128 devices in a mesh: seq: 32 (over y, x, core), batch: 4 (over z).
Axes of the slice: x: 4, y: 4, z: 4, core: 2. Of those that a mesh axis runs over, the one named last changes fastest.
Arguments:
- tokens: bfloat16 [4, 16384, 768], P('batch', 'seq'), may hold values from -6 to 6
- lengths: int32 [4], P('batch'), may hold values from 8192 to 16384, as said below
- w_query: bfloat16 [768, 768], replicated, may hold values from -0.21875 to 0.21875
- b_query: float32 [768], replicated, may hold values from -3 to 3
- w_key: bfloat16 [768, 768], replicated, may hold values from -0.21875 to 0.21875
- b_key: float32 [768], replicated, may hold values from -3 to 3
- w_value: bfloat16 [768, 768], replicated, may hold values from -0.21875 to 0.21875
- b_value: float32 [768], replicated, may hold values from -0.3125 to 0.3125
- w_out: bfloat16 [768, 768], replicated, may hold values from -3 to 3
- b_out: float32 [768], replicated, may hold values from -1.75 to 1.75
- gain_one: float32 [768], replicated, may hold values from 0.1 to 1.9
- shift_one: float32 [768], replicated, may hold values from -1.75 to 1.75
- w_up: bfloat16 [768, 3072], replicated, may hold values from -0.21875 to 0.21875
- b_up: float32 [3072], replicated, may hold values from -1.75 to 1.75
- w_down: bfloat16 [3072, 768], replicated, may hold values from -0.109375 to 0.109375
- b_down: float32 [768], replicated, may hold values from -1.75 to 1.75
- gain_two: float32 [768], replicated, may hold values from 0.1 to 1.9
- shift_two: float32 [768], replicated, may hold values from -1.75 to 1.75
- cotangent: bfloat16 [4, 16384, 768], P('batch', 'seq'), may hold values from -6 to 6
Outputs:
- block_out: bfloat16 [4, 16384, 768], P('batch', 'seq')
- grad_tokens: float32 [4, 16384, 768], P('batch', 'seq')
- grad_w_query: float32 [768, 768], P('seq')
- grad_b_query: float32 [768], P('seq')
- grad_w_key: float32 [768, 768], P('seq')
- grad_b_key: float32 [768], P('seq')
- grad_w_value: float32 [768, 768], P('seq')
- grad_b_value: float32 [768], P('seq')
- grad_w_out: float32 [768, 768], P('seq')
- grad_b_out: float32 [768], P('seq')
- grad_gain_one: float32 [768], P('seq')
- grad_shift_one: float32 [768], P('seq')
- grad_w_up: float32 [768, 3072], P('seq')
- grad_b_up: float32 [3072], P('seq')
- grad_w_down: float32 [3072, 768], P('seq')
- grad_b_down: float32 [768], P('seq')
- grad_gain_two: float32 [768], P('seq')
- grad_shift_two: float32 [768], P('seq')
The draws below stay inside these ranges and needn't reach their ends.
Inputs may be any that keep to these rules, and one draw needn't show every extreme that they name: `lengths`: in every draw one sequence has all 16384 positions real and another has exactly 8192.
All inputs are finite; a program needn't handle non-finite values.
Results may differ from the reference program's by a relative error of at most 0.012.
Values sent between devices are 32-bit elements; how exact they have to be, the bound alone decides.
A program may use at most 192 MiB of HBM per device.

```python
import jax
import jax.numpy as jnp
from jax import lax

D = 768
HEADS = 12
HEAD_DIM = 64
FF = 3072
SEQ_LEN = 16384
SPAN = 512
BATCH = 4


def draw_lengths(key, part):
    key = jax.random.fold_in(key, 7)
    first, second = jax.random.split(key)
    lowest = SEQ_LEN // 2
    drawn_len = jax.random.randint(first, (BATCH,), lowest, SEQ_LEN + 1, dtype=jnp.int32)
    chosen = jax.random.randint(second, (), 0, BATCH, dtype=jnp.int32)
    slot_ids = jnp.arange(BATCH, dtype=jnp.int32)
    drawn_len = jnp.where(slot_ids == chosen, SEQ_LEN, drawn_len)
    drawn_len = jnp.where(slot_ids == (chosen + 1) % BATCH, lowest, drawn_len)
    return drawn_len.astype(jnp.int32)


def block_scale(rng, dims, shards, least, largest):
    level, own = 1.0, jax.random.fold_in(rng, 6)
    for dim, parts in shards:
        steps = jnp.exp(jax.random.uniform(jax.random.fold_in(own, dim), (parts,), jnp.float32, least / len(shards), largest / len(shards)))
        level = level * jnp.repeat(steps, dims[dim] // parts).reshape([-1 if axis == dim else 1 for axis in range(len(dims))])
    return level


def normal_values(rng, dims, scale, limit, cuts=(), held_as=jnp.bfloat16):
    drawn = scale * jax.random.normal(rng, dims, jnp.float32)
    if cuts:
        drawn = drawn * block_scale(rng, dims, cuts, -0.22, 0.18)
    return jnp.clip(drawn, -limit, limit).astype(held_as)


def setup_inputs(seed: int = 0) -> dict:
    streams_of = jax.random.split(jax.random.key(seed), 20)
    return {
        "tokens": normal_values(streams_of[0], (BATCH, SEQ_LEN, D), 1.0, 6.0, ((0, 4), (1, 32))),
        "lengths": draw_lengths(jax.random.fold_in(streams_of[19], 71), 0),
        "w_query": normal_values(streams_of[2], (D, D), D ** -0.5, 0.21875),
        "b_query": normal_values(streams_of[3], (D,), 0.5, 3.0, (), jnp.float32),
        "w_key": normal_values(streams_of[4], (D, D), D ** -0.5, 0.21875),
        "b_key": normal_values(streams_of[5], (D,), 0.5, 3.0, (), jnp.float32),
        "w_value": normal_values(streams_of[6], (D, D), D ** -0.5, 0.21875),
        "b_value": normal_values(streams_of[7], (D,), 0.05, 0.3125, (), jnp.float32),
        "w_out": normal_values(streams_of[8], (D, D), (max(4, 16 * D // SEQ_LEN)) ** -0.5, 3.0),
        "b_out": normal_values(streams_of[9], (D,), 0.3, 1.75, (), jnp.float32),
        "gain_one": jnp.clip(1.0 + 0.18 * jax.random.normal(streams_of[10], (D,), jnp.float32), 0.1, 1.9),
        "shift_one": normal_values(streams_of[11], (D,), 0.3, 1.75, (), jnp.float32),
        "w_up": normal_values(streams_of[12], (D, FF), D ** -0.5, 0.21875),
        "b_up": normal_values(streams_of[13], (FF,), 0.3, 1.75, (), jnp.float32),
        "w_down": normal_values(streams_of[14], (FF, D), FF ** -0.5, 0.109375),
        "b_down": normal_values(streams_of[15], (D,), 0.3, 1.75, (), jnp.float32),
        "gain_two": jnp.clip(1.0 + 0.18 * jax.random.normal(streams_of[16], (D,), jnp.float32), 0.1, 1.9),
        "shift_two": normal_values(streams_of[17], (D,), 0.3, 1.75, (), jnp.float32),
        "cotangent": normal_values(streams_of[18], (BATCH, SEQ_LEN, D), 1.0, 6.0, ((0, 4), (1, 32))),
    }


HALF_PI = 1.5707963267948966
EPSILON = 1e-05
HIGHEST = lax.Precision.HIGHEST

@jax.custom_vjp
def low(v):
    return lax.optimization_barrier(v.astype(jnp.bfloat16)).astype(jnp.float32)

@jax.custom_vjp
def low_back(v):
    return v

def low_keep(v):
    return (low(v), None)

def low_pass(kept, grad):
    return (grad,)

def back_keep(v):
    return (v, None)

def back_low(kept, grad):
    return (low(grad),)
low.defvjp(low_keep, low_pass)
low_back.defvjp(back_keep, back_low)

def project(left_op, right_op):
    return jnp.dot(left_op, right_op, precision=HIGHEST, preferred_element_type=jnp.float32)

def norm_rows(hidden, scale_vec, shift_vec):
    average = lax.optimization_barrier(jnp.mean(hidden, axis=-1, keepdims=True))
    centred = hidden - average
    spread = lax.optimization_barrier(jnp.mean(centred * centred, axis=-1, keepdims=True))
    return centred * lax.rsqrt(spread + EPSILON) * scale_vec + shift_vec

def attend_block(carried, pieces):
    state_cos, state_sin, total_cos, total_sin = carried
    query_cos, query_sin, key_cos, key_sin, values = pieces
    block_rows = query_cos.shape[0]
    counter = jnp.arange(block_rows, dtype=jnp.int32)
    causal = counter[:, None] >= counter[None, :]
    scores = jnp.einsum('thd,jhd->htj', query_cos, key_cos, precision=HIGHEST)
    scores = scores + jnp.einsum('thd,jhd->htj', query_sin, key_sin, precision=HIGHEST)
    scores = jnp.where(causal[None], scores, 0.0)
    numerator = jnp.einsum('htj,jhe->the', scores, values, precision=HIGHEST)
    numerator = numerator + jnp.einsum('thd,hde->the', query_cos, state_cos, precision=HIGHEST)
    numerator = numerator + jnp.einsum('thd,hde->the', query_sin, state_sin, precision=HIGHEST)
    denominator = lax.optimization_barrier(jnp.sum(scores, axis=2)).T
    denominator = denominator + jnp.einsum('thd,hd->th', query_cos, total_cos, precision=HIGHEST)
    denominator = denominator + jnp.einsum('thd,hd->th', query_sin, total_sin, precision=HIGHEST)
    ratios = numerator / denominator[:, :, None]
    state_cos = state_cos + jnp.einsum('jhd,jhe->hde', key_cos, values, precision=HIGHEST)
    state_sin = state_sin + jnp.einsum('jhd,jhe->hde', key_sin, values, precision=HIGHEST)
    total_cos = total_cos + lax.optimization_barrier(jnp.sum(key_cos, axis=0))
    total_sin = total_sin + lax.optimization_barrier(jnp.sum(key_sin, axis=0))
    return ((state_cos, state_sin, total_cos, total_sin), ratios)

def layer(inputs, weights, length):
    w_query, b_query, w_key, b_key, w_value, b_value, w_out, b_out, gain_one, shift_one, w_up, b_up, w_down, b_down, gain_two, shift_two = weights
    positions = jnp.arange(SEQ_LEN, dtype=jnp.int32)
    angles = HALF_PI * jnp.minimum(positions + 1, length).astype(jnp.float32) / length.astype(jnp.float32)
    cosine = jnp.cos(angles)[:, None, None]
    sine_part = jnp.sin(angles)[:, None, None]
    valid_key = (positions < length).astype(jnp.float32)[:, None, None]
    queries = low_back(project(inputs, w_query) + b_query).reshape(SEQ_LEN, HEADS, HEAD_DIM)
    keys_pre = low_back(project(inputs, w_key) + b_key).reshape(SEQ_LEN, HEADS, HEAD_DIM)
    values = low(low_back(project(inputs, w_value) + b_value)).reshape(SEQ_LEN, HEADS, HEAD_DIM)
    soft_query = jax.nn.softplus(queries)
    soft_key = jax.nn.softplus(keys_pre)
    query_cos = low(cosine * soft_query)
    query_sin = low(sine_part * soft_query)
    key_cos = low(valid_key * cosine * soft_key)
    key_sin = low(valid_key * sine_part * soft_key)
    blocks = SEQ_LEN // SPAN

    def split_rows(array):
        return array.reshape(blocks, SPAN, HEADS, HEAD_DIM)
    start_states = (jnp.zeros((HEADS, HEAD_DIM, HEAD_DIM), jnp.float32), jnp.zeros((HEADS, HEAD_DIM, HEAD_DIM), jnp.float32), jnp.zeros((HEADS, HEAD_DIM), jnp.float32), jnp.zeros((HEADS, HEAD_DIM), jnp.float32))
    unused, ratios = lax.scan(jax.checkpoint(attend_block), start_states, (split_rows(query_cos), split_rows(query_sin), split_rows(key_cos), split_rows(key_sin), split_rows(values)))
    mixed = low(ratios.reshape(SEQ_LEN, D))
    projected = low_back(project(mixed, w_out) + b_out)
    hidden_one = inputs + projected
    normed = low(norm_rows(hidden_one, gain_one, shift_one))
    pre_act = low_back(project(normed, w_up) + b_up)
    active = low(jax.nn.gelu(pre_act, approximate=False))
    ffn_out = low_back(project(active, w_down) + b_down)
    hidden_two = normed + ffn_out
    return norm_rows(hidden_two, gain_two, shift_two)

def reference(tokens, lengths, w_query, b_query, w_key, b_key, w_value, b_value, w_out, b_out, gain_one, shift_one, w_up, b_up, w_down, b_down, gain_two, shift_two, cotangent):
    params = tuple((member.astype(jnp.float32) for member in (w_query, b_query, w_key, b_key, w_value, b_value, w_out, b_out, gain_one, shift_one, w_up, b_up, w_down, b_down, gain_two, shift_two)))

    def one_sequence(summed, entry):
        sequence, seq_length, grad_seq = entry

        def forward(inputs, *weights):
            return layer(inputs, weights, seq_length)
        output, pullback = jax.vjp(forward, sequence.astype(jnp.float32), *params)
        gradients = pullback(grad_seq.astype(jnp.float32))
        summed = tuple((running + fresh for running, fresh in zip(summed, gradients[1:])))
        return (summed, (output.astype(jnp.bfloat16), gradients[0]))
    start_sums = tuple((jnp.zeros_like(member) for member in params))
    summed, outputs = lax.scan(one_sequence, start_sums, (tokens, lengths, cotangent))
    block_out, grad_tokens = outputs
    return (block_out, grad_tokens, summed[0], summed[1], summed[2], summed[3], summed[4], summed[5], summed[6], summed[7], summed[8], summed[9], summed[10], summed[11], summed[12], summed[13], summed[14], summed[15])
```

```python
import jax
import jax.numpy as jnp
from jax import lax
from jax.sharding import Mesh
from jax.sharding import PartitionSpec as P
from jax.experimental import pallas as pl
from jax.experimental.pallas import tpu as pltpu

HEAD_DIM = 64
SEQ = ("seq_0", "seq_1", "seq_2")


HALF_PI = 1.5707963267948966
EPSILON = 1e-05
HIGHEST = lax.Precision.HIGHEST


def neutral_like(value, identity):
    return jax.tree.map(
        lambda part, zero: jnp.zeros_like(part) + jnp.asarray(zero, part.dtype), value, identity
    )


def all_in_one(value, axis):
    leaves = jax.tree.leaves(value)
    turns = sorted(range(len(leaves)), key=lambda k: -leaves[k].size)
    width = (1, *leaves[turns[0]].shape)[-1]
    lines = [
        jnp.pad(leaves[k].reshape(-1), (0, -leaves[k].size % width)).reshape(-1, width)
        for k in turns
    ]
    both, at, found = (lax.all_gather(jnp.concatenate(lines), axis), 0, {})
    for k, line in zip(turns, lines):
        section = both[:, at : at + len(line)].reshape(len(both), -1)
        found[k] = section[:, : leaves[k].size].reshape(-1, *leaves[k].shape)
        at += len(line)
    numbers = iter(range(len(leaves)))
    return jax.tree.map(lambda _: found[next(numbers)], value)


def carried_in(value, axes, combine, identity, reverse):
    before = start = neutral_like(value, identity)
    subtotal = value
    for axis in reversed(axes):
        devices, mine = (lax.axis_size(axis), lax.axis_index(axis))
        pieces = all_in_one(subtotal, axis)
        inside, subtotal = (start, start)
        for k in reversed(range(devices)) if reverse else range(devices):
            passed = k > mine if reverse else k < mine
            subtotal = combine(subtotal, jax.tree.map(lambda part: part[k], pieces))
            inside = jax.tree.map(lambda new, old: jnp.where(passed, new, old), subtotal, inside)
        before = combine(inside, before)
    return before


def side_by_side(arrays, axis, dim, along):
    columns = [a.reshape(*a.shape[:along], -1) for a in arrays]
    both = jnp.concatenate(columns, axis=along)
    filled, at, finished = (lax.psum_scatter(both, axis, scatter_dimension=dim, tiled=True), 0, [])
    for a, column in zip(arrays, columns):
        section = filled[..., at : at + column.shape[along]]
        finished.append(section.reshape(*section.shape[:along], *a.shape[along:]))
        at += column.shape[along]
    return tuple(finished)


def sent_to_all(value, axis):
    copies = jnp.broadcast_to(value, (lax.axis_size(axis), *value.shape))
    return lax.all_to_all(copies, axis, split_axis=0, concat_axis=0, tiled=True)


def over_copies(value, axis):
    return sent_to_all(value, axis).sum(axis=0)


def in_one(arrays, axis):
    ends = [0]
    for a in arrays:
        ends.append(ends[-1] + a.size)
    subtotal = over_copies(jnp.concatenate([a.ravel() for a in arrays]), axis)
    return tuple((subtotal[b:e].reshape(a.shape) for a, b, e in zip(arrays, ends, ends[1:])))


def matmul(left_op, right_op):
    return jnp.dot(left_op, right_op, preferred_element_type=jnp.float32)


def transposed(left_op, right_op):
    return lax.dot_general(
        left_op, right_op, (((0,), (0,)), ((), ())), preferred_element_type=jnp.float32
    )


def backward_mul(left_op, right_op):
    return lax.dot_general(
        left_op, right_op, (((1,), (1,)), ((), ())), preferred_element_type=jnp.float32
    )


def mixed_prod(form, first, second):
    return jnp.einsum(form, first, second, precision=HIGHEST, preferred_element_type=jnp.float32)


def norm_rows(hidden, scale_vec, shift_vec):
    average = jnp.mean(hidden, axis=-1, keepdims=True)
    centred = hidden - average
    spread = jnp.mean(centred * centred, axis=-1, keepdims=True)
    return centred * lax.rsqrt(spread + EPSILON) * scale_vec + shift_vec


def gelu_exact(values):
    return jax.nn.gelu(values, approximate=False)


def add_states(earlier_sums, later_sums):
    return tuple((first + second for first, second in zip(earlier_sums, later_sums)))


def column_sum(array):
    return jnp.sum(array.astype(jnp.float32), axis=0)


MESH = pl.DeviceIdType.MESH
AX = ("seq_0", "seq_1", "batch")
CORE = "seq_2"
ORDERS = ((1, 0, 2), (0, 2, 1), (2, 1, 0))
DIRECT = (1, 3, 2)
SUBS = 9
COLS = 256


def rot(k, d):
    return lax.rem(k + d, 4)


def cell(ref, order, picks):
    at = [slice(None)] * 3
    for axis, pick in zip(order, picks):
        at[axis] = pick
    return ref.at[tuple(at)]


def halved(ref, order, pick, half):
    at = [slice(None)] * 3
    at[order[0]] = pick
    at[1 if order[0] == 0 else 0] = half
    return ref.at[tuple(at)]


def add_blocks(dst, srcs, lead):
    total = 1
    for n in lead:
        total *= n

    def step(k, carry):
        at, rest = [], k
        for n in reversed(lead):
            at.append(lax.rem(rest, n))
            rest = rest // n
        at = tuple(reversed(at))
        value = dst[at]
        for src in srcs:
            value = value + src[at]
        dst[at] = value
        return carry

    lax.fori_loop(0, total, step, 0)


def reduce_kernel(
    down, up, w_o, w_q, w_k, w_v, vec,
    out_down, out_up, out_o, out_q, out_k, out_v, out_vec,
    own, core_in, first, second, third, done, vecs,
    load_sem, core_send, core_recv, send, recv, vsend, vrecv,
):
    me = tuple(lax.axis_index(a) for a in AX)
    core = lax.axis_index(CORE)
    other = 1 - core
    barrier = pltpu.get_barrier_semaphore()
    pl.semaphore_signal(barrier, inc=1, device_id={CORE: other}, device_id_type=MESH)
    for axis in range(3):
        for d in DIRECT:
            pl.semaphore_signal(barrier, inc=1, device_id={AX[axis]: rot(me[axis], d)}, device_id_type=MESH)
    pl.semaphore_wait(barrier, 10)

    def source(s, b, half):
        columns = pl.ds(COLS * (s % 3), COLS)
        if s < 3:
            return down.at[:, :, half, b, :, columns]
        if s < 6:
            return up.at[:, :, half, :, pl.ds(768 * b + COLS * (s % 3), COLS)]
        return (w_o, w_q, w_k, w_v)[b].at[:, :, half, :, columns]

    loads, swaps, moves = {}, {}, []
    for s in (0, 4, 8, 3, 7, 2, 6, 1, 5):
        for b in range(4):
            swap = pltpu.make_async_remote_copy(
                src_ref=source(s, b, other), dst_ref=core_in.at[s, :, :, b],
                send_sem=core_send.at[s, b], recv_sem=core_recv.at[s, b],
                device_id={CORE: other}, device_id_type=MESH)
            swap.start()
            load = pltpu.make_async_copy(source(s, b, core), own.at[s, :, :, b], load_sem.at[s, b])
            load.start()
            loads[s, b], swaps[s, b] = load, swap

    def remote(src, dst, s, k, axis, d):
        copy = pltpu.make_async_remote_copy(
            src_ref=src, dst_ref=dst, send_sem=send.at[s, k], recv_sem=recv.at[s, k],
            device_id={AX[axis]: rot(me[axis], d)}, device_id_type=MESH)
        copy.start()
        moves.append(copy)
        return copy

    flight = {}

    def begin(s):
        order = ORDERS[s % 3]
        i = me[order[0]]
        mine, inbox = own.at[s], first.at[s]
        for b in range(4):
            loads[s, b].wait()
            swaps[s, b].wait_recv()
        add_blocks(mine, [core_in.at[s]], (4, 4, 4))
        lo, hi = pl.ds(0, 2), pl.ds(2, 2)
        far = rot(i, 2)
        ax = order[0]
        flight[s, "a"] = (
            remote(halved(mine, order, far, lo), inbox.at[0, pl.ds(0, 2)], s, 0, ax, 1),
            remote(halved(mine, order, far, hi), inbox.at[0, pl.ds(2, 2)], s, 1, ax, 3),
        )
        flight[s, "b"] = (
            remote(halved(mine, order, rot(i, 1), hi), inbox.at[1, pl.ds(2, 2)], s, 2, ax, 1),
            remote(halved(mine, order, rot(i, 3), lo), inbox.at[2, pl.ds(0, 2)], s, 3, ax, 3),
        )

    def relay(s):
        order = ORDERS[s % 3]
        i = me[order[0]]
        mine, inbox = own.at[s], first.at[s]
        lo, hi = pl.ds(0, 2), pl.ds(2, 2)
        ax = order[0]
        flight[s, "a"][0].wait_recv()
        part = halved(mine, order, rot(i, 1), lo)
        add_blocks(part, [inbox.at[0, pl.ds(0, 2)]], (2, 4))
        c0 = remote(part, inbox.at[1, pl.ds(0, 2)], s, 4, ax, 1)
        flight[s, "a"][1].wait_recv()
        part = halved(mine, order, rot(i, 3), hi)
        add_blocks(part, [inbox.at[0, pl.ds(2, 2)]], (2, 4))
        c1 = remote(part, inbox.at[2, pl.ds(2, 2)], s, 5, ax, 3)
        flight[s, "b"] += (c0, c1)

    def middle(s):
        order = ORDERS[s % 3]
        mine = own.at[s]
        for copy in flight[s, "b"]:
            copy.wait_recv()
        i = me[order[0]]
        add_blocks(cell(mine, order, (i,)), [first.at[s, 1], first.at[s, 2]], (4, 4))
        ax = order[1]
        flight[s, 2] = [
            remote(cell(mine, order, (i, rot(me[ax], d))), second.at[s, k], s, 6 + k, ax, d)
            for k, d in enumerate(DIRECT)
        ]

    def last(s):
        order = ORDERS[s % 3]
        mine = own.at[s]
        for copy in flight[s, 2]:
            copy.wait_recv()
        at = (me[order[0]], me[order[1]])
        add_blocks(cell(mine, order, at), [second.at[s, k] for k in range(3)], (4,))
        ax = order[2]
        flight[s, 3] = [
            remote(cell(mine, order, (*at, rot(me[ax], d))), third.at[s, k], s, 9 + k, ax, d)
            for k, d in enumerate(DIRECT)
        ]

    def spread(s):
        for copy in flight[s, 3]:
            copy.wait_recv()
        done[s, me[2]] = own[s, me[0], me[1], me[2]] + third[s, 0] + third[s, 1] + third[s, 2]
        flight[s, 4] = [
            remote(done.at[s, me[2]], done.at[s, me[2]], s, 12 + k, 2, d)
            for k, d in enumerate(DIRECT)
        ]

    def finish(s):
        for copy in flight[s, 4]:
            copy.wait_recv()
        c = pl.ds(COLS * (s % 3), COLS)
        for b in range(4):
            if s < 3:
                out_down[24 * b : 24 * b + 24, c] = done[s, b]
            elif s < 6:
                out_up[:, pl.ds(768 * b + COLS * (s % 3), COLS)] = done[s, b]
            else:
                (out_o, out_q, out_k, out_v)[b][:, c] = done[s, b]

    vecs[0] = vec[...]
    vmoves = {}

    def vector_send(stage):
        if stage == 0:
            targets = [{CORE: other}]
        else:
            ax = stage - 1
            targets = [{AX[ax]: rot(me[ax], d)} for d in DIRECT]
        base = (0, 1, 4, 7)[stage]
        vmoves[stage] = []
        for k, target in enumerate(targets):
            copy = pltpu.make_async_remote_copy(
                src_ref=vecs.at[stage], dst_ref=vecs.at[5 + base + k],
                send_sem=vsend.at[base + k], recv_sem=vrecv.at[base + k],
                device_id=target, device_id_type=MESH)
            copy.start()
            vmoves[stage].append(copy)

    def vector_sum(stage):
        base = (0, 1, 4, 7)[stage]
        total = vecs[stage]
        for k, copy in enumerate(vmoves[stage]):
            copy.wait_recv()
            total = total + vecs[5 + base + k]
        vecs[stage + 1] = total

    G = [(0, 4, 8), (3, 7, 2), (6, 1, 5)]

    def run(step, g):
        for s in G[g]:
            step(s)

    vector_send(0)
    run(begin, 0)
    vector_sum(0)
    vector_send(1)
    run(relay, 0)
    run(begin, 1)
    run(middle, 0)
    vector_sum(1)
    vector_send(2)
    run(relay, 1)
    run(begin, 2)
    run(last, 0)
    run(middle, 1)
    run(relay, 2)
    run(spread, 0)
    vector_sum(2)
    vector_send(3)
    run(last, 1)
    run(middle, 2)
    run(finish, 0)
    run(spread, 1)
    run(last, 2)
    vector_sum(3)
    out_vec[...] = vecs[4]
    run(finish, 1)
    run(spread, 2)
    run(finish, 2)
    for copy in [*moves, *swaps.values(), *(c for cs in vmoves.values() for c in cs)]:
        copy.wait_send()


def reduce_grads(down, up, w_o, w_q, w_k, w_v, vec):
    f32 = jnp.float32
    shapes = [(96, 768), (24, 3072), (24, 768), (24, 768), (24, 768), (24, 768), (16, 768)]
    any_spec = pl.BlockSpec(memory_space=pl.ANY)
    vmem = pl.BlockSpec(memory_space=pltpu.VMEM)
    return pl.pallas_call(
        reduce_kernel,
        out_shape=[jax.ShapeDtypeStruct(s, f32) for s in shapes],
        in_specs=[any_spec] * 6 + [vmem],
        out_specs=[vmem] * 7,
        scratch_shapes=[
            pltpu.VMEM((SUBS, 4, 4, 4, 24, COLS), f32),
            pltpu.VMEM((SUBS, 4, 4, 4, 24, COLS), f32),
            pltpu.VMEM((SUBS, 3, 4, 4, 24, COLS), f32),
            pltpu.VMEM((SUBS, 3, 4, 24, COLS), f32),
            pltpu.VMEM((SUBS, 3, 24, COLS), f32),
            pltpu.VMEM((SUBS, 4, 24, COLS), f32),
            pltpu.VMEM((15, 16, 768), f32),
            pltpu.SemaphoreType.DMA((SUBS, 4)),
            pltpu.SemaphoreType.DMA((SUBS, 4)),
            pltpu.SemaphoreType.DMA((SUBS, 4)),
            pltpu.SemaphoreType.DMA((SUBS, 15)),
            pltpu.SemaphoreType.DMA((SUBS, 15)),
            pltpu.SemaphoreType.DMA((10,)),
            pltpu.SemaphoreType.DMA((10,)),
        ],
        compiler_params=pltpu.CompilerParams(
            collective_id=0, has_side_effects=True, vmem_limit_bytes=60 * 2**20
        ),
    )(
        down.reshape(4, 4, 2, 4, 24, 768),
        up.reshape(4, 4, 2, 24, 3072),
        *(w.reshape(4, 4, 2, 24, 768) for w in (w_o, w_q, w_k, w_v)),
        vec,
    )


def on_device(
    tokens,
    lengths,
    w_query,
    b_query,
    w_key,
    b_key,
    w_value,
    b_value,
    w_out,
    b_out,
    gain_one,
    shift_one,
    w_up,
    b_up,
    w_down,
    b_down,
    gain_two,
    shift_two,
    cotangent,
):
    inputs = tokens[0]
    row_count = inputs.shape[0]
    model_width = inputs.shape[1]
    head_count = model_width // HEAD_DIM
    seq_length = lengths[0]
    positions = lax.axis_index(SEQ) * row_count + jnp.arange(row_count, dtype=jnp.int32)
    angles = (
        HALF_PI
        * jnp.minimum(positions + 1, seq_length).astype(jnp.float32)
        / seq_length.astype(jnp.float32)
    )
    cosine = jnp.cos(angles)[:, None, None]
    sine_part = jnp.sin(angles)[:, None, None]
    valid_key = (positions < seq_length).astype(jnp.float32)[:, None, None]
    queries = (matmul(inputs, w_query) + b_query).reshape(row_count, head_count, HEAD_DIM)
    keys_pre = (matmul(inputs, w_key) + b_key).reshape(row_count, head_count, HEAD_DIM)
    values_low = (
        (matmul(inputs, w_value) + b_value)
        .astype(jnp.bfloat16)
        .reshape(row_count, head_count, HEAD_DIM)
    )
    soft_query = jax.nn.softplus(queries)
    soft_key = jax.nn.softplus(keys_pre)
    query_cos = (cosine * soft_query).astype(jnp.bfloat16)
    query_sin = (sine_part * soft_query).astype(jnp.bfloat16)
    key_cos = (valid_key * cosine * soft_key).astype(jnp.bfloat16)
    key_sin = (valid_key * sine_part * soft_key).astype(jnp.bfloat16)
    local_cos = jnp.einsum("jhd,jhe->hde", key_cos, values_low, preferred_element_type=jnp.float32)
    local_sin = jnp.einsum("jhd,jhe->hde", key_sin, values_low, preferred_element_type=jnp.float32)
    local_zcos = column_sum(key_cos)
    local_zsin = column_sum(key_sin)
    zero_states = (
        jnp.zeros_like(local_cos),
        jnp.zeros_like(local_sin),
        jnp.zeros_like(local_zcos),
        jnp.zeros_like(local_zsin),
    )
    prev_cos, prev_sin, prev_zcos, prev_zsin = carried_in(
        (local_cos, local_sin, local_zcos, local_zsin), SEQ, add_states, zero_states, False
    )
    counter = jnp.arange(row_count, dtype=jnp.int32)
    causal = counter[:, None] >= counter[None, :]
    scores = jnp.einsum("thd,jhd->htj", query_cos, key_cos, preferred_element_type=jnp.float32)
    scores = scores + jnp.einsum(
        "thd,jhd->htj", query_sin, key_sin, preferred_element_type=jnp.float32
    )
    scores = jnp.where(causal[None], scores, 0.0)
    numerator = mixed_prod("htj,jhe->the", scores, values_low)
    numerator = numerator + mixed_prod("thd,hde->the", query_cos, prev_cos)
    numerator = numerator + mixed_prod("thd,hde->the", query_sin, prev_sin)
    denominator = jnp.sum(scores, axis=2).T
    denominator = denominator + mixed_prod("thd,hd->th", query_cos, prev_zcos)
    denominator = denominator + mixed_prod("thd,hd->th", query_sin, prev_zsin)
    ratios = numerator / denominator[:, :, None]
    mixed = ratios.reshape(row_count, model_width).astype(jnp.bfloat16)
    projected = matmul(mixed, w_out) + b_out
    hidden_one = inputs.astype(jnp.float32) + projected
    normed, pull_one = jax.vjp(norm_rows, hidden_one, gain_one, shift_one)
    normed_low = normed.astype(jnp.bfloat16)
    pre_act = matmul(normed_low, w_up) + b_up
    active, pull_gelu = jax.vjp(gelu_exact, pre_act)
    active_low = active.astype(jnp.bfloat16)
    ffn_out = matmul(active_low, w_down) + b_down
    hidden_two = normed_low.astype(jnp.float32) + ffn_out
    block_out, pull_two = jax.vjp(norm_rows, hidden_two, gain_two, shift_two)
    grad_two, grad_gain_two, grad_shift_two = pull_two(cotangent[0].astype(jnp.float32))
    grad_ffn = grad_two.astype(jnp.bfloat16)
    grad_w_down = transposed(active_low, grad_ffn)
    grad_b_down = column_sum(grad_ffn)
    (grad_pre_wide,) = pull_gelu(backward_mul(grad_ffn, w_down))
    grad_pre = grad_pre_wide.astype(jnp.bfloat16)
    grad_w_up = transposed(normed_low, grad_pre)
    grad_b_up = column_sum(grad_pre)
    grad_normed = grad_two + backward_mul(grad_pre, w_up)
    grad_one, grad_gain_one, grad_shift_one = pull_one(grad_normed)
    grad_proj = grad_one.astype(jnp.bfloat16)
    grad_w_out = transposed(mixed, grad_proj)
    grad_b_out = column_sum(grad_proj)
    grad_ratio = backward_mul(grad_proj, w_out).reshape(row_count, head_count, HEAD_DIM)
    grad_num = grad_ratio / denominator[:, :, None]
    grad_den = -jnp.sum(grad_ratio * ratios, axis=2) / denominator
    back_cos = mixed_prod("thd,the->hde", query_cos, grad_num)
    back_sin = mixed_prod("thd,the->hde", query_sin, grad_num)
    back_zcos = mixed_prod("thd,th->hd", query_cos, grad_den)
    back_zsin = mixed_prod("thd,th->hd", query_sin, grad_den)
    next_cos, next_sin, next_zcos, next_zsin = carried_in(
        (back_cos, back_sin, back_zcos, back_zsin), SEQ, add_states, zero_states, True
    )
    grad_weight = mixed_prod("the,jhe->htj", grad_num, values_low) + grad_den.T[:, :, None]
    grad_weight = jnp.where(causal[None], grad_weight, 0.0)
    grad_qc = mixed_prod("htj,jhd->thd", grad_weight, key_cos)
    grad_qc = (
        grad_qc
        + mixed_prod("the,hde->thd", grad_num, prev_cos)
        + grad_den[:, :, None] * prev_zcos[None]
    )
    grad_qs = mixed_prod("htj,jhd->thd", grad_weight, key_sin)
    grad_qs = (
        grad_qs
        + mixed_prod("the,hde->thd", grad_num, prev_sin)
        + grad_den[:, :, None] * prev_zsin[None]
    )
    grad_kc = mixed_prod("htj,thd->jhd", grad_weight, query_cos)
    grad_kc = grad_kc + mixed_prod("hde,jhe->jhd", next_cos, values_low) + next_zcos[None]
    grad_ks = mixed_prod("htj,thd->jhd", grad_weight, query_sin)
    grad_ks = grad_ks + mixed_prod("hde,jhe->jhd", next_sin, values_low) + next_zsin[None]
    grad_val = mixed_prod("htj,the->jhe", scores, grad_num)
    grad_val = grad_val + mixed_prod("hde,jhd->jhe", next_cos, key_cos)
    grad_val = grad_val + mixed_prod("hde,jhd->jhe", next_sin, key_sin)
    grad_query = (
        ((cosine * grad_qc + sine_part * grad_qs) * jax.nn.sigmoid(queries))
        .reshape(row_count, model_width)
        .astype(jnp.bfloat16)
    )
    grad_key = (
        (valid_key * (cosine * grad_kc + sine_part * grad_ks) * jax.nn.sigmoid(keys_pre))
        .reshape(row_count, model_width)
        .astype(jnp.bfloat16)
    )
    grad_value = grad_val.reshape(row_count, model_width).astype(jnp.bfloat16)
    grad_w_query = transposed(inputs, grad_query)
    grad_b_query = column_sum(grad_query)
    grad_w_key = transposed(inputs, grad_key)
    grad_b_key = column_sum(grad_key)
    grad_w_value = transposed(inputs, grad_value)
    grad_b_value = column_sum(grad_value)
    grad_tokens = (
        grad_one
        + backward_mul(grad_query, w_query)
        + backward_mul(grad_key, w_key)
        + backward_mul(grad_value, w_value)
    )
    vec = jnp.concatenate(
        [
            v.reshape(-1, model_width)
            for v in (
                grad_b_query,
                grad_b_key,
                grad_b_value,
                grad_b_out,
                grad_gain_one,
                grad_shift_one,
                grad_b_down,
                grad_gain_two,
                grad_shift_two,
                grad_b_up,
                jnp.zeros((3 * model_width,), jnp.float32),
            )
        ]
    )
    sum_down, sum_up, sum_out, sum_query, sum_key, sum_value, sum_vec = reduce_grads(
        grad_w_down, grad_w_up, grad_w_out, grad_w_query, grad_w_key, grad_w_value, vec
    )
    at = lax.axis_index(SEQ)
    small = lax.dynamic_slice(sum_vec, (0, 24 * at), (9, 24))
    wide = lax.dynamic_slice(sum_vec[9:13].reshape(-1), (96 * at,), (96,))
    totals = (
        sum_query, small[0], sum_key, small[1], sum_value, small[2], sum_out, small[3],
        small[4], small[5], sum_up, wide, sum_down, small[6], small[7], small[8],
    )
    return (block_out.astype(jnp.bfloat16)[None], grad_tokens[None]) + tuple(totals)


def solution(mesh):
    torus = Mesh(
        mesh.devices.reshape(4, 4, 2, mesh.shape["batch"]), ("seq_0", "seq_1", "seq_2", "batch")
    )
    return jax.shard_map(
        on_device,
        mesh=torus,
        in_specs=(
            P("batch", SEQ, None),
            P("batch"),
            P(),
            P(),
            P(),
            P(),
            P(),
            P(),
            P(),
            P(),
            P(),
            P(),
            P(),
            P(),
            P(),
            P(),
            P(),
            P(),
            P("batch", SEQ, None),
        ),
        out_specs=(
            P("batch", SEQ, None),
            P("batch", SEQ, None),
            P(SEQ, None),
            P(SEQ),
            P(SEQ, None),
            P(SEQ),
            P(SEQ, None),
            P(SEQ),
            P(SEQ, None),
            P(SEQ),
            P(SEQ),
            P(SEQ),
            P(SEQ, None),
            P(SEQ),
            P(SEQ, None),
            P(SEQ),
            P(SEQ),
            P(SEQ),
        ),
        check_vma=False,
    )
```

```python
import jax
import jax.numpy as jnp
from jax import lax
from jax.experimental import pallas as pl
from jax.experimental.pallas import tpu as pltpu
from jax.sharding import Mesh
from jax.sharding import PartitionSpec as P

SEQ = ("seq_0", "seq_1", "seq_2")
AX = ("seq_0", "seq_1", "batch")
CORE = "seq_2"
MESH = pl.DeviceIdType.MESH
DIRECT = (1, 3, 2)
F32 = jnp.float32
BF16 = jnp.bfloat16
HALF_PI = 1.5707963267948966
HALF_PI_REST = -4.371139000186241e-08
EPSILON = 1e-05
ROWS = 512
WIDTH = 768
HIDDEN = 3072
HEADS = 12
PAIRS = 6
CHUNK = 256
TILE = 512
VMEM = pltpu.VMEM
LIMIT = 60 * 2**20


def nn(a, b):
    return jnp.dot(a, b, preferred_element_type=F32)


def nt(a, b):
    return lax.dot_general(a, b, (((1,), (1,)), ((), ())), preferred_element_type=F32)


def tn(a, b):
    return lax.dot_general(a, b, (((0,), (0,)), ((), ())), preferred_element_type=F32)


def at(k, size):
    return pl.ds(pl.multiple_of(k * size, size), size)


def rot(k, d):
    return lax.rem(k + d, 4)


def left_lanes(rows):
    return lax.broadcasted_iota(jnp.int32, (rows, 128), 1) < 64


def swap_halves(value):
    return pltpu.roll(value, 64, 1)


def doubled(value):
    return jnp.concatenate([value, value], axis=1)


def halves(value):
    high = value.astype(BF16)
    return high, (value - high.astype(F32)).astype(BF16)


SIN = (1.0, -0.1666666716337204, 0.008333330973982811, -0.00019840864115394652, 2.7525297809916083e-06, -2.3888299338636898e-08)


def sine(x):
    square = x * x
    value = SIN[5]
    for c in SIN[4::-1]:
        value = value * square + c
    return value * x


ERFCX = (
    0.22567586600780487, 0.2256695181131363, 0.2078438699245453, 0.1685338169336319, 0.14146119356155396,
    -0.005668365862220526, 0.16915558278560638, -0.18294405937194824, 0.05027270317077637,
)


def normal_parts(p):
    bell = jnp.exp(-0.5 * p * p)
    t = 1.0 / (1.0 + (0.4 * 0.7071067811865476) * jnp.abs(p))
    value = 0.5 * ERFCX[8]
    for c in ERFCX[7::-1]:
        value = value * t + 0.5 * c
    tail = value * t * bell
    return jnp.where(p >= 0, 1.0 - tail, tail), 0.3989422804014327 * bell


def trig_block(first, rows, length):
    position = first + lax.broadcasted_iota(jnp.int32, (rows, 128), 0)
    size = lax.broadcast_in_dim(length, (rows, 128), ()).astype(F32)
    angle = HALF_PI * jnp.minimum(position + 1, length).astype(F32) / size
    both = sine(jnp.where(left_lanes(rows), (HALF_PI - angle) + HALF_PI_REST, angle))
    return both, (position < length).astype(F32)


def project_kernel(start_ref, len_ref, x_ref, wq, bq, wk, bk, wv, bv,
                   q_ref, k_ref, v_ref, gate_q, gate_k, trig_ref, valid_ref, state_ref, early_ref):
    length = len_ref[0]
    start = start_ref[0]

    def angles(r, carry):
        both, valid = trig_block(start + 128 * r, 128, length)
        trig_ref[at(r, 128)] = both
        valid_ref[at(r, 128)] = both * valid
        return carry

    lax.fori_loop(0, ROWS // 128, angles, 0)
    left = left_lanes(ROWS)

    def columns(n, carry):
        cols = at(n, 256)
        x = x_ref[...]
        for w, b, out, gate, table in ((wq, bq, q_ref, gate_q, trig_ref), (wk, bk, k_ref, gate_k, valid_ref)):
            u = nn(x, w[:, cols]) + b[:, cols]
            small = jnp.exp(-jnp.abs(u))
            soft = jnp.maximum(u, 0.0) + jnp.log1p(small)
            gate[:, cols] = (jnp.where(u >= 0, 1.0, small) / (1.0 + small)).astype(BF16)
            trig = table[...]
            for j in range(2):
                part = soft[:, 128 * j : 128 * j + 128]
                other = swap_halves(part)
                out[4 * n + 2 * j] = (jnp.where(left, part, other) * trig).astype(BF16)
                out[4 * n + 2 * j + 1] = (jnp.where(left, other, part) * trig).astype(BF16)
        u = (nn(x, wv[:, cols]) + bv[:, cols]).astype(BF16).astype(F32)
        for j in range(2):
            part = u[:, 128 * j : 128 * j + 128]
            v_ref[4 * n + 2 * j] = jnp.where(left, part, 1.0).astype(BF16)
            v_ref[4 * n + 2 * j + 1] = jnp.where(left, swap_halves(part), 1.0).astype(BF16)
        return carry

    lax.fori_loop(0, WIDTH // 256, columns, 0)

    def states(p, carry):
        for j in range(2):
            h = 2 * p + j
            early = tn(v_ref[h, 0:CHUNK], k_ref[h, 0:CHUNK])
            early_ref[h] = early
            both = early + tn(v_ref[h, CHUNK:ROWS], k_ref[h, CHUNK:ROWS])
            state_ref[p, 64 * j : 64 * j + 64] = both[0:64]
            state_ref[p, 128 + j : 129 + j] = both[64:65]
        state_ref[p, 130:136] = jnp.zeros((6, 128), F32)
        return carry

    lax.fori_loop(0, PAIRS, states, 0)


def exchange_steps(pay, out, core_in, chip, give, head, tail, total, msgs, xa, ya, yb, xb, send, recv, reverse):
    my, mx = lax.axis_index("seq_0"), lax.axis_index("seq_1")
    core = lax.axis_index(CORE)
    other = 1 - core
    moves = []

    def remote(src, dst, k, target):
        copy = pltpu.make_async_remote_copy(
            src_ref=src, dst_ref=dst, send_sem=send.at[k], recv_sem=recv.at[k],
            device_id=target, device_id_type=MESH)
        copy.start()
        moves.append(copy)
        return copy

    def counts(theirs, mine):
        return theirs > mine if reverse else theirs < mine

    def chosen(flag, value):
        return jnp.where(flag, value, jnp.zeros_like(value))

    def first():
        return remote(pay.at[pl.ds(3 * other, 3)], core_in, 0, {CORE: other})

    def second(copy):
        copy.wait_recv()
        for p in range(3):
            chip[p] = pay[3 * core + p] + core_in[p]
        a = [remote(chip.at[:, pl.ds(0, 72)], xa.at[k], 1 + k, {"seq_1": rot(mx, d)}) for k, d in enumerate(DIRECT)]
        b = [remote(chip.at[:, pl.ds(72, 64)], yb.at[k], 4 + k, {"seq_0": rot(my, d)}) for k, d in enumerate(DIRECT)]
        return a, b

    def third(copies):
        a, b = copies
        for copy in a:
            copy.wait_recv()
        for p in range(3):
            some = jnp.zeros((72, 128), F32)
            every = chip[p, 0:72]
            for k, d in enumerate(DIRECT):
                piece = xa[k, p]
                some = some + chosen(counts(rot(mx, 4 - d), mx), piece)
                every = every + piece
            head[p] = some
            total[p] = every
        a = [remote(total, ya.at[k], 7 + k, {"seq_0": rot(my, d)}) for k, d in enumerate(DIRECT)]
        for copy in b:
            copy.wait_recv()
        for p in range(3):
            some = jnp.zeros((64, 128), F32)
            for k, d in enumerate(DIRECT):
                some = some + chosen(counts(rot(my, 4 - d), my), yb[k, p])
            tail[p] = some
            own = chip[p, 72:136]
            for k, d in enumerate(DIRECT):
                msgs[k, p] = some + chosen(counts(mx, rot(mx, d)), own)
        b = [remote(msgs.at[k], xb.at[k], 10 + k, {"seq_1": rot(mx, d)}) for k, d in enumerate(DIRECT)]
        return a, b

    def fourth(copies):
        a, b = copies
        for copy in a:
            copy.wait_recv()
        for copy in b:
            copy.wait_recv()
        mine = core == (0 if reverse else 1)
        for p in range(3):
            low, high = head[p], tail[p]
            for k, d in enumerate(DIRECT):
                low = low + chosen(counts(rot(my, 4 - d), my), ya[k, p])
                high = high + xb[k, p]
            own = 3 * core + p
            out[own, 0:72] = low + chosen(mine, core_in[p, 0:72])
            out[own, 72:136] = high + chosen(mine, core_in[p, 72:136])
            give[p, 0:72] = low + chosen(jnp.logical_not(mine), pay[own, 0:72])
            give[p, 72:136] = high + chosen(jnp.logical_not(mine), pay[own, 72:136])
        return remote(give, out.at[pl.ds(3 * core, 3)], 13, {CORE: other})

    def fifth(copy):
        copy.wait_recv()
        for move in moves:
            move.wait_send()

    return first, second, third, fourth, fifth


EXCHANGE_SCRATCH = [
    VMEM((3, 136, 128), F32),
    VMEM((3, 136, 128), F32),
    VMEM((3, 136, 128), F32),
    VMEM((3, 72, 128), F32),
    VMEM((3, 64, 128), F32),
    VMEM((3, 72, 128), F32),
    VMEM((3, 3, 64, 128), F32),
    VMEM((3, 3, 72, 128), F32),
    VMEM((3, 3, 72, 128), F32),
    VMEM((3, 3, 64, 128), F32),
    VMEM((3, 3, 64, 128), F32),
    pltpu.SemaphoreType.DMA((14,)),
    pltpu.SemaphoreType.DMA((14,)),
]


def greet(axes):
    barrier = pltpu.get_barrier_semaphore()
    core = lax.axis_index(CORE)
    pl.semaphore_signal(barrier, inc=1, device_id={CORE: 1 - core}, device_id_type=MESH)
    for axis in axes:
        mine = lax.axis_index(axis)
        for d in DIRECT:
            pl.semaphore_signal(barrier, inc=1, device_id={axis: rot(mine, d)}, device_id_type=MESH)
    pl.semaphore_wait(barrier, 1 + 3 * len(axes))


def exchange_kernel(reverse, pay, out, *scratch):
    greet(("seq_0", "seq_1"))
    first, second, third, fourth, fifth = exchange_steps(pay, out, *scratch, reverse)
    fifth(fourth(third(second(first()))))


def exchange(pay, reverse):
    def kernel(*refs):
        exchange_kernel(reverse, *refs)

    vmem = pl.BlockSpec(memory_space=VMEM)
    return pl.pallas_call(
        kernel,
        out_shape=jax.ShapeDtypeStruct((PAIRS, 136, 128), F32),
        in_specs=[vmem],
        out_specs=vmem,
        scratch_shapes=EXCHANGE_SCRATCH,
        compiler_params=pltpu.CompilerParams(
            collective_id=1 if reverse else 2, has_side_effects=True, vmem_limit_bytes=LIMIT),
    )(pay)


def causal_masks():
    row = lax.broadcasted_iota(jnp.int32, (CHUNK, CHUNK), 0)
    col = lax.broadcasted_iota(jnp.int32, (CHUNK, CHUNK), 1)
    return row >= col, row <= col


def prefix_state(before, p, j):
    body = before[p, 64 * j : 64 * j + 64]
    return jnp.concatenate([body, jnp.broadcast_to(before[p, 128 + j : 129 + j], (64, 128))], axis=0)


def attend(p, q_ref, k_ref, v_ref, early_ref, before, ratio_ref, inverse_ref, mixed_ref):
    causal, _ = causal_masks()
    left = left_lanes(CHUNK)
    cols = at(p, 128)
    for c in range(2):
        rows = slice(CHUNK * c, CHUNK * c + CHUNK)
        sums = []
        for j in range(2):
            h = 2 * p + j
            q, k, v = q_ref[h, rows], k_ref[h, rows], v_ref[h, rows]
            weight = jnp.where(causal, nt(q, k), 0.0).astype(BF16)
            state = prefix_state(before, p, j)
            if c == 1:
                state = state + early_ref[h]
            high, low = halves(state)
            sums.append(nn(weight, v) + nt(doubled(q), jnp.concatenate([high, low], axis=1)))
        even, odd = sums
        top = jnp.where(left, even, swap_halves(odd))
        inverse = 1.0 / jnp.where(left, swap_halves(even), odd)
        ratio = top * inverse
        ratio_ref[rows, cols] = ratio
        inverse_ref[rows, cols] = inverse
        mixed_ref[rows, cols] = ratio.astype(BF16)


def mean_rows(value):
    return jnp.mean(value, axis=-1, keepdims=True)


def standard(hidden):
    centred = hidden - mean_rows(hidden)
    scale = lax.rsqrt(mean_rows(centred * centred) + EPSILON)
    return centred * scale, scale


def norm_back(grad, normal, scale, gain):
    scaled = grad * gain
    return scale * (scaled - mean_rows(scaled) - normal * mean_rows(scaled * normal))


def column(value):
    return jnp.sum(value, axis=0, keepdims=True)


def middle_kernel(x_ref, cot_ref, q_ref, k_ref, v_ref, early_ref, before,
                  wo, bo, gain1, shift1, wup, bup, wdown, bdown, gain2, shift2,
                  block_ref, gone_ref, gn_ref, ratio_ref, after_state, late_ref,
                  gw_down, gw_up, gw_out, vec_ref,
                  inverse_ref, mixed_ref, normal_ref, scale_ref, normed_ref, acc_ref, act_ref, slope_ref,
                  gffn_ref, gproj_ref, tile_a, tile_b, store_sem):
    def per_pair(p, carry):
        attend(p, q_ref, k_ref, v_ref, early_ref, before, ratio_ref, inverse_ref, mixed_ref)
        return carry

    lax.fori_loop(0, PAIRS, per_pair, 0)
    vec_ref[...] = jnp.zeros_like(vec_ref)

    def note(k, value):
        vec_ref[k : k + 1, :] += value

    def first_norm(r, carry):
        rows = at(r, 128)
        hidden = x_ref[rows].astype(F32) + (nn(mixed_ref[rows], wo[...]) + bo[...])
        normal, scale = standard(hidden)
        normal_ref[rows] = normal
        scale_ref[rows] = jnp.broadcast_to(scale, (128, 128))
        normed_ref[rows] = (normal * gain1[...] + shift1[...]).astype(BF16)
        return carry

    lax.fori_loop(0, ROWS // 128, first_norm, 0)

    def feed(t, carry):
        cols = at(t, TILE)
        for r in range(2):
            rows = slice(CHUNK * r, CHUNK * r + CHUNK)
            pre = nn(normed_ref[rows], wup[:, cols]) + bup[:, cols]
            whole, bell = normal_parts(pre)
            act = (pre * whole).astype(BF16)
            act_ref[rows, cols] = act
            slope_ref[rows, cols] = (whole + pre * bell).astype(BF16)
            part = nn(act, wdown[cols])
            acc_ref[rows] = part + jnp.where(t == 0, 0.0, acc_ref[rows])
        return carry

    lax.fori_loop(0, HIDDEN // TILE, feed, 0)

    def second_norm(r, carry):
        rows = at(r, 128)
        hidden = normed_ref[rows].astype(F32) + (acc_ref[rows] + bdown[...])
        normal, scale = standard(hidden)
        block_ref[rows] = (normal * gain2[...] + shift2[...]).astype(BF16)
        grad = cot_ref[rows].astype(F32)
        note(7, column(grad * normal))
        note(8, column(grad))
        back = norm_back(grad, normal, scale, gain2[...])
        acc_ref[rows] = back
        low = back.astype(BF16)
        gffn_ref[rows] = low
        note(6, column(low.astype(F32)))
        return carry

    lax.fori_loop(0, ROWS // 128, second_norm, 0)

    def stores(t, slot):
        cols = at(t, TILE)
        return (pltpu.make_async_copy(tile_a.at[slot], gw_down.at[cols], store_sem.at[0, slot]),
                pltpu.make_async_copy(tile_b.at[slot], gw_up.at[:, cols], store_sem.at[1, slot]))

    def feed_back(t, carry):
        cols = at(t, TILE)
        slot = lax.rem(t, 2)

        @pl.when(t >= 2)
        def _():
            for copy in stores(t - 2, slot):
                copy.wait()

        gffn = gffn_ref[...]
        gpre = (nt(gffn, wdown[cols]) * slope_ref[:, cols].astype(F32)).astype(BF16)
        total = column(gpre.astype(F32))
        vec_ref[pl.ds(9 + t, 1), 0:TILE] = total
        tile_a[slot] = tn(act_ref[:, cols], gffn)
        tile_b[slot] = tn(normed_ref[...], gpre)
        acc_ref[...] += nt(gpre, wup[:, cols])
        for copy in stores(t, slot):
            copy.start()
        return carry

    tiles = HIDDEN // TILE
    lax.fori_loop(0, tiles, feed_back, 0)

    def first_back(r, carry):
        rows = at(r, 128)
        normal = normal_ref[rows]
        scale = scale_ref[rows, 0:1]
        grad = acc_ref[rows]
        note(4, column(grad * normal))
        note(5, column(grad))
        back = norm_back(grad, normal, scale, gain1[...])
        gone_ref[rows] = back
        low = back.astype(BF16)
        gproj_ref[rows] = low
        note(3, column(low.astype(F32)))
        acc_ref[rows] = nt(low, wo[...])
        return carry

    lax.fori_loop(0, ROWS // 128, first_back, 0)
    gw_out[...] = tn(mixed_ref[...], gproj_ref[...])

    def heads_back(p, carry):
        cols = at(p, 128)
        lane = lax.broadcasted_iota(jnp.int32, (ROWS, 128), 1)
        left = lane < 64
        gnum = (acc_ref[:, cols] * inverse_ref[:, cols]).astype(BF16).astype(F32)
        product = gnum * ratio_ref[:, cols]
        for j in range(2):
            mine = jnp.where(left, product, 0.0) if j == 0 else jnp.where(left, 0.0, product)
            gden = jnp.broadcast_to(-jnp.sum(mine, axis=1, keepdims=True), (ROWS, 128))
            high = gden.astype(BF16).astype(F32)
            ends = jnp.where(lane == 64, high, jnp.where(lane == 65, gden - high, 0.0))
            grad = jnp.where(left, gnum if j == 0 else swap_halves(gnum), ends).astype(BF16)
            gn_ref[2 * p + j] = grad
            late = tn(grad[CHUNK:ROWS], q_ref[2 * p + j, CHUNK:ROWS])
            late_ref[2 * p + j] = late
            both = late + tn(grad[0:CHUNK], q_ref[2 * p + j, 0:CHUNK])
            after_state[p, 64 * j : 64 * j + 64] = both[0:64]
            after_state[p, 128 + j : 129 + j] = both[64:65] + both[65:66]
        after_state[p, 130:136] = jnp.zeros((6, 128), F32)
        return carry

    lax.fori_loop(0, PAIRS, heads_back, 0)
    for t in (tiles - 2, tiles - 1):
        for copy in stores(t, t % 2):
            copy.wait()


ORDERS = ((1, 0, 2), (0, 2, 1), (2, 1, 0))
SUBS = 9
COLS = 256


def cell(ref, order, picks):
    at = [slice(None)] * 3
    for axis, pick in zip(order, picks):
        at[axis] = pick
    return ref.at[tuple(at)]


def halved(ref, order, pick, half):
    at = [slice(None)] * 3
    at[order[0]] = pick
    at[1 if order[0] == 0 else 0] = half
    return ref.at[tuple(at)]


def add_blocks(dst, srcs, lead):
    total = 1
    for n in lead:
        total *= n

    def step(k, carry):
        at, rest = [], k
        for n in reversed(lead):
            at.append(lax.rem(rest, n))
            rest = rest // n
        at = tuple(reversed(at))
        value = dst[at]
        for src in srcs:
            value = value + src[at]
        dst[at] = value
        return carry

    lax.fori_loop(0, total, step, 0)


def reduce_kernel(
    down, up, w_o, w_q, w_k, w_v, vec,
    out_down, out_up, out_o, out_q, out_k, out_v, out_vec,
    own, core_in, first, second, third, done, vecs,
    load_sem, core_send, core_recv, send, recv, vsend, vrecv,
):
    me = tuple(lax.axis_index(a) for a in AX)
    core = lax.axis_index(CORE)
    other = 1 - core
    barrier = pltpu.get_barrier_semaphore()
    pl.semaphore_signal(barrier, inc=1, device_id={CORE: other}, device_id_type=MESH)
    for axis in range(3):
        for d in DIRECT:
            pl.semaphore_signal(barrier, inc=1, device_id={AX[axis]: rot(me[axis], d)}, device_id_type=MESH)
    pl.semaphore_wait(barrier, 10)

    def source(s, b, half):
        columns = pl.ds(COLS * (s % 3), COLS)
        if s < 3:
            return down.at[:, :, half, b, :, columns]
        if s < 6:
            return up.at[:, :, half, :, pl.ds(768 * b + COLS * (s % 3), COLS)]
        return (w_o, w_q, w_k, w_v)[b].at[:, :, half, :, columns]

    loads, swaps, moves = {}, {}, []
    for s in (0, 4, 8, 3, 7, 2, 6, 1, 5):
        for b in range(4):
            swap = pltpu.make_async_remote_copy(
                src_ref=source(s, b, other), dst_ref=core_in.at[s, :, :, b],
                send_sem=core_send.at[s, b], recv_sem=core_recv.at[s, b],
                device_id={CORE: other}, device_id_type=MESH)
            swap.start()
            load = pltpu.make_async_copy(source(s, b, core), own.at[s, :, :, b], load_sem.at[s, b])
            load.start()
            loads[s, b], swaps[s, b] = load, swap

    def remote(src, dst, s, k, axis, d):
        copy = pltpu.make_async_remote_copy(
            src_ref=src, dst_ref=dst, send_sem=send.at[s, k], recv_sem=recv.at[s, k],
            device_id={AX[axis]: rot(me[axis], d)}, device_id_type=MESH)
        copy.start()
        moves.append(copy)
        return copy

    flight = {}

    def begin(s):
        order = ORDERS[s % 3]
        i = me[order[0]]
        mine, inbox = own.at[s], first.at[s]
        for b in range(4):
            loads[s, b].wait()
            swaps[s, b].wait_recv()
        add_blocks(mine, [core_in.at[s]], (4, 4, 4))
        lo, hi = pl.ds(0, 2), pl.ds(2, 2)
        far = rot(i, 2)
        ax = order[0]
        flight[s, "a"] = (
            remote(halved(mine, order, far, lo), inbox.at[0, pl.ds(0, 2)], s, 0, ax, 1),
            remote(halved(mine, order, far, hi), inbox.at[0, pl.ds(2, 2)], s, 1, ax, 3),
        )
        flight[s, "b"] = (
            remote(halved(mine, order, rot(i, 1), hi), inbox.at[1, pl.ds(2, 2)], s, 2, ax, 1),
            remote(halved(mine, order, rot(i, 3), lo), inbox.at[2, pl.ds(0, 2)], s, 3, ax, 3),
        )

    def relay(s):
        order = ORDERS[s % 3]
        i = me[order[0]]
        mine, inbox = own.at[s], first.at[s]
        lo, hi = pl.ds(0, 2), pl.ds(2, 2)
        ax = order[0]
        flight[s, "a"][0].wait_recv()
        part = halved(mine, order, rot(i, 1), lo)
        add_blocks(part, [inbox.at[0, pl.ds(0, 2)]], (2, 4))
        c0 = remote(part, inbox.at[1, pl.ds(0, 2)], s, 4, ax, 1)
        flight[s, "a"][1].wait_recv()
        part = halved(mine, order, rot(i, 3), hi)
        add_blocks(part, [inbox.at[0, pl.ds(2, 2)]], (2, 4))
        c1 = remote(part, inbox.at[2, pl.ds(2, 2)], s, 5, ax, 3)
        flight[s, "b"] += (c0, c1)

    def middle(s):
        order = ORDERS[s % 3]
        mine = own.at[s]
        for copy in flight[s, "b"]:
            copy.wait_recv()
        i = me[order[0]]
        add_blocks(cell(mine, order, (i,)), [first.at[s, 1], first.at[s, 2]], (4, 4))
        ax = order[1]
        flight[s, 2] = [
            remote(cell(mine, order, (i, rot(me[ax], d))), second.at[s, k], s, 6 + k, ax, d)
            for k, d in enumerate(DIRECT)
        ]

    def last(s):
        order = ORDERS[s % 3]
        mine = own.at[s]
        for copy in flight[s, 2]:
            copy.wait_recv()
        at = (me[order[0]], me[order[1]])
        add_blocks(cell(mine, order, at), [second.at[s, k] for k in range(3)], (4,))
        ax = order[2]
        flight[s, 3] = [
            remote(cell(mine, order, (*at, rot(me[ax], d))), third.at[s, k], s, 9 + k, ax, d)
            for k, d in enumerate(DIRECT)
        ]

    def spread(s):
        for copy in flight[s, 3]:
            copy.wait_recv()
        done[s, me[2]] = own[s, me[0], me[1], me[2]] + third[s, 0] + third[s, 1] + third[s, 2]
        flight[s, 4] = [
            remote(done.at[s, me[2]], done.at[s, me[2]], s, 12 + k, 2, d)
            for k, d in enumerate(DIRECT)
        ]

    def finish(s):
        for copy in flight[s, 4]:
            copy.wait_recv()
        c = pl.ds(COLS * (s % 3), COLS)
        for b in range(4):
            if s < 3:
                out_down[24 * b : 24 * b + 24, c] = done[s, b]
            elif s < 6:
                out_up[:, pl.ds(768 * b + COLS * (s % 3), COLS)] = done[s, b]
            else:
                (out_o, out_q, out_k, out_v)[b][:, c] = done[s, b]

    vecs[0] = vec[...]
    vmoves = {}

    def vector_send(stage):
        if stage == 0:
            targets = [{CORE: other}]
        else:
            ax = stage - 1
            targets = [{AX[ax]: rot(me[ax], d)} for d in DIRECT]
        base = (0, 1, 4, 7)[stage]
        vmoves[stage] = []
        for k, target in enumerate(targets):
            copy = pltpu.make_async_remote_copy(
                src_ref=vecs.at[stage], dst_ref=vecs.at[5 + base + k],
                send_sem=vsend.at[base + k], recv_sem=vrecv.at[base + k],
                device_id=target, device_id_type=MESH)
            copy.start()
            vmoves[stage].append(copy)

    def vector_sum(stage):
        base = (0, 1, 4, 7)[stage]
        total = vecs[stage]
        for k, copy in enumerate(vmoves[stage]):
            copy.wait_recv()
            total = total + vecs[5 + base + k]
        vecs[stage + 1] = total

    G = [(0, 4, 8), (3, 7, 2), (6, 1, 5)]

    def run(step, g):
        for s in G[g]:
            step(s)

    vector_send(0)
    run(begin, 0)
    vector_sum(0)
    vector_send(1)
    run(relay, 0)
    run(begin, 1)
    run(middle, 0)
    vector_sum(1)
    vector_send(2)
    run(relay, 1)
    run(begin, 2)
    run(last, 0)
    run(middle, 1)
    run(relay, 2)
    run(spread, 0)
    vector_sum(2)
    vector_send(3)
    run(last, 1)
    run(middle, 2)
    run(finish, 0)
    run(spread, 1)
    run(last, 2)
    vector_sum(3)
    out_vec[...] = vecs[4]
    run(finish, 1)
    run(spread, 2)
    run(finish, 2)
    for copy in [*moves, *swaps.values(), *(c for cs in vmoves.values() for c in cs)]:
        copy.wait_send()


def reduce_grads(down, up, w_o, w_q, w_k, w_v, vec):
    f32 = jnp.float32
    shapes = [(96, 768), (24, 3072), (24, 768), (24, 768), (24, 768), (24, 768), (16, 768)]
    any_spec = pl.BlockSpec(memory_space=pl.ANY)
    vmem = pl.BlockSpec(memory_space=pltpu.VMEM)
    return pl.pallas_call(
        reduce_kernel,
        out_shape=[jax.ShapeDtypeStruct(s, f32) for s in shapes],
        in_specs=[any_spec] * 6 + [vmem],
        out_specs=[vmem] * 7,
        scratch_shapes=[
            pltpu.VMEM((SUBS, 4, 4, 4, 24, COLS), f32),
            pltpu.VMEM((SUBS, 4, 4, 4, 24, COLS), f32),
            pltpu.VMEM((SUBS, 3, 4, 4, 24, COLS), f32),
            pltpu.VMEM((SUBS, 3, 4, 24, COLS), f32),
            pltpu.VMEM((SUBS, 3, 24, COLS), f32),
            pltpu.VMEM((SUBS, 4, 24, COLS), f32),
            pltpu.VMEM((15, 16, 768), f32),
            pltpu.SemaphoreType.DMA((SUBS, 4)),
            pltpu.SemaphoreType.DMA((SUBS, 4)),
            pltpu.SemaphoreType.DMA((SUBS, 4)),
            pltpu.SemaphoreType.DMA((SUBS, 15)),
            pltpu.SemaphoreType.DMA((SUBS, 15)),
            pltpu.SemaphoreType.DMA((10,)),
            pltpu.SemaphoreType.DMA((10,)),
        ],
        compiler_params=pltpu.CompilerParams(
            collective_id=0, has_side_effects=True, vmem_limit_bytes=60 * 2**20
        ),
    )(
        down.reshape(4, 4, 2, 4, 24, 768),
        up.reshape(4, 4, 2, 24, 3072),
        *(w.reshape(4, 4, 2, 24, 768) for w in (w_o, w_q, w_k, w_v)),
        vec,
    )


def suffix_state(after, p, j):
    body = after[p, 64 * j : 64 * j + 64]
    row = jnp.broadcast_to(after[p, 128 + j : 129 + j], (64, 128))
    first = lax.broadcasted_iota(jnp.int32, (64, 128), 0) == 0
    return jnp.concatenate([body, jnp.where(first, row, 0.0)], axis=0)


def attend_back(p, q_ref, k_ref, v_ref, gn_ref, early_ref, late_ref, before, after, trig_ref, valid_ref,
                gate_q, gate_k, grad_ref):
    causal, flipped = causal_masks()
    left = left_lanes(CHUNK)
    for c in range(2):
        rows = slice(CHUNK * c, CHUNK * c + CHUNK)
        query, keys, value = [], [], []
        for j in range(2):
            h = 2 * p + j
            q, k, v, g = q_ref[h, rows], k_ref[h, rows], v_ref[h, rows], gn_ref[h, rows]
            past = prefix_state(before, p, j)
            if c == 1:
                past = past + early_ref[h]
            future = suffix_state(after, p, j)
            if c == 0:
                future = future + late_ref[h]
            past_high, past_low = halves(past)
            next_high, next_low = halves(future)
            weight = jnp.where(causal, nt(g, v), 0.0).astype(BF16)
            gq = nn(weight, k) + nn(doubled(g), jnp.concatenate([past_high, past_low], axis=0))
            weight = jnp.where(flipped, nt(v, g), 0.0).astype(BF16)
            gk = nn(weight, q) + nn(doubled(v), jnp.concatenate([next_high, next_low], axis=0))
            weight = jnp.where(flipped, nt(k, q), 0.0).astype(BF16)
            gv = nn(weight, g) + nt(doubled(k), jnp.concatenate([next_high, next_low], axis=1))
            gq = gq * trig_ref[rows]
            gk = gk * valid_ref[rows]
            query.append(gq + swap_halves(gq))
            keys.append(gk + swap_halves(gk))
            value.append(gv)
        cols = at(p, 128)
        grad_ref[0, rows, cols] = (jnp.where(left, query[0], query[1]) * gate_q[rows, cols].astype(F32)).astype(BF16)
        grad_ref[1, rows, cols] = (jnp.where(left, keys[0], keys[1]) * gate_k[rows, cols].astype(F32)).astype(BF16)
        grad_ref[2, rows, cols] = jnp.where(left, value[0], swap_halves(value[1])).astype(BF16)


def last_kernel(x_ref, q_ref, k_ref, v_ref, gn_ref, early_ref, late_ref, before, after, trig_ref, valid_ref,
                gate_q, gate_k, gone_ref, wq, wk, wv,
                tokens_ref, gw_q, gw_k, gw_v, vec_ref, grad_ref):
    def per_pair(p, carry):
        attend_back(p, q_ref, k_ref, v_ref, gn_ref, early_ref, late_ref, before, after, trig_ref, valid_ref,
                    gate_q, gate_k, grad_ref)
        return carry

    lax.fori_loop(0, PAIRS, per_pair, 0)
    vec_ref[...] = jnp.zeros_like(vec_ref)
    for i, out in enumerate((gw_q, gw_k, gw_v)):
        vec_ref[i : i + 1, :] = column(grad_ref[i].astype(F32))

        def product(n, carry):
            cols = at(n, 256)
            out[:, cols] = tn(x_ref[...], grad_ref[i, :, cols])
            return carry

        lax.fori_loop(0, WIDTH // 256, product, 0)

    def back(r, carry):
        rows = at(r, 128)
        total = gone_ref[rows]
        for i, w in enumerate((wq, wk, wv)):
            total = total + nt(grad_ref[i, rows], w[...])
        tokens_ref[rows] = total
        return carry

    lax.fori_loop(0, ROWS // 128, back, 0)


def plain_call(kernel, outs, args, specs=None, scratch=(), out_specs=None):
    vmem = pl.BlockSpec(memory_space=VMEM)
    return pl.pallas_call(
        kernel,
        out_shape=[jax.ShapeDtypeStruct(shape, dtype) for shape, dtype in outs],
        in_specs=specs or [vmem] * len(args),
        out_specs=out_specs or [vmem] * len(outs),
        scratch_shapes=list(scratch),
        compiler_params=pltpu.CompilerParams(vmem_limit_bytes=LIMIT),
    )(*args)


def on_device(tokens, lengths, w_query, b_query, w_key, b_key, w_value, b_value, w_out, b_out, gain_one, shift_one,
              w_up, b_up, w_down, b_down, gain_two, shift_two, cotangent):
    x = tokens[0]
    cot = cotangent[0]
    seq = lax.axis_index(SEQ)

    def row(v):
        return v.reshape(1, -1)

    vmem = pl.BlockSpec(memory_space=VMEM)
    smem = pl.BlockSpec(memory_space=pltpu.SMEM)
    anywhere = pl.BlockSpec(memory_space=pl.ANY)
    by_head = ((HEADS, ROWS, 128), BF16)
    wide16, wide32 = ((ROWS, WIDTH), BF16), ((ROWS, WIDTH), F32)
    table = ((ROWS, 128), F32)
    per_head = ((HEADS, 128, 128), F32)
    packed = ((PAIRS, 136, 128), F32)
    q, k, v, gate_q, gate_k, trig, valid, state, early = plain_call(
        project_kernel,
        [by_head, by_head, by_head, wide16, wide16, table, table, packed, per_head],
        [(seq * ROWS).reshape(1), lengths, x, w_query, row(b_query), w_key, row(b_key), w_value, row(b_value)],
        [smem, smem] + [vmem] * 7)
    before = exchange(state, False)
    block, gone, gn, ratio, after_state, late, gw_down, gw_up, gw_out, vec = plain_call(
        middle_kernel,
        [wide16, wide32, by_head, wide32, packed, per_head,
         ((HIDDEN, WIDTH), F32), ((WIDTH, HIDDEN), F32), ((WIDTH, WIDTH), F32), ((16, WIDTH), F32)],
        [x, cot, q, k, v, early, before, w_out, row(b_out), row(gain_one), row(shift_one),
         w_up, row(b_up), w_down, row(b_down), row(gain_two), row(shift_two)],
        scratch=[
            VMEM(*wide32), VMEM(*wide16), VMEM(*wide32), VMEM(*table), VMEM(*wide16), VMEM(*wide32),
            VMEM((ROWS, HIDDEN), BF16), VMEM((ROWS, HIDDEN), BF16), VMEM(*wide16), VMEM(*wide16),
            VMEM((2, TILE, WIDTH), F32), VMEM((2, WIDTH, TILE), F32), pltpu.SemaphoreType.DMA((2, 2))],
        out_specs=[vmem] * 6 + [anywhere, anywhere, vmem, vmem])
    after = exchange(after_state, True)
    tokens_grad, gw_q, gw_k, gw_v, vec_two = plain_call(
        last_kernel,
        [wide32] + [((WIDTH, WIDTH), F32)] * 3 + [((16, WIDTH), F32)],
        [x, q, k, v, gn, early, late, before, after, trig, valid, gate_q, gate_k, gone, w_query, w_key, w_value],
        scratch=[VMEM((3, ROWS, WIDTH), BF16)])
    sum_down, sum_up, sum_out, sum_query, sum_key, sum_value, sums = reduce_grads(
        gw_down, gw_up, gw_out, gw_q, gw_k, gw_v, vec + vec_two)
    small = lax.dynamic_slice(sums, (0, 24 * seq), (9, 24))
    wide = lax.dynamic_slice(sums[9:15, :TILE].reshape(-1), (96 * seq,), (96,))
    return (
        block[None], tokens_grad[None], sum_query, small[0], sum_key, small[1], sum_value, small[2],
        sum_out, small[3], small[4], small[5], sum_up, wide, sum_down, small[6], small[7], small[8],
    )


def solution(mesh):
    torus = Mesh(mesh.devices.reshape(4, 4, 2, mesh.shape["batch"]), (*SEQ, "batch"))
    rows, shares = P("batch", SEQ, None), P(SEQ, None)
    return jax.shard_map(
        on_device,
        mesh=torus,
        in_specs=(rows, P("batch")) + (P(),) * 16 + (rows,),
        out_specs=(rows, rows) + (shares, P(SEQ)) * 4 + (P(SEQ), P(SEQ)) + (shares, P(SEQ)) * 2 + (P(SEQ), P(SEQ)),
        check_vma=False,
    )
```

```python
import jax
import jax.numpy as jnp
from jax import lax
from jax.experimental import pallas as pl
from jax.experimental.pallas import tpu as pltpu
from jax.sharding import Mesh
from jax.sharding import PartitionSpec as P

SEQ = ("seq_0", "seq_1", "seq_2")
AX = ("seq_0", "seq_1", "batch")
CORE = "seq_2"
MESH = pl.DeviceIdType.MESH
DIRECT = (1, 3, 2)
F32 = jnp.float32
BF16 = jnp.bfloat16
HALF_PI = 1.5707963267948966
HALF_PI_REST = -4.371139000186241e-08
EPSILON = 1e-05
ROWS = 512
WIDTH = 768
HIDDEN = 3072
HEADS = 12
PAIRS = 6
CHUNK = 256
TILE = 512
VMEM = pltpu.VMEM
LIMIT = 60 * 2**20


def nn(a, b):
    return jnp.dot(a, b, preferred_element_type=F32)


def nt(a, b):
    return lax.dot_general(a, b, (((1,), (1,)), ((), ())), preferred_element_type=F32)


def tn(a, b):
    return lax.dot_general(a, b, (((0,), (0,)), ((), ())), preferred_element_type=F32)


def at(k, size):
    return pl.ds(pl.multiple_of(k * size, size), size)


def rot(k, d):
    return lax.rem(k + d, 4)


def left_lanes(rows):
    return lax.broadcasted_iota(jnp.int32, (rows, 128), 1) < 64


def swap_halves(value):
    return pltpu.roll(value, 64, 1)


def doubled(value):
    return jnp.concatenate([value, value], axis=1)


def halves(value):
    high = value.astype(BF16)
    return high, (value - high.astype(F32)).astype(BF16)


SIN = (1.0, -0.1666666716337204, 0.008333330973982811, -0.00019840864115394652, 2.7525297809916083e-06, -2.3888299338636898e-08)


def sine(x):
    square = x * x
    value = SIN[5]
    for c in SIN[4::-1]:
        value = value * square + c
    return value * x


ERFCX = (
    0.22567586600780487, 0.2256695181131363, 0.2078438699245453, 0.1685338169336319, 0.14146119356155396,
    -0.005668365862220526, 0.16915558278560638, -0.18294405937194824, 0.05027270317077637,
)


def normal_parts(p):
    bell = jnp.exp(-0.5 * p * p)
    t = 1.0 / (1.0 + (0.4 * 0.7071067811865476) * jnp.abs(p))
    value = 0.5 * ERFCX[8]
    for c in ERFCX[7::-1]:
        value = value * t + 0.5 * c
    tail = value * t * bell
    return jnp.where(p >= 0, 1.0 - tail, tail), 0.3989422804014327 * bell


def trig_block(first, rows, length):
    position = first + lax.broadcasted_iota(jnp.int32, (rows, 128), 0)
    size = lax.broadcast_in_dim(length, (rows, 128), ()).astype(F32)
    angle = HALF_PI * jnp.minimum(position + 1, length).astype(F32) / size
    both = sine(jnp.where(left_lanes(rows), (HALF_PI - angle) + HALF_PI_REST, angle))
    return both, (position < length).astype(F32)


def project_keys(n, x_ref, wk, bk, wv, bv, qk_ref, v_ref, gate_k, valid_ref):
    cols = at(n, 256)
    left = left_lanes(ROWS)
    x = x_ref[...]
    u = (nn(x, wv[:, cols]) + bv[:, cols]).astype(BF16).astype(F32)
    for j in range(2):
        part = u[:, 128 * j : 128 * j + 128]
        v_ref[:, at(4 * n + 2 * j, 128)] = jnp.where(left, part, 1.0).astype(BF16)
        v_ref[:, at(4 * n + 2 * j + 1, 128)] = jnp.where(left, swap_halves(part), 1.0).astype(BF16)
    project_soft(n, HEADS, x, wk, bk, qk_ref, gate_k, valid_ref)


def project_soft(n, first, x, w, b, out, gate, table):
    cols = at(n, 256)
    left = left_lanes(ROWS)
    u = nn(x, w[:, cols]) + b[:, cols]
    small = jnp.exp(-jnp.abs(u))
    soft = jnp.maximum(u, 0.0) + jnp.log1p(small)
    gate[:, cols] = (jnp.where(u >= 0, 1.0, small) / (1.0 + small)).astype(BF16)
    trig = table[...]
    for j in range(2):
        part = soft[:, 128 * j : 128 * j + 128]
        other = swap_halves(part)
        out[:, at(first + 4 * n + 2 * j, 128)] = (jnp.where(left, part, other) * trig).astype(BF16)
        out[:, at(first + 4 * n + 2 * j + 1, 128)] = (jnp.where(left, other, part) * trig).astype(BF16)


def state_sums(p, qk_ref, v_ref, state_ref, early_ref):
    for j in range(2):
        h = 2 * p + j
        keys, values = at(HEADS + h, 128), at(h, 128)
        early = tn(v_ref[0:CHUNK, values], qk_ref[0:CHUNK, keys])
        early_ref[h] = early
        both = early + tn(v_ref[CHUNK:ROWS, values], qk_ref[CHUNK:ROWS, keys])
        state_ref[p, 64 * j : 64 * j + 64] = both[0:64]
        state_ref[p, 128 + j : 129 + j] = both[64:65]
    state_ref[p, 130:136] = jnp.zeros((6, 128), F32)


def exchange_steps(pay, out, core_in, chip, give, head, tail, total, msgs, xa, ya, yb, xb, send, recv, reverse):
    my, mx = lax.axis_index("seq_0"), lax.axis_index("seq_1")
    core = lax.axis_index(CORE)
    other = 1 - core
    moves = []

    def remote(src, dst, k, target):
        copy = pltpu.make_async_remote_copy(
            src_ref=src, dst_ref=dst, send_sem=send.at[k], recv_sem=recv.at[k],
            device_id=target, device_id_type=MESH)
        copy.start()
        moves.append(copy)
        return copy

    def counts(theirs, mine):
        return theirs > mine if reverse else theirs < mine

    def chosen(flag, value):
        return jnp.where(flag, value, jnp.zeros_like(value))

    def first():
        return remote(pay.at[pl.ds(3 * other, 3)], core_in, 0, {CORE: other})

    def second(copy):
        copy.wait_recv()
        for p in range(3):
            chip[p] = pay[3 * core + p] + core_in[p]
        a = [remote(chip.at[:, pl.ds(0, 72)], xa.at[k], 1 + k, {"seq_1": rot(mx, d)}) for k, d in enumerate(DIRECT)]
        b = [remote(chip.at[:, pl.ds(72, 64)], yb.at[k], 4 + k, {"seq_0": rot(my, d)}) for k, d in enumerate(DIRECT)]
        return a, b

    def third(copies):
        a, b = copies
        for copy in a:
            copy.wait_recv()
        for p in range(3):
            some = jnp.zeros((72, 128), F32)
            every = chip[p, 0:72]
            for k, d in enumerate(DIRECT):
                piece = xa[k, p]
                some = some + chosen(counts(rot(mx, 4 - d), mx), piece)
                every = every + piece
            head[p] = some
            total[p] = every
        a = [remote(total, ya.at[k], 7 + k, {"seq_0": rot(my, d)}) for k, d in enumerate(DIRECT)]
        for copy in b:
            copy.wait_recv()
        for p in range(3):
            some = jnp.zeros((64, 128), F32)
            for k, d in enumerate(DIRECT):
                some = some + chosen(counts(rot(my, 4 - d), my), yb[k, p])
            tail[p] = some
            own = chip[p, 72:136]
            for k, d in enumerate(DIRECT):
                msgs[k, p] = some + chosen(counts(mx, rot(mx, d)), own)
        b = [remote(msgs.at[k], xb.at[k], 10 + k, {"seq_1": rot(mx, d)}) for k, d in enumerate(DIRECT)]
        return a, b

    def fourth(copies):
        a, b = copies
        for copy in a:
            copy.wait_recv()
        for copy in b:
            copy.wait_recv()
        mine = core == (0 if reverse else 1)
        for p in range(3):
            low, high = head[p], tail[p]
            for k, d in enumerate(DIRECT):
                low = low + chosen(counts(rot(my, 4 - d), my), ya[k, p])
                high = high + xb[k, p]
            own = 3 * core + p
            out[own, 0:72] = low + chosen(mine, core_in[p, 0:72])
            out[own, 72:136] = high + chosen(mine, core_in[p, 72:136])
            give[p, 0:72] = low + chosen(jnp.logical_not(mine), pay[own, 0:72])
            give[p, 72:136] = high + chosen(jnp.logical_not(mine), pay[own, 72:136])
        return remote(give, out.at[pl.ds(3 * core, 3)], 13, {CORE: other})

    def fifth(copy):
        copy.wait_recv()
        for move in moves:
            move.wait_send()

    return first, second, third, fourth, fifth


EXCHANGE_SCRATCH = [
    VMEM((3, 136, 128), F32),
    VMEM((3, 136, 128), F32),
    VMEM((3, 136, 128), F32),
    VMEM((3, 72, 128), F32),
    VMEM((3, 64, 128), F32),
    VMEM((3, 72, 128), F32),
    VMEM((3, 3, 64, 128), F32),
    VMEM((3, 3, 72, 128), F32),
    VMEM((3, 3, 72, 128), F32),
    VMEM((3, 3, 64, 128), F32),
    VMEM((3, 3, 64, 128), F32),
    pltpu.SemaphoreType.DMA((14,)),
    pltpu.SemaphoreType.DMA((14,)),
]


def greet(axes):
    barrier = pltpu.get_barrier_semaphore()
    core = lax.axis_index(CORE)
    pl.semaphore_signal(barrier, inc=1, device_id={CORE: 1 - core}, device_id_type=MESH)
    for axis in axes:
        mine = lax.axis_index(axis)
        for d in DIRECT:
            pl.semaphore_signal(barrier, inc=1, device_id={axis: rot(mine, d)}, device_id_type=MESH)


def greeted(axes):
    pl.semaphore_wait(pltpu.get_barrier_semaphore(), 1 + 3 * len(axes))


def exchange_kernel(reverse, pay, out, *scratch):
    greet(("seq_0", "seq_1"))
    greeted(("seq_0", "seq_1"))
    first, second, third, fourth, fifth = exchange_steps(pay, out, *scratch, reverse)
    fifth(fourth(third(second(first()))))


def exchange(pay, reverse):
    def kernel(*refs):
        exchange_kernel(reverse, *refs)

    vmem = pl.BlockSpec(memory_space=VMEM)
    return pl.pallas_call(
        kernel,
        out_shape=jax.ShapeDtypeStruct((PAIRS, 136, 128), F32),
        in_specs=[vmem],
        out_specs=vmem,
        scratch_shapes=EXCHANGE_SCRATCH,
        compiler_params=pltpu.CompilerParams(
            collective_id=1 if reverse else 2, has_side_effects=True, vmem_limit_bytes=LIMIT),
    )(pay)


def causal_masks():
    row = lax.broadcasted_iota(jnp.int32, (CHUNK, CHUNK), 0)
    col = lax.broadcasted_iota(jnp.int32, (CHUNK, CHUNK), 1)
    return row >= col, row <= col


def prefix_state(before, p, j):
    body = before[p, 64 * j : 64 * j + 64]
    return jnp.concatenate([body, jnp.broadcast_to(before[p, 128 + j : 129 + j], (64, 128))], axis=0)


def attend_local(p, qk_ref, v_ref, num_ref):
    causal, _ = causal_masks()
    for c in range(2):
        rows = slice(CHUNK * c, CHUNK * c + CHUNK)
        for j in range(2):
            h = 2 * p + j
            weight = nt(qk_ref[rows, at(h, 128)], qk_ref[rows, at(HEADS + h, 128)])
            num_ref[h, rows] = nn(jnp.where(causal, weight, 0.0).astype(BF16), v_ref[rows, at(h, 128)])


def attend_earlier(p, qk_ref, num_ref, early_ref, before, ratio_ref, inverse_ref, mixed_ref):
    left = left_lanes(CHUNK)
    cols = at(p, 128)
    for c in range(2):
        rows = slice(CHUNK * c, CHUNK * c + CHUNK)
        sums = []
        for j in range(2):
            h = 2 * p + j
            state = prefix_state(before, p, j)
            if c == 1:
                state = state + early_ref[h]
            high, low = halves(state)
            q = qk_ref[rows, at(h, 128)]
            sums.append(num_ref[h, rows] + nt(doubled(q), jnp.concatenate([high, low], axis=1)))
        even, odd = sums
        top = jnp.where(left, even, swap_halves(odd))
        inverse = 1.0 / jnp.where(left, swap_halves(even), odd)
        ratio = top * inverse
        ratio_ref[rows, cols] = ratio
        inverse_ref[rows, cols] = inverse
        mixed_ref[rows, cols] = ratio.astype(BF16)


def mean_rows(value):
    return jnp.mean(value, axis=-1, keepdims=True)


def standard(hidden):
    centred = hidden - mean_rows(hidden)
    scale = lax.rsqrt(mean_rows(centred * centred) + EPSILON)
    return centred * scale, scale


def norm_back(grad, normal, scale, gain):
    scaled = grad * gain
    return scale * (scaled - mean_rows(scaled) - normal * mean_rows(scaled * normal))


def column(value):
    return jnp.sum(value, axis=0, keepdims=True)


def front_kernel(len_ref, bq, bk, bv, bo, gain1, shift1, bup, bdown, gain2, shift2,
                 x_hbm, wq_hbm, wk_hbm, wv_hbm, wo_hbm, wup_hbm, wdown_hbm, cot_hbm,
                 qk_out, v_out, gates_out, trigs_out, early_out, before_out, ratio_out, inverse_out, mixed_out,
                 normal_out, scale_out, normed_out, act_out, slope_out, back_out, gffn_out, block_out, vec_out,
                 x_ref, wq, wk, wv, wo, wup, wdown, cot_ref,
                 qk_ref, v_ref, gates, trigs, early_ref, before, ratio_ref, inverse_ref, mixed_ref,
                 normal_ref, scale_ref, normed_ref, act_ref, slope_ref, acc_ref, gffn_ref, block_ref, vec_ref,
                 state_ref, num_ref, load_sem, store_sem, *scratch):
    greet(("seq_0", "seq_1"))
    pairs = ((x_hbm, x_ref), (wk_hbm, wk), (wv_hbm, wv), (wq_hbm, wq), (wo_hbm, wo), (wup_hbm, wup),
             (wdown_hbm, wdown), (cot_hbm, cot_ref))
    loads = [pltpu.make_async_copy(src, dst, load_sem.at[k]) for k, (src, dst) in enumerate(pairs)]
    for load in loads:
        load.start()
    stores = []

    def store(src, dst):
        copy = pltpu.make_async_copy(src, dst, store_sem.at[len(stores)])
        copy.start()
        stores.append(copy)

    length = len_ref[0]
    start = ROWS * ((lax.axis_index("seq_0") * 4 + lax.axis_index("seq_1")) * 2 + lax.axis_index(CORE))

    def angles(r, carry):
        both, valid = trig_block(start + 128 * r, 128, length)
        trigs[0, at(r, 128)] = both
        trigs[1, at(r, 128)] = both * valid
        return carry

    lax.fori_loop(0, ROWS // 128, angles, 0)
    store(trigs, trigs_out)
    for k in range(3):
        loads[k].wait()

    def keys(n, carry):
        project_keys(n, x_ref, wk, bk, wv, bv, qk_ref, v_ref, gates.at[1], trigs.at[1])
        return carry

    lax.fori_loop(0, WIDTH // 256, keys, 0)

    def states(p, carry):
        state_sums(p, qk_ref, v_ref, state_ref, early_ref)
        return carry

    lax.fori_loop(0, PAIRS, states, 0)
    store(v_ref, v_out)
    store(early_ref, early_out)
    greeted(("seq_0", "seq_1"))
    first, second, third, fourth, fifth = exchange_steps(state_ref, before, *scratch, False)
    stage = first()
    loads[3].wait()

    def queries(n, carry):
        project_soft(n, 0, x_ref[...], wq, bq, qk_ref, gates.at[0], trigs.at[0])
        return carry

    def local(p, carry):
        attend_local(p, qk_ref, v_ref, num_ref)
        return carry

    lax.fori_loop(0, 1, queries, 0)
    stage = second(stage)
    lax.fori_loop(1, WIDTH // 256, queries, 0)
    store(qk_ref, qk_out)
    store(gates, gates_out)
    lax.fori_loop(0, 3, local, 0)
    stage = third(stage)
    lax.fori_loop(3, PAIRS, local, 0)
    stage = fourth(stage)
    fifth(stage)
    store(before, before_out)

    def earlier(p, carry):
        attend_earlier(p, qk_ref, num_ref, early_ref, before, ratio_ref, inverse_ref, mixed_ref)
        return carry

    lax.fori_loop(0, PAIRS, earlier, 0)
    store(ratio_ref, ratio_out)
    store(inverse_ref, inverse_out)
    store(mixed_ref, mixed_out)
    vec_ref[...] = jnp.zeros_like(vec_ref)

    def note(k, value):
        vec_ref[k : k + 1, :] += value

    loads[4].wait()

    def first_norm(r, carry):
        rows = at(r, 128)
        hidden = x_ref[rows].astype(F32) + (nn(mixed_ref[rows], wo[...]) + bo[...])
        normal, scale = standard(hidden)
        normal_ref[rows] = normal
        scale_ref[rows] = jnp.broadcast_to(scale, (128, 128))
        normed_ref[rows] = (normal * gain1[...] + shift1[...]).astype(BF16)
        return carry

    lax.fori_loop(0, ROWS // 128, first_norm, 0)
    store(normal_ref, normal_out)
    store(scale_ref, scale_out)
    store(normed_ref, normed_out)
    loads[5].wait()
    loads[6].wait()

    def feed(t, carry):
        cols = at(t, TILE)
        for r in range(2):
            rows = slice(CHUNK * r, CHUNK * r + CHUNK)
            pre = nn(normed_ref[rows], wup[:, cols]) + bup[:, cols]
            whole, bell = normal_parts(pre)
            act = (pre * whole).astype(BF16)
            act_ref[rows, cols] = act
            slope_ref[rows, cols] = (whole + pre * bell).astype(BF16)
            part = nn(act, wdown[cols])
            acc_ref[rows] = part + jnp.where(t == 0, 0.0, acc_ref[rows])
        return carry

    lax.fori_loop(0, HIDDEN // TILE, feed, 0)
    store(act_ref, act_out)
    store(slope_ref, slope_out)
    loads[7].wait()

    def second_norm(r, carry):
        rows = at(r, 128)
        hidden = normed_ref[rows].astype(F32) + (acc_ref[rows] + bdown[...])
        normal, scale = standard(hidden)
        block_ref[rows] = (normal * gain2[...] + shift2[...]).astype(BF16)
        grad = cot_ref[rows].astype(F32)
        note(7, column(grad * normal))
        note(8, column(grad))
        back = norm_back(grad, normal, scale, gain2[...])
        acc_ref[rows] = back
        low = back.astype(BF16)
        gffn_ref[rows] = low
        note(6, column(low.astype(F32)))
        return carry

    lax.fori_loop(0, ROWS // 128, second_norm, 0)
    store(gffn_ref, gffn_out)
    store(acc_ref, back_out)
    store(block_ref, block_out)
    store(vec_ref, vec_out)
    for copy in stores:
        copy.wait()


def middle_kernel(qk_ref, ratio_ref, inverse_ref, mixed_ref, normal_ref, scale_ref, normed_ref, act_ref, slope_ref,
                  acc_ref, gffn_ref, wo, wup, gain1, wdown,
                  gone_ref, gn_ref, after_state, late_ref, gw_down, gw_up, gw_out, vec_ref,
                  gproj_ref, scratch_ref, tile_a, tile_b, store_sem):
    vec_ref[...] = jnp.zeros_like(vec_ref)

    def note(k, value):
        vec_ref[k : k + 1, :] += value

    gone_ref[...] = acc_ref[...]

    def stores(t, slot):
        cols = at(t, TILE)
        return (pltpu.make_async_copy(tile_a.at[slot], gw_down.at[cols], store_sem.at[0, slot]),
                pltpu.make_async_copy(tile_b.at[slot], gw_up.at[:, cols], store_sem.at[1, slot]))

    def feed_back(t, carry):
        cols = at(t, TILE)
        slot = lax.rem(t, 2)

        @pl.when(t >= 2)
        def _():
            for copy in stores(t - 2, slot):
                copy.wait()

        gffn = gffn_ref[...]
        gpre = (nt(gffn, wdown[cols]) * slope_ref[:, cols].astype(F32)).astype(BF16)
        total = column(gpre.astype(F32))
        vec_ref[pl.ds(9 + t, 1), 0:TILE] = total
        tile_a[slot] = tn(act_ref[:, cols], gffn)
        tile_b[slot] = tn(normed_ref[...], gpre)
        gone_ref[...] += nt(gpre, wup[:, cols])
        for copy in stores(t, slot):
            copy.start()
        return carry

    tiles = HIDDEN // TILE
    lax.fori_loop(0, tiles, feed_back, 0)

    def first_back(r, carry):
        rows = at(r, 128)
        normal = normal_ref[rows]
        scale = scale_ref[rows, 0:1]
        grad = gone_ref[rows]
        note(4, column(grad * normal))
        note(5, column(grad))
        back = norm_back(grad, normal, scale, gain1[...])
        gone_ref[rows] = back
        low = back.astype(BF16)
        gproj_ref[rows] = low
        note(3, column(low.astype(F32)))
        scratch_ref[rows] = nt(low, wo[...])
        return carry

    lax.fori_loop(0, ROWS // 128, first_back, 0)
    gw_out[...] = tn(mixed_ref[...], gproj_ref[...])

    def heads_back(p, carry):
        cols = at(p, 128)
        lane = lax.broadcasted_iota(jnp.int32, (ROWS, 128), 1)
        left = lane < 64
        gnum = (scratch_ref[:, cols] * inverse_ref[:, cols]).astype(BF16).astype(F32)
        product = gnum * ratio_ref[:, cols]
        for j in range(2):
            mine = jnp.where(left, product, 0.0) if j == 0 else jnp.where(left, 0.0, product)
            gden = jnp.broadcast_to(-jnp.sum(mine, axis=1, keepdims=True), (ROWS, 128))
            high = gden.astype(BF16).astype(F32)
            ends = jnp.where(lane == 64, high, jnp.where(lane == 65, gden - high, 0.0))
            grad = jnp.where(left, gnum if j == 0 else swap_halves(gnum), ends).astype(BF16)
            gn_ref[:, at(2 * p + j, 128)] = grad
            late = tn(grad[CHUNK:ROWS], qk_ref[CHUNK:ROWS, at(2 * p + j, 128)])
            late_ref[2 * p + j] = late
            both = late + tn(grad[0:CHUNK], qk_ref[0:CHUNK, at(2 * p + j, 128)])
            after_state[p, 64 * j : 64 * j + 64] = both[0:64]
            after_state[p, 128 + j : 129 + j] = both[64:65] + both[65:66]
        after_state[p, 130:136] = jnp.zeros((6, 128), F32)
        return carry

    lax.fori_loop(0, PAIRS, heads_back, 0)
    for t in (tiles - 2, tiles - 1):
        for copy in stores(t, t % 2):
            copy.wait()


ORDERS = ((1, 0, 2), (0, 2, 1), (2, 1, 0))
SUBS = 9
COLS = 256


def cell(ref, order, picks):
    at = [slice(None)] * 3
    for axis, pick in zip(order, picks):
        at[axis] = pick
    return ref.at[tuple(at)]


def halved(ref, order, pick, half):
    at = [slice(None)] * 3
    at[order[0]] = pick
    at[1 if order[0] == 0 else 0] = half
    return ref.at[tuple(at)]


def add_blocks(dst, srcs, lead):
    total = 1
    for n in lead:
        total *= n

    def step(k, carry):
        at, rest = [], k
        for n in reversed(lead):
            at.append(lax.rem(rest, n))
            rest = rest // n
        at = tuple(reversed(at))
        value = dst[at]
        for src in srcs:
            value = value + src[at]
        dst[at] = value
        return carry

    lax.fori_loop(0, total, step, 0)


def reduce_kernel(
    down, up, w_o, w_q, w_k, w_v, vec,
    out_down, out_up, out_o, out_q, out_k, out_v, out_vec,
    own, core_in, first, second, third, done, vecs,
    load_sem, core_send, core_recv, send, recv, vsend, vrecv,
):
    me = tuple(lax.axis_index(a) for a in AX)
    core = lax.axis_index(CORE)
    other = 1 - core
    barrier = pltpu.get_barrier_semaphore()
    pl.semaphore_signal(barrier, inc=1, device_id={CORE: other}, device_id_type=MESH)
    for axis in range(3):
        for d in DIRECT:
            pl.semaphore_signal(barrier, inc=1, device_id={AX[axis]: rot(me[axis], d)}, device_id_type=MESH)
    pl.semaphore_wait(barrier, 10)

    def source(s, b, half):
        columns = pl.ds(COLS * (s % 3), COLS)
        if s < 3:
            return down.at[:, :, half, b, :, columns]
        if s < 6:
            return up.at[:, :, half, :, pl.ds(768 * b + COLS * (s % 3), COLS)]
        return (w_o, w_q, w_k, w_v)[b].at[:, :, half, :, columns]

    loads, swaps, moves = {}, {}, []
    for s in (0, 4, 8, 3, 7, 2, 6, 1, 5):
        for b in range(4):
            swap = pltpu.make_async_remote_copy(
                src_ref=source(s, b, other), dst_ref=core_in.at[s, :, :, b],
                send_sem=core_send.at[s, b], recv_sem=core_recv.at[s, b],
                device_id={CORE: other}, device_id_type=MESH)
            swap.start()
            load = pltpu.make_async_copy(source(s, b, core), own.at[s, :, :, b], load_sem.at[s, b])
            load.start()
            loads[s, b], swaps[s, b] = load, swap

    def remote(src, dst, s, k, axis, d):
        copy = pltpu.make_async_remote_copy(
            src_ref=src, dst_ref=dst, send_sem=send.at[s, k], recv_sem=recv.at[s, k],
            device_id={AX[axis]: rot(me[axis], d)}, device_id_type=MESH)
        copy.start()
        moves.append(copy)
        return copy

    flight = {}

    def begin(s):
        order = ORDERS[s % 3]
        i = me[order[0]]
        mine, inbox = own.at[s], first.at[s]
        for b in range(4):
            loads[s, b].wait()
            swaps[s, b].wait_recv()
        add_blocks(mine, [core_in.at[s]], (4, 4, 4))
        lo, hi = pl.ds(0, 2), pl.ds(2, 2)
        far = rot(i, 2)
        ax = order[0]
        flight[s, "a"] = (
            remote(halved(mine, order, far, lo), inbox.at[0, pl.ds(0, 2)], s, 0, ax, 1),
            remote(halved(mine, order, far, hi), inbox.at[0, pl.ds(2, 2)], s, 1, ax, 3),
        )
        flight[s, "b"] = (
            remote(halved(mine, order, rot(i, 1), hi), inbox.at[1, pl.ds(2, 2)], s, 2, ax, 1),
            remote(halved(mine, order, rot(i, 3), lo), inbox.at[2, pl.ds(0, 2)], s, 3, ax, 3),
        )

    def relay(s):
        order = ORDERS[s % 3]
        i = me[order[0]]
        mine, inbox = own.at[s], first.at[s]
        lo, hi = pl.ds(0, 2), pl.ds(2, 2)
        ax = order[0]
        flight[s, "a"][0].wait_recv()
        part = halved(mine, order, rot(i, 1), lo)
        add_blocks(part, [inbox.at[0, pl.ds(0, 2)]], (2, 4))
        c0 = remote(part, inbox.at[1, pl.ds(0, 2)], s, 4, ax, 1)
        flight[s, "a"][1].wait_recv()
        part = halved(mine, order, rot(i, 3), hi)
        add_blocks(part, [inbox.at[0, pl.ds(2, 2)]], (2, 4))
        c1 = remote(part, inbox.at[2, pl.ds(2, 2)], s, 5, ax, 3)
        flight[s, "b"] += (c0, c1)

    def middle(s):
        order = ORDERS[s % 3]
        mine = own.at[s]
        for copy in flight[s, "b"]:
            copy.wait_recv()
        i = me[order[0]]
        add_blocks(cell(mine, order, (i,)), [first.at[s, 1], first.at[s, 2]], (4, 4))
        ax = order[1]
        flight[s, 2] = [
            remote(cell(mine, order, (i, rot(me[ax], d))), second.at[s, k], s, 6 + k, ax, d)
            for k, d in enumerate(DIRECT)
        ]

    def last(s):
        order = ORDERS[s % 3]
        mine = own.at[s]
        for copy in flight[s, 2]:
            copy.wait_recv()
        at = (me[order[0]], me[order[1]])
        add_blocks(cell(mine, order, at), [second.at[s, k] for k in range(3)], (4,))
        ax = order[2]
        flight[s, 3] = [
            remote(cell(mine, order, (*at, rot(me[ax], d))), third.at[s, k], s, 9 + k, ax, d)
            for k, d in enumerate(DIRECT)
        ]

    def spread(s):
        for copy in flight[s, 3]:
            copy.wait_recv()
        done[s, me[2]] = own[s, me[0], me[1], me[2]] + third[s, 0] + third[s, 1] + third[s, 2]
        flight[s, 4] = [
            remote(done.at[s, me[2]], done.at[s, me[2]], s, 12 + k, 2, d)
            for k, d in enumerate(DIRECT)
        ]

    def finish(s):
        for copy in flight[s, 4]:
            copy.wait_recv()
        c = pl.ds(COLS * (s % 3), COLS)
        for b in range(4):
            if s < 3:
                out_down[24 * b : 24 * b + 24, c] = done[s, b]
            elif s < 6:
                out_up[:, pl.ds(768 * b + COLS * (s % 3), COLS)] = done[s, b]
            else:
                (out_o, out_q, out_k, out_v)[b][:, c] = done[s, b]

    vecs[0] = vec[...]
    vmoves = {}

    def vector_send(stage):
        if stage == 0:
            targets = [{CORE: other}]
        else:
            ax = stage - 1
            targets = [{AX[ax]: rot(me[ax], d)} for d in DIRECT]
        base = (0, 1, 4, 7)[stage]
        vmoves[stage] = []
        for k, target in enumerate(targets):
            copy = pltpu.make_async_remote_copy(
                src_ref=vecs.at[stage], dst_ref=vecs.at[5 + base + k],
                send_sem=vsend.at[base + k], recv_sem=vrecv.at[base + k],
                device_id=target, device_id_type=MESH)
            copy.start()
            vmoves[stage].append(copy)

    def vector_sum(stage):
        base = (0, 1, 4, 7)[stage]
        total = vecs[stage]
        for k, copy in enumerate(vmoves[stage]):
            copy.wait_recv()
            total = total + vecs[5 + base + k]
        vecs[stage + 1] = total

    G = [(0, 4, 8), (3, 7, 2), (6, 1, 5)]

    def run(step, g):
        for s in G[g]:
            step(s)

    vector_send(0)
    run(begin, 0)
    vector_sum(0)
    vector_send(1)
    run(relay, 0)
    run(begin, 1)
    run(middle, 0)
    vector_sum(1)
    vector_send(2)
    run(relay, 1)
    run(begin, 2)
    run(last, 0)
    run(middle, 1)
    run(relay, 2)
    run(spread, 0)
    vector_sum(2)
    vector_send(3)
    run(last, 1)
    run(middle, 2)
    run(finish, 0)
    run(spread, 1)
    run(last, 2)
    vector_sum(3)
    out_vec[...] = vecs[4]
    run(finish, 1)
    run(spread, 2)
    run(finish, 2)
    for copy in [*moves, *swaps.values(), *(c for cs in vmoves.values() for c in cs)]:
        copy.wait_send()


def reduce_grads(down, up, w_o, w_q, w_k, w_v, vec):
    f32 = jnp.float32
    shapes = [(96, 768), (24, 3072), (24, 768), (24, 768), (24, 768), (24, 768), (16, 768)]
    any_spec = pl.BlockSpec(memory_space=pl.ANY)
    vmem = pl.BlockSpec(memory_space=pltpu.VMEM)
    return pl.pallas_call(
        reduce_kernel,
        out_shape=[jax.ShapeDtypeStruct(s, f32) for s in shapes],
        in_specs=[any_spec] * 6 + [vmem],
        out_specs=[vmem] * 7,
        scratch_shapes=[
            pltpu.VMEM((SUBS, 4, 4, 4, 24, COLS), f32),
            pltpu.VMEM((SUBS, 4, 4, 4, 24, COLS), f32),
            pltpu.VMEM((SUBS, 3, 4, 4, 24, COLS), f32),
            pltpu.VMEM((SUBS, 3, 4, 24, COLS), f32),
            pltpu.VMEM((SUBS, 3, 24, COLS), f32),
            pltpu.VMEM((SUBS, 4, 24, COLS), f32),
            pltpu.VMEM((15, 16, 768), f32),
            pltpu.SemaphoreType.DMA((SUBS, 4)),
            pltpu.SemaphoreType.DMA((SUBS, 4)),
            pltpu.SemaphoreType.DMA((SUBS, 4)),
            pltpu.SemaphoreType.DMA((SUBS, 15)),
            pltpu.SemaphoreType.DMA((SUBS, 15)),
            pltpu.SemaphoreType.DMA((10,)),
            pltpu.SemaphoreType.DMA((10,)),
        ],
        compiler_params=pltpu.CompilerParams(
            collective_id=0, has_side_effects=True, vmem_limit_bytes=60 * 2**20
        ),
    )(
        down.reshape(4, 4, 2, 4, 24, 768),
        up.reshape(4, 4, 2, 24, 3072),
        *(w.reshape(4, 4, 2, 24, 768) for w in (w_o, w_q, w_k, w_v)),
        vec,
    )


def suffix_state(after, p, j):
    body = after[p, 64 * j : 64 * j + 64]
    row = jnp.broadcast_to(after[p, 128 + j : 129 + j], (64, 128))
    first = lax.broadcasted_iota(jnp.int32, (64, 128), 0) == 0
    return jnp.concatenate([body, jnp.where(first, row, 0.0)], axis=0)


def attend_back(p, qk_ref, v_ref, gn_ref, early_ref, late_ref, before, after, trigs, gates, grad_ref):
    causal, flipped = causal_masks()
    left = left_lanes(CHUNK)
    for c in range(2):
        rows = slice(CHUNK * c, CHUNK * c + CHUNK)
        query, keys, value = [], [], []
        for j in range(2):
            h = 2 * p + j
            head = at(h, 128)
            q, k, v, g = qk_ref[rows, head], qk_ref[rows, at(HEADS + h, 128)], v_ref[rows, head], gn_ref[rows, head]
            past = prefix_state(before, p, j)
            if c == 1:
                past = past + early_ref[h]
            future = suffix_state(after, p, j)
            if c == 0:
                future = future + late_ref[h]
            past_high, past_low = halves(past)
            next_high, next_low = halves(future)
            weight = jnp.where(causal, nt(g, v), 0.0).astype(BF16)
            gq = nn(weight, k) + nn(doubled(g), jnp.concatenate([past_high, past_low], axis=0))
            weight = jnp.where(flipped, nt(v, g), 0.0).astype(BF16)
            gk = nn(weight, q) + nn(doubled(v), jnp.concatenate([next_high, next_low], axis=0))
            weight = jnp.where(flipped, nt(k, q), 0.0).astype(BF16)
            gv = nn(weight, g) + nt(doubled(k), jnp.concatenate([next_high, next_low], axis=1))
            gq = gq * trigs[0, rows]
            gk = gk * trigs[1, rows]
            query.append(gq + swap_halves(gq))
            keys.append(gk + swap_halves(gk))
            value.append(gv)
        cols = at(p, 128)
        grad_ref[0, rows, cols] = (jnp.where(left, query[0], query[1]) * gates[0, rows, cols].astype(F32)).astype(BF16)
        grad_ref[1, rows, cols] = (jnp.where(left, keys[0], keys[1]) * gates[1, rows, cols].astype(F32)).astype(BF16)
        grad_ref[2, rows, cols] = jnp.where(left, value[0], swap_halves(value[1])).astype(BF16)


def last_kernel(x_ref, qk_ref, v_ref, gn_ref, early_ref, late_ref, before, after, trigs, gates, gone_ref, wq, wk, wv,
                tokens_ref, gw_q, gw_k, gw_v, vec_ref, grad_ref):
    def per_pair(p, carry):
        attend_back(p, qk_ref, v_ref, gn_ref, early_ref, late_ref, before, after, trigs, gates, grad_ref)
        return carry

    lax.fori_loop(0, PAIRS, per_pair, 0)
    vec_ref[...] = jnp.zeros_like(vec_ref)
    for i, out in enumerate((gw_q, gw_k, gw_v)):
        vec_ref[i : i + 1, :] = column(grad_ref[i].astype(F32))

        def product(n, carry):
            cols = at(n, 256)
            out[:, cols] = tn(x_ref[...], grad_ref[i, :, cols])
            return carry

        lax.fori_loop(0, WIDTH // 256, product, 0)

    def back(r, carry):
        rows = at(r, 128)
        total = gone_ref[rows]
        for i, w in enumerate((wq, wk, wv)):
            total = total + nt(grad_ref[i, rows], w[...])
        tokens_ref[rows] = total
        return carry

    lax.fori_loop(0, ROWS // 128, back, 0)


def plain_call(kernel, outs, args, specs=None, scratch=(), out_specs=None):
    vmem = pl.BlockSpec(memory_space=VMEM)
    return pl.pallas_call(
        kernel,
        out_shape=[jax.ShapeDtypeStruct(shape, dtype) for shape, dtype in outs],
        in_specs=specs or [vmem] * len(args),
        out_specs=out_specs or [vmem] * len(outs),
        scratch_shapes=list(scratch),
        compiler_params=pltpu.CompilerParams(vmem_limit_bytes=LIMIT),
    )(*args)


def on_device(tokens, lengths, w_query, b_query, w_key, b_key, w_value, b_value, w_out, b_out, gain_one, shift_one,
              w_up, b_up, w_down, b_down, gain_two, shift_two, cotangent):
    x = tokens[0]
    cot = cotangent[0]
    seq = lax.axis_index(SEQ)

    def row(v):
        return v.reshape(1, -1)

    vmem = pl.BlockSpec(memory_space=VMEM)
    smem = pl.BlockSpec(memory_space=pltpu.SMEM)
    anywhere = pl.BlockSpec(memory_space=pl.ANY)
    wide16, wide32 = ((ROWS, WIDTH), BF16), ((ROWS, WIDTH), F32)
    long16, heads16 = ((ROWS, HIDDEN), BF16), ((ROWS, 128 * HEADS), BF16)
    per_head = ((HEADS, 128, 128), F32)
    packed = ((PAIRS, 136, 128), F32)
    vector = ((16, WIDTH), F32)
    square = ((WIDTH, WIDTH), BF16)
    kept = [long16, heads16, ((2, ROWS, WIDTH), BF16), ((2, ROWS, 128), F32), per_head, packed, wide32, wide32, wide16,
            wide32, ((ROWS, 128), F32), wide16, long16, long16, wide32, wide16, wide16, vector]
    (qk, v, gates, trigs, early, before, ratio, inverse, mixed, normal, scale, normed, act, slope, back, gffn, block,
     vec) = pl.pallas_call(
        front_kernel,
        out_shape=[jax.ShapeDtypeStruct(*shape) for shape in kept],
        in_specs=[smem] + [vmem] * 10 + [anywhere] * 8,
        out_specs=[anywhere] * len(kept),
        scratch_shapes=[VMEM(*shape) for shape in (
            wide16, square, square, square, square, ((WIDTH, HIDDEN), BF16), ((HIDDEN, WIDTH), BF16), wide16,
            *kept, packed, ((HEADS, ROWS, 128), F32))]
        + [pltpu.SemaphoreType.DMA((8,)), pltpu.SemaphoreType.DMA((len(kept),))] + EXCHANGE_SCRATCH,
        compiler_params=pltpu.CompilerParams(collective_id=2, has_side_effects=True, vmem_limit_bytes=LIMIT),
    )(lengths, row(b_query), row(b_key), row(b_value), row(b_out), row(gain_one), row(shift_one), row(b_up),
      row(b_down), row(gain_two), row(shift_two), x, w_query, w_key, w_value, w_out, w_up, w_down, cot)
    gone, gn, after_state, late, gw_down, gw_up, gw_out, vec_one = plain_call(
        middle_kernel,
        [wide32, heads16, packed, per_head, ((HIDDEN, WIDTH), F32), ((WIDTH, HIDDEN), F32), ((WIDTH, WIDTH), F32), vector],
        [qk, ratio, inverse, mixed, normal, scale, normed, act, slope, back, gffn, w_out, w_up, row(gain_one), w_down],
        scratch=[VMEM(*wide16), VMEM(*wide32),
            VMEM((2, TILE, WIDTH), F32), VMEM((2, WIDTH, TILE), F32), pltpu.SemaphoreType.DMA((2, 2))],
        out_specs=[vmem] * 4 + [anywhere, anywhere, vmem, vmem])
    after = exchange(after_state, True)
    tokens_grad, gw_q, gw_k, gw_v, vec_two = plain_call(
        last_kernel,
        [wide32] + [((WIDTH, WIDTH), F32)] * 3 + [vector],
        [x, qk, v, gn, early, late, before, after, trigs, gates, gone, w_query, w_key, w_value],
        scratch=[VMEM((3, ROWS, WIDTH), BF16)])
    sum_down, sum_up, sum_out, sum_query, sum_key, sum_value, sums = reduce_grads(
        gw_down, gw_up, gw_out, gw_q, gw_k, gw_v, vec + vec_one + vec_two)
    small = lax.dynamic_slice(sums, (0, 24 * seq), (9, 24))
    wide = lax.dynamic_slice(sums[9:15, :TILE].reshape(-1), (96 * seq,), (96,))
    return (
        block[None], tokens_grad[None], sum_query, small[0], sum_key, small[1], sum_value, small[2],
        sum_out, small[3], small[4], small[5], sum_up, wide, sum_down, small[6], small[7], small[8],
    )


def solution(mesh):
    torus = Mesh(mesh.devices.reshape(4, 4, 2, mesh.shape["batch"]), (*SEQ, "batch"))
    rows, shares = P("batch", SEQ, None), P(SEQ, None)
    return jax.shard_map(
        on_device,
        mesh=torus,
        in_specs=(rows, P("batch")) + (P(),) * 16 + (rows,),
        out_specs=(rows, rows) + (shares, P(SEQ)) * 4 + (P(SEQ), P(SEQ)) + (shares, P(SEQ)) * 2 + (P(SEQ), P(SEQ)),
        check_vma=False,
    )
```

```python
import jax
import jax.numpy as jnp
from jax import lax
from jax.experimental import pallas as pl
from jax.experimental.pallas import tpu as pltpu
from jax.sharding import Mesh
from jax.sharding import PartitionSpec as P

SEQ = ("seq_0", "seq_1", "seq_2")
AX = ("seq_0", "seq_1", "batch")
CORE = "seq_2"
MESH = pl.DeviceIdType.MESH
DIRECT = (1, 3, 2)
F32 = jnp.float32
BF16 = jnp.bfloat16
HALF_PI = 1.5707963267948966
HALF_PI_REST = -4.371139000186241e-08
EPSILON = 1e-05
ROWS = 512
WIDTH = 768
HIDDEN = 3072
HEADS = 12
PAIRS = 6
CHUNK = 256
TILE = 512
VMEM = pltpu.VMEM
LIMIT = 60 * 2**20
BACK_LIMIT = 63 * 2**20


def nn(a, b):
    return jnp.dot(a, b, preferred_element_type=F32)


def nt(a, b):
    return lax.dot_general(a, b, (((1,), (1,)), ((), ())), preferred_element_type=F32)


def tn(a, b):
    return lax.dot_general(a, b, (((0,), (0,)), ((), ())), preferred_element_type=F32)


def at(k, size):
    return pl.ds(pl.multiple_of(k * size, size), size)


def rot(k, d):
    return lax.rem(k + d, 4)


def left_lanes(rows):
    return lax.broadcasted_iota(jnp.int32, (rows, 128), 1) < 64


def swap_halves(value):
    return pltpu.roll(value, 64, 1)


def doubled(value):
    return jnp.concatenate([value, value], axis=1)


def halves(value):
    high = value.astype(BF16)
    return high, (value - high.astype(F32)).astype(BF16)


SIN = (1.0, -0.1666666716337204, 0.008333330973982811, -0.00019840864115394652, 2.7525297809916083e-06, -2.3888299338636898e-08)


def sine(x):
    square = x * x
    value = SIN[5]
    for c in SIN[4::-1]:
        value = value * square + c
    return value * x


ERFCX = (
    0.22567586600780487, 0.2256695181131363, 0.2078438699245453, 0.1685338169336319, 0.14146119356155396,
    -0.005668365862220526, 0.16915558278560638, -0.18294405937194824, 0.05027270317077637,
)


def normal_parts(p):
    bell = jnp.exp(-0.5 * p * p)
    t = 1.0 / (1.0 + (0.4 * 0.7071067811865476) * jnp.abs(p))
    value = 0.5 * ERFCX[8]
    for c in ERFCX[7::-1]:
        value = value * t + 0.5 * c
    tail = value * t * bell
    return jnp.where(p >= 0, 1.0 - tail, tail), 0.3989422804014327 * bell


def trig_block(first, rows, length):
    position = first + lax.broadcasted_iota(jnp.int32, (rows, 128), 0)
    size = lax.broadcast_in_dim(length, (rows, 128), ()).astype(F32)
    angle = HALF_PI * jnp.minimum(position + 1, length).astype(F32) / size
    both = sine(jnp.where(left_lanes(rows), (HALF_PI - angle) + HALF_PI_REST, angle))
    return both, (position < length).astype(F32)


def project_keys(n, x_ref, wk, bk, wv, bv, qk_ref, v_ref, gate_k, valid_ref):
    cols = at(n, 256)
    left = left_lanes(ROWS)
    x = x_ref[...]
    u = (nn(x, wv[:, cols]) + bv[:, cols]).astype(BF16).astype(F32)
    for j in range(2):
        part = u[:, 128 * j : 128 * j + 128]
        v_ref[:, at(4 * n + 2 * j, 128)] = jnp.where(left, part, 1.0).astype(BF16)
        v_ref[:, at(4 * n + 2 * j + 1, 128)] = jnp.where(left, swap_halves(part), 1.0).astype(BF16)
    project_soft(n, HEADS, x, wk, bk, qk_ref, gate_k, valid_ref)


def project_soft(n, first, x, w, b, out, gate, table):
    cols = at(n, 256)
    left = left_lanes(ROWS)
    u = nn(x, w[:, cols]) + b[:, cols]
    small = jnp.exp(-jnp.abs(u))
    soft = jnp.maximum(u, 0.0) + jnp.log1p(small)
    gate[:, cols] = (jnp.where(u >= 0, 1.0, small) / (1.0 + small)).astype(BF16)
    trig = table[...]
    for j in range(2):
        part = soft[:, 128 * j : 128 * j + 128]
        other = swap_halves(part)
        out[:, at(first + 4 * n + 2 * j, 128)] = (jnp.where(left, part, other) * trig).astype(BF16)
        out[:, at(first + 4 * n + 2 * j + 1, 128)] = (jnp.where(left, other, part) * trig).astype(BF16)


def state_sums(p, qk_ref, v_ref, state_ref, early_ref):
    for j in range(2):
        h = 2 * p + j
        keys, values = at(HEADS + h, 128), at(h, 128)
        early = tn(v_ref[0:CHUNK, values], qk_ref[0:CHUNK, keys])
        early_ref[h] = early
        both = early + tn(v_ref[CHUNK:ROWS, values], qk_ref[CHUNK:ROWS, keys])
        state_ref[p, 64 * j : 64 * j + 64] = both[0:64]
        state_ref[p, 128 + j : 129 + j] = both[64:65]
    state_ref[p, 130:136] = jnp.zeros((6, 128), F32)


def exchange_steps(pay, out, core_in, chip, give, head, tail, total, msgs, xa, ya, yb, xb, send, recv, reverse):
    my, mx = lax.axis_index("seq_0"), lax.axis_index("seq_1")
    core = lax.axis_index(CORE)
    other = 1 - core
    moves = []

    def remote(src, dst, k, target):
        copy = pltpu.make_async_remote_copy(
            src_ref=src, dst_ref=dst, send_sem=send.at[k], recv_sem=recv.at[k],
            device_id=target, device_id_type=MESH)
        copy.start()
        moves.append(copy)
        return copy

    def counts(theirs, mine):
        return theirs > mine if reverse else theirs < mine

    def chosen(flag, value):
        return jnp.where(flag, value, jnp.zeros_like(value))

    def first():
        return remote(pay.at[pl.ds(3 * other, 3)], core_in, 0, {CORE: other})

    def second(copy):
        copy.wait_recv()
        for p in range(3):
            chip[p] = pay[3 * core + p] + core_in[p]
        a = [remote(chip.at[:, pl.ds(0, 72)], xa.at[k], 1 + k, {"seq_1": rot(mx, d)}) for k, d in enumerate(DIRECT)]
        b = [remote(chip.at[:, pl.ds(72, 64)], yb.at[k], 4 + k, {"seq_0": rot(my, d)}) for k, d in enumerate(DIRECT)]
        return a, b

    def third(copies):
        a, b = copies
        for copy in a:
            copy.wait_recv()
        for p in range(3):
            some = jnp.zeros((72, 128), F32)
            every = chip[p, 0:72]
            for k, d in enumerate(DIRECT):
                piece = xa[k, p]
                some = some + chosen(counts(rot(mx, 4 - d), mx), piece)
                every = every + piece
            head[p] = some
            total[p] = every
        a = [remote(total, ya.at[k], 7 + k, {"seq_0": rot(my, d)}) for k, d in enumerate(DIRECT)]
        for copy in b:
            copy.wait_recv()
        for p in range(3):
            some = jnp.zeros((64, 128), F32)
            for k, d in enumerate(DIRECT):
                some = some + chosen(counts(rot(my, 4 - d), my), yb[k, p])
            tail[p] = some
            own = chip[p, 72:136]
            for k, d in enumerate(DIRECT):
                msgs[k, p] = some + chosen(counts(mx, rot(mx, d)), own)
        b = [remote(msgs.at[k], xb.at[k], 10 + k, {"seq_1": rot(mx, d)}) for k, d in enumerate(DIRECT)]
        return a, b

    def fourth(copies):
        a, b = copies
        for copy in a:
            copy.wait_recv()
        for copy in b:
            copy.wait_recv()
        mine = core == (0 if reverse else 1)
        for p in range(3):
            low, high = head[p], tail[p]
            for k, d in enumerate(DIRECT):
                low = low + chosen(counts(rot(my, 4 - d), my), ya[k, p])
                high = high + xb[k, p]
            own = 3 * core + p
            out[own, 0:72] = low + chosen(mine, core_in[p, 0:72])
            out[own, 72:136] = high + chosen(mine, core_in[p, 72:136])
            give[p, 0:72] = low + chosen(jnp.logical_not(mine), pay[own, 0:72])
            give[p, 72:136] = high + chosen(jnp.logical_not(mine), pay[own, 72:136])
        return remote(give, out.at[pl.ds(3 * core, 3)], 13, {CORE: other})

    def fifth(copy):
        copy.wait_recv()
        for move in moves:
            move.wait_send()

    return first, second, third, fourth, fifth


EXCHANGE_SCRATCH = [
    VMEM((3, 136, 128), F32),
    VMEM((3, 136, 128), F32),
    VMEM((3, 136, 128), F32),
    VMEM((3, 72, 128), F32),
    VMEM((3, 64, 128), F32),
    VMEM((3, 72, 128), F32),
    VMEM((3, 3, 64, 128), F32),
    VMEM((3, 3, 72, 128), F32),
    VMEM((3, 3, 72, 128), F32),
    VMEM((3, 3, 64, 128), F32),
    VMEM((3, 3, 64, 128), F32),
    pltpu.SemaphoreType.DMA((14,)),
    pltpu.SemaphoreType.DMA((14,)),
]


def greet(axes):
    barrier = pltpu.get_barrier_semaphore()
    core = lax.axis_index(CORE)
    pl.semaphore_signal(barrier, inc=1, device_id={CORE: 1 - core}, device_id_type=MESH)
    for axis in axes:
        mine = lax.axis_index(axis)
        for d in DIRECT:
            pl.semaphore_signal(barrier, inc=1, device_id={axis: rot(mine, d)}, device_id_type=MESH)


def greeted(axes):
    pl.semaphore_wait(pltpu.get_barrier_semaphore(), 1 + 3 * len(axes))


def causal_masks():
    row = lax.broadcasted_iota(jnp.int32, (CHUNK, CHUNK), 0)
    col = lax.broadcasted_iota(jnp.int32, (CHUNK, CHUNK), 1)
    return row >= col, row <= col


def prefix_state(before, p, j):
    body = before[p, 64 * j : 64 * j + 64]
    return jnp.concatenate([body, jnp.broadcast_to(before[p, 128 + j : 129 + j], (64, 128))], axis=0)


def attend_local(p, qk_ref, v_ref, num_ref):
    causal, _ = causal_masks()
    for c in range(2):
        rows = slice(CHUNK * c, CHUNK * c + CHUNK)
        for j in range(2):
            h = 2 * p + j
            weight = nt(qk_ref[rows, at(h, 128)], qk_ref[rows, at(HEADS + h, 128)])
            num_ref[h, rows] = nn(jnp.where(causal, weight, 0.0).astype(BF16), v_ref[rows, at(h, 128)])


def attend_earlier(p, qk_ref, num_ref, early_ref, before, ratio_ref, inverse_ref, mixed_ref):
    left = left_lanes(CHUNK)
    cols = at(p, 128)
    for c in range(2):
        rows = slice(CHUNK * c, CHUNK * c + CHUNK)
        sums = []
        for j in range(2):
            h = 2 * p + j
            state = prefix_state(before, p, j)
            if c == 1:
                state = state + early_ref[h]
            high, low = halves(state)
            q = qk_ref[rows, at(h, 128)]
            sums.append(num_ref[h, rows] + nt(doubled(q), jnp.concatenate([high, low], axis=1)))
        even, odd = sums
        top = jnp.where(left, even, swap_halves(odd))
        inverse = 1.0 / jnp.where(left, swap_halves(even), odd)
        ratio = top * inverse
        ratio_ref[rows, cols] = ratio
        inverse_ref[rows, cols] = inverse
        mixed_ref[rows, cols] = ratio.astype(BF16)


def mean_rows(value):
    return jnp.mean(value, axis=-1, keepdims=True)


def standard(hidden):
    centred = hidden - mean_rows(hidden)
    scale = lax.rsqrt(mean_rows(centred * centred) + EPSILON)
    return centred * scale, scale


def norm_back(grad, normal, scale, gain):
    scaled = grad * gain
    return scale * (scaled - mean_rows(scaled) - normal * mean_rows(scaled * normal))


def column(value):
    return jnp.sum(value, axis=0, keepdims=True)


def front_kernel(len_ref, bq, bk, bv, bo, gain1, shift1, bup, bdown, gain2, shift2,
                 x_hbm, wq_hbm, wk_hbm, wv_hbm, wo_hbm, wup_hbm, wdown_hbm, cot_hbm,
                 qk_out, v_out, gates_out, trigs_out, early_out, before_out, ratio_out, inverse_out, mixed_out,
                 normal_out, scale_out, normed_out, act_out, slope_out, back_out, gffn_out, block_out, vec_out,
                 x_ref, wq, wk, wv, wo, wup, wdown, cot_ref,
                 qk_ref, v_ref, gates, trigs, early_ref, before, ratio_ref, inverse_ref, mixed_ref,
                 normal_ref, scale_ref, normed_ref, act_ref, slope_ref, acc_ref, gffn_ref, block_ref, vec_ref,
                 state_ref, num_ref, load_sem, store_sem, *scratch):
    greet(("seq_0", "seq_1"))
    pairs = ((x_hbm, x_ref), (wk_hbm, wk), (wv_hbm, wv), (wq_hbm, wq), (wo_hbm, wo), (wup_hbm, wup),
             (wdown_hbm, wdown), (cot_hbm, cot_ref))
    loads = [pltpu.make_async_copy(src, dst, load_sem.at[k]) for k, (src, dst) in enumerate(pairs)]
    for load in loads:
        load.start()
    stores = []

    def store(src, dst):
        copy = pltpu.make_async_copy(src, dst, store_sem.at[len(stores)])
        copy.start()
        stores.append(copy)

    length = len_ref[0]
    start = ROWS * ((lax.axis_index("seq_0") * 4 + lax.axis_index("seq_1")) * 2 + lax.axis_index(CORE))

    def angles(r, carry):
        both, valid = trig_block(start + 128 * r, 128, length)
        trigs[0, at(r, 128)] = both
        trigs[1, at(r, 128)] = both * valid
        return carry

    lax.fori_loop(0, ROWS // 128, angles, 0)
    store(trigs, trigs_out)
    for k in range(3):
        loads[k].wait()

    def keys(n, carry):
        project_keys(n, x_ref, wk, bk, wv, bv, qk_ref, v_ref, gates.at[1], trigs.at[1])
        return carry

    lax.fori_loop(0, WIDTH // 256, keys, 0)

    def states(p, carry):
        state_sums(p, qk_ref, v_ref, state_ref, early_ref)
        return carry

    lax.fori_loop(0, PAIRS, states, 0)
    store(v_ref, v_out)
    store(early_ref, early_out)
    greeted(("seq_0", "seq_1"))
    first, second, third, fourth, fifth = exchange_steps(state_ref, before, *scratch, False)
    stage = first()
    loads[3].wait()

    def queries(n, carry):
        project_soft(n, 0, x_ref[...], wq, bq, qk_ref, gates.at[0], trigs.at[0])
        return carry

    def local(p, carry):
        attend_local(p, qk_ref, v_ref, num_ref)
        return carry

    lax.fori_loop(0, 1, queries, 0)
    stage = second(stage)
    lax.fori_loop(1, WIDTH // 256, queries, 0)
    store(qk_ref, qk_out)
    store(gates, gates_out)
    lax.fori_loop(0, 3, local, 0)
    stage = third(stage)
    lax.fori_loop(3, PAIRS, local, 0)
    stage = fourth(stage)
    fifth(stage)
    store(before, before_out)

    def earlier(p, carry):
        attend_earlier(p, qk_ref, num_ref, early_ref, before, ratio_ref, inverse_ref, mixed_ref)
        return carry

    lax.fori_loop(0, PAIRS, earlier, 0)
    store(ratio_ref, ratio_out)
    store(inverse_ref, inverse_out)
    store(mixed_ref, mixed_out)
    vec_ref[...] = jnp.zeros_like(vec_ref)

    def note(k, value):
        vec_ref[k : k + 1, :] += value

    loads[4].wait()

    def first_norm(r, carry):
        rows = at(r, 128)
        hidden = x_ref[rows].astype(F32) + (nn(mixed_ref[rows], wo[...]) + bo[...])
        normal, scale = standard(hidden)
        normal_ref[rows] = normal
        scale_ref[rows] = jnp.broadcast_to(scale, (128, 128))
        normed_ref[rows] = (normal * gain1[...] + shift1[...]).astype(BF16)
        return carry

    lax.fori_loop(0, ROWS // 128, first_norm, 0)
    store(normal_ref, normal_out)
    store(scale_ref, scale_out)
    store(normed_ref, normed_out)
    loads[5].wait()
    loads[6].wait()

    def feed(t, carry):
        cols = at(t, TILE)
        for r in range(2):
            rows = slice(CHUNK * r, CHUNK * r + CHUNK)
            pre = nn(normed_ref[rows], wup[:, cols]) + bup[:, cols]
            whole, bell = normal_parts(pre)
            act = (pre * whole).astype(BF16)
            act_ref[rows, cols] = act
            slope_ref[rows, cols] = (whole + pre * bell).astype(BF16)
            part = nn(act, wdown[cols])
            acc_ref[rows] = part + jnp.where(t == 0, 0.0, acc_ref[rows])
        return carry

    lax.fori_loop(0, HIDDEN // TILE, feed, 0)
    store(act_ref, act_out)
    store(slope_ref, slope_out)
    loads[7].wait()

    def second_norm(r, carry):
        rows = at(r, 128)
        hidden = normed_ref[rows].astype(F32) + (acc_ref[rows] + bdown[...])
        normal, scale = standard(hidden)
        block_ref[rows] = (normal * gain2[...] + shift2[...]).astype(BF16)
        grad = cot_ref[rows].astype(F32)
        note(7, column(grad * normal))
        note(8, column(grad))
        back = norm_back(grad, normal, scale, gain2[...])
        acc_ref[rows] = back
        low = back.astype(BF16)
        gffn_ref[rows] = low
        note(6, column(low.astype(F32)))
        return carry

    lax.fori_loop(0, ROWS // 128, second_norm, 0)
    store(gffn_ref, gffn_out)
    store(acc_ref, back_out)
    store(block_ref, block_out)
    store(vec_ref, vec_out)
    for copy in stores:
        copy.wait()


ORDERS = ((1, 0, 2), (0, 2, 1), (2, 1, 0))
SUBS = 9
COLS = 256


def cell(ref, order, picks):
    at = [slice(None)] * 3
    for axis, pick in zip(order, picks):
        at[axis] = pick
    return ref.at[tuple(at)]


def halved(ref, order, pick, half):
    at = [slice(None)] * 3
    at[order[0]] = pick
    at[1 if order[0] == 0 else 0] = half
    return ref.at[tuple(at)]


def add_blocks(dst, srcs, lead):
    total = 1
    for n in lead:
        total *= n

    def step(k, carry):
        where, rest = [], k
        for n in reversed(lead):
            where.append(lax.rem(rest, n))
            rest = rest // n
        where = tuple(reversed(where))
        value = dst[where]
        for src in srcs:
            value = value + src[where]
        dst[where] = value
        return carry

    lax.fori_loop(0, total, step, 0)


GROUPS = ((0, 0, 256), (1, 0, 256), (0, 0, 128), (0, 128, 128))
DONE = (0, 1, 2, 2)


class Reduction:
    def __init__(self, stage, sums, first, second, third, done, core_send, core_recv, send, recv):
        self.stage, self.sums, self.first, self.second, self.third, self.done = stage, sums, first, second, third, done
        self.core_send, self.core_recv, self.send, self.recv = core_send, core_recv, send, recv
        self.me = tuple(lax.axis_index(a) for a in AX)
        self.core = lax.axis_index(CORE)
        self.other = 1 - self.core
        self.moves, self.flight = {0: [], 1: [], 2: [], 3: []}, {}

    def swap(self, g, s, part):
        slot, start, width = GROUPS[g]
        where = (part,) if g == 0 else (slice(None), slice(None), part, slice(None), pl.ds(start, width))
        return pltpu.make_async_remote_copy(
            src_ref=self.stage.at[(s, self.other, *where)], dst_ref=self.sums.at[(slot, s, *where)],
            send_sem=self.core_send.at[g, s, part], recv_sem=self.core_recv.at[g, s, part],
            device_id={CORE: self.other}, device_id_type=MESH)

    def remote(self, src, dst, g, s, k, axis, d):
        copy = pltpu.make_async_remote_copy(
            src_ref=src, dst_ref=dst, send_sem=self.send.at[g, s, k], recv_sem=self.recv.at[g, s, k],
            device_id={AX[axis]: rot(self.me[axis], d)}, device_id_type=MESH)
        copy.start()
        self.moves[g].append(copy)
        return copy

    def views(self, g, s):
        slot, start, width = GROUPS[g]
        cols = pl.ds(start, width)
        return (self.sums.at[slot, s, :, :, :, :, cols], self.first.at[slot, s, :, :, :, :, cols],
                self.second.at[slot, s, :, :, :, cols], self.third.at[slot, s, :, :, cols],
                self.done.at[DONE[g], s, :, :, cols], self.stage.at[s, self.core, :, :, :, :, cols])

    def begin(self, g, s):
        mine, inbox, _, _, _, own = self.views(g, s)
        for part in range(4):
            copy = self.swap(g, s, part)
            copy.wait_recv()
            copy.wait_send()
        add_blocks(mine, [own], (4, 4))
        order = ORDERS[s]
        ax = order[0]
        i = self.me[ax]
        lo, hi = pl.ds(0, 2), pl.ds(2, 2)
        far = rot(i, 2)
        self.flight[g, s, 0] = (
            self.remote(halved(mine, order, far, lo), inbox.at[0, lo], g, s, 0, ax, 1),
            self.remote(halved(mine, order, far, hi), inbox.at[0, hi], g, s, 1, ax, 3),
        )
        self.flight[g, s, 1] = (
            self.remote(halved(mine, order, rot(i, 1), hi), inbox.at[1, hi], g, s, 2, ax, 1),
            self.remote(halved(mine, order, rot(i, 3), lo), inbox.at[2, lo], g, s, 3, ax, 3),
        )

    def relay(self, g, s):
        mine, inbox = self.views(g, s)[:2]
        order = ORDERS[s]
        ax = order[0]
        i = self.me[ax]
        lo, hi = pl.ds(0, 2), pl.ds(2, 2)
        first, second = self.flight[g, s, 0]
        first.wait_recv()
        part = halved(mine, order, rot(i, 1), lo)
        add_blocks(part, [inbox.at[0, lo]], (2, 4))
        third = self.remote(part, inbox.at[1, lo], g, s, 4, ax, 1)
        second.wait_recv()
        part = halved(mine, order, rot(i, 3), hi)
        add_blocks(part, [inbox.at[0, hi]], (2, 4))
        fourth = self.remote(part, inbox.at[2, hi], g, s, 5, ax, 3)
        self.flight[g, s, 1] += (third, fourth)

    def middle(self, g, s):
        mine, inbox, second = self.views(g, s)[:3]
        order = ORDERS[s]
        for copy in self.flight[g, s, 1]:
            copy.wait_recv()
        i, ax = self.me[order[0]], order[1]
        add_blocks(cell(mine, order, (i,)), [inbox.at[1], inbox.at[2]], (4,))
        self.flight[g, s, 2] = [
            self.remote(cell(mine, order, (i, rot(self.me[ax], d))), second.at[k], g, s, 6 + k, ax, d)
            for k, d in enumerate(DIRECT)
        ]

    def last(self, g, s):
        mine, _, second, third = self.views(g, s)[:4]
        order = ORDERS[s]
        for copy in self.flight[g, s, 2]:
            copy.wait_recv()
        where = (self.me[order[0]], self.me[order[1]])
        add_blocks(cell(mine, order, where), [second.at[k] for k in range(3)], (4,))
        ax = order[2]
        self.flight[g, s, 3] = [
            self.remote(cell(mine, order, (*where, rot(self.me[ax], d))), third.at[k], g, s, 9 + k, ax, d)
            for k, d in enumerate(DIRECT)
        ]

    def spread(self, g, s):
        mine, _, _, third, done = self.views(g, s)[:5]
        for copy in self.flight[g, s, 3]:
            copy.wait_recv()
        y, x, z = self.me
        done[z] = mine[y, x, z] + third[0] + third[1] + third[2]
        self.flight[g, s, 4] = [
            self.remote(done.at[z], done.at[z], g, s, 12 + k, 2, d) for k, d in enumerate(DIRECT)
        ]

    def finish(self, g, s):
        for copy in self.flight[g, s, 4]:
            copy.wait_recv()

    def sent(self, g):
        for copy in self.moves[g]:
            copy.wait_send()

    def each(self, step, g):
        for s in range(3):
            step(g, s)


def vector_steps(vec, vecs, send, recv):
    me = tuple(lax.axis_index(a) for a in AX)
    core = lax.axis_index(CORE)
    moves = {}
    bases = (0, 1, 4, 7)

    def start(stage):
        if stage == 0:
            targets = [{CORE: 1 - core}]
            vecs[0] = vec[...]
        else:
            ax = stage - 1
            targets = [{AX[ax]: rot(me[ax], d)} for d in DIRECT]
        moves[stage] = []
        for k, target in enumerate(targets):
            n = bases[stage] + k
            copy = pltpu.make_async_remote_copy(
                src_ref=vecs.at[stage], dst_ref=vecs.at[5 + n], send_sem=send.at[n], recv_sem=recv.at[n],
                device_id=target, device_id_type=MESH)
            copy.start()
            moves[stage].append(copy)

    def end(stage):
        total = vecs[stage]
        for k, copy in enumerate(moves[stage]):
            copy.wait_recv()
            total = total + vecs[5 + bases[stage] + k]
        vecs[stage + 1] = total

    def sent():
        for copies in moves.values():
            for copy in copies:
                copy.wait_send()

    return start, end, sent


def suffix_state(after, p, j):
    body = after[p, 64 * j : 64 * j + 64]
    row = jnp.broadcast_to(after[p, 128 + j : 129 + j], (64, 128))
    first = lax.broadcasted_iota(jnp.int32, (64, 128), 0) == 0
    return jnp.concatenate([body, jnp.where(first, row, 0.0)], axis=0)


def attend_back_local(p, act, bufu, early_ref, before, trigs, ratio_ref, inverse_ref, grads):
    causal, flipped = causal_masks()
    left = left_lanes(CHUNK)
    for c in range(2):
        rows = slice(CHUNK * c, CHUNK * c + CHUNK)
        query, keys, value = [], [], []
        for j in range(2):
            h = 2 * p + j
            q, k = bufu[rows, at(h, 128)], bufu[rows, at(HEADS + h, 128)]
            v, g = act[rows, at(h, 128)], act[rows, at(HEADS + h, 128)]
            past = prefix_state(before, p, j)
            if c == 1:
                past = past + early_ref[h]
            high, low = halves(past)
            weight = jnp.where(causal, nt(g, v), 0.0).astype(BF16)
            gq = nn(weight, k) + nn(doubled(g), jnp.concatenate([high, low], axis=0))
            weight = jnp.where(flipped, nt(v, g), 0.0).astype(BF16)
            gk = nn(weight, q)
            weight = jnp.where(flipped, nt(k, q), 0.0).astype(BF16)
            value.append(nn(weight, g))
            gq = gq * trigs[0, rows]
            gk = gk * trigs[1, rows]
            query.append(gq + swap_halves(gq))
            keys.append(gk + swap_halves(gk))
        cols = at(p, 128)
        gate = bufu[ROWS:WIDTH, at(PAIRS * c + p, 128)].astype(F32)
        grads[rows, cols] = (jnp.where(left, query[0], query[1]) * gate).astype(BF16)
        ratio_ref[rows, cols] = jnp.where(left, keys[0], keys[1])
        inverse_ref[rows, cols] = jnp.where(left, value[0], swap_halves(value[1]))


def attend_back_later(p, act, bufu, late_ref, after, trigs, ratio_ref, inverse_ref, grads):
    left = left_lanes(CHUNK)
    for c in range(2):
        rows = slice(CHUNK * c, CHUNK * c + CHUNK)
        keys, value = [], []
        for j in range(2):
            h = 2 * p + j
            k, v = bufu[rows, at(HEADS + h, 128)], act[rows, at(h, 128)]
            future = suffix_state(after, p, j)
            if c == 0:
                future = future + late_ref[h]
            high, low = halves(future)
            gk = nn(doubled(v), jnp.concatenate([high, low], axis=0)) * trigs[1, rows]
            keys.append(gk + swap_halves(gk))
            value.append(nt(doubled(k), jnp.concatenate([high, low], axis=1)))
        cols = at(p, 128)
        gate = bufu[ROWS:WIDTH, at(2 * PAIRS + PAIRS * c + p, 128)].astype(F32)
        gk = (ratio_ref[rows, cols] + jnp.where(left, keys[0], keys[1])) * gate
        grads[rows, at(PAIRS + p, 128)] = gk.astype(BF16)
        gv = inverse_ref[rows, cols] + jnp.where(left, value[0], swap_halves(value[1]))
        grads[rows, at(2 * PAIRS + p, 128)] = gv.astype(BF16)


def back_kernel(gain1, qk_hbm, v_hbm, gates_hbm, trigs_hbm, early_hbm, before_hbm, ratio_hbm, inverse_hbm, mixed_hbm,
                normal_hbm, scale_hbm, normed_hbm, act_hbm, slope_hbm, back_hbm, gffn_hbm, vec_hbm,
                x_hbm, wq_hbm, wk_hbm, wv_hbm, wo_hbm, wup_hbm, wdown_hbm,
                tokens_out, done_out, vec_out,
                trigs, early_ref, before, ratio_ref, inverse_ref, mixed_ref, normal_ref, scale_ref, normed_ref,
                act, slope, acc_ref, gffn_ref, vec_ref, wo, bufu, bufd,
                late_ref, pay, after, turned, stage, sums, first_in, second_in, third_in, done, vecs,
                load_sem, store_sem, core_send, core_recv, send, recv, vec_send, vec_recv, free_sem, *scratch):
    everywhere = ("seq_0", "seq_1", "batch")
    greet(everywhere)
    loads = {}

    def load(name, src, dst):
        copy = pltpu.make_async_copy(src, dst, load_sem.at[len(loads)])
        copy.start()
        loads[name] = copy

    def ready(*names):
        for name in names:
            loads[name].wait()

    load("gffn", gffn_hbm, gffn_ref)
    load("act", act_hbm, act)
    load("wdown", wdown_hbm, bufd)
    load("slope", slope_hbm, slope)
    load("wup", wup_hbm, bufu)
    load("back", back_hbm, acc_ref)
    load("vec", vec_hbm, vec_ref)
    load("normed", normed_hbm, normed_ref)
    load("normal", normal_hbm, normal_ref)
    load("scale", scale_hbm, scale_ref)
    load("wo", wo_hbm, wo)
    load("mixed", mixed_hbm, mixed_ref)
    load("ratio", ratio_hbm, ratio_ref)
    load("inverse", inverse_hbm, inverse_ref)
    load("early", early_hbm, early_ref)
    load("before", before_hbm, before)
    load("trigs", trigs_hbm, trigs)
    red = Reduction(stage, sums, first_in, second_in, third_in, done, core_send, core_recv, send, recv)

    def note(k, value):
        vec_ref[k : k + 1, :] += value

    ready("gffn", "act")
    greeted(everywhere)

    def down_rows(y, carry):
        turned[...] = act[:, at(y, WIDTH)].T
        for s in range(3):
            value = nn(turned[...], gffn_ref[:, 256 * s : 256 * s + 256]).reshape(4, 2, 4, 24, 256)
            for side in range(2):
                stage[s, side, y] = value[:, side]
            red.swap(0, s, y).start()
        return carry

    lax.fori_loop(0, 4, down_rows, 0)
    ready("wdown", "slope", "wup", "back", "vec")

    def feed_back(t, carry):
        cols = at(t, WIDTH)
        gpre = (nt(gffn_ref[...], bufd[cols]) * slope[:, cols].astype(F32)).astype(BF16)
        slope[:, cols] = gpre
        vec_ref[pl.ds(9 + t, 1), :] = column(gpre.astype(F32))
        acc_ref[...] += nt(gpre, bufu[:, cols])
        return carry

    lax.fori_loop(0, 2, feed_back, 0)
    red.begin(0, 0)
    lax.fori_loop(2, 3, feed_back, 0)
    red.begin(0, 1)
    lax.fori_loop(3, 4, feed_back, 0)
    red.begin(0, 2)
    load("wq", wq_hbm, bufd.at[0:WIDTH])
    load("wk", wk_hbm, bufd.at[WIDTH : 2 * WIDTH])
    load("wv", wv_hbm, bufd.at[2 * WIDTH : 3 * WIDTH])
    load("x", x_hbm, bufd.at[3 * WIDTH : 3 * WIDTH + ROWS])
    load("qk", qk_hbm, bufu.at[0:ROWS])
    load("v", v_hbm, act.at[:, 0 : 128 * HEADS])
    for i in range(2):
        for c in range(2):
            load(f"gate{i}{c}", gates_hbm.at[i, CHUNK * c : CHUNK * c + CHUNK],
                 bufu.at[ROWS:WIDTH, pl.ds(2 * WIDTH * i + WIDTH * c, WIDTH)])
    ready("normal", "scale", "wo")

    def first_back(r, carry):
        rows = at(r, 128)
        normal = normal_ref[rows]
        scale = scale_ref[rows, 0:1]
        grad = acc_ref[rows]
        note(4, column(grad * normal))
        note(5, column(grad))
        back = norm_back(grad, normal, scale, gain1[...])
        acc_ref[rows] = back
        low = back.astype(BF16)
        gffn_ref[rows] = low
        note(3, column(low.astype(F32)))
        normal_ref[rows] = nt(low, wo[...])
        return carry

    lax.fori_loop(0, ROWS // 128, first_back, 0)
    ready("ratio", "inverse", "qk")

    def heads_back(p, carry):
        cols = at(p, 128)
        lane = lax.broadcasted_iota(jnp.int32, (ROWS, 128), 1)
        left = lane < 64
        gnum = (normal_ref[:, cols] * inverse_ref[:, cols]).astype(BF16).astype(F32)
        product = gnum * ratio_ref[:, cols]
        for j in range(2):
            h = 2 * p + j
            mine = jnp.where(left, product, 0.0) if j == 0 else jnp.where(left, 0.0, product)
            gden = jnp.broadcast_to(-jnp.sum(mine, axis=1, keepdims=True), (ROWS, 128))
            high = gden.astype(BF16).astype(F32)
            ends = jnp.where(lane == 64, high, jnp.where(lane == 65, gden - high, 0.0))
            grad = jnp.where(left, gnum if j == 0 else swap_halves(gnum), ends).astype(BF16)
            act[:, at(HEADS + h, 128)] = grad
            late = tn(grad[CHUNK:ROWS], bufu[CHUNK:ROWS, at(h, 128)])
            late_ref[h] = late
            both = late + tn(grad[0:CHUNK], bufu[0:CHUNK, at(h, 128)])
            pay[p, 64 * j : 64 * j + 64] = both[0:64]
            pay[p, 128 + j : 129 + j] = both[64:65] + both[65:66]
        pay[p, 130:136] = jnp.zeros((6, 128), F32)
        return carry

    lax.fori_loop(0, PAIRS, heads_back, 0)
    first, second, third, fourth, fifth = exchange_steps(pay, after, *scratch, True)
    step = first()
    red.each(red.relay, 0)
    ready("normed", "mixed")
    turned[...] = normed_ref[...].T

    def up_columns(b, carry):
        for s in range(3):
            cols = pl.ds(pl.multiple_of(WIDTH * b + 256 * s, 256), 256)
            value = nn(turned[...], slope[:, cols]).reshape(4, 4, 2, 24, 256)
            for side in range(2):
                stage[s, side, :, :, b] = value[:, :, side]
            red.swap(1, s, b).start()
        return carry

    lax.fori_loop(0, 1, up_columns, 0)
    step = second(step)
    lax.fori_loop(1, 4, up_columns, 0)
    red.each(red.middle, 0)
    step = third(step)
    ready("v", "early", "before", "trigs", "gate00", "gate01", "gate10", "gate11")

    def local(p, carry):
        attend_back_local(p, act, bufu, early_ref, before, trigs, ratio_ref, inverse_ref, slope)
        return carry

    lax.fori_loop(0, 2, local, 0)
    red.each(red.last, 0)
    red.begin(1, 0)
    lax.fori_loop(2, 4, local, 0)
    red.each(red.spread, 0)
    red.begin(1, 1)
    red.begin(1, 2)
    step = fourth(step)
    lax.fori_loop(4, 6, local, 0)
    red.each(red.finish, 0)
    red.sent(0)
    axes_of = ((CORE, (1,)),) + tuple((a, DIRECT) for a in everywhere)
    for axis, steps in axes_of:
        size = 2 if axis == CORE else 4
        for d in steps:
            pl.semaphore_signal(free_sem, inc=1, device_id={axis: lax.rem(lax.axis_index(axis) + d, size)},
                                device_id_type=MESH)
    red.each(red.relay, 1)

    def product(rhs, base, group, b0):
        _, start, width = GROUPS[group]
        for n in range(3):
            value = nn(turned[...], rhs[:, base + 256 * n : base + 256 * n + 256]).reshape(4, 4, 2, 24, 256)
            for half in range(2):
                unit = 2 * n + half
                for side in range(2):
                    stage[unit % 3, side, :, :, b0 + unit // 3, :, start : start + width] = (
                        value[:, :, side, :, 128 * half : 128 * half + 128])

    turned[...] = mixed_ref[...].T
    product(gffn_ref, 0, 2, 0)
    ready("wq", "wk", "wv", "x")
    turned[...] = bufd[3 * WIDTH : 3 * WIDTH + ROWS].T
    product(slope, 0, 2, 2)
    pl.semaphore_wait(free_sem, 10)
    for s in range(3):
        for b in range(4):
            red.swap(2, s, b).start()
    fifth(step)

    def later(p, carry):
        attend_back_later(p, act, bufu, late_ref, after, trigs, ratio_ref, inverse_ref, slope)
        return carry

    lax.fori_loop(0, 6, later, 0)
    product(slope, WIDTH, 3, 0)
    product(slope, 2 * WIDTH, 3, 2)
    for s in range(3):
        for b in range(4):
            red.swap(3, s, b).start()
    for i in range(3):
        note(i, column(slope[:, WIDTH * i : WIDTH * i + WIDTH].astype(F32)))
    start, end, vector_sent = vector_steps(vec_ref, vecs, vec_send, vec_recv)
    start(0)
    red.each(red.begin, 2)
    red.each(red.middle, 1)
    end(0)
    start(1)
    red.each(red.relay, 2)
    red.each(red.begin, 3)

    def back(r, carry):
        rows = at(r, 128)
        total = acc_ref[rows]
        for i in range(3):
            total = total + nt(slope[rows, WIDTH * i : WIDTH * i + WIDTH], bufd[WIDTH * i : WIDTH * i + WIDTH])
        acc_ref[rows] = total
        return carry

    lax.fori_loop(0, 2, back, 0)
    red.each(red.last, 1)
    red.each(red.relay, 3)
    lax.fori_loop(2, 4, back, 0)
    tokens_copy = pltpu.make_async_copy(acc_ref, tokens_out, store_sem.at[0])
    tokens_copy.start()
    end(1)
    start(2)
    red.each(red.middle, 2)
    red.each(red.spread, 1)
    red.each(red.middle, 3)
    end(2)
    start(3)
    red.each(red.last, 2)
    red.each(red.last, 3)
    red.each(red.finish, 1)
    red.each(red.spread, 2)
    red.each(red.spread, 3)
    end(3)
    vec_copy = pltpu.make_async_copy(vecs.at[4], vec_out, store_sem.at[1])
    vec_copy.start()
    red.each(red.finish, 2)
    red.each(red.finish, 3)
    done_copy = pltpu.make_async_copy(done, done_out, store_sem.at[2])
    done_copy.start()
    vector_sent()
    for g in range(1, 4):
        red.sent(g)
    tokens_copy.wait()
    vec_copy.wait()
    done_copy.wait()


def final_kernel(done, vecs, tokens, block, block_out, tokens_out, out_q, out_bq, out_k, out_bk, out_v, out_bv, out_o,
                 out_bo, out_g1, out_s1, out_up, out_bup, out_down, out_bdown, out_g2, out_s2, sem):
    copies = (pltpu.make_async_copy(tokens, tokens_out, sem.at[0]), pltpu.make_async_copy(block, block_out, sem.at[1]))
    for copy in copies:
        copy.start()
    for s in range(3):
        for b in range(4):
            out_down[24 * b : 24 * b + 24, 256 * s : 256 * s + 256] = done[0, s, b]
            out_up[:, 768 * b + 256 * s : 768 * b + 256 * s + 256] = done[1, s, b]
            cols = slice(384 * (b % 2) + 128 * s, 384 * (b % 2) + 128 * s + 128)
            (out_o, out_q)[b // 2][:, cols] = done[2, s, b, :, 0:128]
            (out_k, out_v)[b // 2][:, cols] = done[2, s, b, :, 128:256]
    seq = (lax.axis_index("seq_0") * 4 + lax.axis_index("seq_1")) * 2 + lax.axis_index(CORE)
    values = vecs[...]
    mine = pltpu.roll(values, lax.rem(WIDTH - 24 * seq, WIDTH), 1)
    for k, out in enumerate((out_bq, out_bk, out_bv, out_bo, out_g1, out_s1, out_bdown, out_g2, out_s2)):
        out[...] = mine[k, 0:24]
    spun = pltpu.roll(values, lax.rem(WIDTH - 96 * lax.rem(seq, 8), WIDTH), 1)
    row = lax.broadcasted_iota(jnp.int32, (16, WIDTH), 0)
    out_bup[...] = jnp.sum(jnp.where(row == 9 + seq // 8, spun, 0.0), axis=0)[0:96]
    for copy in copies:
        copy.wait()


def on_device(tokens, lengths, w_query, b_query, w_key, b_key, w_value, b_value, w_out, b_out, gain_one, shift_one,
              w_up, b_up, w_down, b_down, gain_two, shift_two, cotangent):
    x = tokens[0]
    cot = cotangent[0]
    seq = lax.axis_index(SEQ)

    def row(v):
        return v.reshape(1, -1)

    vmem = pl.BlockSpec(memory_space=VMEM)
    smem = pl.BlockSpec(memory_space=pltpu.SMEM)
    anywhere = pl.BlockSpec(memory_space=pl.ANY)
    wide16, wide32 = ((ROWS, WIDTH), BF16), ((ROWS, WIDTH), F32)
    long16, heads16 = ((ROWS, HIDDEN), BF16), ((ROWS, 128 * HEADS), BF16)
    per_head = ((HEADS, 128, 128), F32)
    packed = ((PAIRS, 136, 128), F32)
    vector = ((16, WIDTH), F32)
    square = ((WIDTH, WIDTH), BF16)
    kept = [long16, heads16, ((2, ROWS, WIDTH), BF16), ((2, ROWS, 128), F32), per_head, packed, wide32, wide32, wide16,
            wide32, ((ROWS, 128), F32), wide16, long16, long16, wide32, wide16, wide16, vector]
    (qk, v, gates, trigs, early, before, ratio, inverse, mixed, normal, scale, normed, act, slope, back, gffn, block,
     vec) = pl.pallas_call(
        front_kernel,
        out_shape=[jax.ShapeDtypeStruct(*shape) for shape in kept],
        in_specs=[smem] + [vmem] * 10 + [anywhere] * 8,
        out_specs=[anywhere] * len(kept),
        scratch_shapes=[VMEM(*shape) for shape in (
            wide16, square, square, square, square, ((WIDTH, HIDDEN), BF16), ((HIDDEN, WIDTH), BF16), wide16,
            *kept, packed, ((HEADS, ROWS, 128), F32))]
        + [pltpu.SemaphoreType.DMA((8,)), pltpu.SemaphoreType.DMA((len(kept),))] + EXCHANGE_SCRATCH,
        compiler_params=pltpu.CompilerParams(collective_id=2, has_side_effects=True, vmem_limit_bytes=LIMIT),
    )(lengths, row(b_query), row(b_key), row(b_value), row(b_out), row(gain_one), row(shift_one), row(b_up),
      row(b_down), row(gain_two), row(shift_two), x, w_query, w_key, w_value, w_out, w_up, w_down, cot)
    anywhere_of = [qk, v, gates, trigs, early, before, ratio, inverse, mixed, normal, scale, normed, act, slope, back, gffn,
                   vec, x, w_query, w_key, w_value, w_out, w_up, w_down]
    tokens_grad, done, sums = pl.pallas_call(
        back_kernel,
        out_shape=[jax.ShapeDtypeStruct(*wide32), jax.ShapeDtypeStruct((3, 3, 4, 24, 256), F32),
                   jax.ShapeDtypeStruct(*vector)],
        in_specs=[vmem] + [anywhere] * len(anywhere_of),
        out_specs=[anywhere] * 3,
        scratch_shapes=[VMEM(*shape) for shape in (
            ((2, ROWS, 128), F32), per_head, packed, wide32, wide32, wide16, wide32, ((ROWS, 128), F32), wide16,
            long16, long16, wide32, wide16, vector, square, ((WIDTH, HIDDEN), BF16), ((HIDDEN, WIDTH), BF16),
            per_head, packed, packed, ((WIDTH, ROWS), BF16),
            ((3, 2, 4, 4, 4, 24, 256), F32), ((2, 3, 4, 4, 4, 24, 256), F32), ((2, 3, 3, 4, 4, 24, 256), F32),
            ((2, 3, 3, 4, 24, 256), F32), ((2, 3, 3, 24, 256), F32), ((3, 3, 4, 24, 256), F32), ((15, 16, WIDTH), F32))]
        + [pltpu.SemaphoreType.DMA((32,)), pltpu.SemaphoreType.DMA((3,)), pltpu.SemaphoreType.DMA((4, 3, 4)),
           pltpu.SemaphoreType.DMA((4, 3, 4)), pltpu.SemaphoreType.DMA((4, 3, 15)), pltpu.SemaphoreType.DMA((4, 3, 15)),
           pltpu.SemaphoreType.DMA((10,)), pltpu.SemaphoreType.DMA((10,)), pltpu.SemaphoreType.REGULAR]
        + EXCHANGE_SCRATCH,
        compiler_params=pltpu.CompilerParams(collective_id=1, has_side_effects=True, vmem_limit_bytes=BACK_LIMIT),
    )(row(gain_one), *anywhere_of)
    out = jax.ShapeDtypeStruct
    square_share, vector_share = out((24, WIDTH), F32), out((24,), F32)
    results = pl.pallas_call(
        final_kernel,
        out_shape=[out(*wide16), out(*wide32)] + [square_share, vector_share] * 4 + [vector_share] * 2
        + [out((24, HIDDEN), F32), out((96,), F32), out((96, WIDTH), F32)] + [vector_share] * 3,
        in_specs=[vmem, vmem, anywhere, anywhere],
        out_specs=[anywhere] * 2 + [vmem] * 16,
        scratch_shapes=[pltpu.SemaphoreType.DMA((2,))],
        compiler_params=pltpu.CompilerParams(vmem_limit_bytes=32 * 2**20),
    )(done, sums, tokens_grad, block)
    return (results[0][None], results[1][None], *results[2:])


def solution(mesh):
    torus = Mesh(mesh.devices.reshape(4, 4, 2, mesh.shape["batch"]), (*SEQ, "batch"))
    rows, shares = P("batch", SEQ, None), P(SEQ, None)
    return jax.shard_map(
        on_device,
        mesh=torus,
        in_specs=(rows, P("batch")) + (P(),) * 16 + (rows,),
        out_specs=(rows, rows) + (shares, P(SEQ)) * 4 + (P(SEQ), P(SEQ)) + (shares, P(SEQ)) * 2 + (P(SEQ), P(SEQ)),
        check_vma=False,
    )
```

```python
import jax
import jax.numpy as jnp
from jax import lax
from jax.experimental import pallas as pl
from jax.experimental.pallas import tpu as pltpu
from jax.sharding import Mesh
from jax.sharding import PartitionSpec as P

SEQ = ("seq_0", "seq_1", "seq_2")
AX = ("seq_0", "seq_1", "batch")
CORE = "seq_2"
MESH = pl.DeviceIdType.MESH
DIRECT = (1, 3, 2)
F32 = jnp.float32
BF16 = jnp.bfloat16
HALF_PI = 1.5707963267948966
HALF_PI_REST = -4.371139000186241e-08
EPSILON = 1e-05
ROWS = 512
WIDTH = 768
HIDDEN = 3072
HEADS = 12
PAIRS = 6
CHUNK = 256
FEED = 1024
TILE = 1536
VMEM = pltpu.VMEM
LIMIT = 63 * 2**20


def loop(lo, hi, body):
    with jax.named_scope(body.__name__):
        lax.fori_loop(lo, hi, body, 0)


def nn(a, b):
    return jnp.dot(a, b, preferred_element_type=F32)


def nt(a, b):
    return lax.dot_general(a, b, (((1,), (1,)), ((), ())), preferred_element_type=F32)


def tn(a, b):
    return lax.dot_general(a, b, (((0,), (0,)), ((), ())), preferred_element_type=F32)


def at(k, size):
    return pl.ds(pl.multiple_of(k * size, size), size)


def rot(k, d):
    return lax.rem(k + d, 4)


def left_lanes(rows):
    return lax.broadcasted_iota(jnp.int32, (rows, 128), 1) < 64


def swap_halves(value):
    return pltpu.roll(value, 64, 1)


def doubled(value):
    return jnp.concatenate([value, value], axis=1)


def halves(value):
    high = value.astype(BF16)
    return high, (value - high.astype(F32)).astype(BF16)


SIN = (1.0, -0.1666666716337204, 0.008333330973982811, -0.00019840864115394652, 2.7525297809916083e-06, -2.3888299338636898e-08)


def sine(x):
    square = x * x
    value = SIN[5]
    for c in SIN[4::-1]:
        value = value * square + c
    return value * x


def normal_parts(p):
    return 0.5 + 0.5 * lax.erf(p * 0.7071067811865476), 0.3989422804014327 * jnp.exp(-0.5 * p * p)


def trig_block(first, rows, length):
    position = first + lax.broadcasted_iota(jnp.int32, (rows, 128), 0)
    size = lax.broadcast_in_dim(length, (rows, 128), ()).astype(F32)
    angle = HALF_PI * jnp.minimum(position + 1, length).astype(F32) / size
    both = sine(jnp.where(left_lanes(rows), (HALF_PI - angle) + HALF_PI_REST, angle))
    return both, (position < length).astype(F32)


def project_values(n, x_ref, w, b, out):
    left = left_lanes(ROWS)
    u = (nn(x_ref[...], w[:, at(n, 256)]) + b[:, at(n, 256)]).astype(BF16).astype(F32)
    for j in range(2):
        part = u[:, 128 * j : 128 * j + 128]
        out[:, at(4 * n + 2 * j, 128)] = jnp.where(left, part, 1.0).astype(BF16)
        out[:, at(4 * n + 2 * j + 1, 128)] = jnp.where(left, swap_halves(part), 1.0).astype(BF16)


def project_soft(n, x_ref, w, b, table, out, first, gates, gate):
    left = left_lanes(ROWS)
    u = nn(x_ref[...], w[:, at(n, 256)]) + b[:, at(n, 256)]
    small = jnp.exp(-jnp.abs(u))
    soft = jnp.maximum(u, 0.0) + jnp.log1p(small)
    gates[:, at(gate + n, 256)] = (jnp.where(u >= 0, 1.0, small) / (1.0 + small)).astype(BF16)
    trig = table[...]
    for j in range(2):
        part = soft[:, 128 * j : 128 * j + 128]
        other = swap_halves(part)
        out[:, at(first + 4 * n + 2 * j, 128)] = (jnp.where(left, part, other) * trig).astype(BF16)
        out[:, at(first + 4 * n + 2 * j + 1, 128)] = (jnp.where(left, other, part) * trig).astype(BF16)


def state_sums(p, qk_ref, v_ref, state_ref, early_ref):
    for j in range(2):
        h = 2 * p + j
        keys, values = at(HEADS + h, 128), at(h, 128)
        early = tn(v_ref[0:CHUNK, values], qk_ref[0:CHUNK, keys])
        early_ref[h] = early[0:72]
        both = early + tn(v_ref[CHUNK:ROWS, values], qk_ref[CHUNK:ROWS, keys])
        state_ref[p, 64 * j : 64 * j + 64] = both[0:64]
        state_ref[p, 128 + j : 129 + j] = both[64:65]
    state_ref[p, 130:136] = jnp.zeros((6, 128), F32)


def exchange_steps(n, pay, out, core_in, chip, head, tail, total, msgs, xa, ya, yb, xb, send, recv, reverse):
    my, mx = lax.axis_index("seq_0"), lax.axis_index("seq_1")
    core = lax.axis_index(CORE)
    other = 1 - core
    own = 2 * n + core

    def remote(src, dst, stage, k, target):
        pltpu.make_async_remote_copy(
            src_ref=src, dst_ref=dst, send_sem=send.at[n, stage], recv_sem=recv.at[n, k],
            device_id=target, device_id_type=MESH).start()

    def counts(theirs, mine):
        return theirs > mine if reverse else theirs < mine

    def chosen(flag, value):
        return jnp.where(flag, value, jnp.zeros_like(value))

    def first():
        remote(pay.at[2 * n + other], core_in.at[n], 0, 0, {CORE: other})

    def second():
        arrived(core_in.at[n], recv.at[n, 0])
        chip[n] = pay[own] + core_in[n]
        for k, d in enumerate(DIRECT):
            remote(chip.at[n, pl.ds(0, 72)], xa.at[n, k], 1, 1, {"seq_1": rot(mx, d)})
        for k, d in enumerate(DIRECT):
            remote(chip.at[n, pl.ds(72, 64)], yb.at[n, k], 1, 2, {"seq_0": rot(my, d)})

    def third():
        arrived(xa.at[n], recv.at[n, 1])
        some, every = jnp.zeros((72, 128), F32), chip[n, 0:72]
        for k, d in enumerate(DIRECT):
            some = some + chosen(counts(rot(mx, 4 - d), mx), xa[n, k])
            every = every + xa[n, k]
        head[n] = some
        total[n] = every
        for k, d in enumerate(DIRECT):
            remote(total.at[n], ya.at[n, k], 2, 3, {"seq_0": rot(my, d)})
        arrived(yb.at[n], recv.at[n, 2])
        some = jnp.zeros((64, 128), F32)
        for k, d in enumerate(DIRECT):
            some = some + chosen(counts(rot(my, 4 - d), my), yb[n, k])
        tail[n] = some
        for k, d in enumerate(DIRECT):
            msgs[n, k] = some + chosen(counts(mx, rot(mx, d)), chip[n, 72:136])
        for k, d in enumerate(DIRECT):
            remote(msgs.at[n, k], xb.at[n, k], 2, 4, {"seq_1": rot(mx, d)})

    def fourth():
        arrived(ya.at[n], recv.at[n, 3])
        arrived(xb.at[n], recv.at[n, 4])
        arrived(chip, send.at[n, 1])
        mine = core == (0 if reverse else 1)
        low, high = head[n], tail[n]
        for k, d in enumerate(DIRECT):
            low = low + chosen(counts(rot(my, 4 - d), my), ya[n, k])
            high = high + xb[n, k]
        out[own, 0:72] = low + chosen(mine, core_in[n, 0:72])
        out[own, 72:136] = high + chosen(mine, core_in[n, 72:136])
        chip[n, 0:72] = low + chosen(jnp.logical_not(mine), pay[own, 0:72])
        chip[n, 72:136] = high + chosen(jnp.logical_not(mine), pay[own, 72:136])
        remote(chip.at[n], out.at[own], 3, 5, {CORE: other})

    def fifth():
        arrived(out.at[2 * n + other], recv.at[n, 5])

    def sent():
        arrived(core_in.at[n], send.at[n, 0])
        arrived(chip, send.at[n, 2])
        arrived(chip.at[n], send.at[n, 3])

    return first, second, third, fourth, fifth, sent


EXCHANGE_SCRATCH = [
    VMEM((3, 136, 128), F32),
    VMEM((3, 136, 128), F32),
    VMEM((3, 72, 128), F32),
    VMEM((3, 64, 128), F32),
    VMEM((3, 72, 128), F32),
    VMEM((3, 3, 64, 128), F32),
    VMEM((3, 3, 72, 128), F32),
    VMEM((3, 3, 72, 128), F32),
    VMEM((3, 3, 64, 128), F32),
    VMEM((3, 3, 64, 128), F32),
    pltpu.SemaphoreType.DMA((3, 4)),
    pltpu.SemaphoreType.DMA((3, 6)),
]


class Exchange:
    def __init__(self, pay, out, scratch, reverse):
        self.parts = [exchange_steps(n, pay, out, *scratch, reverse) for n in range(3)]

    def step(self, k, n):
        with jax.named_scope(("swap", "begin", "turn", "end", "share", "sent")[k]):
            self.parts[n][k]()


def greet(axes):
    barrier = pltpu.get_barrier_semaphore()
    core = lax.axis_index(CORE)
    pl.semaphore_signal(barrier, inc=1, device_id={CORE: 1 - core}, device_id_type=MESH)
    for axis in axes:
        mine = lax.axis_index(axis)
        for d in DIRECT:
            pl.semaphore_signal(barrier, inc=1, device_id={axis: rot(mine, d)}, device_id_type=MESH)


def greeted(axes):
    pl.semaphore_wait(pltpu.get_barrier_semaphore(), 1 + 3 * len(axes))


def causal_masks():
    row = lax.broadcasted_iota(jnp.int32, (CHUNK, CHUNK), 0)
    col = lax.broadcasted_iota(jnp.int32, (CHUNK, CHUNK), 1)
    return row >= col, row <= col


def prefix_state(before, p, j, early_ref, c):
    body, row = before[p, 64 * j : 64 * j + 64], before[p, 128 + j : 129 + j]
    if c == 1:
        body, row = body + early_ref[2 * p + j, 0:64], row + early_ref[2 * p + j, 64:65]
    return jnp.concatenate([body, jnp.broadcast_to(row, (64, 128))], axis=0)


def attend_local(p, qk_ref, v_ref, top_ref, under_ref):
    causal, _ = causal_masks()
    left = left_lanes(CHUNK)
    cols = at(p, 128)
    for c in range(2):
        rows = slice(CHUNK * c, CHUNK * c + CHUNK)
        sums = []
        for j in range(2):
            h = 2 * p + j
            weight = nt(qk_ref[rows, at(h, 128)], qk_ref[rows, at(HEADS + h, 128)])
            sums.append(nn(jnp.where(causal, weight, 0.0).astype(BF16), v_ref[rows, at(h, 128)]))
        even, odd = sums
        top_ref[rows, cols] = jnp.where(left, even, swap_halves(odd))
        under_ref[rows, cols] = jnp.where(left, swap_halves(even), odd)


def attend_earlier(p, qk_ref, early_ref, before, ratio_ref, inverse_ref, mixed_ref):
    left = left_lanes(CHUNK)
    cols = at(p, 128)
    for c in range(2):
        rows = slice(CHUNK * c, CHUNK * c + CHUNK)
        sums = []
        for j in range(2):
            h = 2 * p + j
            high, low = halves(prefix_state(before, p, j, early_ref, c))
            sums.append(nt(doubled(qk_ref[rows, at(h, 128)]), jnp.concatenate([high, low], axis=1)))
        even, odd = sums
        inverse = 1.0 / (inverse_ref[rows, cols] + jnp.where(left, swap_halves(even), odd))
        ratio = (ratio_ref[rows, cols] + jnp.where(left, even, swap_halves(odd))) * inverse
        ratio_ref[rows, cols] = ratio
        inverse_ref[rows, cols] = inverse
        mixed_ref[rows, cols] = ratio.astype(BF16)


def mean_rows(value):
    return jnp.mean(value, axis=-1, keepdims=True)


def standard(hidden):
    centred = hidden - mean_rows(hidden)
    scale = lax.rsqrt(mean_rows(centred * centred) + EPSILON)
    return centred * scale, scale


def norm_back(grad, normal, scale, gain):
    scaled = grad * gain
    return scale * (scaled - mean_rows(scaled) - normal * mean_rows(scaled * normal))


def column(value):
    return jnp.sum(value, axis=0, keepdims=True)


ORDERS = ((1, 0, 2), (0, 2, 1), (2, 1, 0))
SUBS = 9
COLS = 256


def cell(ref, order, picks):
    at = [slice(None)] * 3
    for axis, pick in zip(order, picks):
        at[axis] = pick
    return ref.at[tuple(at)]


def halved(ref, order, pick, half):
    at = [slice(None)] * 3
    at[order[0]] = pick
    at[1 if order[0] == 0 else 0] = half
    return ref.at[tuple(at)]


def add_blocks(dst, srcs, lead):
    total = 1
    for n in lead:
        total *= n

    def step(k, carry):
        where, rest = [], k
        for n in reversed(lead):
            where.append(lax.rem(rest, n))
            rest = rest // n
        where = tuple(reversed(where))
        value = dst[where]
        for src in srcs:
            value = value + src[where]
        dst[where] = value
        return carry

    lax.fori_loop(0, total, step, 0)


SLOTS = (0, 1, 2, 3, 0, 1)


def arrived(ref, sem):
    pltpu.make_async_copy(ref, ref, sem).wait()


class Reduction:
    def __init__(self, stage, sums, first, second, third, done, core_send, core_recv, send, recv, keep,
                 spread_recv):
        self.stage, self.sums, self.first, self.second, self.third, self.done = stage, sums, first, second, third, done
        self.core_send, self.core_recv, self.send, self.recv, self.keep = core_send, core_recv, send, recv, keep
        self.spread_recv = spread_recv
        self.me = tuple(lax.axis_index(a) for a in AX)
        self.core = lax.axis_index(CORE)
        self.other = 1 - self.core

    def swap(self, g, s, part):
        where = (part,) if g < 2 else (slice(None), slice(None), part)
        return pltpu.make_async_remote_copy(
            src_ref=self.stage.at[(g % 2, s, self.other, *where)], dst_ref=self.sums.at[(SLOTS[g], s, *where)],
            send_sem=self.core_send.at[SLOTS[g], s], recv_sem=self.core_recv.at[SLOTS[g], s],
            device_id={CORE: self.other}, device_id_type=MESH)

    def swaps(self, g):
        for s in range(3):
            for part in range(4):
                self.swap(g, s, part).start()

    def remote(self, src, dst, g, s, stage, k, axis, d):
        pltpu.make_async_remote_copy(
            src_ref=src, dst_ref=dst, send_sem=self.send.at[SLOTS[g], stage],
            recv_sem=self.recv.at[SLOTS[g], s, k] if k < 5 else self.spread_recv.at[g, s],
            device_id={AX[axis]: rot(self.me[axis], d)}, device_id_type=MESH).start()

    def views(self, g, s):
        slot = SLOTS[g]
        return (self.sums.at[slot, s], self.first.at[slot, s], self.second.at[slot, s], self.third.at[slot, s],
                self.done.at[g, s], self.stage.at[g % 2, s, self.core], self.recv.at[slot, s])

    def begin(self, g, s):
        mine, inbox, _, _, _, own, _ = self.views(g, s)
        arrived(mine, self.core_recv.at[SLOTS[g], s])
        arrived(own, self.core_send.at[SLOTS[g], s])
        add_blocks(mine, [own], (4, 4))
        order = ORDERS[s]
        ax = order[0]
        far = rot(self.me[ax], 2)
        lo, hi = pl.ds(0, 2), pl.ds(2, 2)
        self.remote(halved(mine, order, far, lo), inbox.at[0, lo], g, s, 0, 0, ax, 1)
        self.remote(halved(mine, order, far, hi), inbox.at[0, hi], g, s, 0, 1, ax, 3)

    def follow(self, g, s):
        mine, inbox = self.views(g, s)[:2]
        order = ORDERS[s]
        ax = order[0]
        i = self.me[ax]
        lo, hi = pl.ds(0, 2), pl.ds(2, 2)
        self.remote(halved(mine, order, rot(i, 1), hi), inbox.at[1, hi], g, s, 0, 2, ax, 1)
        self.remote(halved(mine, order, rot(i, 3), lo), inbox.at[2, lo], g, s, 0, 2, ax, 3)

    def relay(self, g, s):
        mine, inbox, _, _, _, _, recv = self.views(g, s)
        order = ORDERS[s]
        ax = order[0]
        i = self.me[ax]
        lo, hi = pl.ds(0, 2), pl.ds(2, 2)
        arrived(inbox.at[0, lo], recv.at[0])
        part = halved(mine, order, rot(i, 1), lo)
        add_blocks(part, [inbox.at[0, lo]], (2, 4))
        self.remote(part, inbox.at[1, lo], g, s, 0, 2, ax, 1)
        arrived(inbox.at[0, hi], recv.at[1])
        part = halved(mine, order, rot(i, 3), hi)
        add_blocks(part, [inbox.at[0, hi]], (2, 4))
        self.remote(part, inbox.at[2, hi], g, s, 0, 2, ax, 3)

    def middle(self, g, s):
        mine, inbox, second, _, _, _, recv = self.views(g, s)
        order = ORDERS[s]
        arrived(inbox.at[pl.ds(1, 2)], recv.at[2])
        i, ax = self.me[order[0]], order[1]
        add_blocks(cell(mine, order, (i,)), [inbox.at[1], inbox.at[2]], (4,))
        for k, d in enumerate(DIRECT):
            self.remote(cell(mine, order, (i, rot(self.me[ax], d))), second.at[k], g, s, 1, 3, ax, d)

    def last(self, g, s):
        mine, _, second, third, _, _, recv = self.views(g, s)
        order = ORDERS[s]
        arrived(second, recv.at[3])
        where = (self.me[order[0]], self.me[order[1]])
        add_blocks(cell(mine, order, where), [second.at[k] for k in range(3)], (4,))
        ax = order[2]
        for k, d in enumerate(DIRECT):
            self.remote(cell(mine, order, (*where, rot(self.me[ax], d))), third.at[k], g, s, 2, 4, ax, d)

    def spread(self, g, s):
        mine, _, _, third, done, _, recv = self.views(g, s)
        arrived(third, recv.at[4])
        y, x, z = self.me
        mine[y, x, z] = mine[y, x, z] + third[0] + third[1] + third[2]
        part = mine.at[y, x, z]
        for k, d in enumerate(DIRECT):
            self.remote(part, done.at[z], g, s, 3, 5, 2, d)
        pltpu.make_async_copy(part, done.at[z], self.keep.at[SLOTS[g]]).start()

    def finish(self, g, s):
        third = self.views(g, s)[3]
        arrived(third, self.spread_recv.at[g, s])

    def sent(self, g):
        slot = SLOTS[g]
        arrived(self.first.at[slot], self.send.at[slot, 0])
        arrived(self.second.at[slot], self.send.at[slot, 1])
        arrived(self.third.at[slot], self.send.at[slot, 2])
        arrived(self.third.at[slot], self.send.at[slot, 3])
        arrived(self.third.at[slot, 0], self.keep.at[slot])

    def each(self, step, g):
        with jax.named_scope(f"{step.__name__} {g}"):
            for s in range(3):
                step(g, s)


def vector_steps(vec, vecs, send, recv):
    me = tuple(lax.axis_index(a) for a in AX)
    core = lax.axis_index(CORE)
    bases = (0, 1, 4, 7)

    def start(stage):
        if stage == 0:
            targets = [{CORE: 1 - core}]
        else:
            ax = stage - 1
            targets = [{AX[ax]: rot(me[ax], d)} for d in DIRECT]
        for k, target in enumerate(targets):
            pltpu.make_async_remote_copy(
                src_ref=vec, dst_ref=vecs.at[bases[stage] + k], send_sem=send.at[stage], recv_sem=recv.at[stage],
                device_id=target, device_id_type=MESH).start()

    def end(stage):
        with jax.named_scope("vector"):
            count = 3 if stage else 1
            part = vecs.at[pl.ds(bases[stage], count)]
            arrived(part, recv.at[stage])
            arrived(part, send.at[stage])
            total = vec[...]
            for k in range(count):
                total = total + vecs[bases[stage] + k]
            vec[...] = total

    return start, end


def suffix_state(after, p, j, late_ref, c):
    body, row = after[p, 64 * j : 64 * j + 64], after[p, 128 + j : 129 + j]
    if c == 0:
        h = 2 * p + j
        body, row = body + late_ref[h, 0:64], row + (late_ref[h, 64:65] + late_ref[h, 65:66])
    first = lax.broadcasted_iota(jnp.int32, (64, 128), 0) == 0
    return jnp.concatenate([body, jnp.where(first, jnp.broadcast_to(row, (64, 128)), 0.0)], axis=0)


def attend_back_query(p, act, bufu, early_ref, before, trigs, grads):
    causal, _ = causal_masks()
    left = left_lanes(CHUNK)
    for c in range(2):
        rows = slice(CHUNK * c, CHUNK * c + CHUNK)
        query = []
        for j in range(2):
            h = 2 * p + j
            k = bufu[rows, at(HEADS + h, 128)]
            v, g = act[rows, at(h, 128)], act[rows, at(HEADS + h, 128)]
            high, low = halves(prefix_state(before, p, j, early_ref, c))
            weight = jnp.where(causal, nt(g, v), 0.0).astype(BF16)
            gq = nn(weight, k) + nn(doubled(g), jnp.concatenate([high, low], axis=0))
            gq = gq * trigs[0, rows]
            query.append(gq + swap_halves(gq))
        gate = bufu[ROWS:WIDTH, at(PAIRS * c + p, 128)].astype(F32)
        grads[rows, at(p, 128)] = (jnp.where(left, query[0], query[1]) * gate).astype(BF16)


def attend_back_local(p, act, bufu, trigs, key_ref, value_ref):
    _, flipped = causal_masks()
    left = left_lanes(CHUNK)
    cols = at(p, 128)
    for c in range(2):
        rows = slice(CHUNK * c, CHUNK * c + CHUNK)
        keys, value = [], []
        for j in range(2):
            h = 2 * p + j
            q, k = bufu[rows, at(h, 128)], bufu[rows, at(HEADS + h, 128)]
            v, g = act[rows, at(h, 128)], act[rows, at(HEADS + h, 128)]
            gk = nn(jnp.where(flipped, nt(v, g), 0.0).astype(BF16), q) * trigs[1, rows]
            keys.append(gk + swap_halves(gk))
            value.append(nn(jnp.where(flipped, nt(k, q), 0.0).astype(BF16), g))
        key_ref[rows, cols] = jnp.where(left, keys[0], keys[1])
        value_ref[rows, cols] = jnp.where(left, value[0], swap_halves(value[1]))


def attend_back_later(p, act, bufu, late_ref, after, trigs, ratio_ref, inverse_ref, grads):
    left = left_lanes(CHUNK)
    for c in range(2):
        rows = slice(CHUNK * c, CHUNK * c + CHUNK)
        keys, value = [], []
        for j in range(2):
            h = 2 * p + j
            k, v = bufu[rows, at(HEADS + h, 128)], act[rows, at(h, 128)]
            high, low = halves(suffix_state(after, p, j, late_ref, c))
            gk = nn(doubled(v), jnp.concatenate([high, low], axis=0)) * trigs[1, rows]
            keys.append(gk + swap_halves(gk))
            value.append(nt(doubled(k), jnp.concatenate([high, low], axis=1)))
        cols = at(p, 128)
        gate = bufu[ROWS:WIDTH, at(2 * PAIRS + PAIRS * c + p, 128)].astype(F32)
        gk = (ratio_ref[rows, cols] + jnp.where(left, keys[0], keys[1])) * gate
        grads[rows, at(PAIRS + p, 128)] = gk.astype(BF16)
        gv = inverse_ref[rows, cols] + jnp.where(left, value[0], swap_halves(value[1]))
        grads[rows, at(2 * PAIRS + p, 128)] = gv.astype(BF16)


def layer_kernel(len_ref, bq_in, bk_in, bv_in, bo_in, gain1_in, shift1_in, bdown_in, gain2_in, shift2_in, bup_in,
                 x_hbm, wq_hbm, wk_hbm, wv_hbm, wo_hbm, wup_hbm, wdown_hbm, cot_hbm,
                 block_out, tokens_out, done_out, vec_out, act_spill, slope_spill,
                 x_ref, act, slope, bufu, bufd, trigs, early_ref, late_ref, pay, before, after,
                 ratio_ref, inverse_ref, normal_ref, acc_ref, scale_ref, mixed_ref, normed_ref, gffn_ref, vec_ref, rows_ref,
                 bup, turned, stage, sums, first_in, second_in, third_in, vecs,
                 load_sem, core_send, core_recv, send, recv, keep_sem, spread_recv, vec_send, vec_recv, free_sem, *scratch):
    everywhere = ("seq_0", "seq_1", "batch")
    greet(everywhere)
    loads = {}

    def load(name, src, dst):
        copy = pltpu.make_async_copy(src, dst, load_sem.at[len(loads)])
        copy.start()
        loads[name] = copy

    def ready(*names):
        with jax.named_scope("ready"):
            for name in names:
                loads[name].wait()

    def note(k, value):
        vec_ref[k : k + 1, :] += value

    load("x", x_hbm, x_ref)
    load("wk", wk_hbm, bufd.at[WIDTH : 2 * WIDTH])
    load("wv", wv_hbm, bufd.at[2 * WIDTH : 3 * WIDTH])
    load("wq", wq_hbm, bufd.at[0:WIDTH])
    for k, vector in enumerate((bq_in, bk_in, bv_in, bo_in, gain1_in, shift1_in, bdown_in, gain2_in, shift2_in)):
        rows_ref[k : k + 1, :] = vector[...].reshape(1, WIDTH)
    bup[...] = bup_in[...].reshape(1, HIDDEN)
    bq, bk, bv, bo, gain1, shift1, bdown, gain2, shift2 = (rows_ref.at[k : k + 1] for k in range(9))
    vec_ref[...] = jnp.zeros_like(vec_ref)
    length = len_ref[0]
    start = ROWS * ((lax.axis_index("seq_0") * 4 + lax.axis_index("seq_1")) * 2 + lax.axis_index(CORE))

    def angles(r, carry):
        both, valid = trig_block(start + 128 * r, 128, length)
        trigs[0, at(r, 128)] = both
        trigs[1, at(r, 128)] = both * valid
        return carry

    loop(0, ROWS // 128, angles)
    ready("x", "wk", "wv")
    load("wup", wup_hbm, bufu)
    wo = bufd.at[3 * WIDTH : HIDDEN]
    load("wo", wo_hbm, wo)
    load("cot", cot_hbm, gffn_ref)
    earlier_sums = Exchange(pay, before, scratch[: len(EXCHANGE_SCRATCH)], False)
    later_sums = Exchange(pay, after, scratch[len(EXCHANGE_SCRATCH) :], True)

    def keys(n, carry):
        project_values(n, x_ref, bufd.at[2 * WIDTH : 3 * WIDTH], bv, slope)
        project_soft(n, x_ref, bufd.at[WIDTH : 2 * WIDTH], bk, trigs.at[1], act, HEADS, slope, 9)
        return carry

    def states(p, carry):
        state_sums(p, act, slope, pay, early_ref)
        return carry

    def queries(n, carry):
        project_soft(n, x_ref, bufd.at[0:WIDTH], bq, trigs.at[0], act, 0, slope, 6)
        return carry

    def own(p, carry):
        attend_local(p, act, slope, ratio_ref, inverse_ref)
        return carry

    def earlier(p, carry):
        attend_earlier(p, act, early_ref, before, ratio_ref, inverse_ref, mixed_ref)
        return carry

    for n in range(3):
        loop(n, n + 1, keys)
        loop(2 * n, 2 * n + 2, states)
        if n == 0:
            greeted(everywhere)
        earlier_sums.step(0, n)
        if n > 0:
            earlier_sums.step(1, n - 1)
    ready("wq")
    loop(0, 1, queries)
    earlier_sums.step(1, 2)
    loop(1, 3, queries)
    load("wdown", wdown_hbm.at[0 : 3 * WIDTH], bufd.at[0 : 3 * WIDTH])
    load("qk_out", act, act_spill)
    load("v_out", slope, slope_spill)
    earlier_sums.step(2, 0)
    loop(0, 2, own)
    earlier_sums.step(2, 1)
    loop(2, 4, own)
    earlier_sums.step(2, 2)
    loop(4, 6, own)
    for n in range(3):
        earlier_sums.step(3, n)
    for n in range(3):
        earlier_sums.step(4, n)
        loop(2 * n, 2 * n + 2, earlier)
    ready("wo")

    def first_norm(r, carry):
        rows = at(r, CHUNK)
        hidden = x_ref[rows].astype(F32) + (nn(mixed_ref[rows], wo[...]) + bo[...])
        normal, scale = standard(hidden)
        normal_ref[rows] = normal
        scale_ref[rows] = jnp.broadcast_to(scale, (CHUNK, 128))
        normed_ref[rows] = (normal * gain1[...] + shift1[...]).astype(BF16)
        return carry

    loop(0, ROWS // CHUNK, first_norm)
    load("wdown end", wdown_hbm.at[3 * WIDTH : HIDDEN], wo)
    ready("qk_out", "v_out", "wup", "wdown")

    def feed(t, carry):
        cols = at(t, FEED)
        for r in range(2):
            rows = slice(CHUNK * r, CHUNK * r + CHUNK)
            pre = nn(normed_ref[rows], bufu[:, cols]) + bup[:, cols]
            whole, bell = normal_parts(pre)
            active = (pre * whole).astype(BF16)
            act[rows, cols] = active
            slope[rows, cols] = (whole + pre * bell).astype(BF16)
            acc_ref[rows] = nn(active, bufd[cols]) + jnp.where(t == 0, 0.0, acc_ref[rows])
        return carry

    loop(0, 2, feed)
    ready("wdown end")
    loop(2, 3, feed)
    ready("cot")

    def second_norm(r, carry):
        rows = at(r, CHUNK)
        hidden = normed_ref[rows].astype(F32) + (acc_ref[rows] + bdown[...])
        normal, scale = standard(hidden)
        x_ref[rows] = (normal * gain2[...] + shift2[...]).astype(BF16)
        grad = gffn_ref[rows].astype(F32)
        note(7, column(grad * normal))
        note(8, column(grad))
        back = norm_back(grad, normal, scale, gain2[...])
        acc_ref[rows] = back
        low = back.astype(BF16)
        gffn_ref[rows] = low
        note(6, column(low.astype(F32)))
        return carry

    loop(0, ROWS // CHUNK, second_norm)
    load("block", x_ref, block_out)
    red = Reduction(stage, sums, first_in, second_in, third_in, done_out, core_send, core_recv, send, recv, keep_sem,
                    spread_recv)

    def down_rows(y, carry):
        turned[...] = act[:, at(y, WIDTH)].T
        for n in range(3):
            value = nn(turned[...], gffn_ref[:, 256 * n : 256 * n + 256]).reshape(4, 2, 4, 24, 256)
            for half in range(2):
                unit = 2 * n + half
                for side in range(2):
                    stage[unit // 3, unit % 3, side, y] = value[:, side, :, :, 128 * half : 128 * half + 128]
        for s in range(3):
            red.swap(0, s, y).start()
        return carry

    loop(0, 4, down_rows)
    red.swaps(1)
    load("v", slope_spill.at[:, 0 : 128 * HEADS], act.at[:, 0 : 128 * HEADS])

    def feed_back(k, carry):
        t = 1 - k
        cols = at(t, TILE)
        total = jnp.zeros((1, TILE), F32)
        for r in range(2):
            rows = slice(CHUNK * r, CHUNK * r + CHUNK)
            gpre = (nt(gffn_ref[rows], bufd[cols]) * slope[rows, cols].astype(F32)).astype(BF16)
            slope[rows, cols] = gpre
            total = total + column(gpre.astype(F32))
            acc_ref[rows] += nt(gpre, bufu[:, cols])
        for half in range(2):
            vec_ref[pl.ds(9 + 2 * t + half, 1), :] = total[:, WIDTH * half : WIDTH * half + WIDTH]
        return carry

    loop(0, 1, feed_back)
    load("wo again", wo_hbm, wo)
    red.each(red.begin, 0)
    loop(1, 2, feed_back)
    red.each(red.follow, 0)
    red.each(red.begin, 1)
    ready("block")
    load("x again", x_hbm, x_ref)
    load("wq again", wq_hbm, bufd.at[0:WIDTH])
    load("wk again", wk_hbm, bufd.at[WIDTH : 2 * WIDTH])
    load("wv again", wv_hbm, bufd.at[2 * WIDTH : 3 * WIDTH])
    load("qk", act_spill, bufu.at[0:ROWS])
    gates = []
    for i in range(2):
        for c in range(2):
            gates.append(f"gate {i}{c}")
            load(gates[-1], slope_spill.at[CHUNK * c : CHUNK * c + CHUNK, pl.ds(128 * HEADS + WIDTH * i, WIDTH)],
                 bufu.at[ROWS:WIDTH, pl.ds(2 * WIDTH * i + WIDTH * c, WIDTH)])
    def up_columns(b, carry):
        for n in range(3):
            cols = pl.ds(pl.multiple_of(WIDTH * b + 256 * n, 256), 256)
            value = nn(turned[...], slope[:, cols]).reshape(4, 4, 2, 24, 256)
            for half in range(2):
                unit = 2 * n + half
                for side in range(2):
                    stage[unit // 3, unit % 3, side, :, :, b] = value[:, :, side, :, 128 * half : 128 * half + 128]
        for s in range(3):
            red.swap(2, s, b).start()
        return carry

    def first_back(r, carry):
        rows = at(r, CHUNK)
        normal = normal_ref[rows]
        scale = scale_ref[rows, 0:1]
        grad = acc_ref[rows]
        note(4, column(grad * normal))
        note(5, column(grad))
        back = norm_back(grad, normal, scale, gain1[...])
        acc_ref[rows] = back
        low = back.astype(BF16)
        gffn_ref[rows] = low
        note(3, column(low.astype(F32)))
        normal_ref[rows] = nt(low, wo[...])
        return carry

    def heads_back(p, carry):
        cols = at(p, 128)
        lane = lax.broadcasted_iota(jnp.int32, (ROWS, 128), 1)
        left = lane < 64
        gnum = (normal_ref[:, cols] * inverse_ref[:, cols]).astype(BF16).astype(F32)
        product = gnum * ratio_ref[:, cols]
        for j in range(2):
            h = 2 * p + j
            mine = jnp.where(left, product, 0.0) if j == 0 else jnp.where(left, 0.0, product)
            gden = jnp.broadcast_to(-jnp.sum(mine, axis=1, keepdims=True), (ROWS, 128))
            high = gden.astype(BF16).astype(F32)
            ends = jnp.where(lane == 64, high, jnp.where(lane == 65, gden - high, 0.0))
            grad = jnp.where(left, gnum if j == 0 else swap_halves(gnum), ends).astype(BF16)
            act[:, at(HEADS + h, 128)] = grad
            late = tn(grad[CHUNK:ROWS], bufu[CHUNK:ROWS, at(h, 128)])
            late_ref[h] = late[0:72]
            both = late + tn(grad[0:CHUNK], bufu[0:CHUNK, at(h, 128)])
            pay[p, 64 * j : 64 * j + 64] = both[0:64]
            pay[p, 128 + j : 129 + j] = both[64:65] + both[65:66]
        pay[p, 130:136] = jnp.zeros((6, 128), F32)
        return carry

    def query_back(p, carry):
        attend_back_query(p, act, bufu, early_ref, before, trigs, slope)
        return carry

    def own_back(p, carry):
        attend_back_local(p, act, bufu, trigs, ratio_ref, inverse_ref)
        return carry

    def later(p, carry):
        attend_back_later(p, act, bufu, late_ref, after, trigs, ratio_ref, inverse_ref, slope)
        return carry

    def back(r, carry):
        rows = at(r, CHUNK)
        total = acc_ref[rows]
        for i in range(3):
            total = total + nt(slope[rows, WIDTH * i : WIDTH * i + WIDTH], bufd[WIDTH * i : WIDTH * i + WIDTH])
        acc_ref[rows] = total
        return carry

    def product(rhs, base, g, b0, n):
        with jax.named_scope("product"):
            value = nn(turned[...], rhs[:, base + 256 * n : base + 256 * n + 256]).reshape(4, 4, 2, 24, 256)
            for part in range(2):
                unit = 2 * n + part
                for side in range(2):
                    stage[g % 2, unit % 3, side, :, :, b0 + unit // 3] = value[:, :, side, :, 128 * part : 128 * part + 128]
                red.swap(g, unit % 3, b0 + unit // 3).start()

    def release(k):
        for axis, steps in ((CORE, (1,)),) + tuple((a, DIRECT) for a in everywhere):
            size = 2 if axis == CORE else 4
            for d in steps:
                pl.semaphore_signal(free_sem.at[k], inc=1, device_id_type=MESH,
                                    device_id={axis: lax.rem(lax.axis_index(axis) + d, size)})

    def released(k):
        with jax.named_scope("released"):
            pl.semaphore_wait(free_sem.at[k], 10)

    ready("wo again")
    loop(0, ROWS // CHUNK, first_back)
    red.each(red.relay, 0)
    red.each(red.follow, 1)
    for n in range(3):
        earlier_sums.step(5, n)
    ready("qk", "v")
    for n in range(3):
        loop(2 * n, 2 * n + 2, heads_back)
        later_sums.step(0, n)
        if n > 0:
            later_sums.step(1, n - 1)
    turned[...] = normed_ref[...].T
    loop(0, 1, up_columns)
    later_sums.step(1, 2)
    red.each(red.relay, 1)
    loop(1, 3, up_columns)
    red.each(red.middle, 0)
    loop(3, 4, up_columns)
    red.swaps(3)
    ready(*gates)
    loop(0, 2, query_back)
    later_sums.step(2, 0)
    loop(2, 4, query_back)
    red.each(red.middle, 1)
    red.each(red.begin, 2)
    later_sums.step(2, 1)
    later_sums.step(2, 2)
    loop(4, 6, query_back)
    red.each(red.begin, 3)
    red.each(red.follow, 2)
    red.each(red.last, 0)
    loop(0, 1, own_back)
    red.each(red.relay, 2)
    red.each(red.follow, 3)
    loop(1, 3, own_back)
    red.each(red.last, 1)
    red.each(red.spread, 0)
    loop(3, 4, own_back)
    red.each(red.relay, 3)
    red.sent(0)
    release(0)
    for n in range(3):
        later_sums.step(3, n)
    loop(4, 5, own_back)
    red.each(red.spread, 1)
    red.each(red.middle, 2)
    loop(5, 6, own_back)
    red.sent(1)
    release(1)
    turned[...] = mixed_ref[...].T
    released(0)
    for n in range(3):
        product(gffn_ref, 0, 4, 0, n)
    ready("x again")
    turned[...] = x_ref[...].T
    for n in range(3):
        product(slope, 0, 4, 2, n)
    red.each(red.middle, 3)
    for n in range(3):
        later_sums.step(4, n)
        loop(2 * n, 2 * n + 2, later)
        if n == 0:
            released(1)
        product(slope, WIDTH, 5, 0, n)
        product(slope, 2 * WIDTH, 5, 2, n)
        if n == 0:
            red.each(red.begin, 4)
        if n == 1:
            red.each(red.follow, 4)
    for i in range(3):
        note(i, column(slope[:, WIDTH * i : WIDTH * i + WIDTH].astype(F32)))
    vector_start, vector_end = vector_steps(vec_ref, vecs, vec_send, vec_recv)
    vector_start(0)
    red.each(red.begin, 5)
    red.each(red.relay, 4)
    red.each(red.follow, 5)
    vector_end(0)
    vector_start(1)
    ready("wq again", "wk again", "wv again")
    loop(0, 1, back)
    red.each(red.last, 2)
    red.each(red.relay, 5)
    loop(1, 2, back)
    load("tokens", acc_ref, tokens_out)
    red.each(red.middle, 4)
    vector_end(1)
    vector_start(2)
    red.each(red.last, 3)
    red.each(red.middle, 5)
    red.each(red.spread, 2)
    red.each(red.last, 4)
    red.each(red.last, 5)
    vector_end(2)
    vector_start(3)
    red.each(red.spread, 3)
    red.each(red.spread, 4)
    red.each(red.spread, 5)
    vector_end(3)
    load("vec", vec_ref, vec_out)
    for g in range(6):
        red.each(red.finish, g)
    for g in range(2, 6):
        red.sent(g)
    for n in range(3):
        later_sums.step(5, n)
    ready("tokens", "vec")


def final_kernel(done, vecs, tokens, block, block_out, tokens_out, out_q, out_bq, out_k, out_bk, out_v, out_bv, out_o,
                 out_bo, out_g1, out_s1, out_up, out_bup, out_down, out_bdown, out_g2, out_s2):
    tokens_out[...] = tokens[...]
    block_out[...] = block[...]
    for s in range(3):
        for b in range(4):
            for half in range(2):
                at_col = 384 * half + 128 * s
                out_down[24 * b : 24 * b + 24, at_col : at_col + 128] = done[half, s, b]
                out_up[:, 768 * b + at_col : 768 * b + at_col + 128] = done[2 + half, s, b]
            cols = slice(384 * (b % 2) + 128 * s, 384 * (b % 2) + 128 * s + 128)
            (out_o, out_q)[b // 2][:, cols] = done[4, s, b]
            (out_k, out_v)[b // 2][:, cols] = done[5, s, b]
    seq = (lax.axis_index("seq_0") * 4 + lax.axis_index("seq_1")) * 2 + lax.axis_index(CORE)
    values = vecs[...]
    mine = pltpu.roll(values, lax.rem(WIDTH - 24 * seq, WIDTH), 1)
    for k, out in enumerate((out_bq, out_bk, out_bv, out_bo, out_g1, out_s1, out_bdown, out_g2, out_s2)):
        out[...] = mine[k, 0:24]
    spun = pltpu.roll(values, lax.rem(WIDTH - 96 * lax.rem(seq, 8), WIDTH), 1)
    row = lax.broadcasted_iota(jnp.int32, (16, WIDTH), 0)
    out_bup[...] = jnp.sum(jnp.where(row == 9 + seq // 8, spun, 0.0), axis=0)[0:96]


def on_device(tokens, lengths, w_query, b_query, w_key, b_key, w_value, b_value, w_out, b_out, gain_one, shift_one,
              w_up, b_up, w_down, b_down, gain_two, shift_two, cotangent):
    vmem = pl.BlockSpec(memory_space=VMEM)
    smem = pl.BlockSpec(memory_space=pltpu.SMEM)
    anywhere = pl.BlockSpec(memory_space=pl.ANY)
    out = jax.ShapeDtypeStruct
    wide16, wide32, long16 = ((ROWS, WIDTH), BF16), ((ROWS, WIDTH), F32), ((ROWS, HIDDEN), BF16)
    per_head, packed = ((HEADS, 72, 128), F32), ((PAIRS, 136, 128), F32)
    vector = ((16, WIDTH), F32)
    finished = ((6, 3, 4, 24, 128), F32)
    block, tokens_grad, done, sums, _, _ = pl.pallas_call(
        layer_kernel,
        out_shape=[out(*shape) for shape in (wide16, wide32, finished, vector, long16, long16)],
        in_specs=[smem] + [vmem] * 10 + [anywhere] * 8,
        out_specs=[anywhere] * 6,
        scratch_shapes=[VMEM(*shape) for shape in (
            wide16, long16, long16, ((WIDTH, HIDDEN), BF16), ((HIDDEN, WIDTH), BF16),
            ((2, ROWS, 128), F32), per_head, per_head, packed, packed, packed,
            wide32, wide32, wide32, wide32, ((ROWS, 128), F32), wide16, wide16, wide16, vector, vector,
            ((1, HIDDEN), F32), ((WIDTH, ROWS), BF16),
            ((2, 3, 2, 4, 4, 4, 24, 128), F32), ((4, 3, 4, 4, 4, 24, 128), F32), ((4, 3, 3, 4, 4, 24, 128), F32),
            ((4, 3, 3, 4, 24, 128), F32), ((4, 3, 3, 24, 128), F32), ((10, 16, WIDTH), F32))]
        + [pltpu.SemaphoreType.DMA((32,)), pltpu.SemaphoreType.DMA((4, 3)), pltpu.SemaphoreType.DMA((4, 3)),
           pltpu.SemaphoreType.DMA((4, 4)), pltpu.SemaphoreType.DMA((4, 3, 5)), pltpu.SemaphoreType.DMA((4,)), pltpu.SemaphoreType.DMA((6, 3)),
           pltpu.SemaphoreType.DMA((4,)), pltpu.SemaphoreType.DMA((4,)), pltpu.SemaphoreType.REGULAR((2,))]
        + EXCHANGE_SCRATCH * 2,
        compiler_params=pltpu.CompilerParams(collective_id=1, has_side_effects=True, vmem_limit_bytes=LIMIT),
    )(lengths, b_query, b_key, b_value, b_out, gain_one, shift_one, b_down, gain_two, shift_two, b_up,
      tokens[0], w_query, w_key, w_value, w_out, w_up, w_down, cotangent[0])
    square_share, vector_share = out((24, WIDTH), F32), out((24,), F32)
    results = pl.pallas_call(
        final_kernel,
        out_shape=[out(*wide16), out(*wide32)] + [square_share, vector_share] * 4 + [vector_share] * 2
        + [out((24, HIDDEN), F32), out((96,), F32), out((96, WIDTH), F32)] + [vector_share] * 3,
        in_specs=[vmem] * 4,
        out_specs=[vmem] * 18,
        compiler_params=pltpu.CompilerParams(vmem_limit_bytes=LIMIT),
    )(done, sums, tokens_grad, block)
    return (results[0][None], results[1][None], *results[2:])


def solution(mesh):
    torus = Mesh(mesh.devices.reshape(4, 4, 2, mesh.shape["batch"]), (*SEQ, "batch"))
    rows, shares = P("batch", SEQ, None), P(SEQ, None)
    return jax.shard_map(
        on_device,
        mesh=torus,
        in_specs=(rows, P("batch")) + (P(),) * 16 + (rows,),
        out_specs=(rows, rows) + (shares, P(SEQ)) * 4 + (P(SEQ), P(SEQ)) + (shares, P(SEQ)) * 2 + (P(SEQ), P(SEQ)),
        check_vma=False,
    )
```

```python
import jax
import jax.numpy as jnp
from jax import lax
from jax.experimental import pallas as pl
from jax.experimental.pallas import tpu as pltpu
from jax.sharding import Mesh
from jax.sharding import PartitionSpec as P

SEQ = ("seq_0", "seq_1", "seq_2")
AX = ("seq_0", "seq_1", "batch")
CORE = "seq_2"
MESH = pl.DeviceIdType.MESH
DIRECT = (1, 3, 2)
F32 = jnp.float32
BF16 = jnp.bfloat16
HALF_PI = 1.5707963267948966
HALF_PI_REST = -4.371139000186241e-08
EPSILON = 1e-05
ROWS = 512
WIDTH = 768
HIDDEN = 3072
HEADS = 12
PAIRS = 6
CHUNK = 256
FEED = 1024
TILE = 1536
VMEM = pltpu.VMEM
LIMIT = 63 * 2**20


def loop(count, body, after=None):
    def step(k, carry):
        with jax.named_scope(body.__name__):
            body(k)
        for n, then in (after or {}).items():
            pl.when(k == n)(then)

    lax.fori_loop(0, count, step, None)


def each_of(count, body):
    lax.fori_loop(0, count, lambda k, carry: body(k), None)


def nn(a, b):
    return jnp.dot(a, b, preferred_element_type=F32)


def nt(a, b):
    return lax.dot_general(a, b, (((1,), (1,)), ((), ())), preferred_element_type=F32)


def tn(a, b):
    return lax.dot_general(a, b, (((0,), (0,)), ((), ())), preferred_element_type=F32)


def at(k, size):
    return pl.ds(pl.multiple_of(k * size, size), size)


def rot(k, d):
    return lax.rem(k + d, 4)


def left_lanes(rows):
    return lax.broadcasted_iota(jnp.int32, (rows, 128), 1) < 64


def swap_halves(value):
    return pltpu.roll(value, 64, 1)


def doubled(value):
    return jnp.concatenate([value, value], axis=1)


def halves(value):
    high = value.astype(BF16)
    return high, (value - high.astype(F32)).astype(BF16)


SIN = (1.0, -0.1666666716337204, 0.008333330973982811, -0.00019840864115394652, 2.7525297809916083e-06, -2.3888299338636898e-08)


def sine(x):
    square = x * x
    value = SIN[5]
    for c in SIN[4::-1]:
        value = value * square + c
    return value * x


def normal_parts(p):
    return 0.5 + 0.5 * lax.erf(p * 0.7071067811865476), 0.3989422804014327 * jnp.exp(-0.5 * p * p)


def trig_block(first, rows, length):
    position = first + lax.broadcasted_iota(jnp.int32, (rows, 128), 0)
    size = lax.broadcast_in_dim(length, (rows, 128), ()).astype(F32)
    angle = HALF_PI * jnp.minimum(position + 1, length).astype(F32) / size
    both = sine(jnp.where(left_lanes(rows), (HALF_PI - angle) + HALF_PI_REST, angle))
    return both, (position < length).astype(F32)


def project_values(n, x_ref, w, b, out):
    left = left_lanes(ROWS)
    u = (nn(x_ref[...], w[:, at(n, 256)]) + b[:, at(n, 256)]).astype(BF16).astype(F32)
    for j in range(2):
        part = u[:, 128 * j : 128 * j + 128]
        out[:, at(4 * n + 2 * j, 128)] = jnp.where(left, part, 1.0).astype(BF16)
        out[:, at(4 * n + 2 * j + 1, 128)] = jnp.where(left, swap_halves(part), 1.0).astype(BF16)


def project_soft(n, x_ref, w, b, table, out, first, gates, gate):
    left = left_lanes(ROWS)
    u = nn(x_ref[...], w[:, at(n, 256)]) + b[:, at(n, 256)]
    small = jnp.exp(-jnp.abs(u))
    soft = jnp.maximum(u, 0.0) + jnp.log1p(small)
    gates[:, at(gate + n, 256)] = (0.5 + 0.5 * jnp.tanh(0.5 * u)).astype(BF16)
    trig = table[...]
    for j in range(2):
        part = soft[:, 128 * j : 128 * j + 128]
        other = swap_halves(part)
        out[:, at(first + 4 * n + 2 * j, 128)] = (jnp.where(left, part, other) * trig).astype(BF16)
        out[:, at(first + 4 * n + 2 * j + 1, 128)] = (jnp.where(left, other, part) * trig).astype(BF16)


def state_sums(p, qk_ref, v_ref, state_ref, early_ref):
    for j in range(2):
        h = 2 * p + j
        keys, values = at(HEADS + h, 128), at(h, 128)
        early = tn(v_ref[0:CHUNK, values], qk_ref[0:CHUNK, keys])
        early_ref[h] = early[0:72]
        both = early + tn(v_ref[CHUNK:ROWS, values], qk_ref[CHUNK:ROWS, keys])
        state_ref[p, 64 * j : 64 * j + 64] = both[0:64]
        state_ref[p, 128 + j : 129 + j] = both[64:65]
    state_ref[p, 130:136] = jnp.zeros((6, 128), F32)


def exchange_steps(n, pay, out, core_in, chip, head, tail, total, msgs, xa, ya, yb, xb, send, recv):
    my, mx = lax.axis_index("seq_0"), lax.axis_index("seq_1")
    core = lax.axis_index(CORE)
    other = 1 - core
    own = 2 * n + core

    def remote(src, dst, stage, k, target):
        pltpu.make_async_remote_copy(
            src_ref=src, dst_ref=dst, send_sem=send.at[n, stage], recv_sem=recv.at[n, k],
            device_id=target, device_id_type=MESH).start()

    def counts(theirs, mine):
        return theirs < mine

    def chosen(flag, value):
        return jnp.where(flag, value, jnp.zeros_like(value))

    def first():
        remote(pay.at[2 * n + other], core_in.at[n], 0, 0, {CORE: other})

    def second():
        arrived(core_in.at[n], recv.at[n, 0])
        chip[n] = pay[own] + core_in[n]
        for k, d in enumerate(DIRECT):
            remote(chip.at[n, pl.ds(0, 72)], xa.at[n, k], 1, 1, {"seq_1": rot(mx, d)})
        for k, d in enumerate(DIRECT):
            remote(chip.at[n, pl.ds(72, 64)], yb.at[n, k], 1, 2, {"seq_0": rot(my, d)})

    def third():
        arrived(xa.at[n], recv.at[n, 1])
        some, every = jnp.zeros((72, 128), F32), chip[n, 0:72]
        for k, d in enumerate(DIRECT):
            some = some + chosen(counts(rot(mx, 4 - d), mx), xa[n, k])
            every = every + xa[n, k]
        head[n] = some
        total[n] = every
        for k, d in enumerate(DIRECT):
            remote(total.at[n], ya.at[n, k], 2, 3, {"seq_0": rot(my, d)})
        arrived(yb.at[n], recv.at[n, 2])
        some = jnp.zeros((64, 128), F32)
        for k, d in enumerate(DIRECT):
            some = some + chosen(counts(rot(my, 4 - d), my), yb[n, k])
        tail[n] = some
        for k, d in enumerate(DIRECT):
            msgs[n, k] = some + chosen(counts(mx, rot(mx, d)), chip[n, 72:136])
        for k, d in enumerate(DIRECT):
            remote(msgs.at[n, k], xb.at[n, k], 2, 4, {"seq_1": rot(mx, d)})

    def fourth():
        arrived(ya.at[n], recv.at[n, 3])
        arrived(xb.at[n], recv.at[n, 4])
        arrived(chip, send.at[n, 1])
        mine = core == 1
        low, high = head[n], tail[n]
        for k, d in enumerate(DIRECT):
            low = low + chosen(counts(rot(my, 4 - d), my), ya[n, k])
            high = high + xb[n, k]
        out[own, 0:72] = low + chosen(mine, core_in[n, 0:72])
        out[own, 72:136] = high + chosen(mine, core_in[n, 72:136])
        chip[n, 0:72] = low + chosen(jnp.logical_not(mine), pay[own, 0:72])
        chip[n, 72:136] = high + chosen(jnp.logical_not(mine), pay[own, 72:136])
        remote(chip.at[n], out.at[own], 3, 5, {CORE: other})

    def fifth():
        arrived(out.at[2 * n + other], recv.at[n, 5])

    def sent():
        arrived(core_in.at[n], send.at[n, 0])
        arrived(chip, send.at[n, 2])
        arrived(chip.at[n], send.at[n, 3])

    return first, second, third, fourth, fifth, sent


EXCHANGE_SCRATCH = [
    VMEM((3, 136, 128), F32),
    VMEM((3, 136, 128), F32),
    VMEM((3, 72, 128), F32),
    VMEM((3, 64, 128), F32),
    VMEM((3, 72, 128), F32),
    VMEM((3, 3, 64, 128), F32),
    VMEM((3, 3, 72, 128), F32),
    VMEM((3, 3, 72, 128), F32),
    VMEM((3, 3, 64, 128), F32),
    VMEM((3, 3, 64, 128), F32),
    pltpu.SemaphoreType.DMA((3, 4)),
    pltpu.SemaphoreType.DMA((3, 6)),
]


def quarter_steps(n, pay, out, core_in, chip, xa, total, ya, msgs, got, send, recv):
    my, mx = lax.axis_index("seq_0"), lax.axis_index("seq_1")
    core = lax.axis_index(CORE)
    other = 1 - core
    own = 2 * n + core

    def remote(src, dst, stage, k, target):
        pltpu.make_async_remote_copy(
            src_ref=src, dst_ref=dst, send_sem=send.at[n, stage], recv_sem=recv.at[n, k],
            device_id=target, device_id_type=MESH).start()

    def chosen(flag, value):
        return jnp.where(flag, value, jnp.zeros_like(value))

    def first():
        remote(pay.at[2 * n + other], core_in.at[n], 0, 0, {CORE: other})

    def second():
        arrived(core_in.at[n], recv.at[n, 0])
        chip[n] = pay[own] + core_in[n]
        for k, d in enumerate(DIRECT):
            remote(chip.at[n, rot(mx, d)], xa.at[n, k], 1, 1, {"seq_1": rot(mx, d)})

    def third():
        arrived(xa.at[n], recv.at[n, 1])
        total[n] = chip[n, mx] + xa[n, 0] + xa[n, 1] + xa[n, 2]
        for k, d in enumerate(DIRECT):
            remote(total.at[n], ya.at[n, k], 2, 2, {"seq_0": rot(my, d)})

    def cross():
        arrived(ya.at[n], recv.at[n, 2])
        behind = jnp.zeros((40, 128), F32)
        for k, d in enumerate(DIRECT):
            behind = behind + chosen(rot(my, 4 - d) > my, ya[n, k])

        def for_column(column):
            value = behind + chosen(mx > column, chip[n, mx])
            for k, d in enumerate(DIRECT):
                value = value + chosen(rot(mx, 4 - d) > column, xa[n, k])
            return value

        for k, d in enumerate(DIRECT):
            msgs[n, k] = for_column(rot(mx, d))
            remote(msgs.at[n, k], got.at[n, mx], 3, 3, {"seq_1": rot(mx, d)})
        got[n, mx] = for_column(mx)

    def fourth():
        arrived(xa.at[n], recv.at[n, 3])
        arrived(xa.at[n], send.at[n, 1])
        out[own] = got[n] + chosen(core == 0, core_in[n])
        chip[n] = got[n] + chosen(core == 1, pay[own])
        remote(chip.at[n], out.at[own], 4, 4, {CORE: other})

    def fifth():
        arrived(out.at[2 * n + other], recv.at[n, 4])

    def sent():
        arrived(chip.at[n], send.at[n, 0])
        arrived(xa.at[n], send.at[n, 2])
        arrived(xa.at[n], send.at[n, 3])
        arrived(chip.at[n], send.at[n, 4])

    return first, second, third, fourth, fifth, sent, cross


QUARTER_SCRATCH = [
    VMEM((3, 4, 40, 128), F32),
    VMEM((3, 4, 40, 128), F32),
    VMEM((3, 3, 40, 128), F32),
    VMEM((3, 40, 128), F32),
    VMEM((3, 3, 40, 128), F32),
    VMEM((3, 3, 40, 128), F32),
    VMEM((3, 4, 40, 128), F32),
    pltpu.SemaphoreType.DMA((3, 5)),
    pltpu.SemaphoreType.DMA((3, 5)),
]


class Exchange:
    def __init__(self, steps, *refs):
        self.steps = lambda n: steps(n, *refs)

    def step(self, k, n):
        with jax.named_scope(("swap", "begin", "turn", "end", "share", "sent", "cross")[k]):
            self.steps(n)[k]()


def greet(axes):
    barrier = pltpu.get_barrier_semaphore()
    core = lax.axis_index(CORE)
    pl.semaphore_signal(barrier, inc=1, device_id={CORE: 1 - core}, device_id_type=MESH)
    for axis in axes:
        mine = lax.axis_index(axis)
        for d in DIRECT:
            pl.semaphore_signal(barrier, inc=1, device_id={axis: rot(mine, d)}, device_id_type=MESH)


def greeted(axes):
    pl.semaphore_wait(pltpu.get_barrier_semaphore(), 1 + 3 * len(axes))


def causal_masks():
    row = lax.broadcasted_iota(jnp.int32, (CHUNK, CHUNK), 0)
    col = lax.broadcasted_iota(jnp.int32, (CHUNK, CHUNK), 1)
    return row >= col, row <= col


def prefix_state(before, p, j, early_ref, c):
    body, row = before[p, 64 * j : 64 * j + 64], before[p, 128 + j : 129 + j]
    if c == 1:
        body, row = body + early_ref[2 * p + j, 0:64], row + early_ref[2 * p + j, 64:65]
    return jnp.concatenate([body, jnp.broadcast_to(row, (64, 128))], axis=0)


def attend_local(p, qk_ref, v_ref, top_ref, under_ref):
    causal, _ = causal_masks()
    left = left_lanes(CHUNK)
    cols = at(p, 128)
    for c in range(2):
        rows = slice(CHUNK * c, CHUNK * c + CHUNK)
        sums = []
        for j in range(2):
            h = 2 * p + j
            weight = nt(qk_ref[rows, at(h, 128)], qk_ref[rows, at(HEADS + h, 128)])
            sums.append(nn(jnp.where(causal, weight, 0.0).astype(BF16), v_ref[rows, at(h, 128)]))
        even, odd = sums
        top_ref[rows, cols] = jnp.where(left, even, swap_halves(odd))
        under_ref[rows, cols] = jnp.where(left, swap_halves(even), odd)


def attend_earlier(p, qk_ref, early_ref, before, ratio_ref, inverse_ref, mixed_ref):
    left = left_lanes(CHUNK)
    cols = at(p, 128)
    for c in range(2):
        rows = slice(CHUNK * c, CHUNK * c + CHUNK)
        sums = []
        for j in range(2):
            h = 2 * p + j
            high, low = halves(prefix_state(before, p, j, early_ref, c))
            sums.append(nt(doubled(qk_ref[rows, at(h, 128)]), jnp.concatenate([high, low], axis=1)))
        even, odd = sums
        inverse = 1.0 / (inverse_ref[rows, cols] + jnp.where(left, swap_halves(even), odd))
        ratio = (ratio_ref[rows, cols] + jnp.where(left, even, swap_halves(odd))) * inverse
        ratio_ref[rows, cols] = ratio
        inverse_ref[rows, cols] = inverse
        mixed_ref[rows, cols] = ratio.astype(BF16)


def mean_rows(value):
    return jnp.mean(value, axis=-1, keepdims=True)


def standard(hidden):
    centred = hidden - mean_rows(hidden)
    scale = lax.rsqrt(mean_rows(centred * centred) + EPSILON)
    return centred * scale, scale


def norm_back(grad, normal, scale, gain):
    scaled = grad * gain
    return scale * (scaled - mean_rows(scaled) - normal * mean_rows(scaled * normal))


def column(value):
    return jnp.sum(value, axis=0, keepdims=True)


ORDERS = ((1, 0, 2), (0, 2, 1), (2, 1, 0))
SUBS = 9
COLS = 256


def cell(ref, order, picks):
    at = [slice(None)] * 3
    for axis, pick in zip(order, picks):
        at[axis] = pick
    return ref.at[tuple(at)]


def rest(ref, order, pick):
    return ref.at[pick] if order[1] < order[2] else ref.at[:, pick]


def halved(ref, order, pick, half):
    at = [slice(None)] * 3
    at[order[0]] = pick
    at[1 if order[0] == 0 else 0] = half
    return ref.at[tuple(at)]


def add_blocks(dst, srcs, lead, fresh=False):
    total = 1
    for n in lead:
        total *= n

    def step(k, carry):
        where, rest = [], k
        for n in reversed(lead):
            where.append(lax.rem(rest, n))
            rest = rest // n
        where = tuple(reversed(where))
        value = srcs[0][where] if fresh else dst[where] + srcs[0][where]
        for src in srcs[1:]:
            value = value + src[where]
        dst[where] = value

    lax.fori_loop(0, total, step, None)


SLOTS = (0, 1, 2, 3, 0, 1)


def arrived(ref, sem):
    pltpu.make_async_copy(ref, ref, sem).wait()


class Reduction:
    def __init__(self, stage, sums, first, second, third, done, core_send, core_recv, send, recv, keep,
                 spread_recv, spread_send, final):
        self.stage, self.sums, self.first, self.second, self.third, self.done = stage, sums, first, second, third, done
        self.core_send, self.core_recv, self.send, self.recv, self.keep = core_send, core_recv, send, recv, keep
        self.spread_recv, self.spread_send, self.final = spread_recv, spread_send, final
        self.me = tuple(lax.axis_index(a) for a in AX)
        self.core = lax.axis_index(CORE)
        self.other = 1 - self.core

    def swap(self, g, s, part):
        where = (part,) if g < 2 else (slice(None), slice(None), part)
        return pltpu.make_async_remote_copy(
            src_ref=self.stage.at[(g % 2, s, self.other, *where)], dst_ref=self.sums.at[(SLOTS[g], s, *where)],
            send_sem=self.core_send.at[SLOTS[g], s], recv_sem=self.core_recv.at[SLOTS[g], s],
            device_id={CORE: self.other}, device_id_type=MESH)

    def swaps(self, g):
        for s in range(3):
            for part in range(4):
                self.swap(g, s, part).start()

    def remote(self, src, dst, g, s, stage, k, axis, d):
        pltpu.make_async_remote_copy(
            src_ref=src, dst_ref=dst, send_sem=self.send.at[SLOTS[g], stage] if k < 5 else self.spread_send.at[g],
            recv_sem=self.recv.at[SLOTS[g], s, k] if k < 5 else self.spread_recv.at[g, s],
            device_id={AX[axis]: rot(self.me[axis], d)}, device_id_type=MESH).start()

    def views(self, g, s):
        slot = SLOTS[g]
        return (self.sums.at[slot, s], self.first.at[slot, s], self.second.at[slot, s], self.third.at[slot, s],
                self.done.at[g, s], self.stage.at[g % 2, s, self.core], self.recv.at[slot, s])

    def begin(self, g, s):
        mine, inbox, _, _, _, own, _ = self.views(g, s)
        arrived(mine, self.core_recv.at[SLOTS[g], s])
        arrived(own, self.core_send.at[SLOTS[g], s])
        add_blocks(mine, [own], (4, 4))
        order = ORDERS[s]
        ax = order[0]
        far = rot(self.me[ax], 2)
        lo, hi = pl.ds(0, 2), pl.ds(2, 2)
        self.remote(halved(mine, order, far, lo), inbox.at[0, lo], g, s, 0, 0, ax, 1)
        self.remote(halved(mine, order, far, hi), inbox.at[0, hi], g, s, 0, 1, ax, 3)

    def follow(self, g, s):
        mine, inbox = self.views(g, s)[:2]
        order = ORDERS[s]
        ax = order[0]
        i = self.me[ax]
        lo, hi = pl.ds(0, 2), pl.ds(2, 2)
        self.remote(halved(mine, order, rot(i, 1), hi), inbox.at[1, hi], g, s, 0, 2, ax, 1)
        self.remote(halved(mine, order, rot(i, 3), lo), inbox.at[2, lo], g, s, 0, 2, ax, 3)

    def relay(self, g, s):
        mine, inbox, _, _, _, _, recv = self.views(g, s)
        order = ORDERS[s]
        ax = order[0]
        i = self.me[ax]
        lo, hi = pl.ds(0, 2), pl.ds(2, 2)
        arrived(inbox.at[0, lo], recv.at[0])
        part = halved(mine, order, rot(i, 1), lo)
        add_blocks(part, [inbox.at[0, lo]], (2, 4))
        self.remote(part, inbox.at[1, lo], g, s, 0, 2, ax, 1)
        arrived(inbox.at[0, hi], recv.at[1])
        part = halved(mine, order, rot(i, 3), hi)
        add_blocks(part, [inbox.at[0, hi]], (2, 4))
        self.remote(part, inbox.at[2, hi], g, s, 0, 2, ax, 3)

    def middle(self, g, s):
        mine, inbox, second, _, _, _, recv = self.views(g, s)
        order = ORDERS[s]
        arrived(inbox.at[pl.ds(1, 2)], recv.at[2])
        i, ax = self.me[order[0]], order[1]
        add_blocks(inbox.at[0], [cell(mine, order, (i,)), inbox.at[1], inbox.at[2]], (4,), fresh=True)
        for k, d in enumerate(DIRECT):
            self.remote(rest(inbox.at[0], order, rot(self.me[ax], d)), second.at[k], g, s, 1, 3, ax, d)

    def cleared(self, g):
        arrived(self.first.at[SLOTS[g]], self.send.at[SLOTS[g], 0])

    def last(self, g, s):
        _, inbox, second, third, _, _, recv = self.views(g, s)
        order = ORDERS[s]
        arrived(second, recv.at[3])
        mine = rest(inbox.at[0], order, self.me[order[1]])
        add_blocks(mine, [second.at[k] for k in range(3)], (4,))
        ax = order[2]
        for k, d in enumerate(DIRECT):
            self.remote(mine.at[rot(self.me[ax], d)], third.at[k], g, s, 2, 4, ax, d)

    def spread(self, g, s):
        _, inbox, _, third, done, _, recv = self.views(g, s)
        order = ORDERS[s]
        arrived(third, recv.at[4])
        part = rest(inbox.at[0], order, self.me[order[1]]).at[self.me[order[2]]]
        self.final[g, s] = part[...] + third[0] + third[1] + third[2]
        part = self.final.at[g, s]
        z = self.me[2]
        for k, d in enumerate(DIRECT):
            self.remote(part, done.at[z], g, s, 3, 5, 2, d)
        pltpu.make_async_copy(part, done.at[z], self.keep.at[g]).start()

    def finish(self, g, s):
        third = self.views(g, s)[3]
        arrived(third, self.spread_recv.at[g, s])

    def sent(self, g):
        slot = SLOTS[g]
        arrived(self.second.at[slot], self.send.at[slot, 1])
        arrived(self.third.at[slot], self.send.at[slot, 2])

    def spread_sent(self, g):
        arrived(self.final.at[g], self.keep.at[g])
        arrived(self.third.at[SLOTS[g]], self.spread_send.at[g])

    def each(self, step, g):
        with jax.named_scope(f"{step.__name__} {g}"):
            for s in range(3):
                step(g, s)


def vector_steps(vec, vecs, send, recv):
    me = tuple(lax.axis_index(a) for a in AX)
    core = lax.axis_index(CORE)
    bases = (0, 1, 4, 7)

    def start(stage):
        if stage == 0:
            targets = [{CORE: 1 - core}]
        else:
            ax = stage - 1
            targets = [{AX[ax]: rot(me[ax], d)} for d in DIRECT]
        for k, target in enumerate(targets):
            pltpu.make_async_remote_copy(
                src_ref=vec, dst_ref=vecs.at[bases[stage] + k], send_sem=send.at[stage], recv_sem=recv.at[stage],
                device_id=target, device_id_type=MESH).start()

    def end(stage):
        with jax.named_scope("vector"):
            count = 3 if stage else 1
            part = vecs.at[pl.ds(bases[stage], count)]
            arrived(part, recv.at[stage])
            arrived(part, send.at[stage])
            total = vec[...]
            for k in range(count):
                total = total + vecs[bases[stage] + k]
            vec[...] = total

    return start, end


def suffix_state(after, p, j, late_ref, c):
    body, row = after[p, 2 * j : 2 * j + 2, 0:32].reshape(64, 128), after[p, 0, 32 + j : 33 + j]
    if c == 0:
        h = 2 * p + j
        body, row = body + late_ref[h, 0:64], row + (late_ref[h, 64:65] + late_ref[h, 65:66])
    first = lax.broadcasted_iota(jnp.int32, (64, 128), 0) == 0
    return jnp.concatenate([body, jnp.where(first, jnp.broadcast_to(row, (64, 128)), 0.0)], axis=0)


def attend_back_query(p, act, bufu, early_ref, before, trigs, grads):
    causal, _ = causal_masks()
    left = left_lanes(CHUNK)
    for c in range(2):
        rows = slice(CHUNK * c, CHUNK * c + CHUNK)
        query = []
        for j in range(2):
            h = 2 * p + j
            k = bufu[rows, at(HEADS + h, 128)]
            v, g = act[rows, at(h, 128)], act[rows, at(HEADS + h, 128)]
            high, low = halves(prefix_state(before, p, j, early_ref, c))
            weight = jnp.where(causal, nt(g, v), 0.0).astype(BF16)
            gq = nn(weight, k) + nn(doubled(g), jnp.concatenate([high, low], axis=0))
            gq = gq * trigs[0, rows]
            query.append(gq + swap_halves(gq))
        gate = bufu[ROWS:WIDTH, at(PAIRS * c + p, 128)].astype(F32)
        grads[rows, at(p, 128)] = (jnp.where(left, query[0], query[1]) * gate).astype(BF16)


def attend_back_local(p, act, bufu, trigs, key_ref, value_ref):
    _, flipped = causal_masks()
    left = left_lanes(CHUNK)
    cols = at(p, 128)
    for c in range(2):
        rows = slice(CHUNK * c, CHUNK * c + CHUNK)
        keys, value = [], []
        for j in range(2):
            h = 2 * p + j
            q, k = bufu[rows, at(h, 128)], bufu[rows, at(HEADS + h, 128)]
            v, g = act[rows, at(h, 128)], act[rows, at(HEADS + h, 128)]
            gk = nn(jnp.where(flipped, nt(v, g), 0.0).astype(BF16), q) * trigs[1, rows]
            keys.append(gk + swap_halves(gk))
            value.append(nn(jnp.where(flipped, nt(k, q), 0.0).astype(BF16), g))
        key_ref[rows, cols] = jnp.where(left, keys[0], keys[1])
        value_ref[rows, cols] = jnp.where(left, value[0], swap_halves(value[1]))


def attend_back_later(p, act, bufu, late_ref, after, trigs, ratio_ref, inverse_ref, grads):
    left = left_lanes(CHUNK)
    for c in range(2):
        rows = slice(CHUNK * c, CHUNK * c + CHUNK)
        keys, value = [], []
        for j in range(2):
            h = 2 * p + j
            k, v = bufu[rows, at(HEADS + h, 128)], act[rows, at(h, 128)]
            high, low = halves(suffix_state(after, p, j, late_ref, c))
            gk = nn(doubled(v), jnp.concatenate([high, low], axis=0)) * trigs[1, rows]
            keys.append(gk + swap_halves(gk))
            value.append(nt(doubled(k), jnp.concatenate([high, low], axis=1)))
        cols = at(p, 128)
        gate = bufu[ROWS:WIDTH, at(2 * PAIRS + PAIRS * c + p, 128)].astype(F32)
        gk = (ratio_ref[rows, cols] + jnp.where(left, keys[0], keys[1])) * gate
        grads[rows, at(PAIRS + p, 128)] = gk.astype(BF16)
        gv = inverse_ref[rows, cols] + jnp.where(left, value[0], swap_halves(value[1]))
        grads[rows, at(2 * PAIRS + p, 128)] = gv.astype(BF16)


def layer_kernel(len_ref, bq_in, bk_in, bv_in, bo_in, gain1_in, shift1_in, bdown_in, gain2_in, shift2_in, bup_in,
                 x_hbm, wq_hbm, wk_hbm, wv_hbm, wo_hbm, wup_hbm, wdown_hbm, cot_hbm,
                 block_out, tokens_out, done_out, vec_out, act_spill, slope_spill,
                 x_ref, act, slope, bufu, bufd, trigs, early_ref, late_ref, state, before, pay, after,
                 ratio_ref, inverse_ref, normal_ref, acc_ref, scale_ref, mixed_ref, normed_ref, gffn_ref, vec_ref, rows_ref,
                 bup, turned, stage, sums, first_in, second_in, third_in, final_ref, vecs,
                 load_sem, core_send, core_recv, send, recv, keep_sem, spread_recv, spread_send, vec_send, vec_recv, free_sem, open_sem, *scratch):
    everywhere = ("seq_0", "seq_1", "batch")
    greet(everywhere)
    loads = {}

    def load(name, src, dst):
        copy = pltpu.make_async_copy(src, dst, load_sem.at[len(loads)])
        copy.start()
        loads[name] = copy

    def ready(*names):
        with jax.named_scope("ready"):
            for name in names:
                loads[name].wait()

    def note(k, value):
        vec_ref[k : k + 1, :] += value

    load("x", x_hbm, x_ref)
    for n in range(3):
        cols = pl.ds(256 * n, 256)
        load(f"wv{n}", wv_hbm.at[:, cols], bufd.at[2 * WIDTH : 3 * WIDTH, cols])
        load(f"wk{n}", wk_hbm.at[:, cols], bufd.at[WIDTH : 2 * WIDTH, cols])
    load("wq", wq_hbm, bufd.at[0:WIDTH])
    for k, vector in enumerate((bq_in, bk_in, bv_in, bo_in, gain1_in, shift1_in, bdown_in, gain2_in, shift2_in)):
        rows_ref[k : k + 1, :] = vector[...].reshape(1, WIDTH)
    bup[...] = bup_in[...].reshape(1, HIDDEN)
    bq, bk, bv, bo, gain1, shift1, bdown, gain2, shift2 = (rows_ref.at[k : k + 1] for k in range(9))
    vec_ref[...] = jnp.zeros_like(vec_ref)
    length = len_ref[0]
    start = ROWS * ((lax.axis_index("seq_0") * 4 + lax.axis_index("seq_1")) * 2 + lax.axis_index(CORE))

    def angles(r):
        both, valid = trig_block(start + 128 * r, 128, length)
        trigs[0, at(r, 128)] = both
        trigs[1, at(r, 128)] = both * valid

    loop(ROWS // 128, angles)
    ready("x", "wv0", "wk0")
    load("wup", wup_hbm, bufu)
    wo = bufd.at[3 * WIDTH : HIDDEN]
    load("wo", wo_hbm, wo)
    load("cot", cot_hbm, gffn_ref)
    earlier_sums = Exchange(exchange_steps, state, before, *scratch[: len(EXCHANGE_SCRATCH)])
    later_sums = Exchange(quarter_steps, pay, after, *scratch[len(EXCHANGE_SCRATCH) :])

    def keys(n):
        project_values(n, x_ref, bufd.at[2 * WIDTH : 3 * WIDTH], bv, slope)
        project_soft(n, x_ref, bufd.at[WIDTH : 2 * WIDTH], bk, trigs.at[1], act, HEADS, slope, 9)
        each_of(2, lambda j: state_sums(2 * n + j, act, slope, state, early_ref))
        pl.when(n == 0)(lambda: greeted(everywhere))
        earlier_sums.step(0, n)
        pl.when(n > 0)(lambda: earlier_sums.step(1, n - 1))

    def queries(n):
        project_soft(n, x_ref, bufd.at[0:WIDTH], bq, trigs.at[0], act, 0, slope, 6)
        pl.when(n == 0)(lambda: earlier_sums.step(1, 2))

    def own(p):
        pl.when(lax.rem(p, 2) == 0)(lambda: earlier_sums.step(2, p // 2))
        attend_local(p, act, slope, ratio_ref, inverse_ref)

    def earlier(p):
        pl.when(lax.rem(p, 2) == 0)(lambda: earlier_sums.step(4, p // 2))
        attend_earlier(p, act, early_ref, before, ratio_ref, inverse_ref, mixed_ref)

    loop(3, keys, {n: lambda n=n: ready(f"wv{n + 1}", f"wk{n + 1}") for n in range(2)})
    ready("wq")
    loop(3, queries)
    load("wdown", wdown_hbm.at[0 : 3 * WIDTH], bufd.at[0 : 3 * WIDTH])
    load("qk_out", act, act_spill)
    load("v_out", slope, slope_spill)
    loop(PAIRS, own)
    each_of(3, lambda n: earlier_sums.step(3, n))
    loop(PAIRS, earlier)
    ready("wo")

    def first_norm(r):
        rows = at(r, CHUNK)
        hidden = x_ref[rows].astype(F32) + (nn(mixed_ref[rows], wo[...]) + bo[...])
        normal, scale = standard(hidden)
        normal_ref[rows] = normal
        scale_ref[rows] = jnp.broadcast_to(scale, (CHUNK, 128))
        normed_ref[rows] = (normal * gain1[...] + shift1[...]).astype(BF16)

    loop(ROWS // CHUNK, first_norm)
    load("wdown end", wdown_hbm.at[3 * WIDTH : HIDDEN], wo)
    ready("qk_out", "v_out", "wup", "wdown")

    def feed(t):
        cols = at(t, FEED)
        for r in range(2):
            rows = slice(CHUNK * r, CHUNK * r + CHUNK)
            pre = nn(normed_ref[rows], bufu[:, cols]) + bup[:, cols]
            whole, bell = normal_parts(pre)
            active = (pre * whole).astype(BF16)
            act[rows, cols] = active
            slope[rows, cols] = (whole + pre * bell).astype(BF16)
            acc_ref[rows] = nn(active, bufd[cols]) + jnp.where(t == 0, 0.0, acc_ref[rows])

    loop(3, feed, {1: lambda: ready("wdown end")})
    ready("cot")

    def second_norm(r):
        rows = at(r, CHUNK)
        hidden = normed_ref[rows].astype(F32) + (acc_ref[rows] + bdown[...])
        normal, scale = standard(hidden)
        x_ref[rows] = (normal * gain2[...] + shift2[...]).astype(BF16)
        grad = gffn_ref[rows].astype(F32)
        note(7, column(grad * normal))
        note(8, column(grad))
        back = norm_back(grad, normal, scale, gain2[...])
        acc_ref[rows] = back
        low = back.astype(BF16)
        gffn_ref[rows] = low
        note(6, column(low.astype(F32)))

    loop(ROWS // CHUNK, second_norm)
    load("block", x_ref, block_out)
    red = Reduction(stage, sums, first_in, second_in, third_in, done_out, core_send, core_recv, send, recv, keep_sem,
                    spread_recv, spread_send, final_ref)

    def down_rows(y):
        turned[...] = act[:, at(y, WIDTH)].T
        for n in range(3):
            value = nn(turned[...], gffn_ref[:, 256 * n : 256 * n + 256]).reshape(4, 2, 4, 24, 256)
            for half in range(2):
                unit = 2 * n + half
                for side in range(2):
                    stage[unit // 3, unit % 3, side, y] = value[:, side, :, :, 128 * half : 128 * half + 128]
        for s in range(3):
            red.swap(0, s, y).start()

    loop(4, down_rows)
    red.swaps(1)
    load("v", slope_spill.at[:, 0 : 128 * HEADS], act.at[:, 0 : 128 * HEADS])

    def feed_back(k):
        t = 1 - k
        cols = at(t, TILE)
        total = jnp.zeros((1, TILE), F32)
        for r in range(2):
            rows = slice(CHUNK * r, CHUNK * r + CHUNK)
            gpre = (nt(gffn_ref[rows], bufd[cols]) * slope[rows, cols].astype(F32)).astype(BF16)
            slope[rows, cols] = gpre
            total = total + column(gpre.astype(F32))
            acc_ref[rows] += nt(gpre, bufu[:, cols])
        for half in range(2):
            vec_ref[pl.ds(9 + 2 * t + half, 1), :] = total[:, WIDTH * half : WIDTH * half + WIDTH]

    loads["wo again"] = pltpu.make_async_copy(wo_hbm, wo, load_sem.at[31])

    def down_begun():
        red.each(red.begin, 0)
        loads["wo again"].start()

    loop(2, feed_back, {0: down_begun})
    red.each(red.follow, 0)
    red.each(red.begin, 1)
    ready("block")
    load("x again", x_hbm, x_ref)
    load("wq again", wq_hbm, bufd.at[0:WIDTH])
    load("wk again", wk_hbm, bufd.at[WIDTH : 2 * WIDTH])
    load("wv again", wv_hbm, bufd.at[2 * WIDTH : 3 * WIDTH])
    load("qk", act_spill, bufu.at[0:ROWS])
    gates = []
    for i in range(2):
        for c in range(2):
            gates.append(f"gate {i}{c}")
            load(gates[-1], slope_spill.at[CHUNK * c : CHUNK * c + CHUNK, pl.ds(128 * HEADS + WIDTH * i, WIDTH)],
                 bufu.at[ROWS:WIDTH, pl.ds(2 * WIDTH * i + WIDTH * c, WIDTH)])
    def up_columns(b):
        for n in range(3):
            cols = pl.ds(pl.multiple_of(WIDTH * b + 256 * n, 256), 256)
            value = nn(turned[...], slope[:, cols]).reshape(4, 4, 2, 24, 256)
            for half in range(2):
                unit = 2 * n + half
                for side in range(2):
                    stage[unit // 3, unit % 3, side, :, :, b] = value[:, :, side, :, 128 * half : 128 * half + 128]
        for s in range(3):
            red.swap(2, s, b).start()

    def first_back(r):
        rows = at(r, CHUNK)
        normal = normal_ref[rows]
        scale = scale_ref[rows, 0:1]
        grad = acc_ref[rows]
        note(4, column(grad * normal))
        note(5, column(grad))
        back = norm_back(grad, normal, scale, gain1[...])
        acc_ref[rows] = back
        low = back.astype(BF16)
        gffn_ref[rows] = low
        note(3, column(low.astype(F32)))
        normal_ref[rows] = nt(low, wo[...])

    def heads_back(p):
        cols = at(p, 128)
        lane = lax.broadcasted_iota(jnp.int32, (ROWS, 128), 1)
        left = lane < 64
        gnum = (normal_ref[:, cols] * inverse_ref[:, cols]).astype(BF16).astype(F32)
        product = gnum * ratio_ref[:, cols]
        ends_of = []
        for j in range(2):
            h = 2 * p + j
            mine = jnp.where(left, product, 0.0) if j == 0 else jnp.where(left, 0.0, product)
            gden = jnp.broadcast_to(-jnp.sum(mine, axis=1, keepdims=True), (ROWS, 128))
            high = gden.astype(BF16).astype(F32)
            ends = jnp.where(lane == 64, high, jnp.where(lane == 65, gden - high, 0.0))
            grad = jnp.where(left, gnum if j == 0 else swap_halves(gnum), ends).astype(BF16)
            act[:, at(HEADS + h, 128)] = grad
            late = tn(grad[CHUNK:ROWS], bufu[CHUNK:ROWS, at(h, 128)])
            late_ref[h] = late[0:72]
            both = late + tn(grad[0:CHUNK], bufu[0:CHUNK, at(h, 128)])
            for half in range(2):
                pay[p, 2 * j + half, 0:32] = both[32 * half : 32 * half + 32]
                pay[p, 2 * j + half, 32:40] = jnp.zeros((8, 128), F32)
            ends_of.append(both[64:65] + both[65:66])
        for j in range(2):
            pay[p, 0, 32 + j : 33 + j] = ends_of[j]

    def query_back(p):
        attend_back_query(p, act, bufu, early_ref, before, trigs, slope)

    def own_back(p):
        attend_back_local(p, act, bufu, trigs, ratio_ref, inverse_ref)

    def later(p):
        attend_back_later(p, act, bufu, late_ref, after, trigs, ratio_ref, inverse_ref, slope)

    def back(r):
        rows = at(r, CHUNK)
        total = acc_ref[rows]
        for i in range(3):
            total = total + nt(slope[rows, WIDTH * i : WIDTH * i + WIDTH], bufd[WIDTH * i : WIDTH * i + WIDTH])
        acc_ref[rows] = total

    def product(rhs, base, g, b0, n):
        with jax.named_scope("product"):
            value = nn(turned[...], rhs[:, at(base + n, 256)]).reshape(4, 4, 2, 24, 256)
            for part in range(2):
                unit = 2 * n + part
                half, s = unit // 3, lax.rem(unit, 3)
                for side in range(2):
                    stage[g % 2, s, side, :, :, b0 + half] = value[:, :, side, :, 128 * part : 128 * part + 128]
                red.swap(g, s, b0 + half).start()

    def free(k):
        red.cleared(k)
        pl.semaphore_signal(free_sem.at[k], inc=1, device_id={CORE: red.other}, device_id_type=MESH)

    def freed(k):
        with jax.named_scope("freed"):
            pl.semaphore_wait(free_sem.at[k], 1)

    def release(k):
        red.sent(k)
        for axis in everywhere:
            for d in DIRECT:
                pl.semaphore_signal(open_sem.at[k], inc=1, device_id={axis: rot(lax.axis_index(axis), d)},
                                    device_id_type=MESH)

    def released(k):
        with jax.named_scope("released"):
            pl.semaphore_wait(open_sem.at[k], 9)

    ready("wo again")
    loop(ROWS // CHUNK, first_back)
    red.each(red.relay, 0)
    red.each(red.follow, 1)
    each_of(3, lambda n: earlier_sums.step(5, n))
    ready("qk", "v")

    def heads_sent(p):
        heads_back(p)

        @pl.when(lax.rem(p, 2) == 1)
        def _():
            later_sums.step(0, p // 2)
            pl.when(p > 1)(lambda: later_sums.step(1, p // 2 - 1))

    loop(PAIRS, heads_sent)
    turned[...] = normed_ref[...].T

    def up_first():
        later_sums.step(1, 2)
        red.each(red.relay, 1)

    loop(4, up_columns, {0: up_first, 2: lambda: red.each(red.middle, 0)})
    red.swaps(3)
    later_sums.step(2, 0)
    free(0)
    ready(*gates)

    def query_two(n):
        query_back(2 * n)
        query_back(2 * n + 1)

    def query_second():
        later_sums.step(2, 1)
        red.each(red.begin, 2)

    def query_fourth():
        later_sums.step(2, 2)
        later_sums.step(6, 0)
        red.each(red.middle, 1)

    loop(3, query_two, {0: query_second, 1: query_fourth})
    red.each(red.begin, 3)
    red.each(red.follow, 2)
    later_sums.step(6, 1)
    red.each(red.last, 0)
    free(1)
    turned[...] = mixed_ref[...].T
    freed(0)
    loop(3, lambda n: product(gffn_ref, 0, 4, 0, n))
    later_sums.step(6, 2)
    ready("x again")
    turned[...] = x_ref[...].T
    loop(3, lambda n: product(slope, 0, 4, 2, n))

    def own_two(n):
        own_back(2 * n)
        own_back(2 * n + 1)

    def own_fourth():
        red.each(red.relay, 2)
        red.each(red.follow, 3)
        red.each(red.last, 1)

    loop(3, own_two, {1: own_fourth})
    red.each(red.relay, 3)
    each_of(3, lambda n: later_sums.step(3, n))
    red.each(red.spread, 0)
    release(0)
    freed(1)

    def keys_values(n):
        later_sums.step(4, n)
        each_of(2, lambda j: later(2 * n + j))
        each_of(2, lambda i: product(slope, 3 + 3 * i, 5, 2 * i, n))

    def keys_first():
        red.each(red.middle, 2)
        red.each(red.spread, 1)
        release(1)

    def keys_second():
        released(0)
        red.each(red.begin, 4)
        red.each(red.middle, 3)

    loop(3, keys_values, {0: keys_first, 1: keys_second})
    red.each(red.follow, 4)
    for i in range(3):
        note(i, column(slope[:, WIDTH * i : WIDTH * i + WIDTH].astype(F32)))
    vector_start, vector_end = vector_steps(vec_ref, vecs, vec_send, vec_recv)
    vector_start(0)
    released(1)
    red.each(red.begin, 5)
    red.each(red.relay, 4)
    vector_end(0)
    ready("wq again", "wk again", "wv again")

    def back_first():
        red.each(red.follow, 5)
        red.each(red.last, 2)

    loop(ROWS // CHUNK, back, {0: back_first})
    load("tokens", acc_ref, tokens_out)
    red.each(red.relay, 5)
    vector_start(1)
    red.each(red.middle, 4)
    red.each(red.last, 3)
    red.each(red.spread, 2)
    vector_end(1)
    vector_start(2)
    red.each(red.middle, 5)
    red.each(red.last, 4)
    red.each(red.spread, 3)
    vector_end(2)
    vector_start(3)
    red.each(red.last, 5)
    red.each(red.spread, 4)
    vector_end(3)
    load("vec", vec_ref, vec_out)
    red.each(red.spread, 5)
    for g in range(6):
        red.each(red.finish, g)
        red.spread_sent(g)
    for g in range(2, 6):
        red.cleared(g)
        red.sent(g)
    each_of(3, lambda n: later_sums.step(5, n))
    ready("tokens", "vec")


def final_kernel(done, vecs, tokens, block, block_out, tokens_out, out_q, out_bq, out_k, out_bk, out_v, out_bv, out_o,
                 out_bo, out_g1, out_s1, out_up, out_bup, out_down, out_bdown, out_g2, out_s2):
    tokens_out[...] = tokens[...]
    block_out[...] = block[...]
    for s in range(3):
        for b in range(4):
            for half in range(2):
                at_col = 384 * half + 128 * s
                out_down[24 * b : 24 * b + 24, at_col : at_col + 128] = done[half, s, b]
                out_up[:, 768 * b + at_col : 768 * b + at_col + 128] = done[2 + half, s, b]
            cols = slice(384 * (b % 2) + 128 * s, 384 * (b % 2) + 128 * s + 128)
            (out_o, out_q)[b // 2][:, cols] = done[4, s, b]
            (out_k, out_v)[b // 2][:, cols] = done[5, s, b]
    seq = (lax.axis_index("seq_0") * 4 + lax.axis_index("seq_1")) * 2 + lax.axis_index(CORE)
    values = vecs[...]
    mine = pltpu.roll(values, lax.rem(WIDTH - 24 * seq, WIDTH), 1)
    for k, out in enumerate((out_bq, out_bk, out_bv, out_bo, out_g1, out_s1, out_bdown, out_g2, out_s2)):
        out[...] = mine[k, 0:24]
    spun = pltpu.roll(values, lax.rem(WIDTH - 96 * lax.rem(seq, 8), WIDTH), 1)
    row = lax.broadcasted_iota(jnp.int32, (16, WIDTH), 0)
    out_bup[...] = jnp.sum(jnp.where(row == 9 + seq // 8, spun, 0.0), axis=0)[0:96]


def on_device(tokens, lengths, w_query, b_query, w_key, b_key, w_value, b_value, w_out, b_out, gain_one, shift_one,
              w_up, b_up, w_down, b_down, gain_two, shift_two, cotangent):
    vmem = pl.BlockSpec(memory_space=VMEM)
    smem = pl.BlockSpec(memory_space=pltpu.SMEM)
    anywhere = pl.BlockSpec(memory_space=pl.ANY)
    out = jax.ShapeDtypeStruct
    wide16, wide32, long16 = ((ROWS, WIDTH), BF16), ((ROWS, WIDTH), F32), ((ROWS, HIDDEN), BF16)
    per_head, packed = ((HEADS, 72, 128), F32), ((PAIRS, 136, 128), F32)
    quarters = ((PAIRS, 4, 40, 128), F32)
    vector = ((16, WIDTH), F32)
    finished = ((6, 3, 4, 24, 128), F32)
    block, tokens_grad, done, sums, _, _ = pl.pallas_call(
        layer_kernel,
        out_shape=[out(*shape) for shape in (wide16, wide32, finished, vector, long16, long16)],
        in_specs=[smem] + [vmem] * 10 + [anywhere] * 8,
        out_specs=[anywhere] * 6,
        scratch_shapes=[VMEM(*shape) for shape in (
            wide16, long16, long16, ((WIDTH, HIDDEN), BF16), ((HIDDEN, WIDTH), BF16),
            ((2, ROWS, 128), F32), per_head, per_head, packed, packed, quarters, quarters,
            wide32, wide32, wide32, wide32, ((ROWS, 128), F32), wide16, wide16, wide16, vector, vector,
            ((1, HIDDEN), F32), ((WIDTH, ROWS), BF16),
            ((2, 3, 2, 4, 4, 4, 24, 128), F32), ((4, 3, 4, 4, 4, 24, 128), F32), ((4, 3, 3, 4, 4, 24, 128), F32),
            ((4, 3, 3, 4, 24, 128), F32), ((4, 3, 3, 24, 128), F32), ((6, 3, 24, 128), F32), ((10, 16, WIDTH), F32))]
        + [pltpu.SemaphoreType.DMA((32,)), pltpu.SemaphoreType.DMA((4, 3)), pltpu.SemaphoreType.DMA((4, 3)),
           pltpu.SemaphoreType.DMA((4, 3)), pltpu.SemaphoreType.DMA((4, 3, 5)), pltpu.SemaphoreType.DMA((6,)), pltpu.SemaphoreType.DMA((6, 3)),
           pltpu.SemaphoreType.DMA((6,)),
           pltpu.SemaphoreType.DMA((4,)), pltpu.SemaphoreType.DMA((4,)), pltpu.SemaphoreType.REGULAR((2,)), pltpu.SemaphoreType.REGULAR((2,))]
        + EXCHANGE_SCRATCH + QUARTER_SCRATCH,
        compiler_params=pltpu.CompilerParams(collective_id=1, has_side_effects=True, vmem_limit_bytes=LIMIT),
    )(lengths, b_query, b_key, b_value, b_out, gain_one, shift_one, b_down, gain_two, shift_two, b_up,
      tokens[0], w_query, w_key, w_value, w_out, w_up, w_down, cotangent[0])
    square_share, vector_share = out((24, WIDTH), F32), out((24,), F32)
    results = pl.pallas_call(
        final_kernel,
        out_shape=[out(*wide16), out(*wide32)] + [square_share, vector_share] * 4 + [vector_share] * 2
        + [out((24, HIDDEN), F32), out((96,), F32), out((96, WIDTH), F32)] + [vector_share] * 3,
        in_specs=[vmem] * 4,
        out_specs=[vmem] * 18,
        compiler_params=pltpu.CompilerParams(vmem_limit_bytes=LIMIT),
    )(done, sums, tokens_grad, block)
    return (results[0][None], results[1][None], *results[2:])


def solution(mesh):
    torus = Mesh(mesh.devices.reshape(4, 4, 2, mesh.shape["batch"]), (*SEQ, "batch"))
    rows, shares = P("batch", SEQ, None), P(SEQ, None)
    return jax.shard_map(
        on_device,
        mesh=torus,
        in_specs=(rows, P("batch")) + (P(),) * 16 + (rows,),
        out_specs=(rows, rows) + (shares, P(SEQ)) * 4 + (P(SEQ), P(SEQ)) + (shares, P(SEQ)) * 2 + (P(SEQ), P(SEQ)),
        check_vma=False,
    )
```

```python
import jax
import jax.numpy as jnp
from jax import lax
from jax.experimental import pallas as pl
from jax.experimental.pallas import tpu as pltpu
from jax.sharding import Mesh
from jax.sharding import PartitionSpec as P

SEQ = ("seq_0", "seq_1", "seq_2")
AX = ("seq_0", "seq_1", "batch")
CORE = "seq_2"
MESH = pl.DeviceIdType.MESH
DIRECT = (1, 3, 2)
F32 = jnp.float32
BF16 = jnp.bfloat16
HALF_PI = 1.5707963267948966
HALF_PI_REST = -4.371139000186241e-08
EPSILON = 1e-05
ROWS = 512
WIDTH = 768
HIDDEN = 3072
HEADS = 12
PAIRS = 6
CHUNK = 256
FEED = 1536
TILE = 1536
VMEM = pltpu.VMEM
LIMIT = 63 * 2**20


def loop(count, body, after=None):
    def step(k, carry):
        with jax.named_scope(body.__name__):
            body(k)
        for n, then in (after or {}).items():
            pl.when(k == n)(then)

    lax.fori_loop(0, count, step, None)


def each_of(count, body):
    lax.fori_loop(0, count, lambda k, carry: body(k), None)


def nn(a, b):
    return jnp.dot(a, b, preferred_element_type=F32)


def nt(a, b):
    return lax.dot_general(a, b, (((1,), (1,)), ((), ())), preferred_element_type=F32)


def tn(a, b):
    return lax.dot_general(a, b, (((0,), (0,)), ((), ())), preferred_element_type=F32)


def at(k, size):
    return pl.ds(pl.multiple_of(k * size, size), size)


def rot(k, d):
    return lax.rem(k + d, 4)


def left_lanes(rows):
    return lax.broadcasted_iota(jnp.int32, (rows, 128), 1) < 64


def swap_halves(value):
    return pltpu.roll(value, 64, 1)


def doubled(value):
    return jnp.concatenate([value, value], axis=1)


def halves(value):
    high = value.astype(BF16)
    return high, (value - high.astype(F32)).astype(BF16)


SIN = (1.0, -0.1666666716337204, 0.008333330973982811, -0.00019840864115394652, 2.7525297809916083e-06, -2.3888299338636898e-08)


def sine(x):
    square = x * x
    value = SIN[5]
    for c in SIN[4::-1]:
        value = value * square + c
    return value * x


def normal_parts(p):
    return 0.5 + 0.5 * lax.erf(p * 0.7071067811865476), 0.3989422804014327 * jnp.exp(-0.5 * p * p)


def trig_block(first, rows, length):
    position = first + lax.broadcasted_iota(jnp.int32, (rows, 128), 0)
    length = jnp.broadcast_to(length, (rows, 128))
    angle = HALF_PI * jnp.minimum(position + 1, length).astype(F32) / length.astype(F32)
    both = sine(jnp.where(left_lanes(rows), (HALF_PI - angle) + HALF_PI_REST, angle))
    return both, (position < length).astype(F32)


def project_values(n, x_ref, w, b, out):
    left = left_lanes(ROWS)
    u = (nn(x_ref[...], w[:, at(n, 256)]) + b[:, at(n, 256)]).astype(BF16).astype(F32)
    for j in range(2):
        part = u[:, 128 * j : 128 * j + 128]
        out[:, at(4 * n + 2 * j, 128)] = jnp.where(left, part, 1.0).astype(BF16)
        out[:, at(4 * n + 2 * j + 1, 128)] = jnp.where(left, swap_halves(part), 1.0).astype(BF16)


def project_soft(n, x_ref, w, b, table, out, first, gates, gate):
    left = left_lanes(ROWS)
    u = nn(x_ref[...], w[:, at(n, 256)]) + b[:, at(n, 256)]
    small = jnp.exp(-jnp.abs(u))
    soft = jnp.maximum(u, 0.0) + jnp.log1p(small)
    gates[:, at(gate + n, 256)] = (0.5 + 0.5 * jnp.tanh(0.5 * u)).astype(BF16)
    trig = table[...]
    for j in range(2):
        part = soft[:, 128 * j : 128 * j + 128]
        other = swap_halves(part)
        out[:, at(first + 4 * n + 2 * j, 128)] = (jnp.where(left, part, other) * trig).astype(BF16)
        out[:, at(first + 4 * n + 2 * j + 1, 128)] = (jnp.where(left, other, part) * trig).astype(BF16)


def state_sums(p, qk_ref, v_ref, state_ref, early_ref):
    for j in range(2):
        h = 2 * p + j
        keys, values = at(HEADS + h, 128), at(h, 128)
        early = tn(v_ref[0:CHUNK, values], qk_ref[0:CHUNK, keys])
        early_ref[h] = early[0:72]
        both = early + tn(v_ref[CHUNK:ROWS, values], qk_ref[CHUNK:ROWS, keys])
        state_ref[p, 64 * j : 64 * j + 64] = both[0:64]
        state_ref[p, 128 + j : 129 + j] = both[64:65]
    state_ref[p, 130:136] = jnp.zeros((6, 128), F32)


def exchange_steps(n, pay, out, core_in, chip, head, tail, total, msgs, xa, ya, yb, xb, send, recv):
    my, mx = lax.axis_index("seq_0"), lax.axis_index("seq_1")
    core = lax.axis_index(CORE)
    other = 1 - core
    own = 2 * n + core

    def remote(src, dst, stage, k, target):
        pltpu.make_async_remote_copy(
            src_ref=src, dst_ref=dst, send_sem=send.at[n, stage], recv_sem=recv.at[n, k],
            device_id=target, device_id_type=MESH).start()

    def counts(theirs, mine):
        return theirs < mine

    def chosen(flag, value):
        return jnp.where(flag, value, jnp.zeros_like(value))

    def first():
        remote(pay.at[2 * n + other], core_in.at[n], 0, 0, {CORE: other})

    def second():
        arrived(core_in.at[n], recv.at[n, 0])
        chip[n] = pay[own] + core_in[n]
        for k, d in enumerate(DIRECT):
            remote(chip.at[n, pl.ds(0, 72)], xa.at[n, k], 1, 1, {"seq_1": rot(mx, d)})
        for k, d in enumerate(DIRECT):
            remote(chip.at[n, pl.ds(72, 64)], yb.at[n, k], 1, 2, {"seq_0": rot(my, d)})

    def third():
        arrived(xa.at[n], recv.at[n, 1])
        some, every = jnp.zeros((72, 128), F32), chip[n, 0:72]
        for k, d in enumerate(DIRECT):
            some = some + chosen(counts(rot(mx, 4 - d), mx), xa[n, k])
            every = every + xa[n, k]
        head[n] = some
        total[n] = every
        for k, d in enumerate(DIRECT):
            remote(total.at[n], ya.at[n, k], 2, 3, {"seq_0": rot(my, d)})
        arrived(yb.at[n], recv.at[n, 2])
        some = jnp.zeros((64, 128), F32)
        for k, d in enumerate(DIRECT):
            some = some + chosen(counts(rot(my, 4 - d), my), yb[n, k])
        tail[n] = some
        for k, d in enumerate(DIRECT):
            msgs[n, k] = some + chosen(counts(mx, rot(mx, d)), chip[n, 72:136])
        for k, d in enumerate(DIRECT):
            remote(msgs.at[n, k], xb.at[n, k], 2, 4, {"seq_1": rot(mx, d)})

    def fourth():
        arrived(ya.at[n], recv.at[n, 3])
        arrived(xb.at[n], recv.at[n, 4])
        arrived(chip, send.at[n, 1])
        mine = core == 1
        low, high = head[n], tail[n]
        for k, d in enumerate(DIRECT):
            low = low + chosen(counts(rot(my, 4 - d), my), ya[n, k])
            high = high + xb[n, k]
        out[own, 0:72] = low + chosen(mine, core_in[n, 0:72])
        out[own, 72:136] = high + chosen(mine, core_in[n, 72:136])
        chip[n, 0:72] = low + chosen(jnp.logical_not(mine), pay[own, 0:72])
        chip[n, 72:136] = high + chosen(jnp.logical_not(mine), pay[own, 72:136])
        remote(chip.at[n], out.at[own], 3, 5, {CORE: other})

    def fifth():
        arrived(out.at[2 * n + other], recv.at[n, 5])

    def sent():
        arrived(core_in.at[n], send.at[n, 0])
        arrived(chip, send.at[n, 2])
        arrived(chip.at[n], send.at[n, 3])

    return first, second, third, fourth, fifth, sent


EXCHANGE_SCRATCH = [
    VMEM((3, 136, 128), F32),
    VMEM((3, 136, 128), F32),
    VMEM((3, 72, 128), F32),
    VMEM((3, 64, 128), F32),
    VMEM((3, 72, 128), F32),
    VMEM((3, 3, 64, 128), F32),
    VMEM((3, 3, 72, 128), F32),
    VMEM((3, 3, 72, 128), F32),
    VMEM((3, 3, 64, 128), F32),
    VMEM((3, 3, 64, 128), F32),
    pltpu.SemaphoreType.DMA((3, 4)),
    pltpu.SemaphoreType.DMA((3, 6)),
]


def quarter_steps(n, pay, out, core_in, chip, xa, total, ya, msgs, got, send, recv):
    my, mx = lax.axis_index("seq_0"), lax.axis_index("seq_1")
    core = lax.axis_index(CORE)
    other = 1 - core
    own = 2 * n + core

    def remote(src, dst, stage, k, target):
        pltpu.make_async_remote_copy(
            src_ref=src, dst_ref=dst, send_sem=send.at[n, stage], recv_sem=recv.at[n, k],
            device_id=target, device_id_type=MESH).start()

    def chosen(flag, value):
        return jnp.where(flag, value, jnp.zeros_like(value))

    def first():
        remote(pay.at[2 * n + other], core_in.at[n], 0, 0, {CORE: other})

    def second():
        arrived(core_in.at[n], recv.at[n, 0])
        chip[n] = pay[own] + core_in[n]
        for k, d in enumerate(DIRECT):
            remote(chip.at[n, rot(mx, d)], xa.at[n, k], 1, 1, {"seq_1": rot(mx, d)})

    def third():
        arrived(xa.at[n], recv.at[n, 1])
        total[n] = chip[n, mx] + xa[n, 0] + xa[n, 1] + xa[n, 2]
        for k, d in enumerate(DIRECT):
            remote(total.at[n], ya.at[n, k], 2, 2, {"seq_0": rot(my, d)})

    def cross():
        arrived(ya.at[n], recv.at[n, 2])
        behind = jnp.zeros((40, 128), F32)
        for k, d in enumerate(DIRECT):
            behind = behind + chosen(rot(my, 4 - d) > my, ya[n, k])

        def for_column(column):
            value = behind + chosen(mx > column, chip[n, mx])
            for k, d in enumerate(DIRECT):
                value = value + chosen(rot(mx, 4 - d) > column, xa[n, k])
            return value

        for k, d in enumerate(DIRECT):
            msgs[n, k] = for_column(rot(mx, d))
            remote(msgs.at[n, k], got.at[n, mx], 3, 3, {"seq_1": rot(mx, d)})
        got[n, mx] = for_column(mx)

    def fourth():
        arrived(xa.at[n], recv.at[n, 3])
        arrived(xa.at[n], send.at[n, 1])
        out[own] = got[n] + chosen(core == 0, core_in[n])
        chip[n] = got[n] + chosen(core == 1, pay[own])
        remote(chip.at[n], out.at[own], 4, 4, {CORE: other})

    def fifth():
        arrived(out.at[2 * n + other], recv.at[n, 4])

    def sent():
        arrived(chip.at[n], send.at[n, 0])
        arrived(xa.at[n], send.at[n, 2])
        arrived(xa.at[n], send.at[n, 3])
        arrived(chip.at[n], send.at[n, 4])

    return first, second, third, fourth, fifth, sent, cross


QUARTER_SCRATCH = [
    VMEM((3, 4, 40, 128), F32),
    VMEM((3, 4, 40, 128), F32),
    VMEM((3, 3, 40, 128), F32),
    VMEM((3, 40, 128), F32),
    VMEM((3, 3, 40, 128), F32),
    VMEM((3, 3, 40, 128), F32),
    VMEM((3, 4, 40, 128), F32),
    pltpu.SemaphoreType.DMA((3, 5)),
    pltpu.SemaphoreType.DMA((3, 5)),
]


class Exchange:
    def __init__(self, steps, *refs):
        self.steps = lambda n: steps(n, *refs)

    def step(self, k, n):
        with jax.named_scope(("swap", "begin", "turn", "end", "share", "sent", "cross")[k]):
            self.steps(n)[k]()


def greet(axes):
    barrier = pltpu.get_barrier_semaphore()
    core = lax.axis_index(CORE)
    pl.semaphore_signal(barrier, inc=1, device_id={CORE: 1 - core}, device_id_type=MESH)
    for axis in axes:
        mine = lax.axis_index(axis)
        for d in DIRECT:
            pl.semaphore_signal(barrier, inc=1, device_id={axis: rot(mine, d)}, device_id_type=MESH)


def greeted(axes):
    pl.semaphore_wait(pltpu.get_barrier_semaphore(), 1 + 3 * len(axes))


def causal_masks():
    row = lax.broadcasted_iota(jnp.int32, (CHUNK, CHUNK), 0)
    col = lax.broadcasted_iota(jnp.int32, (CHUNK, CHUNK), 1)
    return row >= col, row <= col


def prefix_state(before, p, j, early_ref, c):
    body, row = before[p, 64 * j : 64 * j + 64], before[p, 128 + j : 129 + j]
    if c == 1:
        body, row = body + early_ref[2 * p + j, 0:64], row + early_ref[2 * p + j, 64:65]
    return jnp.concatenate([body, jnp.broadcast_to(row, (64, 128))], axis=0)


def attend_local(p, qk_ref, v_ref, top_ref, under_ref):
    causal, _ = causal_masks()
    left = left_lanes(CHUNK)
    cols = at(p, 128)
    for c in range(2):
        rows = slice(CHUNK * c, CHUNK * c + CHUNK)
        sums = []
        for j in range(2):
            h = 2 * p + j
            weight = nt(qk_ref[rows, at(h, 128)], qk_ref[rows, at(HEADS + h, 128)])
            sums.append(nn(jnp.where(causal, weight, 0.0).astype(BF16), v_ref[rows, at(h, 128)]))
        even, odd = sums
        top_ref[rows, cols] = jnp.where(left, even, swap_halves(odd))
        under_ref[rows, cols] = jnp.where(left, swap_halves(even), odd)


def attend_earlier(p, qk_ref, early_ref, before, ratio_ref, inverse_ref, mixed_ref):
    left = left_lanes(CHUNK)
    cols = at(p, 128)
    for c in range(2):
        rows = slice(CHUNK * c, CHUNK * c + CHUNK)
        sums = []
        for j in range(2):
            h = 2 * p + j
            high, low = halves(prefix_state(before, p, j, early_ref, c))
            sums.append(nt(doubled(qk_ref[rows, at(h, 128)]), jnp.concatenate([high, low], axis=1)))
        even, odd = sums
        inverse = 1.0 / (inverse_ref[rows, cols] + jnp.where(left, swap_halves(even), odd))
        ratio = (ratio_ref[rows, cols] + jnp.where(left, even, swap_halves(odd))) * inverse
        ratio_ref[rows, cols] = ratio
        inverse_ref[rows, cols] = inverse
        mixed_ref[rows, cols] = ratio.astype(BF16)


def mean_rows(value):
    return jnp.mean(value, axis=-1, keepdims=True)


def standard(hidden):
    centred = hidden - mean_rows(hidden)
    scale = lax.rsqrt(mean_rows(centred * centred) + EPSILON)
    return centred * scale, scale


def norm_back(grad, normal, scale, gain):
    scaled = grad * gain
    return scale * (scaled - mean_rows(scaled) - normal * mean_rows(scaled * normal))


def column(value):
    return jnp.sum(value, axis=0, keepdims=True)


ORDERS = ((1, 0, 2), (0, 2, 1), (2, 1, 0))
SUBS = 9
COLS = 256


def cell(ref, order, picks):
    at = [slice(None)] * 3
    for axis, pick in zip(order, picks):
        at[axis] = pick
    return ref.at[tuple(at)]


def rest(ref, order, pick):
    return ref.at[pick] if order[1] < order[2] else ref.at[:, pick]


def halved(ref, order, pick, half):
    at = [slice(None)] * 3
    at[order[0]] = pick
    at[1 if order[0] == 0 else 0] = half
    return ref.at[tuple(at)]


def add_blocks(dst, srcs, count, fresh=False):
    def step(k, carry):
        value = srcs[0][k] if fresh else dst[k] + srcs[0][k]
        for src in srcs[1:]:
            value = value + src[k]
        dst[k] = value

    lax.fori_loop(0, count, step, None)


SLOTS = (0, 1, 2, 3, 0, 1)


def arrived(ref, sem):
    pltpu.make_async_copy(ref, ref, sem).wait()


class Reduction:
    def __init__(self, stage, sums, first, second, third, done, core_send, core_recv, send, recv, keep,
                 spread_recv, spread_send, final):
        self.stage, self.sums, self.first, self.second, self.third, self.done = stage, sums, first, second, third, done
        self.core_send, self.core_recv, self.send, self.recv, self.keep = core_send, core_recv, send, recv, keep
        self.spread_recv, self.spread_send, self.final = spread_recv, spread_send, final
        self.me = tuple(lax.axis_index(a) for a in AX)
        self.core = lax.axis_index(CORE)
        self.other = 1 - self.core

    def swap(self, g, s, part):
        where = (part,) if g < 2 else (slice(None), slice(None), part)
        return pltpu.make_async_remote_copy(
            src_ref=self.stage.at[(g % 2, s, self.other, *where)], dst_ref=self.sums.at[(SLOTS[g], s, *where)],
            send_sem=self.core_send.at[SLOTS[g], s], recv_sem=self.core_recv.at[SLOTS[g], s],
            device_id={CORE: self.other}, device_id_type=MESH)

    def swaps(self, g):
        for s in range(3):
            for part in range(4):
                self.swap(g, s, part).start()

    def remote(self, src, dst, g, s, stage, k, axis, d):
        pltpu.make_async_remote_copy(
            src_ref=src, dst_ref=dst, send_sem=self.send.at[SLOTS[g], stage] if k < 5 else self.spread_send.at[g],
            recv_sem=self.recv.at[SLOTS[g], s, k] if k < 5 else self.spread_recv.at[g, s],
            device_id={AX[axis]: rot(self.me[axis], d)}, device_id_type=MESH).start()

    def views(self, g, s):
        slot = SLOTS[g]
        return (self.sums.at[slot, s], self.first.at[slot, s], self.second.at[slot, s], self.third.at[slot, s],
                self.done.at[g, s], self.stage.at[g % 2, s, self.core], self.recv.at[slot, s])

    def begin(self, g, s):
        mine, inbox, _, _, _, own, _ = self.views(g, s)
        arrived(mine, self.core_recv.at[SLOTS[g], s])
        arrived(own, self.core_send.at[SLOTS[g], s])
        add_blocks(mine, [own], 4)
        order = ORDERS[s]
        ax = order[0]
        far = rot(self.me[ax], 2)
        lo, hi = pl.ds(0, 2), pl.ds(2, 2)
        self.remote(halved(mine, order, far, lo), inbox.at[0, lo], g, s, 0, 0, ax, 1)
        self.remote(halved(mine, order, far, hi), inbox.at[0, hi], g, s, 0, 1, ax, 3)

    def follow(self, g, s):
        mine, inbox = self.views(g, s)[:2]
        order = ORDERS[s]
        ax = order[0]
        i = self.me[ax]
        lo, hi = pl.ds(0, 2), pl.ds(2, 2)
        self.remote(halved(mine, order, rot(i, 1), hi), inbox.at[1, hi], g, s, 0, 2, ax, 1)
        self.remote(halved(mine, order, rot(i, 3), lo), inbox.at[2, lo], g, s, 0, 2, ax, 3)

    def relay(self, g, s):
        mine, inbox, _, _, _, _, recv = self.views(g, s)
        order = ORDERS[s]
        ax = order[0]
        i = self.me[ax]
        lo, hi = pl.ds(0, 2), pl.ds(2, 2)
        arrived(inbox.at[0, lo], recv.at[0])
        part = halved(mine, order, rot(i, 1), lo)
        add_blocks(part, [inbox.at[0, lo]], 2)
        self.remote(part, inbox.at[1, lo], g, s, 0, 2, ax, 1)
        arrived(inbox.at[0, hi], recv.at[1])
        part = halved(mine, order, rot(i, 3), hi)
        add_blocks(part, [inbox.at[0, hi]], 2)
        self.remote(part, inbox.at[2, hi], g, s, 0, 2, ax, 3)

    def middle(self, g, s):
        mine, inbox, second, _, _, _, recv = self.views(g, s)
        order = ORDERS[s]
        arrived(inbox.at[pl.ds(1, 2)], recv.at[2])
        i, ax = self.me[order[0]], order[1]
        add_blocks(inbox.at[0], [cell(mine, order, (i,)), inbox.at[1], inbox.at[2]], 4, fresh=True)
        for k, d in enumerate(DIRECT):
            self.remote(rest(inbox.at[0], order, rot(self.me[ax], d)), second.at[k], g, s, 1, 3, ax, d)

    def cleared(self, g):
        arrived(self.first.at[SLOTS[g]], self.send.at[SLOTS[g], 0])

    def last(self, g, s):
        _, inbox, second, third, _, _, recv = self.views(g, s)
        order = ORDERS[s]
        arrived(second, recv.at[3])
        mine = rest(inbox.at[0], order, self.me[order[1]])
        mine[...] = mine[...] + second[0] + second[1] + second[2]
        ax = order[2]
        for k, d in enumerate(DIRECT):
            self.remote(mine.at[rot(self.me[ax], d)], third.at[k], g, s, 2, 4, ax, d)

    def spread(self, g, s):
        _, inbox, _, third, done, _, recv = self.views(g, s)
        order = ORDERS[s]
        arrived(third, recv.at[4])
        part = rest(inbox.at[0], order, self.me[order[1]]).at[self.me[order[2]]]
        self.final[g, s] = part[...] + third[0] + third[1] + third[2]
        part = self.final.at[g, s]
        z = self.me[2]
        for k, d in enumerate(DIRECT):
            self.remote(part, done.at[z], g, s, 3, 5, 2, d)
        pltpu.make_async_copy(part, done.at[z], self.keep.at[g]).start()

    def finish(self, g, s):
        third = self.views(g, s)[3]
        arrived(third, self.spread_recv.at[g, s])

    def sent(self, g):
        slot = SLOTS[g]
        arrived(self.second.at[slot], self.send.at[slot, 1])
        arrived(self.third.at[slot], self.send.at[slot, 2])

    def spread_sent(self, g):
        arrived(self.final.at[g], self.keep.at[g])
        arrived(self.third.at[SLOTS[g]], self.spread_send.at[g])

    def each(self, step, g):
        with jax.named_scope(f"{step.__name__} {g}"):
            for s in range(3):
                step(g, s)


def vector_steps(vec, vecs, send, recv):
    me = tuple(lax.axis_index(a) for a in AX)
    core = lax.axis_index(CORE)
    other = 1 - core
    bases = (0, 1, 4, 7, 10)
    mine = vec.at[pl.ds(pl.multiple_of(8 * core, 8), 8)]
    theirs = vec.at[pl.ds(pl.multiple_of(8 * other, 8), 8)]

    def start(stage):
        source = theirs if stage == 0 else mine
        if stage in (0, 4):
            targets = [{CORE: other}]
        else:
            ax = stage - 1
            targets = [{AX[ax]: rot(me[ax], d)} for d in DIRECT]
        for k, target in enumerate(targets):
            pltpu.make_async_remote_copy(
                src_ref=source, dst_ref=vecs.at[bases[stage] + k],
                send_sem=send.at[stage], recv_sem=recv.at[stage], device_id=target, device_id_type=MESH).start()

    def end(stage):
        with jax.named_scope("vector"):
            part = vecs.at[pl.ds(bases[stage], 3)] if stage in (1, 2, 3) else vecs.at[pl.ds(0, 1)]
            arrived(part, recv.at[stage])
            arrived(part, send.at[stage])
            if stage < 4:
                total = mine[...]
                for k in range(3 if stage else 1):
                    total = total + vecs[bases[stage] + k]
                mine[...] = total
            else:
                theirs[...] = vecs[10]

    return start, end


def suffix_state(after, p, j, late_ref, c):
    body, row = after[p, 2 * j : 2 * j + 2, 0:32].reshape(64, 128), after[p, 0, 32 + j : 33 + j]
    if c == 0:
        h = 2 * p + j
        body, row = body + late_ref[h, 0:64], row + (late_ref[h, 64:65] + late_ref[h, 65:66])
    first = lax.broadcasted_iota(jnp.int32, (64, 128), 0) == 0
    return jnp.concatenate([body, jnp.where(first, jnp.broadcast_to(row, (64, 128)), 0.0)], axis=0)


def attend_back_query(p, act, bufu, early_ref, before, trigs, grads):
    causal, _ = causal_masks()
    left = left_lanes(CHUNK)
    for c in range(2):
        rows = slice(CHUNK * c, CHUNK * c + CHUNK)
        query = []
        for j in range(2):
            h = 2 * p + j
            k = bufu[rows, at(HEADS + h, 128)]
            v, g = act[rows, at(h, 128)], act[rows, at(HEADS + h, 128)]
            high, low = halves(prefix_state(before, p, j, early_ref, c))
            weight = jnp.where(causal, nt(g, v), 0.0).astype(BF16)
            gq = nn(weight, k) + nn(doubled(g), jnp.concatenate([high, low], axis=0))
            gq = gq * trigs[0, rows]
            query.append(gq + swap_halves(gq))
        gate = bufu[ROWS:WIDTH, at(PAIRS * c + p, 128)].astype(F32)
        grads[rows, at(p, 128)] = (jnp.where(left, query[0], query[1]) * gate).astype(BF16)


def attend_back_local(p, act, bufu, trigs, key_ref, value_ref):
    _, flipped = causal_masks()
    left = left_lanes(CHUNK)
    cols = at(p, 128)
    for c in range(2):
        rows = slice(CHUNK * c, CHUNK * c + CHUNK)
        keys, value = [], []
        for j in range(2):
            h = 2 * p + j
            q, k = bufu[rows, at(h, 128)], bufu[rows, at(HEADS + h, 128)]
            v, g = act[rows, at(h, 128)], act[rows, at(HEADS + h, 128)]
            gk = nn(jnp.where(flipped, nt(v, g), 0.0).astype(BF16), q) * trigs[1, rows]
            keys.append(gk + swap_halves(gk))
            value.append(nn(jnp.where(flipped, nt(k, q), 0.0).astype(BF16), g))
        key_ref[rows, cols] = jnp.where(left, keys[0], keys[1])
        value_ref[rows, cols] = jnp.where(left, value[0], swap_halves(value[1]))


def attend_back_later(p, act, bufu, late_ref, after, trigs, ratio_ref, inverse_ref, grads):
    left = left_lanes(CHUNK)
    for c in range(2):
        rows = slice(CHUNK * c, CHUNK * c + CHUNK)
        keys, value = [], []
        for j in range(2):
            h = 2 * p + j
            k, v = bufu[rows, at(HEADS + h, 128)], act[rows, at(h, 128)]
            high, low = halves(suffix_state(after, p, j, late_ref, c))
            gk = nn(doubled(v), jnp.concatenate([high, low], axis=0)) * trigs[1, rows]
            keys.append(gk + swap_halves(gk))
            value.append(nt(doubled(k), jnp.concatenate([high, low], axis=1)))
        cols = at(p, 128)
        gate = bufu[ROWS:WIDTH, at(2 * PAIRS + PAIRS * c + p, 128)].astype(F32)
        gk = (ratio_ref[rows, cols] + jnp.where(left, keys[0], keys[1])) * gate
        grads[rows, at(PAIRS + p, 128)] = gk.astype(BF16)
        gv = inverse_ref[rows, cols] + jnp.where(left, value[0], swap_halves(value[1]))
        grads[rows, at(2 * PAIRS + p, 128)] = gv.astype(BF16)


def layer_kernel(len_ref, bq_in, bk_in, bv_in, bo_in, gain1_in, shift1_in, bdown_in, gain2_in, shift2_in, bup_in,
                 x_hbm, wq_hbm, wk_hbm, wv_hbm, wo_hbm, wup_hbm, wdown_hbm, cot_hbm,
                 block_out, tokens_out, done_out, vec_out, act_spill, slope_spill,
                 x_ref, act, slope, bufu, bufd, trigs, early_ref, late_ref, state, before, pay, after,
                 ratio_ref, inverse_ref, normal_ref, acc_ref, scale_ref, mixed_ref, normed_ref, gffn_ref, vec_ref, rows_ref,
                 bup, turned, stage, sums, first_in, second_in, third_in, final_ref, vecs,
                 load_sem, core_send, core_recv, send, recv, keep_sem, spread_recv, spread_send, vec_send, vec_recv, free_sem, open_sem, *scratch):
    everywhere = ("seq_0", "seq_1", "batch")
    greet(everywhere)
    loads = {}

    def load(name, src, dst):
        copy = pltpu.make_async_copy(src, dst, load_sem.at[len(loads)])
        copy.start()
        loads[name] = copy

    def ready(*names):
        with jax.named_scope("ready"):
            for name in names:
                loads[name].wait()

    def note(k, value):
        vec_ref[k : k + 1, :] += value

    load("x", x_hbm, x_ref)
    for n in range(3):
        cols = pl.ds(256 * n, 256)
        load(f"wv{n}", wv_hbm.at[:, cols], bufd.at[2 * WIDTH : 3 * WIDTH, cols])
        load(f"wk{n}", wk_hbm.at[:, cols], bufd.at[WIDTH : 2 * WIDTH, cols])
    load("wq", wq_hbm, bufd.at[0:WIDTH])
    for k, vector in enumerate((bq_in, bk_in, bv_in, bo_in, gain1_in, shift1_in, bdown_in, gain2_in, shift2_in)):
        load(f"row {k}", vector, rows_ref.at[k])
    load("bup", bup_in, bup.at[0])
    bq, bk, bv, bo, gain1, shift1, bdown, gain2, shift2 = (rows_ref.at[k : k + 1] for k in range(9))
    vec_ref[...] = jnp.zeros_like(vec_ref)
    length = len_ref[...].reshape(1, 1)
    start = ROWS * ((lax.axis_index("seq_0") * 4 + lax.axis_index("seq_1")) * 2 + lax.axis_index(CORE))

    def angles(r):
        both, valid = trig_block(start + 128 * r, 128, length)
        trigs[0, at(r, 128)] = both
        trigs[1, at(r, 128)] = both * valid

    loop(ROWS // 128, angles)
    ready("x", "wv0", "wk0", *(f"row {k}" for k in range(9)), "bup")
    load("wup", wup_hbm, bufu)
    wo = bufd.at[3 * WIDTH : HIDDEN]
    load("wo", wo_hbm, wo)
    load("cot", cot_hbm, gffn_ref)
    earlier_sums = Exchange(exchange_steps, state, before, *scratch[: len(EXCHANGE_SCRATCH)])
    later_sums = Exchange(quarter_steps, pay, after, *scratch[len(EXCHANGE_SCRATCH) :])

    def keys(n):
        project_values(n, x_ref, bufd.at[2 * WIDTH : 3 * WIDTH], bv, slope)
        project_soft(n, x_ref, bufd.at[WIDTH : 2 * WIDTH], bk, trigs.at[1], act, HEADS, slope, 9)
        pl.when(n == 0)(lambda: greeted(everywhere))
        pl.when(n > 0)(lambda: earlier_sums.step(1, n - 1))
        each_of(2, lambda j: state_sums(2 * n + j, act, slope, state, early_ref))
        earlier_sums.step(0, n)

    def queries(n):
        project_soft(n, x_ref, bufd.at[0:WIDTH], bq, trigs.at[0], act, 0, slope, 6)
        pl.when(n == 0)(lambda: earlier_sums.step(1, 2))

    def own(p):
        pl.when(lax.rem(p, 2) == 0)(lambda: earlier_sums.step(2, p // 2))
        attend_local(p, act, slope, ratio_ref, inverse_ref)

    def earlier(p):
        pl.when(lax.rem(p, 2) == 0)(lambda: earlier_sums.step(4, p // 2))
        attend_earlier(p, act, early_ref, before, ratio_ref, inverse_ref, mixed_ref)

    loop(3, keys, {n: lambda n=n: ready(f"wv{n + 1}", f"wk{n + 1}") for n in range(2)})
    ready("wq")
    loop(3, queries)
    load("wdown", wdown_hbm.at[0 : 3 * WIDTH], bufd.at[0 : 3 * WIDTH])
    load("qk_out", act, act_spill)
    load("v_out", slope, slope_spill)
    loop(PAIRS, own)
    each_of(3, lambda n: earlier_sums.step(3, n))
    loop(PAIRS, earlier)
    ready("wo")

    def first_norm(r):
        rows = at(r, CHUNK)
        hidden = x_ref[rows].astype(F32) + (nn(mixed_ref[rows], wo[...]) + bo[...])
        normal, scale = standard(hidden)
        normal_ref[rows] = normal
        scale_ref[rows] = jnp.broadcast_to(scale, (CHUNK, 128))
        normed_ref[rows] = (normal * gain1[...] + shift1[...]).astype(BF16)

    loop(ROWS // CHUNK, first_norm)
    load("wdown end", wdown_hbm.at[3 * WIDTH : HIDDEN], wo)
    ready("qk_out", "v_out", "wup", "wdown")

    def feed(t):
        cols = at(t, FEED)
        for r in range(2):
            rows = slice(CHUNK * r, CHUNK * r + CHUNK)
            pre = nn(normed_ref[rows], bufu[:, cols]) + bup[:, cols]
            whole, bell = normal_parts(pre)
            active = (pre * whole).astype(BF16)
            act[rows, cols] = active
            slope[rows, cols] = (whole + pre * bell).astype(BF16)
            acc_ref[rows] = nn(active, bufd[cols]) + jnp.where(t == 0, 0.0, acc_ref[rows])

    loop(2, feed, {0: lambda: ready("wdown end")})
    ready("cot")

    def second_norm(r):
        rows = at(r, CHUNK)
        hidden = normed_ref[rows].astype(F32) + (acc_ref[rows] + bdown[...])
        normal, scale = standard(hidden)
        x_ref[rows] = (normal * gain2[...] + shift2[...]).astype(BF16)
        grad = gffn_ref[rows].astype(F32)
        note(7, column(grad * normal))
        note(8, column(grad))
        back = norm_back(grad, normal, scale, gain2[...])
        acc_ref[rows] = back
        low = back.astype(BF16)
        gffn_ref[rows] = low
        note(6, column(low.astype(F32)))

    loop(ROWS // CHUNK, second_norm)
    load("block", x_ref, block_out)
    red = Reduction(stage, sums, first_in, second_in, third_in, done_out, core_send, core_recv, send, recv, keep_sem,
                    spread_recv, spread_send, final_ref)

    def down_rows(y):
        turned[...] = act[:, at(y, WIDTH)].T
        for n in range(3):
            value = nn(turned[...], gffn_ref[:, 256 * n : 256 * n + 256]).reshape(4, 2, 4, 24, 256)
            for half in range(2):
                unit = 2 * n + half
                for side in range(2):
                    stage[unit // 3, unit % 3, side, y] = value[:, side, :, :, 128 * half : 128 * half + 128]
        for s in range(3):
            red.swap(0, s, y).start()

    loop(4, down_rows)
    red.swaps(1)
    load("v", slope_spill.at[:, 0 : 128 * HEADS], act.at[:, 0 : 128 * HEADS])

    def feed_back(k):
        t = 1 - k
        cols = at(t, TILE)
        total = jnp.zeros((1, TILE), F32)
        for r in range(2):
            rows = slice(CHUNK * r, CHUNK * r + CHUNK)
            gpre = (nt(gffn_ref[rows], bufd[cols]) * slope[rows, cols].astype(F32)).astype(BF16)
            slope[rows, cols] = gpre
            total = total + column(gpre.astype(F32))
            acc_ref[rows] += nt(gpre, bufu[:, cols])
        for half in range(2):
            vec_ref[pl.ds(9 + 2 * t + half, 1), :] = total[:, WIDTH * half : WIDTH * half + WIDTH]

    loads["wo again"] = pltpu.make_async_copy(wo_hbm, wo, load_sem.at[39])

    def down_begun():
        red.each(red.begin, 0)
        loads["wo again"].start()

    loop(2, feed_back, {0: down_begun})
    red.each(red.follow, 0)
    red.each(red.begin, 1)
    ready("block")
    load("x again", x_hbm, x_ref)
    load("wq again", wq_hbm, bufd.at[0:WIDTH])
    load("wk again", wk_hbm, bufd.at[WIDTH : 2 * WIDTH])
    load("wv again", wv_hbm, bufd.at[2 * WIDTH : 3 * WIDTH])
    load("qk", act_spill, bufu.at[0:ROWS])
    gates = []
    for i in range(2):
        for c in range(2):
            gates.append(f"gate {i}{c}")
            load(gates[-1], slope_spill.at[CHUNK * c : CHUNK * c + CHUNK, pl.ds(128 * HEADS + WIDTH * i, WIDTH)],
                 bufu.at[ROWS:WIDTH, pl.ds(2 * WIDTH * i + WIDTH * c, WIDTH)])
    def up_columns(b):
        for n in range(3):
            cols = pl.ds(pl.multiple_of(WIDTH * b + 256 * n, 256), 256)
            value = nn(turned[...], slope[:, cols]).reshape(4, 4, 2, 24, 256)
            for half in range(2):
                unit = 2 * n + half
                for side in range(2):
                    stage[unit // 3, unit % 3, side, :, :, b] = value[:, :, side, :, 128 * half : 128 * half + 128]
        for s in range(3):
            red.swap(2, s, b).start()

    def first_back(r):
        rows = at(r, CHUNK)
        normal = normal_ref[rows]
        scale = scale_ref[rows, 0:1]
        grad = acc_ref[rows]
        note(4, column(grad * normal))
        note(5, column(grad))
        back = norm_back(grad, normal, scale, gain1[...])
        acc_ref[rows] = back
        low = back.astype(BF16)
        gffn_ref[rows] = low
        note(3, column(low.astype(F32)))
        normal_ref[rows] = nt(low, wo[...])

    def heads_back(p):
        cols = at(p, 128)
        lane = lax.broadcasted_iota(jnp.int32, (ROWS, 128), 1)
        left = lane < 64
        gnum = (normal_ref[:, cols] * inverse_ref[:, cols]).astype(BF16).astype(F32)
        product = gnum * ratio_ref[:, cols]
        ends_of = []
        for j in range(2):
            h = 2 * p + j
            mine = jnp.where(left, product, 0.0) if j == 0 else jnp.where(left, 0.0, product)
            gden = jnp.broadcast_to(-jnp.sum(mine, axis=1, keepdims=True), (ROWS, 128))
            high = gden.astype(BF16).astype(F32)
            ends = jnp.where(lane == 64, high, jnp.where(lane == 65, gden - high, 0.0))
            grad = jnp.where(left, gnum if j == 0 else swap_halves(gnum), ends).astype(BF16)
            act[:, at(HEADS + h, 128)] = grad
            late = tn(grad[CHUNK:ROWS], bufu[CHUNK:ROWS, at(h, 128)])
            late_ref[h] = late[0:72]
            both = late + tn(grad[0:CHUNK], bufu[0:CHUNK, at(h, 128)])
            for half in range(2):
                pay[p, 2 * j + half, 0:32] = both[32 * half : 32 * half + 32]
                pay[p, 2 * j + half, 32:40] = jnp.zeros((8, 128), F32)
            ends_of.append(both[64:65] + both[65:66])
        for j in range(2):
            pay[p, 0, 32 + j : 33 + j] = ends_of[j]

    def query_back(p):
        attend_back_query(p, act, bufu, early_ref, before, trigs, slope)

    def own_back(p):
        attend_back_local(p, act, bufu, trigs, ratio_ref, inverse_ref)

    def later(p):
        attend_back_later(p, act, bufu, late_ref, after, trigs, ratio_ref, inverse_ref, slope)

    def back(r):
        rows = at(r, CHUNK)
        total = acc_ref[rows]
        for i in range(3):
            total = total + nt(slope[rows, WIDTH * i : WIDTH * i + WIDTH], bufd[WIDTH * i : WIDTH * i + WIDTH])
        acc_ref[rows] = total

    def product(rhs, base, g, b0, n):
        with jax.named_scope("product"):
            value = nn(turned[...], rhs[:, at(base + n, 256)]).reshape(4, 4, 2, 24, 256)
            for part in range(2):
                unit = 2 * n + part
                half, s = unit // 3, lax.rem(unit, 3)
                for side in range(2):
                    stage[g % 2, s, side, :, :, b0 + half] = value[:, :, side, :, 128 * part : 128 * part + 128]
                red.swap(g, s, b0 + half).start()

    def free(k):
        red.cleared(k)
        pl.semaphore_signal(free_sem.at[k], inc=1, device_id={CORE: red.other}, device_id_type=MESH)

    def freed(k):
        with jax.named_scope("freed"):
            pl.semaphore_wait(free_sem.at[k], 1)

    def release(k):
        red.sent(k)
        for axis in everywhere:
            for d in DIRECT:
                pl.semaphore_signal(open_sem.at[k], inc=1, device_id={axis: rot(lax.axis_index(axis), d)},
                                    device_id_type=MESH)

    def released(k):
        with jax.named_scope("released"):
            pl.semaphore_wait(open_sem.at[k], 9)

    ready("wo again")
    loop(ROWS // CHUNK, first_back)
    red.each(red.relay, 0)
    red.each(red.follow, 1)
    each_of(3, lambda n: earlier_sums.step(5, n))
    ready("qk", "v")

    def heads_sent(p):
        heads_back(p)

        @pl.when(lax.rem(p, 2) == 1)
        def _():
            later_sums.step(0, p // 2)
            pl.when(p > 1)(lambda: later_sums.step(1, p // 2 - 1))

    loop(PAIRS, heads_sent)
    turned[...] = normed_ref[...].T

    def up_first():
        later_sums.step(1, 2)
        red.each(red.relay, 1)

    loop(4, up_columns, {0: up_first, 2: lambda: red.each(red.middle, 0)})
    red.swaps(3)
    later_sums.step(2, 0)
    free(0)
    ready(*gates)

    def query_two(n):
        query_back(2 * n)
        query_back(2 * n + 1)

    def query_second():
        later_sums.step(2, 1)
        red.each(red.begin, 2)

    def query_fourth():
        later_sums.step(2, 2)
        later_sums.step(6, 0)
        red.each(red.middle, 1)

    loop(3, query_two, {0: query_second, 1: query_fourth})
    red.each(red.begin, 3)
    red.each(red.follow, 2)
    later_sums.step(6, 1)
    red.each(red.last, 0)
    free(1)
    turned[...] = mixed_ref[...].T
    freed(0)
    loop(3, lambda n: product(gffn_ref, 0, 4, 0, n))
    later_sums.step(6, 2)
    ready("x again")
    turned[...] = x_ref[...].T
    loop(3, lambda n: product(slope, 0, 4, 2, n))

    def own_two(n):
        own_back(2 * n)
        own_back(2 * n + 1)

    def own_fourth():
        red.each(red.relay, 2)
        red.each(red.follow, 3)
        red.each(red.last, 1)

    loop(3, own_two, {1: own_fourth})
    red.each(red.relay, 3)
    each_of(3, lambda n: later_sums.step(3, n))
    red.each(red.spread, 0)
    release(0)
    freed(1)

    def keys_values(n):
        later_sums.step(4, n)
        each_of(2, lambda j: later(2 * n + j))
        each_of(2, lambda i: product(slope, 3 + 3 * i, 5, 2 * i, n))

    def keys_first():
        released(0)
        red.each(red.begin, 4)
        red.each(red.middle, 2)

    def keys_second():
        red.each(red.spread, 1)
        release(1)
        red.each(red.middle, 3)

    loop(3, keys_values, {0: keys_first, 1: keys_second})
    for i in range(3):
        note(i, column(slope[:, WIDTH * i : WIDTH * i + WIDTH].astype(F32)))
    vector_start, vector_end = vector_steps(vec_ref, vecs, vec_send, vec_recv)
    vector_start(0)
    released(1)
    red.each(red.begin, 5)
    vector_end(0)
    vector_start(1)
    ready("wq again", "wk again", "wv again")

    def back_first():
        red.each(red.follow, 4)
        red.each(red.relay, 4)
        red.each(red.last, 2)

    loop(ROWS // CHUNK, back, {0: back_first})
    load("tokens", acc_ref, tokens_out)
    red.each(red.relay, 5)
    red.each(red.follow, 5)
    red.each(red.last, 3)
    red.each(red.middle, 4)
    red.each(red.spread, 2)
    vector_end(1)
    vector_start(2)
    red.each(red.middle, 5)
    red.each(red.last, 4)
    red.each(red.spread, 3)
    vector_end(2)
    vector_start(3)
    red.each(red.last, 5)
    red.each(red.spread, 4)
    red.each(red.spread, 5)
    vector_end(3)
    vector_start(4)
    vector_end(4)
    load("vec", vec_ref, vec_out)
    for g in range(6):
        red.each(red.finish, g)
        red.spread_sent(g)
    for g in range(2, 6):
        red.cleared(g)
        red.sent(g)
    each_of(3, lambda n: later_sums.step(5, n))
    ready("tokens", "vec")


def final_kernel(done, vecs, tokens, block, block_out, tokens_out, out_q, out_bq, out_k, out_bk, out_v, out_bv, out_o,
                 out_bo, out_g1, out_s1, out_up, out_bup, out_down, out_bdown, out_g2, out_s2):
    tokens_out[...] = tokens[...]
    block_out[...] = block[...]
    for s in range(3):
        for b in range(4):
            for half in range(2):
                at_col = 384 * half + 128 * s
                out_down[24 * b : 24 * b + 24, at_col : at_col + 128] = done[half, s, b]
                out_up[:, 768 * b + at_col : 768 * b + at_col + 128] = done[2 + half, s, b]
            cols = slice(384 * (b % 2) + 128 * s, 384 * (b % 2) + 128 * s + 128)
            (out_o, out_q)[b // 2][:, cols] = done[4, s, b]
            (out_k, out_v)[b // 2][:, cols] = done[5, s, b]
    seq = (lax.axis_index("seq_0") * 4 + lax.axis_index("seq_1")) * 2 + lax.axis_index(CORE)
    values = vecs[...]
    mine = pltpu.roll(values, lax.rem(WIDTH - 24 * seq, WIDTH), 1)
    for k, out in enumerate((out_bq, out_bk, out_bv, out_bo, out_g1, out_s1, out_bdown, out_g2, out_s2)):
        out[...] = mine[k, 0:24]
    spun = pltpu.roll(values, lax.rem(WIDTH - 96 * lax.rem(seq, 8), WIDTH), 1)
    row = lax.broadcasted_iota(jnp.int32, (16, WIDTH), 0)
    out_bup[...] = jnp.sum(jnp.where(row == 9 + seq // 8, spun, 0.0), axis=0)[0:96]


def on_device(tokens, lengths, w_query, b_query, w_key, b_key, w_value, b_value, w_out, b_out, gain_one, shift_one,
              w_up, b_up, w_down, b_down, gain_two, shift_two, cotangent):
    vmem = pl.BlockSpec(memory_space=VMEM)
    anywhere = pl.BlockSpec(memory_space=pl.ANY)
    out = jax.ShapeDtypeStruct
    wide16, wide32, long16 = ((ROWS, WIDTH), BF16), ((ROWS, WIDTH), F32), ((ROWS, HIDDEN), BF16)
    per_head, packed = ((HEADS, 72, 128), F32), ((PAIRS, 136, 128), F32)
    quarters = ((PAIRS, 4, 40, 128), F32)
    vector = ((16, WIDTH), F32)
    finished = ((6, 3, 4, 24, 128), F32)
    block, tokens_grad, done, sums, _, _ = pl.pallas_call(
        layer_kernel,
        out_shape=[out(*shape) for shape in (wide16, wide32, finished, vector, long16, long16)],
        in_specs=[vmem] + [anywhere] * 18,
        out_specs=[anywhere] * 6,
        scratch_shapes=[VMEM(*shape) for shape in (
            wide16, long16, long16, ((WIDTH, HIDDEN), BF16), ((HIDDEN, WIDTH), BF16),
            ((2, ROWS, 128), F32), per_head, per_head, packed, packed, quarters, quarters,
            wide32, wide32, wide32, wide32, ((ROWS, 128), F32), wide16, wide16, wide16, vector, vector,
            ((1, HIDDEN), F32), ((WIDTH, ROWS), BF16),
            ((2, 3, 2, 4, 4, 4, 24, 128), F32), ((4, 3, 4, 4, 4, 24, 128), F32), ((4, 3, 3, 4, 4, 24, 128), F32),
            ((4, 3, 3, 4, 24, 128), F32), ((4, 3, 3, 24, 128), F32), ((6, 3, 24, 128), F32), ((11, 8, WIDTH), F32))]
        + [pltpu.SemaphoreType.DMA((40,)), pltpu.SemaphoreType.DMA((4, 3)), pltpu.SemaphoreType.DMA((4, 3)),
           pltpu.SemaphoreType.DMA((4, 3)), pltpu.SemaphoreType.DMA((4, 3, 5)), pltpu.SemaphoreType.DMA((6,)), pltpu.SemaphoreType.DMA((6, 3)),
           pltpu.SemaphoreType.DMA((6,)),
           pltpu.SemaphoreType.DMA((5,)), pltpu.SemaphoreType.DMA((5,)), pltpu.SemaphoreType.REGULAR((2,)), pltpu.SemaphoreType.REGULAR((2,))]
        + EXCHANGE_SCRATCH + QUARTER_SCRATCH,
        compiler_params=pltpu.CompilerParams(collective_id=1, has_side_effects=True, vmem_limit_bytes=LIMIT),
    )(lengths, b_query, b_key, b_value, b_out, gain_one, shift_one, b_down, gain_two, shift_two, b_up,
      tokens[0], w_query, w_key, w_value, w_out, w_up, w_down, cotangent[0])
    square_share, vector_share = out((24, WIDTH), F32), out((24,), F32)
    results = pl.pallas_call(
        final_kernel,
        out_shape=[out(*wide16), out(*wide32)] + [square_share, vector_share] * 4 + [vector_share] * 2
        + [out((24, HIDDEN), F32), out((96,), F32), out((96, WIDTH), F32)] + [vector_share] * 3,
        in_specs=[vmem] * 4,
        out_specs=[vmem] * 18,
        compiler_params=pltpu.CompilerParams(vmem_limit_bytes=LIMIT),
    )(done, sums, tokens_grad, block)
    return (results[0][None], results[1][None], *results[2:])


def solution(mesh):
    torus = Mesh(mesh.devices.reshape(4, 4, 2, mesh.shape["batch"]), (*SEQ, "batch"))
    rows, shares = P("batch", SEQ, None), P(SEQ, None)
    return jax.shard_map(
        on_device,
        mesh=torus,
        in_specs=(rows, P("batch")) + (P(),) * 16 + (rows,),
        out_specs=(rows, rows) + (shares, P(SEQ)) * 4 + (P(SEQ), P(SEQ)) + (shares, P(SEQ)) * 2 + (P(SEQ), P(SEQ)),
        check_vma=False,
    )
```

```python
import jax
import jax.numpy as jnp
from jax import lax
from jax.experimental import pallas as pl
from jax.experimental.pallas import tpu as pltpu
from jax.sharding import Mesh
from jax.sharding import PartitionSpec as P

SEQ = ("seq_0", "seq_1", "seq_2")
AX = ("seq_0", "seq_1", "batch")
CORE = "seq_2"
MESH = pl.DeviceIdType.MESH
DIRECT = (1, 3, 2)
F32 = jnp.float32
BF16 = jnp.bfloat16
HALF_PI = 1.5707963267948966
HALF_PI_REST = -4.371139000186241e-08
EPSILON = 1e-05
ROWS = 512
WIDTH = 768
HIDDEN = 3072
HEADS = 12
PAIRS = 6
CHUNK = 256
FEED = 1536
TILE = 1536
VMEM = pltpu.VMEM
LIMIT = 63 * 2**20


def loop(count, body, after=None):
    def step(k, carry):
        with jax.named_scope(body.__name__):
            body(k)
        for n, then in (after or {}).items():
            pl.when(k == n)(then)

    lax.fori_loop(0, count, step, None)


def each_of(count, body):
    lax.fori_loop(0, count, lambda k, carry: body(k), None)


def nn(a, b):
    return jnp.dot(a, b, preferred_element_type=F32)


def nt(a, b):
    return lax.dot_general(a, b, (((1,), (1,)), ((), ())), preferred_element_type=F32)


def tn(a, b):
    return lax.dot_general(a, b, (((0,), (0,)), ((), ())), preferred_element_type=F32)


def at(k, size):
    return pl.ds(pl.multiple_of(k * size, size), size)


def rot(k, d):
    return lax.rem(k + d, 4)


def left_lanes(rows):
    return lax.broadcasted_iota(jnp.int32, (rows, 128), 1) < 64


def swap_halves(value):
    return pltpu.roll(value, 64, 1)


def doubled(value):
    return jnp.concatenate([value, value], axis=1)


def halves(value):
    high = value.astype(BF16)
    return high, (value - high.astype(F32)).astype(BF16)


SIN = (1.0, -0.1666666716337204, 0.008333330973982811, -0.00019840864115394652, 2.7525297809916083e-06, -2.3888299338636898e-08)


def sine(x):
    square = x * x
    value = SIN[5]
    for c in SIN[4::-1]:
        value = value * square + c
    return value * x


def normal_parts(p):
    return 0.5 + 0.5 * lax.erf(p * 0.7071067811865476), 0.3989422804014327 * jnp.exp(-0.5 * p * p)


def trig_block(first, rows, length):
    position = first + lax.broadcasted_iota(jnp.int32, (rows, 128), 0)
    length = jnp.broadcast_to(length, (rows, 128))
    angle = HALF_PI * jnp.minimum(position + 1, length).astype(F32) / length.astype(F32)
    both = sine(jnp.where(left_lanes(rows), (HALF_PI - angle) + HALF_PI_REST, angle))
    return both, (position < length).astype(F32)


def project_values(n, x_ref, w, b, out):
    left = left_lanes(ROWS)
    u = (nn(x_ref[...], w[:, at(n, 256)]) + b[:, at(n, 256)]).astype(BF16).astype(F32)
    for j in range(2):
        part = u[:, 128 * j : 128 * j + 128]
        out[:, at(4 * n + 2 * j, 128)] = jnp.where(left, part, 1.0).astype(BF16)
        out[:, at(4 * n + 2 * j + 1, 128)] = jnp.where(left, swap_halves(part), 1.0).astype(BF16)


def project_soft(n, x_ref, w, b, table, out, first, gates, gate):
    left = left_lanes(ROWS)
    u = nn(x_ref[...], w[:, at(n, 256)]) + b[:, at(n, 256)]
    small = jnp.exp(-jnp.abs(u))
    soft = jnp.maximum(u, 0.0) + jnp.log1p(small)
    gates[:, at(gate + n, 256)] = (0.5 + 0.5 * jnp.tanh(0.5 * u)).astype(BF16)
    trig = table[...]
    for j in range(2):
        part = soft[:, 128 * j : 128 * j + 128]
        other = swap_halves(part)
        out[:, at(first + 4 * n + 2 * j, 128)] = (jnp.where(left, part, other) * trig).astype(BF16)
        out[:, at(first + 4 * n + 2 * j + 1, 128)] = (jnp.where(left, other, part) * trig).astype(BF16)


def state_sums(p, qk_ref, v_ref, state_ref, early_ref):
    for j in range(2):
        h = 2 * p + j
        keys, values = at(HEADS + h, 128), at(h, 128)
        early = tn(v_ref[0:CHUNK, values], qk_ref[0:CHUNK, keys])
        early_ref[h] = early[0:72]
        both = early + tn(v_ref[CHUNK:ROWS, values], qk_ref[CHUNK:ROWS, keys])
        state_ref[p, 64 * j : 64 * j + 64] = both[0:64]
        state_ref[p, 128 + j : 129 + j] = both[64:65]
    state_ref[p, 130:136] = jnp.zeros((6, 128), F32)


def exchange_steps(n, pay, out, core_in, chip, head, tail, total, msgs, xa, ya, yb, xb, send, recv):
    my, mx = lax.axis_index("seq_0"), lax.axis_index("seq_1")
    core = lax.axis_index(CORE)
    other = 1 - core
    own = 2 * n + core

    def remote(src, dst, stage, k, target):
        pltpu.make_async_remote_copy(
            src_ref=src, dst_ref=dst, send_sem=send.at[n, stage], recv_sem=recv.at[n, k],
            device_id=target, device_id_type=MESH).start()

    def counts(theirs, mine):
        return theirs < mine

    def chosen(flag, value):
        return jnp.where(flag, value, jnp.zeros_like(value))

    def first():
        remote(pay.at[2 * n + other], core_in.at[n], 0, 0, {CORE: other})

    def second():
        arrived(core_in.at[n], recv.at[n, 0])
        chip[n] = pay[own] + core_in[n]
        for k, d in enumerate(DIRECT):
            remote(chip.at[n, pl.ds(0, 72)], xa.at[n, k], 1, 1, {"seq_1": rot(mx, d)})
        for k, d in enumerate(DIRECT):
            remote(chip.at[n, pl.ds(72, 64)], yb.at[n, k], 1, 2, {"seq_0": rot(my, d)})

    def third():
        arrived(xa.at[n], recv.at[n, 1])
        some, every = jnp.zeros((72, 128), F32), chip[n, 0:72]
        for k, d in enumerate(DIRECT):
            some = some + chosen(counts(rot(mx, 4 - d), mx), xa[n, k])
            every = every + xa[n, k]
        head[n] = some
        total[n] = every
        for k, d in enumerate(DIRECT):
            remote(total.at[n], ya.at[n, k], 2, 3, {"seq_0": rot(my, d)})
        arrived(yb.at[n], recv.at[n, 2])
        some = jnp.zeros((64, 128), F32)
        for k, d in enumerate(DIRECT):
            some = some + chosen(counts(rot(my, 4 - d), my), yb[n, k])
        tail[n] = some
        for k, d in enumerate(DIRECT):
            msgs[n, k] = some + chosen(counts(mx, rot(mx, d)), chip[n, 72:136])
        for k, d in enumerate(DIRECT):
            remote(msgs.at[n, k], xb.at[n, k], 2, 4, {"seq_1": rot(mx, d)})

    def fourth():
        arrived(ya.at[n], recv.at[n, 3])
        arrived(xb.at[n], recv.at[n, 4])
        arrived(chip, send.at[n, 1])
        mine = core == 1
        low, high = head[n], tail[n]
        for k, d in enumerate(DIRECT):
            low = low + chosen(counts(rot(my, 4 - d), my), ya[n, k])
            high = high + xb[n, k]
        out[own, 0:72] = low + chosen(mine, core_in[n, 0:72])
        out[own, 72:136] = high + chosen(mine, core_in[n, 72:136])
        chip[n, 0:72] = low + chosen(jnp.logical_not(mine), pay[own, 0:72])
        chip[n, 72:136] = high + chosen(jnp.logical_not(mine), pay[own, 72:136])
        remote(chip.at[n], out.at[own], 3, 5, {CORE: other})

    def fifth():
        arrived(out.at[2 * n + other], recv.at[n, 5])

    def sent():
        arrived(core_in.at[n], send.at[n, 0])
        arrived(chip, send.at[n, 2])
        arrived(chip.at[n], send.at[n, 3])

    return first, second, third, fourth, fifth, sent


EXCHANGE_SCRATCH = [
    VMEM((3, 136, 128), F32),
    VMEM((3, 136, 128), F32),
    VMEM((3, 72, 128), F32),
    VMEM((3, 64, 128), F32),
    VMEM((3, 72, 128), F32),
    VMEM((3, 3, 64, 128), F32),
    VMEM((3, 3, 72, 128), F32),
    VMEM((3, 3, 72, 128), F32),
    VMEM((3, 3, 64, 128), F32),
    VMEM((3, 3, 64, 128), F32),
    pltpu.SemaphoreType.DMA((3, 4)),
    pltpu.SemaphoreType.DMA((3, 6)),
]


def quarter_steps(n, pay, out, core_in, chip, xa, total, ya, msgs, got, send, recv):
    my, mx = lax.axis_index("seq_0"), lax.axis_index("seq_1")
    core = lax.axis_index(CORE)
    other = 1 - core
    own = 2 * n + core

    def remote(src, dst, stage, k, target):
        pltpu.make_async_remote_copy(
            src_ref=src, dst_ref=dst, send_sem=send.at[n, stage], recv_sem=recv.at[n, k],
            device_id=target, device_id_type=MESH).start()

    def chosen(flag, value):
        return jnp.where(flag, value, jnp.zeros_like(value))

    def first():
        remote(pay.at[2 * n + other], core_in.at[n], 0, 0, {CORE: other})

    def second():
        arrived(core_in.at[n], recv.at[n, 0])
        chip[n] = pay[own] + core_in[n]
        for k, d in enumerate(DIRECT):
            remote(chip.at[n, rot(mx, d)], xa.at[n, k], 1, 1, {"seq_1": rot(mx, d)})

    def third():
        arrived(xa.at[n], recv.at[n, 1])
        total[n] = chip[n, mx] + xa[n, 0] + xa[n, 1] + xa[n, 2]
        for k, d in enumerate(DIRECT):
            remote(total.at[n], ya.at[n, k], 2, 2, {"seq_0": rot(my, d)})

    def cross():
        arrived(ya.at[n], recv.at[n, 2])
        behind = jnp.zeros((40, 128), F32)
        for k, d in enumerate(DIRECT):
            behind = behind + chosen(rot(my, 4 - d) > my, ya[n, k])

        def for_column(column):
            value = behind + chosen(mx > column, chip[n, mx])
            for k, d in enumerate(DIRECT):
                value = value + chosen(rot(mx, 4 - d) > column, xa[n, k])
            return value

        for k, d in enumerate(DIRECT):
            msgs[n, k] = for_column(rot(mx, d))
            remote(msgs.at[n, k], got.at[n, mx], 3, 3, {"seq_1": rot(mx, d)})
        got[n, mx] = for_column(mx)

    def fourth():
        arrived(xa.at[n], recv.at[n, 3])
        arrived(xa.at[n], send.at[n, 1])
        out[own] = got[n] + chosen(core == 0, core_in[n])
        chip[n] = got[n] + chosen(core == 1, pay[own])
        remote(chip.at[n], out.at[own], 4, 4, {CORE: other})

    def fifth():
        arrived(out.at[2 * n + other], recv.at[n, 4])

    def sent():
        arrived(chip.at[n], send.at[n, 0])
        arrived(xa.at[n], send.at[n, 2])
        arrived(xa.at[n], send.at[n, 3])
        arrived(chip.at[n], send.at[n, 4])

    return first, second, third, fourth, fifth, sent, cross


QUARTER_SCRATCH = [
    VMEM((3, 4, 40, 128), F32),
    VMEM((3, 4, 40, 128), F32),
    VMEM((3, 3, 40, 128), F32),
    VMEM((3, 40, 128), F32),
    VMEM((3, 3, 40, 128), F32),
    VMEM((3, 3, 40, 128), F32),
    VMEM((3, 4, 40, 128), F32),
    pltpu.SemaphoreType.DMA((3, 5)),
    pltpu.SemaphoreType.DMA((3, 5)),
]


class Exchange:
    def __init__(self, steps, *refs):
        self.steps = lambda n: steps(n, *refs)

    def step(self, k, n):
        with jax.named_scope(("swap", "begin", "turn", "end", "share", "sent", "cross")[k]):
            self.steps(n)[k]()


def greet(axes):
    barrier = pltpu.get_barrier_semaphore()
    core = lax.axis_index(CORE)
    pl.semaphore_signal(barrier, inc=1, device_id={CORE: 1 - core}, device_id_type=MESH)
    for axis in axes:
        mine = lax.axis_index(axis)
        for d in DIRECT:
            pl.semaphore_signal(barrier, inc=1, device_id={axis: rot(mine, d)}, device_id_type=MESH)


def greeted(axes):
    pl.semaphore_wait(pltpu.get_barrier_semaphore(), 1 + 3 * len(axes))


def causal_masks():
    row = lax.broadcasted_iota(jnp.int32, (CHUNK, CHUNK), 0)
    col = lax.broadcasted_iota(jnp.int32, (CHUNK, CHUNK), 1)
    return row >= col, row <= col


def prefix_state(before, p, j, early_ref, c):
    body, row = before[p, 64 * j : 64 * j + 64], before[p, 128 + j : 129 + j]
    if c == 1:
        body, row = body + early_ref[2 * p + j, 0:64], row + early_ref[2 * p + j, 64:65]
    return jnp.concatenate([body, jnp.broadcast_to(row, (64, 128))], axis=0)


def attend_local(p, qk_ref, v_ref, top_ref, under_ref):
    causal, _ = causal_masks()
    left = left_lanes(CHUNK)
    cols = at(p, 128)
    for c in range(2):
        rows = slice(CHUNK * c, CHUNK * c + CHUNK)
        sums = []
        for j in range(2):
            h = 2 * p + j
            weight = nt(qk_ref[rows, at(h, 128)], qk_ref[rows, at(HEADS + h, 128)])
            sums.append(nn(jnp.where(causal, weight, 0.0).astype(BF16), v_ref[rows, at(h, 128)]))
        even, odd = sums
        top_ref[rows, cols] = jnp.where(left, even, swap_halves(odd))
        under_ref[rows, cols] = jnp.where(left, swap_halves(even), odd)


def attend_earlier(p, qk_ref, early_ref, before, ratio_ref, inverse_ref, mixed_ref):
    left = left_lanes(CHUNK)
    cols = at(p, 128)
    for c in range(2):
        rows = slice(CHUNK * c, CHUNK * c + CHUNK)
        sums = []
        for j in range(2):
            h = 2 * p + j
            high, low = halves(prefix_state(before, p, j, early_ref, c))
            sums.append(nt(doubled(qk_ref[rows, at(h, 128)]), jnp.concatenate([high, low], axis=1)))
        even, odd = sums
        inverse = 1.0 / (inverse_ref[rows, cols] + jnp.where(left, swap_halves(even), odd))
        ratio = (ratio_ref[rows, cols] + jnp.where(left, even, swap_halves(odd))) * inverse
        ratio_ref[rows, cols] = ratio
        inverse_ref[rows, cols] = inverse
        mixed_ref[rows, cols] = ratio.astype(BF16)


def mean_rows(value):
    return jnp.mean(value, axis=-1, keepdims=True)


def standard(hidden):
    centred = hidden - mean_rows(hidden)
    scale = lax.rsqrt(mean_rows(centred * centred) + EPSILON)
    return centred * scale, scale


def norm_back(grad, normal, scale, gain):
    scaled = grad * gain
    return scale * (scaled - mean_rows(scaled) - normal * mean_rows(scaled * normal))


def column(value):
    return jnp.sum(value, axis=0, keepdims=True)


USUAL = ((1, 0, 2), (0, 2, 1), (2, 1, 0))
ORDERS = (USUAL, USUAL, (USUAL[0], USUAL[1], (2, 0, 1)), (USUAL[0], (0, 1, 2), USUAL[2]), USUAL, USUAL)
SUBS = 9
COLS = 256


def cell(ref, order, picks):
    at = [slice(None)] * 3
    for axis, pick in zip(order, picks):
        at[axis] = pick
    return ref.at[tuple(at)]


def rest(ref, order, pick):
    return ref.at[pick] if order[1] < order[2] else ref.at[:, pick]


def halved(ref, order, pick, half):
    at = [slice(None)] * 3
    at[order[0]] = pick
    at[1 if order[0] == 0 else 0] = half
    return ref.at[tuple(at)]


def add_blocks(dst, srcs, count, fresh=False):
    def step(k, carry):
        value = srcs[0][k] if fresh else dst[k] + srcs[0][k]
        for src in srcs[1:]:
            value = value + src[k]
        dst[k] = value

    lax.fori_loop(0, count, step, None)


SLOTS = (0, 1, 2, 3, 0, 1)


def arrived(ref, sem):
    pltpu.make_async_copy(ref, ref, sem).wait()


class Reduction:
    def __init__(self, stage, sums, first, second, third, done, core_send, core_recv, send, recv, keep,
                 spread_recv, spread_send, third_recv, final):
        self.stage, self.sums, self.first, self.second, self.third, self.done = stage, sums, first, second, third, done
        self.core_send, self.core_recv, self.send, self.recv, self.keep = core_send, core_recv, send, recv, keep
        self.spread_recv, self.spread_send, self.third_recv, self.final = spread_recv, spread_send, third_recv, final
        self.me = tuple(lax.axis_index(a) for a in AX)
        self.core = lax.axis_index(CORE)
        self.other = 1 - self.core

    def swap(self, g, s, part):
        where = (part,) if g < 2 else (slice(None), slice(None), part)
        return pltpu.make_async_remote_copy(
            src_ref=self.stage.at[(g % 2, s, self.other, *where)], dst_ref=self.sums.at[(SLOTS[g], s, *where)],
            send_sem=self.core_send.at[SLOTS[g], s], recv_sem=self.core_recv.at[SLOTS[g], s],
            device_id={CORE: self.other}, device_id_type=MESH)

    def swaps(self, g):
        for s in range(3):
            for part in range(4):
                self.swap(g, s, part).start()

    def remote(self, src, dst, g, s, stage, k, axis, d):
        pltpu.make_async_remote_copy(
            src_ref=src, dst_ref=dst, send_sem=self.send.at[SLOTS[g], stage] if k < 5 else self.spread_send.at[g],
            recv_sem=(self.recv.at[SLOTS[g], s, k] if k < 4 else
                      self.third_recv.at[SLOTS[g]] if k == 4 else self.spread_recv.at[g]),
            device_id={AX[axis]: rot(self.me[axis], d)}, device_id_type=MESH).start()

    def views(self, g, s):
        slot = SLOTS[g]
        return (self.sums.at[slot, s], self.first.at[slot, s], self.second.at[slot, s], self.third.at[slot, s],
                self.done.at[g, s], self.stage.at[g % 2, s, self.core], self.recv.at[slot, s])

    def begin(self, g, s):
        mine, inbox, _, _, _, own, _ = self.views(g, s)
        arrived(mine, self.core_recv.at[SLOTS[g], s])
        arrived(own, self.core_send.at[SLOTS[g], s])
        add_blocks(mine, [own], 4)
        order = ORDERS[g][s]
        ax = order[0]
        far = rot(self.me[ax], 2)
        lo, hi = pl.ds(0, 2), pl.ds(2, 2)
        self.remote(halved(mine, order, far, lo), inbox.at[0, lo], g, s, 0, 0, ax, 1)
        self.remote(halved(mine, order, far, hi), inbox.at[0, hi], g, s, 0, 1, ax, 3)

    def follow(self, g, s):
        mine, inbox = self.views(g, s)[:2]
        order = ORDERS[g][s]
        ax = order[0]
        i = self.me[ax]
        lo, hi = pl.ds(0, 2), pl.ds(2, 2)
        self.remote(halved(mine, order, rot(i, 1), hi), inbox.at[1, hi], g, s, 0, 2, ax, 1)
        self.remote(halved(mine, order, rot(i, 3), lo), inbox.at[2, lo], g, s, 0, 2, ax, 3)

    def relay(self, g, s):
        mine, inbox, _, _, _, _, recv = self.views(g, s)
        order = ORDERS[g][s]
        ax = order[0]
        i = self.me[ax]
        lo, hi = pl.ds(0, 2), pl.ds(2, 2)
        arrived(inbox.at[0, lo], recv.at[0])
        part = halved(mine, order, rot(i, 1), lo)
        add_blocks(part, [inbox.at[0, lo]], 2)
        self.remote(part, inbox.at[1, lo], g, s, 0, 2, ax, 1)
        arrived(inbox.at[0, hi], recv.at[1])
        part = halved(mine, order, rot(i, 3), hi)
        add_blocks(part, [inbox.at[0, hi]], 2)
        self.remote(part, inbox.at[2, hi], g, s, 0, 2, ax, 3)

    def middle(self, g, s):
        mine, inbox, second, _, _, _, recv = self.views(g, s)
        order = ORDERS[g][s]
        arrived(inbox.at[pl.ds(1, 2)], recv.at[2])
        i, ax = self.me[order[0]], order[1]
        add_blocks(inbox.at[0], [cell(mine, order, (i,)), inbox.at[1], inbox.at[2]], 4, fresh=True)
        for k, d in enumerate(DIRECT):
            self.remote(rest(inbox.at[0], order, rot(self.me[ax], d)), second.at[k], g, s, 1, 3, ax, d)

    def cleared(self, g):
        arrived(self.first.at[SLOTS[g]], self.send.at[SLOTS[g], 0])

    def last(self, g, s):
        _, inbox, second, third, _, _, recv = self.views(g, s)
        order = ORDERS[g][s]
        arrived(second, recv.at[3])
        mine = rest(inbox.at[0], order, self.me[order[1]])
        mine[...] = mine[...] + second[0] + second[1] + second[2]
        ax = order[2]
        for k, d in enumerate(DIRECT):
            self.remote(mine.at[rot(self.me[ax], d)], third.at[k], g, s, 2, 4, ax, d)

    def spread(self, g, s):
        _, inbox, _, third, done, _, recv = self.views(g, s)
        order = ORDERS[g][s]
        if s == 0:
            arrived(self.third.at[SLOTS[g]], self.third_recv.at[SLOTS[g]])
        part = rest(inbox.at[0], order, self.me[order[1]]).at[self.me[order[2]]]
        self.final[g, s] = part[...] + third[0] + third[1] + third[2]
        part = self.final.at[g, s]
        z = self.me[2]
        for k, d in enumerate(DIRECT):
            self.remote(part, done.at[z], g, s, 3, 5, 2, d)
        pltpu.make_async_copy(part, done.at[z], self.keep.at[g]).start()

    def finish(self, g, s):
        if s == 0:
            arrived(self.third.at[SLOTS[g]], self.spread_recv.at[g])

    def sent(self, g):
        slot = SLOTS[g]
        arrived(self.second.at[slot], self.send.at[slot, 1])
        arrived(self.third.at[slot], self.send.at[slot, 2])

    def spread_sent(self, g):
        arrived(self.final.at[g], self.keep.at[g])
        arrived(self.third.at[SLOTS[g]], self.spread_send.at[g])

    def each(self, step, g):
        with jax.named_scope(f"{step.__name__} {g}"):
            for s in range(3):
                step(g, s)


def vector_steps(vec, vecs, send, recv):
    me = tuple(lax.axis_index(a) for a in AX)
    core = lax.axis_index(CORE)
    other = 1 - core
    bases = (0, 1, 4, 7, 10)
    mine = vec.at[pl.ds(pl.multiple_of(8 * core, 8), 8)]
    theirs = vec.at[pl.ds(pl.multiple_of(8 * other, 8), 8)]

    def start(stage):
        source = theirs if stage == 0 else mine
        if stage in (0, 4):
            targets = [{CORE: other}]
        else:
            ax = stage - 1
            targets = [{AX[ax]: rot(me[ax], d)} for d in DIRECT]
        for k, target in enumerate(targets):
            pltpu.make_async_remote_copy(
                src_ref=source, dst_ref=vecs.at[bases[stage] + k],
                send_sem=send.at[stage], recv_sem=recv.at[stage], device_id=target, device_id_type=MESH).start()

    def end(stage):
        with jax.named_scope("vector"):
            part = vecs.at[pl.ds(bases[stage], 3)] if stage in (1, 2, 3) else vecs.at[pl.ds(0, 1)]
            arrived(part, recv.at[stage])
            arrived(part, send.at[stage])
            if stage < 4:
                total = mine[...]
                for k in range(3 if stage else 1):
                    total = total + vecs[bases[stage] + k]
                mine[...] = total
            else:
                theirs[...] = vecs[10]

    return start, end


def suffix_state(after, p, j, late_ref, c):
    body, row = after[p, 2 * j : 2 * j + 2, 0:32].reshape(64, 128), after[p, 0, 32 + j : 33 + j]
    if c == 0:
        h = 2 * p + j
        body, row = body + late_ref[h, 0:64], row + (late_ref[h, 64:65] + late_ref[h, 65:66])
    first = lax.broadcasted_iota(jnp.int32, (64, 128), 0) == 0
    return jnp.concatenate([body, jnp.where(first, jnp.broadcast_to(row, (64, 128)), 0.0)], axis=0)


def attend_back_query(p, act, bufu, early_ref, before, trigs, grads):
    causal, _ = causal_masks()
    left = left_lanes(CHUNK)
    for c in range(2):
        rows = slice(CHUNK * c, CHUNK * c + CHUNK)
        query = []
        for j in range(2):
            h = 2 * p + j
            k = bufu[rows, at(HEADS + h, 128)]
            v, g = act[rows, at(h, 128)], act[rows, at(HEADS + h, 128)]
            high, low = halves(prefix_state(before, p, j, early_ref, c))
            weight = jnp.where(causal, nt(g, v), 0.0).astype(BF16)
            gq = nn(weight, k) + nn(doubled(g), jnp.concatenate([high, low], axis=0))
            gq = gq * trigs[0, rows]
            query.append(gq + swap_halves(gq))
        gate = bufu[ROWS:WIDTH, at(PAIRS * c + p, 128)].astype(F32)
        grads[rows, at(p, 128)] = (jnp.where(left, query[0], query[1]) * gate).astype(BF16)


def attend_back_local(p, act, bufu, trigs, key_ref, value_ref):
    _, flipped = causal_masks()
    left = left_lanes(CHUNK)
    cols = at(p, 128)
    for c in range(2):
        rows = slice(CHUNK * c, CHUNK * c + CHUNK)
        keys, value = [], []
        for j in range(2):
            h = 2 * p + j
            q, k = bufu[rows, at(h, 128)], bufu[rows, at(HEADS + h, 128)]
            v, g = act[rows, at(h, 128)], act[rows, at(HEADS + h, 128)]
            gk = nn(jnp.where(flipped, nt(v, g), 0.0).astype(BF16), q) * trigs[1, rows]
            keys.append(gk + swap_halves(gk))
            value.append(nn(jnp.where(flipped, nt(k, q), 0.0).astype(BF16), g))
        key_ref[rows, cols] = jnp.where(left, keys[0], keys[1])
        value_ref[rows, cols] = jnp.where(left, value[0], swap_halves(value[1]))


def attend_back_later(p, act, bufu, late_ref, after, trigs, ratio_ref, inverse_ref, grads):
    left = left_lanes(CHUNK)
    for c in range(2):
        rows = slice(CHUNK * c, CHUNK * c + CHUNK)
        keys, value = [], []
        for j in range(2):
            h = 2 * p + j
            k, v = bufu[rows, at(HEADS + h, 128)], act[rows, at(h, 128)]
            high, low = halves(suffix_state(after, p, j, late_ref, c))
            gk = nn(doubled(v), jnp.concatenate([high, low], axis=0)) * trigs[1, rows]
            keys.append(gk + swap_halves(gk))
            value.append(nt(doubled(k), jnp.concatenate([high, low], axis=1)))
        cols = at(p, 128)
        gate = bufu[ROWS:WIDTH, at(2 * PAIRS + PAIRS * c + p, 128)].astype(F32)
        gk = (ratio_ref[rows, cols] + jnp.where(left, keys[0], keys[1])) * gate
        grads[rows, at(PAIRS + p, 128)] = gk.astype(BF16)
        gv = inverse_ref[rows, cols] + jnp.where(left, value[0], swap_halves(value[1]))
        grads[rows, at(2 * PAIRS + p, 128)] = gv.astype(BF16)


def layer_kernel(len_ref, bq_in, bk_in, bv_in, bo_in, gain1_in, shift1_in, bdown_in, gain2_in, shift2_in, bup_in,
                 x_hbm, wq_hbm, wk_hbm, wv_hbm, wo_hbm, wup_hbm, wdown_hbm, cot_hbm,
                 block_out, tokens_out, done_out, vec_out, act_spill, slope_spill,
                 x_ref, act, slope, bufu, bufd, trigs, early_ref, late_ref, state, before, pay, after,
                 ratio_ref, inverse_ref, normal_ref, acc_ref, scale_ref, mixed_ref, normed_ref, gffn_ref, vec_ref, rows_ref,
                 bup, turned, stage, sums, first_in, second_in, third_in, final_ref, vecs,
                 load_sem, core_send, core_recv, send, recv, keep_sem, spread_recv, spread_send, third_recv, vec_send, vec_recv, free_sem, open_sem, *scratch):
    everywhere = ("seq_0", "seq_1", "batch")
    loads = {}

    def load(name, src, dst):
        copy = pltpu.make_async_copy(src, dst, load_sem.at[len(loads)])
        copy.start()
        loads[name] = copy

    def load_shared(k, src, dst):
        pltpu.make_async_copy(src, dst, load_sem.at[k]).start()

    def ready(*names):
        with jax.named_scope("ready"):
            for name in names:
                loads[name].wait()

    def note(k, value):
        vec_ref[k : k + 1, :] += value

    load("x", x_hbm, x_ref)
    for n in range(3):
        cols = pl.ds(256 * n, 256)
        load(f"wv{n}", wv_hbm.at[:, cols], bufd.at[2 * WIDTH : 3 * WIDTH, cols])
        load(f"wk{n}", wk_hbm.at[:, cols], bufd.at[WIDTH : 2 * WIDTH, cols])
    load("wq", wq_hbm, bufd.at[0:WIDTH])
    greet(everywhere)
    for k, vector in enumerate((bq_in, bk_in, bv_in, bo_in, gain1_in, shift1_in, bdown_in, gain2_in, shift2_in)):
        load(f"row {k}", vector, rows_ref.at[k])
    load("bup", bup_in, bup.at[0])
    bq, bk, bv, bo, gain1, shift1, bdown, gain2, shift2 = (rows_ref.at[k : k + 1] for k in range(9))
    vec_ref[...] = jnp.zeros_like(vec_ref)
    length = len_ref[...].reshape(1, 1)
    start = ROWS * ((lax.axis_index("seq_0") * 4 + lax.axis_index("seq_1")) * 2 + lax.axis_index(CORE))

    def angles(r):
        both, valid = trig_block(start + 128 * r, 128, length)
        trigs[0, at(r, 128)] = both
        trigs[1, at(r, 128)] = both * valid

    loop(ROWS // 128, angles)
    ready("x", "wv0", "wk0", *(f"row {k}" for k in range(9)), "bup")
    load("wup", wup_hbm, bufu)
    wo = bufd.at[3 * WIDTH : HIDDEN]
    load("wo", wo_hbm, wo)
    load("cot", cot_hbm, gffn_ref)
    earlier_sums = Exchange(exchange_steps, state, before, *scratch[: len(EXCHANGE_SCRATCH)])
    later_sums = Exchange(quarter_steps, pay, after, *scratch[len(EXCHANGE_SCRATCH) :])

    def keys(n):
        project_values(n, x_ref, bufd.at[2 * WIDTH : 3 * WIDTH], bv, slope)
        project_soft(n, x_ref, bufd.at[WIDTH : 2 * WIDTH], bk, trigs.at[1], act, HEADS, slope, 9)
        pl.when(n == 0)(lambda: greeted(everywhere))
        pl.when(n > 0)(lambda: earlier_sums.step(1, n - 1))
        for j in range(2):
            state_sums(2 * n + j, act, slope, state, early_ref)
        earlier_sums.step(0, n)

    def queries(n):
        project_soft(n, x_ref, bufd.at[0:WIDTH], bq, trigs.at[0], act, 0, slope, 6)
        pl.when(n == 0)(lambda: earlier_sums.step(1, 2))

    def own(n):
        pl.when(n == 2)(lambda: earlier_sums.step(2, 2))
        for j in range(2):
            attend_local(2 * n + j, act, slope, ratio_ref, inverse_ref)
        pl.when(n == 0)(lambda: earlier_sums.step(2, 1))

    def earlier(n):
        pl.when(n < 2)(lambda: earlier_sums.step(3, n + 1))
        earlier_sums.step(4, n)
        for j in range(2):
            attend_earlier(2 * n + j, act, early_ref, before, ratio_ref, inverse_ref, mixed_ref)

    loop(3, keys, {n: lambda n=n: ready(f"wv{n + 1}", f"wk{n + 1}") for n in range(2)})
    ready("wq")
    loop(3, queries)
    load("wdown", wdown_hbm.at[0 : 3 * WIDTH], bufd.at[0 : 3 * WIDTH])
    load("qk_out", act, act_spill)
    load("v_out", slope, slope_spill)
    earlier_sums.step(2, 0)
    loop(3, own)
    earlier_sums.step(3, 0)
    loop(3, earlier)
    ready("wo")

    def first_norm(r):
        rows = at(r, CHUNK)
        hidden = x_ref[rows].astype(F32) + (nn(mixed_ref[rows], wo[...]) + bo[...])
        normal, scale = standard(hidden)
        normal_ref[rows] = normal
        scale_ref[rows] = jnp.broadcast_to(scale, (CHUNK, 128))
        normed_ref[rows] = (normal * gain1[...] + shift1[...]).astype(BF16)

    loop(ROWS // CHUNK, first_norm)
    load("wdown end", wdown_hbm.at[3 * WIDTH : HIDDEN], wo)
    ready("qk_out", "v_out", "wup", "wdown")

    def feed(t):
        cols = at(t, FEED)
        for r in range(2):
            rows = slice(CHUNK * r, CHUNK * r + CHUNK)
            pre = nn(normed_ref[rows], bufu[:, cols]) + bup[:, cols]
            whole, bell = normal_parts(pre)
            active = (pre * whole).astype(BF16)
            act[rows, cols] = active
            slope[rows, cols] = (whole + pre * bell).astype(BF16)
            acc_ref[rows] = nn(active, bufd[cols]) + jnp.where(t == 0, 0.0, acc_ref[rows])

    loop(2, feed, {0: lambda: ready("wdown end")})
    ready("cot")

    def second_norm(r):
        rows = at(r, CHUNK)
        hidden = normed_ref[rows].astype(F32) + (acc_ref[rows] + bdown[...])
        normal, scale = standard(hidden)
        x_ref[rows] = (normal * gain2[...] + shift2[...]).astype(BF16)
        grad = gffn_ref[rows].astype(F32)
        note(7, column(grad * normal))
        note(8, column(grad))
        back = norm_back(grad, normal, scale, gain2[...])
        acc_ref[rows] = back
        low = back.astype(BF16)
        gffn_ref[rows] = low
        note(6, column(low.astype(F32)))

    loop(ROWS // CHUNK, second_norm)
    load("block", x_ref, block_out)
    red = Reduction(stage, sums, first_in, second_in, third_in, done_out, core_send, core_recv, send, recv, keep_sem,
                    spread_recv, spread_send, third_recv, final_ref)

    def down_rows(y):
        turned[...] = act[:, at(y, WIDTH)].T
        for n in range(3):
            value = nn(turned[...], gffn_ref[:, 256 * n : 256 * n + 256]).reshape(4, 2, 4, 24, 256)
            for half in range(2):
                unit = 2 * n + half
                for side in range(2):
                    stage[unit // 3, unit % 3, side, y] = value[:, side, :, :, 128 * half : 128 * half + 128]
        for s in range(3):
            red.swap(0, s, y).start()

    loop(4, down_rows)
    red.swaps(1)
    load("v", slope_spill.at[:, 0 : 128 * HEADS], act.at[:, 0 : 128 * HEADS])

    def feed_back(k):
        t = 1 - k
        cols = at(t, TILE)
        total = jnp.zeros((1, TILE), F32)
        for r in range(2):
            rows = slice(CHUNK * r, CHUNK * r + CHUNK)
            gpre = (nt(gffn_ref[rows], bufd[cols]) * slope[rows, cols].astype(F32)).astype(BF16)
            slope[rows, cols] = gpre
            total = total + column(gpre.astype(F32))
            acc_ref[rows] += nt(gpre, bufu[:, cols])
        for half in range(2):
            vec_ref[pl.ds(9 + 2 * t + half, 1), :] = total[:, WIDTH * half : WIDTH * half + WIDTH]

    loads["wo again"] = pltpu.make_async_copy(wo_hbm, wo, load_sem.at[34])

    def down_begun():
        red.each(red.begin, 0)
        loads["wo again"].start()

    loop(2, feed_back, {0: down_begun})
    red.each(red.follow, 0)
    red.each(red.begin, 1)
    ready("block")
    load("x again", x_hbm, x_ref)
    for k, w in enumerate((wq_hbm, wk_hbm, wv_hbm)):
        load_shared(35, w, bufd.at[WIDTH * k : WIDTH * k + WIDTH])
    load("qk", act_spill, bufu.at[0:ROWS])
    for i in range(2):
        for c in range(2):
            load_shared(36, slope_spill.at[CHUNK * c : CHUNK * c + CHUNK, pl.ds(128 * HEADS + WIDTH * i, WIDTH)],
                 bufu.at[ROWS:WIDTH, pl.ds(2 * WIDTH * i + WIDTH * c, WIDTH)])
    def up_columns(b):
        for n in range(3):
            cols = pl.ds(pl.multiple_of(WIDTH * b + 256 * n, 256), 256)
            value = nn(turned[...], slope[:, cols]).reshape(4, 4, 2, 24, 256)
            for half in range(2):
                unit = 2 * n + half
                for side in range(2):
                    stage[unit // 3, unit % 3, side, :, :, b] = value[:, :, side, :, 128 * half : 128 * half + 128]
        for s in range(3):
            red.swap(2, s, b).start()

    def first_back(r):
        rows = at(r, CHUNK)
        normal = normal_ref[rows]
        scale = scale_ref[rows, 0:1]
        grad = acc_ref[rows]
        note(4, column(grad * normal))
        note(5, column(grad))
        back = norm_back(grad, normal, scale, gain1[...])
        acc_ref[rows] = back
        low = back.astype(BF16)
        gffn_ref[rows] = low
        note(3, column(low.astype(F32)))
        normal_ref[rows] = nt(low, wo[...])

    def heads_back(p):
        cols = at(p, 128)
        lane = lax.broadcasted_iota(jnp.int32, (ROWS, 128), 1)
        left = lane < 64
        gnum = (normal_ref[:, cols] * inverse_ref[:, cols]).astype(BF16).astype(F32)
        product = gnum * ratio_ref[:, cols]
        ends_of = []
        for j in range(2):
            h = 2 * p + j
            mine = jnp.where(left, product, 0.0) if j == 0 else jnp.where(left, 0.0, product)
            gden = jnp.broadcast_to(-jnp.sum(mine, axis=1, keepdims=True), (ROWS, 128))
            high = gden.astype(BF16).astype(F32)
            ends = jnp.where(lane == 64, high, jnp.where(lane == 65, gden - high, 0.0))
            grad = jnp.where(left, gnum if j == 0 else swap_halves(gnum), ends).astype(BF16)
            act[:, at(HEADS + h, 128)] = grad
            late = tn(grad[CHUNK:ROWS], bufu[CHUNK:ROWS, at(h, 128)])
            late_ref[h] = late[0:72]
            both = late + tn(grad[0:CHUNK], bufu[0:CHUNK, at(h, 128)])
            for half in range(2):
                pay[p, 2 * j + half, 0:32] = both[32 * half : 32 * half + 32]
                pay[p, 2 * j + half, 32:40] = jnp.zeros((8, 128), F32)
            ends_of.append(both[64:65] + both[65:66])
        for j in range(2):
            pay[p, 0, 32 + j : 33 + j] = ends_of[j]

    def query_back(p):
        attend_back_query(p, act, bufu, early_ref, before, trigs, slope)

    def own_back(p):
        attend_back_local(p, act, bufu, trigs, ratio_ref, inverse_ref)

    def later(p):
        attend_back_later(p, act, bufu, late_ref, after, trigs, ratio_ref, inverse_ref, slope)

    def back(r):
        rows = at(r, CHUNK)
        total = acc_ref[rows]
        for i in range(3):
            total = total + nt(slope[rows, WIDTH * i : WIDTH * i + WIDTH], bufd[WIDTH * i : WIDTH * i + WIDTH])
        acc_ref[rows] = total

    def product(rhs, base, g, b0, n):
        with jax.named_scope("product"):
            value = nn(turned[...], rhs[:, at(base + n, 256)]).reshape(4, 4, 2, 24, 256)
            for part in range(2):
                unit = 2 * n + part
                half, s = unit // 3, lax.rem(unit, 3)
                for side in range(2):
                    stage[g % 2, s, side, :, :, b0 + half] = value[:, :, side, :, 128 * part : 128 * part + 128]
                red.swap(g, s, b0 + half).start()

    def free(k):
        red.cleared(k)
        pl.semaphore_signal(free_sem.at[k], inc=1, device_id={CORE: red.other}, device_id_type=MESH)

    def freed(k):
        with jax.named_scope("freed"):
            pl.semaphore_wait(free_sem.at[k], 1)

    def release(k):
        red.sent(k)
        for axis in everywhere:
            for d in DIRECT:
                pl.semaphore_signal(open_sem.at[k], inc=1, device_id={axis: rot(lax.axis_index(axis), d)},
                                    device_id_type=MESH)

    def released(k):
        with jax.named_scope("released"):
            pl.semaphore_wait(open_sem.at[k], 9)

    ready("wo again")
    loop(ROWS // CHUNK, first_back)
    red.each(red.relay, 0)
    red.each(red.follow, 1)
    each_of(3, lambda n: earlier_sums.step(5, n))
    ready("qk", "v")

    def heads_sent(n):
        for j in range(2):
            heads_back(2 * n + j)
        later_sums.step(0, n)
        pl.when(n > 0)(lambda: later_sums.step(1, n - 1))

    loop(3, heads_sent)
    turned[...] = normed_ref[...].T

    def up_first():
        later_sums.step(1, 2)
        red.each(red.relay, 1)

    loop(4, up_columns, {0: up_first, 2: lambda: red.each(red.middle, 0)})
    red.swaps(3)
    later_sums.step(2, 0)
    free(0)
    arrived(bufu.at[ROWS:WIDTH], load_sem.at[36])

    def query_two(n):
        query_back(2 * n)
        query_back(2 * n + 1)

    def query_second():
        later_sums.step(2, 1)
        red.each(red.begin, 2)

    def query_fourth():
        later_sums.step(2, 2)
        later_sums.step(6, 0)
        red.each(red.middle, 1)

    loop(3, query_two, {0: query_second, 1: query_fourth})
    red.each(red.begin, 3)
    red.each(red.follow, 2)
    later_sums.step(6, 1)
    red.each(red.last, 0)
    free(1)
    turned[...] = mixed_ref[...].T
    freed(0)
    loop(3, lambda n: product(gffn_ref, 0, 4, 0, n))
    later_sums.step(6, 2)
    ready("x again")
    turned[...] = x_ref[...].T
    loop(3, lambda n: product(slope, 0, 4, 2, n))

    def own_two(n):
        own_back(2 * n)
        own_back(2 * n + 1)

    def own_fourth():
        red.each(red.relay, 2)
        red.each(red.follow, 3)
        red.each(red.last, 1)

    loop(3, own_two, {1: own_fourth})
    red.each(red.relay, 3)
    red.each(red.spread, 0)
    release(0)
    each_of(3, lambda n: later_sums.step(3, n))
    freed(1)

    def keys_values(n):
        later_sums.step(4, n)
        for j in range(2):
            later(2 * n + j)
        each_of(2, lambda i: product(slope, 3 + 3 * i, 5, 2 * i, n))

    def keys_first():
        released(0)
        red.each(red.begin, 4)
        red.each(red.middle, 2)

    def keys_second():
        red.each(red.follow, 4)
        red.each(red.spread, 1)
        release(1)

    loop(3, keys_values, {0: keys_first, 1: keys_second})
    for i in range(3):
        note(i, column(slope[:, WIDTH * i : WIDTH * i + WIDTH].astype(F32)))
    vector_start, vector_end = vector_steps(vec_ref, vecs, vec_send, vec_recv)
    vector_start(0)
    released(1)
    red.each(red.begin, 5)
    vector_end(0)
    vector_start(1)
    arrived(bufd.at[0 : 3 * WIDTH], load_sem.at[35])

    def back_first():
        red.each(red.relay, 4)
        red.each(red.middle, 3)
        red.each(red.last, 2)

    loop(ROWS // CHUNK, back, {0: back_first})
    load("tokens", acc_ref, tokens_out)
    red.each(red.relay, 5)
    red.each(red.follow, 5)
    red.each(red.middle, 4)
    red.each(red.last, 3)
    vector_end(1)
    vector_start(2)
    red.each(red.middle, 5)
    red.each(red.spread, 2)
    red.each(red.last, 4)
    vector_end(2)
    vector_start(3)
    red.each(red.last, 5)
    red.each(red.spread, 3)
    red.each(red.spread, 4)
    red.each(red.spread, 5)
    vector_end(3)
    vector_start(4)
    vector_end(4)
    load("vec", vec_ref, vec_out)
    for g in range(6):
        red.each(red.finish, g)
        red.spread_sent(g)
    for g in range(2, 6):
        red.cleared(g)
        red.sent(g)
    each_of(3, lambda n: later_sums.step(5, n))
    ready("tokens", "vec")


def final_kernel(done, vecs, tokens, block, block_out, tokens_out, out_q, out_bq, out_k, out_bk, out_v, out_bv, out_o,
                 out_bo, out_g1, out_s1, out_up, out_bup, out_down, out_bdown, out_g2, out_s2):
    tokens_out[...] = tokens[...]
    block_out[...] = block[...]
    for s in range(3):
        for b in range(4):
            for half in range(2):
                at_col = 384 * half + 128 * s
                out_down[24 * b : 24 * b + 24, at_col : at_col + 128] = done[half, s, b]
                out_up[:, 768 * b + at_col : 768 * b + at_col + 128] = done[2 + half, s, b]
            cols = slice(384 * (b % 2) + 128 * s, 384 * (b % 2) + 128 * s + 128)
            (out_o, out_q)[b // 2][:, cols] = done[4, s, b]
            (out_k, out_v)[b // 2][:, cols] = done[5, s, b]
    seq = (lax.axis_index("seq_0") * 4 + lax.axis_index("seq_1")) * 2 + lax.axis_index(CORE)
    values = vecs[...]
    mine = pltpu.roll(values, lax.rem(WIDTH - 24 * seq, WIDTH), 1)
    for k, out in enumerate((out_bq, out_bk, out_bv, out_bo, out_g1, out_s1, out_bdown, out_g2, out_s2)):
        out[...] = mine[k, 0:24]
    spun = pltpu.roll(values, lax.rem(WIDTH - 96 * lax.rem(seq, 8), WIDTH), 1)
    row = lax.broadcasted_iota(jnp.int32, (16, WIDTH), 0)
    out_bup[...] = jnp.sum(jnp.where(row == 9 + seq // 8, spun, 0.0), axis=0)[0:96]


def on_device(tokens, lengths, w_query, b_query, w_key, b_key, w_value, b_value, w_out, b_out, gain_one, shift_one,
              w_up, b_up, w_down, b_down, gain_two, shift_two, cotangent):
    vmem = pl.BlockSpec(memory_space=VMEM)
    anywhere = pl.BlockSpec(memory_space=pl.ANY)
    out = jax.ShapeDtypeStruct
    wide16, wide32, long16 = ((ROWS, WIDTH), BF16), ((ROWS, WIDTH), F32), ((ROWS, HIDDEN), BF16)
    per_head, packed = ((HEADS, 72, 128), F32), ((PAIRS, 136, 128), F32)
    quarters = ((PAIRS, 4, 40, 128), F32)
    vector = ((16, WIDTH), F32)
    finished = ((6, 3, 4, 24, 128), F32)
    block, tokens_grad, done, sums, _, _ = pl.pallas_call(
        layer_kernel,
        out_shape=[out(*shape) for shape in (wide16, wide32, finished, vector, long16, long16)],
        in_specs=[vmem] + [anywhere] * 18,
        out_specs=[anywhere] * 6,
        scratch_shapes=[VMEM(*shape) for shape in (
            wide16, long16, long16, ((WIDTH, HIDDEN), BF16), ((HIDDEN, WIDTH), BF16),
            ((2, ROWS, 128), F32), per_head, per_head, packed, packed, quarters, quarters,
            wide32, wide32, wide32, wide32, ((ROWS, 128), F32), wide16, wide16, wide16, vector, vector,
            ((1, HIDDEN), F32), ((WIDTH, ROWS), BF16),
            ((2, 3, 2, 4, 4, 4, 24, 128), F32), ((4, 3, 4, 4, 4, 24, 128), F32), ((4, 3, 3, 4, 4, 24, 128), F32),
            ((4, 3, 3, 4, 24, 128), F32), ((4, 3, 3, 24, 128), F32), ((6, 3, 24, 128), F32), ((11, 8, WIDTH), F32))]
        + [pltpu.SemaphoreType.DMA((37,)), pltpu.SemaphoreType.DMA((4, 3)), pltpu.SemaphoreType.DMA((4, 3)),
           pltpu.SemaphoreType.DMA((4, 3)), pltpu.SemaphoreType.DMA((4, 3, 4)), pltpu.SemaphoreType.DMA((6,)), pltpu.SemaphoreType.DMA((6,)),
           pltpu.SemaphoreType.DMA((6,)), pltpu.SemaphoreType.DMA((4,)),
           pltpu.SemaphoreType.DMA((5,)), pltpu.SemaphoreType.DMA((5,)), pltpu.SemaphoreType.REGULAR((2,)), pltpu.SemaphoreType.REGULAR((2,))]
        + EXCHANGE_SCRATCH + QUARTER_SCRATCH,
        compiler_params=pltpu.CompilerParams(collective_id=1, has_side_effects=True, vmem_limit_bytes=LIMIT),
    )(lengths, b_query, b_key, b_value, b_out, gain_one, shift_one, b_down, gain_two, shift_two, b_up,
      tokens[0], w_query, w_key, w_value, w_out, w_up, w_down, cotangent[0])
    square_share, vector_share = out((24, WIDTH), F32), out((24,), F32)
    results = pl.pallas_call(
        final_kernel,
        out_shape=[out(*wide16), out(*wide32)] + [square_share, vector_share] * 4 + [vector_share] * 2
        + [out((24, HIDDEN), F32), out((96,), F32), out((96, WIDTH), F32)] + [vector_share] * 3,
        in_specs=[vmem] * 4,
        out_specs=[vmem] * 18,
        compiler_params=pltpu.CompilerParams(vmem_limit_bytes=LIMIT),
    )(done, sums, tokens_grad, block)
    return (results[0][None], results[1][None], *results[2:])


def solution(mesh):
    torus = Mesh(mesh.devices.reshape(4, 4, 2, mesh.shape["batch"]), (*SEQ, "batch"))
    rows, shares = P("batch", SEQ, None), P(SEQ, None)
    return jax.shard_map(
        on_device,
        mesh=torus,
        in_specs=(rows, P("batch")) + (P(),) * 16 + (rows,),
        out_specs=(rows, rows) + (shares, P(SEQ)) * 4 + (P(SEQ), P(SEQ)) + (shares, P(SEQ)) * 2 + (P(SEQ), P(SEQ)),
        check_vma=False,
    )
```

```python
import jax
import jax.numpy as jnp
from jax import lax
from jax.experimental import pallas as pl
from jax.experimental.pallas import tpu as pltpu
from jax.sharding import Mesh
from jax.sharding import PartitionSpec as P

SEQ = ("seq_0", "seq_1", "seq_2")
AX = ("seq_0", "seq_1", "batch")
CORE = "seq_2"
MESH = pl.DeviceIdType.MESH
DIRECT = (1, 3, 2)
F32 = jnp.float32
BF16 = jnp.bfloat16
HALF_PI = 1.5707963267948966
HALF_PI_REST = -4.371139000186241e-08
EPSILON = 1e-05
ROWS = 512
WIDTH = 768
HIDDEN = 3072
HEADS = 12
PAIRS = 6
CHUNK = 256
FEED = 1536
TILE = 1536
VMEM = pltpu.VMEM
LIMIT = 63 * 2**20


def loop(count, body, after=None):
    def step(k, carry):
        with jax.named_scope(body.__name__):
            body(k)
        for n, then in (after or {}).items():
            pl.when(k == n)(then)

    lax.fori_loop(0, count, step, None)


def each_of(count, body):
    lax.fori_loop(0, count, lambda k, carry: body(k), None)


def nn(a, b):
    return jnp.dot(a, b, preferred_element_type=F32)


def nt(a, b):
    return lax.dot_general(a, b, (((1,), (1,)), ((), ())), preferred_element_type=F32)


def tn(a, b):
    return lax.dot_general(a, b, (((0,), (0,)), ((), ())), preferred_element_type=F32)


def at(k, size):
    return pl.ds(pl.multiple_of(k * size, size), size)


def rot(k, d):
    return lax.rem(k + d, 4)


def left_lanes(rows):
    return lax.broadcasted_iota(jnp.int32, (rows, 128), 1) < 64


def swap_halves(value):
    return pltpu.roll(value, 64, 1)


def doubled(value):
    return jnp.concatenate([value, value], axis=1)


def halves(value):
    high = value.astype(BF16)
    return high, (value - high.astype(F32)).astype(BF16)


SIN = (1.0, -0.1666666716337204, 0.008333330973982811, -0.00019840864115394652, 2.7525297809916083e-06, -2.3888299338636898e-08)


def sine(x):
    square = x * x
    value = SIN[5]
    for c in SIN[4::-1]:
        value = value * square + c
    return value * x


def normal_parts(p):
    return 0.5 + 0.5 * lax.erf(p * 0.7071067811865476), 0.3989422804014327 * jnp.exp(-0.5 * p * p)


def trig_block(first, rows, length):
    position = first + lax.broadcasted_iota(jnp.int32, (rows, 128), 0)
    length = jnp.broadcast_to(length, (rows, 128))
    angle = HALF_PI * jnp.minimum(position + 1, length).astype(F32) / length.astype(F32)
    both = sine(jnp.where(left_lanes(rows), (HALF_PI - angle) + HALF_PI_REST, angle))
    return both, (position < length).astype(F32)


def project_values(n, x_ref, w, b, out):
    left = left_lanes(ROWS)
    u = (nn(x_ref[...], w[:, at(n, 256)]) + b[:, at(n, 256)]).astype(BF16).astype(F32)
    for j in range(2):
        part = u[:, 128 * j : 128 * j + 128]
        out[:, at(4 * n + 2 * j, 128)] = jnp.where(left, part, 1.0).astype(BF16)
        out[:, at(4 * n + 2 * j + 1, 128)] = jnp.where(left, swap_halves(part), 1.0).astype(BF16)


def project_soft(n, x_ref, w, b, table, out, first, gates, gate):
    left = left_lanes(ROWS)
    u = nn(x_ref[...], w[:, at(n, 256)]) + b[:, at(n, 256)]
    small = jnp.exp(-jnp.abs(u))
    soft = jnp.maximum(u, 0.0) + jnp.log1p(small)
    gates[:, at(gate + n, 256)] = (0.5 + 0.5 * jnp.tanh(0.5 * u)).astype(BF16)
    trig = table[...]
    for j in range(2):
        part = soft[:, 128 * j : 128 * j + 128]
        other = swap_halves(part)
        out[:, at(first + 4 * n + 2 * j, 128)] = (jnp.where(left, part, other) * trig).astype(BF16)
        out[:, at(first + 4 * n + 2 * j + 1, 128)] = (jnp.where(left, other, part) * trig).astype(BF16)


def state_sums(p, qk_ref, v_ref, state_ref, early_ref):
    for j in range(2):
        h = 2 * p + j
        keys, values = at(HEADS + h, 128), at(h, 128)
        early = tn(v_ref[0:CHUNK, values], qk_ref[0:CHUNK, keys])
        early_ref[h] = early[0:72]
        both = early + tn(v_ref[CHUNK:ROWS, values], qk_ref[CHUNK:ROWS, keys])
        state_ref[p, 64 * j : 64 * j + 64] = both[0:64]
        state_ref[p, 128 + j : 129 + j] = both[64:65]
    state_ref[p, 130:136] = jnp.zeros((6, 128), F32)


def exchange_steps(n, pay, out, core_in, chip, head, tail, total, msgs, xa, ya, yb, xb, send, recv):
    my, mx = lax.axis_index("seq_0"), lax.axis_index("seq_1")
    core = lax.axis_index(CORE)
    other = 1 - core
    own = 2 * n + core

    def remote(src, dst, stage, k, target):
        pltpu.make_async_remote_copy(
            src_ref=src, dst_ref=dst, send_sem=send.at[n, stage], recv_sem=recv.at[n, k],
            device_id=target, device_id_type=MESH).start()

    def counts(theirs, mine):
        return theirs < mine

    def chosen(flag, value):
        return jnp.where(flag, value, jnp.zeros_like(value))

    def first():
        remote(pay.at[2 * n + other], core_in.at[n], 0, 0, {CORE: other})

    def second():
        arrived(core_in.at[n], recv.at[n, 0])
        chip[n] = pay[own] + core_in[n]
        for k, d in enumerate(DIRECT):
            remote(chip.at[n, pl.ds(0, 72)], xa.at[n, k], 1, 1, {"seq_1": rot(mx, d)})
        for k, d in enumerate(DIRECT):
            remote(chip.at[n, pl.ds(72, 64)], yb.at[n, k], 1, 2, {"seq_0": rot(my, d)})

    def third():
        arrived(xa.at[n], recv.at[n, 1])
        some, every = jnp.zeros((72, 128), F32), chip[n, 0:72]
        for k, d in enumerate(DIRECT):
            some = some + chosen(counts(rot(mx, 4 - d), mx), xa[n, k])
            every = every + xa[n, k]
        head[n] = some
        total[n] = every
        for k, d in enumerate(DIRECT):
            remote(total.at[n], ya.at[n, k], 2, 3, {"seq_0": rot(my, d)})
        arrived(yb.at[n], recv.at[n, 2])
        some = jnp.zeros((64, 128), F32)
        for k, d in enumerate(DIRECT):
            some = some + chosen(counts(rot(my, 4 - d), my), yb[n, k])
        tail[n] = some
        for k, d in enumerate(DIRECT):
            msgs[n, k] = some + chosen(counts(mx, rot(mx, d)), chip[n, 72:136])
        for k, d in enumerate(DIRECT):
            remote(msgs.at[n, k], xb.at[n, k], 2, 4, {"seq_1": rot(mx, d)})

    def fourth():
        arrived(ya.at[n], recv.at[n, 3])
        arrived(xb.at[n], recv.at[n, 4])
        arrived(chip, send.at[n, 1])
        mine = core == 1
        low, high = head[n], tail[n]
        for k, d in enumerate(DIRECT):
            low = low + chosen(counts(rot(my, 4 - d), my), ya[n, k])
            high = high + xb[n, k]
        out[own, 0:72] = low + chosen(mine, core_in[n, 0:72])
        out[own, 72:136] = high + chosen(mine, core_in[n, 72:136])
        chip[n, 0:72] = low + chosen(jnp.logical_not(mine), pay[own, 0:72])
        chip[n, 72:136] = high + chosen(jnp.logical_not(mine), pay[own, 72:136])
        remote(chip.at[n], out.at[own], 3, 5, {CORE: other})

    def fifth():
        arrived(out.at[2 * n + other], recv.at[n, 5])

    def sent():
        arrived(core_in.at[n], send.at[n, 0])
        arrived(chip, send.at[n, 2])
        arrived(chip.at[n], send.at[n, 3])

    return first, second, third, fourth, fifth, sent


EXCHANGE_SCRATCH = [
    VMEM((3, 136, 128), F32),
    VMEM((3, 136, 128), F32),
    VMEM((3, 72, 128), F32),
    VMEM((3, 64, 128), F32),
    VMEM((3, 72, 128), F32),
    VMEM((3, 3, 64, 128), F32),
    VMEM((3, 3, 72, 128), F32),
    VMEM((3, 3, 72, 128), F32),
    VMEM((3, 3, 64, 128), F32),
    VMEM((3, 3, 64, 128), F32),
    pltpu.SemaphoreType.DMA((3, 4)),
    pltpu.SemaphoreType.DMA((3, 6)),
]


def quarter_steps(n, pay, out, core_in, chip, xa, total, ya, msgs, got, send, recv):
    my, mx = lax.axis_index("seq_0"), lax.axis_index("seq_1")
    core = lax.axis_index(CORE)
    other = 1 - core
    own = 2 * n + core

    def remote(src, dst, stage, k, target):
        pltpu.make_async_remote_copy(
            src_ref=src, dst_ref=dst, send_sem=send.at[n, stage], recv_sem=recv.at[n, k],
            device_id=target, device_id_type=MESH).start()

    def chosen(flag, value):
        return jnp.where(flag, value, jnp.zeros_like(value))

    def first():
        remote(pay.at[2 * n + other], core_in.at[n], 0, 0, {CORE: other})

    def second():
        arrived(core_in.at[n], recv.at[n, 0])
        chip[n] = pay[own] + core_in[n]
        for k, d in enumerate(DIRECT):
            remote(chip.at[n, rot(mx, d)], xa.at[n, k], 1, 1, {"seq_1": rot(mx, d)})

    def third():
        arrived(xa.at[n], recv.at[n, 1])
        total[n] = chip[n, mx] + xa[n, 0] + xa[n, 1] + xa[n, 2]
        for k, d in enumerate(DIRECT):
            remote(total.at[n], ya.at[n, k], 2, 2, {"seq_0": rot(my, d)})

    def cross():
        arrived(ya.at[n], recv.at[n, 2])
        behind = jnp.zeros((40, 128), F32)
        for k, d in enumerate(DIRECT):
            behind = behind + chosen(rot(my, 4 - d) > my, ya[n, k])

        def for_column(column):
            value = behind + chosen(mx > column, chip[n, mx])
            for k, d in enumerate(DIRECT):
                value = value + chosen(rot(mx, 4 - d) > column, xa[n, k])
            return value

        for k, d in enumerate(DIRECT):
            msgs[n, k] = for_column(rot(mx, d))
            remote(msgs.at[n, k], got.at[n, mx], 3, 3, {"seq_1": rot(mx, d)})
        got[n, mx] = for_column(mx)

    def fourth():
        arrived(xa.at[n], recv.at[n, 3])
        arrived(xa.at[n], send.at[n, 1])
        out[own] = got[n] + chosen(core == 0, core_in[n])
        chip[n] = got[n] + chosen(core == 1, pay[own])
        remote(chip.at[n], out.at[own], 4, 4, {CORE: other})

    def fifth():
        arrived(out.at[2 * n + other], recv.at[n, 4])

    def sent():
        arrived(chip.at[n], send.at[n, 0])
        arrived(xa.at[n], send.at[n, 2])
        arrived(xa.at[n], send.at[n, 3])
        arrived(chip.at[n], send.at[n, 4])

    return first, second, third, fourth, fifth, sent, cross


QUARTER_SCRATCH = [
    VMEM((3, 4, 40, 128), F32),
    VMEM((3, 4, 40, 128), F32),
    VMEM((3, 3, 40, 128), F32),
    VMEM((3, 40, 128), F32),
    VMEM((3, 3, 40, 128), F32),
    VMEM((3, 3, 40, 128), F32),
    VMEM((3, 4, 40, 128), F32),
    pltpu.SemaphoreType.DMA((3, 5)),
    pltpu.SemaphoreType.DMA((3, 5)),
]


class Exchange:
    def __init__(self, steps, *refs):
        self.steps = lambda n: steps(n, *refs)

    def step(self, k, n):
        with jax.named_scope(("swap", "begin", "turn", "end", "share", "sent", "cross")[k]):
            self.steps(n)[k]()


def greet(axes):
    barrier = pltpu.get_barrier_semaphore()
    core = lax.axis_index(CORE)
    pl.semaphore_signal(barrier, inc=1, device_id={CORE: 1 - core}, device_id_type=MESH)
    for axis in axes:
        mine = lax.axis_index(axis)
        for d in DIRECT:
            pl.semaphore_signal(barrier, inc=1, device_id={axis: rot(mine, d)}, device_id_type=MESH)


def greeted(axes):
    pl.semaphore_wait(pltpu.get_barrier_semaphore(), 1 + 3 * len(axes))


def causal_masks():
    row = lax.broadcasted_iota(jnp.int32, (CHUNK, CHUNK), 0)
    col = lax.broadcasted_iota(jnp.int32, (CHUNK, CHUNK), 1)
    return row >= col, row <= col


def prefix_state(before, p, j, early_ref, c):
    body, row = before[p, 64 * j : 64 * j + 64], before[p, 128 + j : 129 + j]
    if c == 1:
        body, row = body + early_ref[2 * p + j, 0:64], row + early_ref[2 * p + j, 64:65]
    return jnp.concatenate([body, jnp.broadcast_to(row, (64, 128))], axis=0)


def attend_local(p, qk_ref, v_ref, top_ref, under_ref):
    causal, _ = causal_masks()
    left = left_lanes(CHUNK)
    cols = at(p, 128)
    for c in range(2):
        rows = slice(CHUNK * c, CHUNK * c + CHUNK)
        sums = []
        for j in range(2):
            h = 2 * p + j
            weight = nt(qk_ref[rows, at(h, 128)], qk_ref[rows, at(HEADS + h, 128)])
            sums.append(nn(jnp.where(causal, weight, 0.0).astype(BF16), v_ref[rows, at(h, 128)]))
        even, odd = sums
        top_ref[rows, cols] = jnp.where(left, even, swap_halves(odd))
        under_ref[rows, cols] = jnp.where(left, swap_halves(even), odd)


def attend_earlier(p, qk_ref, early_ref, before, ratio_ref, inverse_ref, mixed_ref):
    left = left_lanes(CHUNK)
    cols = at(p, 128)
    for c in range(2):
        rows = slice(CHUNK * c, CHUNK * c + CHUNK)
        sums = []
        for j in range(2):
            h = 2 * p + j
            high, low = halves(prefix_state(before, p, j, early_ref, c))
            sums.append(nt(doubled(qk_ref[rows, at(h, 128)]), jnp.concatenate([high, low], axis=1)))
        even, odd = sums
        inverse = 1.0 / (inverse_ref[rows, cols] + jnp.where(left, swap_halves(even), odd))
        ratio = (ratio_ref[rows, cols] + jnp.where(left, even, swap_halves(odd))) * inverse
        ratio_ref[rows, cols] = ratio
        inverse_ref[rows, cols] = inverse
        mixed_ref[rows, cols] = ratio.astype(BF16)


def mean_rows(value):
    return jnp.mean(value, axis=-1, keepdims=True)


def standard(hidden):
    centred = hidden - mean_rows(hidden)
    scale = lax.rsqrt(mean_rows(centred * centred) + EPSILON)
    return centred * scale, scale


def norm_back(grad, normal, scale, gain):
    scaled = grad * gain
    return scale * (scaled - mean_rows(scaled) - normal * mean_rows(scaled * normal))


def column(value):
    return jnp.sum(value, axis=0, keepdims=True)


USUAL = ((1, 0, 2), (0, 2, 1), (2, 1, 0))
ORDERS = (USUAL, USUAL, (USUAL[0], USUAL[1], (2, 0, 1)), (USUAL[0], (0, 1, 2), USUAL[2]), USUAL, USUAL)
SUBS = 9
COLS = 256


def cell(ref, order, picks):
    at = [slice(None)] * 3
    for axis, pick in zip(order, picks):
        at[axis] = pick
    return ref.at[tuple(at)]


def rest(ref, order, pick):
    return ref.at[pick] if order[1] < order[2] else ref.at[:, pick]


def halved(ref, order, pick, half):
    at = [slice(None)] * 3
    at[order[0]] = pick
    at[1 if order[0] == 0 else 0] = half
    return ref.at[tuple(at)]


def add_blocks(dst, srcs, count, fresh=False):
    def step(k, carry):
        value = srcs[0][k] if fresh else dst[k] + srcs[0][k]
        for src in srcs[1:]:
            value = value + src[k]
        dst[k] = value

    lax.fori_loop(0, count, step, None)


SLOTS = (0, 1, 2, 3, 0, 1)


def arrived(ref, sem):
    pltpu.make_async_copy(ref, ref, sem).wait()


class Reduction:
    def __init__(self, stage, sums, first, second, third, done, core_send, core_recv, send, recv, keep,
                 spread_recv, spread_send, third_recv, final):
        self.stage, self.sums, self.first, self.second, self.third, self.done = stage, sums, first, second, third, done
        self.core_send, self.core_recv, self.send, self.recv, self.keep = core_send, core_recv, send, recv, keep
        self.spread_recv, self.spread_send, self.third_recv, self.final = spread_recv, spread_send, third_recv, final
        self.me = tuple(lax.axis_index(a) for a in AX)
        self.core = lax.axis_index(CORE)
        self.other = 1 - self.core

    def swap(self, g, s, part):
        where = (part,) if g < 2 else (slice(None), slice(None), part)
        return pltpu.make_async_remote_copy(
            src_ref=self.stage.at[(g % 2, s, self.other, *where)], dst_ref=self.sums.at[(SLOTS[g], s, *where)],
            send_sem=self.core_send.at[SLOTS[g], s], recv_sem=self.core_recv.at[SLOTS[g], s],
            device_id={CORE: self.other}, device_id_type=MESH)

    def swaps(self, g):
        for s in range(3):
            for part in range(4):
                self.swap(g, s, part).start()

    def remote(self, src, dst, g, s, stage, k, axis, d):
        pltpu.make_async_remote_copy(
            src_ref=src, dst_ref=dst, send_sem=self.send.at[SLOTS[g], stage] if k < 5 else self.spread_send.at[g],
            recv_sem=(self.recv.at[SLOTS[g], s, k] if k < 4 else
                      self.third_recv.at[SLOTS[g]] if k == 4 else self.spread_recv.at[g]),
            device_id={AX[axis]: rot(self.me[axis], d)}, device_id_type=MESH).start()

    def views(self, g, s):
        slot = SLOTS[g]
        return (self.sums.at[slot, s], self.first.at[slot, s], self.second.at[slot, s], self.third.at[slot, s],
                self.done.at[g, s], self.stage.at[g % 2, s, self.core], self.recv.at[slot, s])

    def begin(self, g, s):
        mine, inbox, _, _, _, own, _ = self.views(g, s)
        arrived(mine, self.core_recv.at[SLOTS[g], s])
        arrived(own, self.core_send.at[SLOTS[g], s])
        add_blocks(mine, [own], 4)
        order = ORDERS[g][s]
        ax = order[0]
        far = rot(self.me[ax], 2)
        lo, hi = pl.ds(0, 2), pl.ds(2, 2)
        self.remote(halved(mine, order, far, lo), inbox.at[0, lo], g, s, 0, 0, ax, 1)
        self.remote(halved(mine, order, far, hi), inbox.at[0, hi], g, s, 0, 1, ax, 3)

    def follow(self, g, s):
        mine, inbox = self.views(g, s)[:2]
        order = ORDERS[g][s]
        ax = order[0]
        i = self.me[ax]
        lo, hi = pl.ds(0, 2), pl.ds(2, 2)
        self.remote(halved(mine, order, rot(i, 1), hi), inbox.at[1, hi], g, s, 0, 2, ax, 1)
        self.remote(halved(mine, order, rot(i, 3), lo), inbox.at[2, lo], g, s, 0, 2, ax, 3)

    def relay(self, g, s):
        mine, inbox, _, _, _, _, recv = self.views(g, s)
        order = ORDERS[g][s]
        ax = order[0]
        i = self.me[ax]
        lo, hi = pl.ds(0, 2), pl.ds(2, 2)
        arrived(inbox.at[0, lo], recv.at[0])
        part = halved(mine, order, rot(i, 1), lo)
        add_blocks(part, [inbox.at[0, lo]], 2)
        self.remote(part, inbox.at[1, lo], g, s, 0, 2, ax, 1)
        arrived(inbox.at[0, hi], recv.at[1])
        part = halved(mine, order, rot(i, 3), hi)
        add_blocks(part, [inbox.at[0, hi]], 2)
        self.remote(part, inbox.at[2, hi], g, s, 0, 2, ax, 3)

    def middle(self, g, s):
        mine, inbox, second, _, _, _, recv = self.views(g, s)
        order = ORDERS[g][s]
        arrived(inbox.at[pl.ds(1, 2)], recv.at[2])
        i, ax = self.me[order[0]], order[1]
        add_blocks(inbox.at[0], [cell(mine, order, (i,)), inbox.at[1], inbox.at[2]], 4, fresh=True)
        for k, d in enumerate(DIRECT):
            self.remote(rest(inbox.at[0], order, rot(self.me[ax], d)), second.at[k], g, s, 1, 3, ax, d)

    def cleared(self, g):
        arrived(self.first.at[SLOTS[g]], self.send.at[SLOTS[g], 0])

    def last(self, g, s):
        _, inbox, second, third, _, _, recv = self.views(g, s)
        order = ORDERS[g][s]
        arrived(second, recv.at[3])
        mine = rest(inbox.at[0], order, self.me[order[1]])
        mine[...] = mine[...] + second[0] + second[1] + second[2]
        ax = order[2]
        for k, d in enumerate(DIRECT):
            self.remote(mine.at[rot(self.me[ax], d)], third.at[k], g, s, 2, 4, ax, d)

    def spread(self, g, s):
        _, inbox, _, third, done, _, recv = self.views(g, s)
        order = ORDERS[g][s]
        if s == 0:
            arrived(self.third.at[SLOTS[g]], self.third_recv.at[SLOTS[g]])
        part = rest(inbox.at[0], order, self.me[order[1]]).at[self.me[order[2]]]
        self.final[g, s] = part[...] + third[0] + third[1] + third[2]
        part = self.final.at[g, s]
        z = self.me[2]
        for k, d in enumerate(DIRECT):
            self.remote(part, done.at[z], g, s, 3, 5, 2, d)
        pltpu.make_async_copy(part, done.at[z], self.keep.at[g]).start()

    def finish(self, g, s):
        if s == 0:
            arrived(self.third.at[SLOTS[g]], self.spread_recv.at[g])

    def sent(self, g):
        slot = SLOTS[g]
        arrived(self.second.at[slot], self.send.at[slot, 1])
        arrived(self.third.at[slot], self.send.at[slot, 2])

    def spread_sent(self, g):
        arrived(self.final.at[g], self.keep.at[g])
        arrived(self.third.at[SLOTS[g]], self.spread_send.at[g])

    def each(self, step, g):
        with jax.named_scope(f"{step.__name__} {g}"):
            for s in range(3):
                step(g, s)


def vector_steps(vec, vecs, send, recv):
    me = tuple(lax.axis_index(a) for a in AX)
    core = lax.axis_index(CORE)
    other = 1 - core
    bases = (0, 1, 4, 7, 10)
    mine = vec.at[pl.ds(pl.multiple_of(8 * core, 8), 8)]
    theirs = vec.at[pl.ds(pl.multiple_of(8 * other, 8), 8)]

    def start(stage):
        source = theirs if stage == 0 else mine
        if stage in (0, 4):
            targets = [{CORE: other}]
        else:
            ax = stage - 1
            targets = [{AX[ax]: rot(me[ax], d)} for d in DIRECT]
        for k, target in enumerate(targets):
            pltpu.make_async_remote_copy(
                src_ref=source, dst_ref=vecs.at[bases[stage] + k],
                send_sem=send.at[stage], recv_sem=recv.at[stage], device_id=target, device_id_type=MESH).start()

    def end(stage):
        with jax.named_scope("vector"):
            part = vecs.at[pl.ds(bases[stage], 3)] if stage in (1, 2, 3) else vecs.at[pl.ds(0, 1)]
            arrived(part, recv.at[stage])
            arrived(part, send.at[stage])
            if stage < 4:
                total = mine[...]
                for k in range(3 if stage else 1):
                    total = total + vecs[bases[stage] + k]
                mine[...] = total
            else:
                theirs[...] = vecs[10]

    return start, end


def suffix_state(after, p, j, late_ref, c):
    body, row = after[p, 2 * j : 2 * j + 2, 0:32].reshape(64, 128), after[p, 0, 32 + j : 33 + j]
    if c == 0:
        h = 2 * p + j
        body, row = body + late_ref[h, 0:64], row + (late_ref[h, 64:65] + late_ref[h, 65:66])
    first = lax.broadcasted_iota(jnp.int32, (64, 128), 0) == 0
    return jnp.concatenate([body, jnp.where(first, jnp.broadcast_to(row, (64, 128)), 0.0)], axis=0)


def attend_back_query(p, act, bufu, early_ref, before, trigs, grads):
    causal, _ = causal_masks()
    left = left_lanes(CHUNK)
    for c in range(2):
        rows = slice(CHUNK * c, CHUNK * c + CHUNK)
        query = []
        for j in range(2):
            h = 2 * p + j
            k = bufu[rows, at(HEADS + h, 128)]
            v, g = act[rows, at(h, 128)], act[rows, at(HEADS + h, 128)]
            high, low = halves(prefix_state(before, p, j, early_ref, c))
            weight = jnp.where(causal, nt(g, v), 0.0).astype(BF16)
            gq = nn(weight, k) + nn(doubled(g), jnp.concatenate([high, low], axis=0))
            gq = gq * trigs[0, rows]
            query.append(gq + swap_halves(gq))
        gate = bufu[ROWS:WIDTH, at(PAIRS * c + p, 128)].astype(F32)
        grads[rows, at(p, 128)] = (jnp.where(left, query[0], query[1]) * gate).astype(BF16)


def attend_back_local(p, act, bufu, trigs, key_ref, value_ref):
    _, flipped = causal_masks()
    left = left_lanes(CHUNK)
    cols = at(p, 128)
    for c in range(2):
        rows = slice(CHUNK * c, CHUNK * c + CHUNK)
        keys, value = [], []
        for j in range(2):
            h = 2 * p + j
            q, k = bufu[rows, at(h, 128)], bufu[rows, at(HEADS + h, 128)]
            v, g = act[rows, at(h, 128)], act[rows, at(HEADS + h, 128)]
            gk = nn(jnp.where(flipped, nt(v, g), 0.0).astype(BF16), q) * trigs[1, rows]
            keys.append(gk + swap_halves(gk))
            value.append(nn(jnp.where(flipped, nt(k, q), 0.0).astype(BF16), g))
        key_ref[rows, cols] = jnp.where(left, keys[0], keys[1])
        value_ref[rows, cols] = jnp.where(left, value[0], swap_halves(value[1]))


def attend_back_later(p, act, bufu, late_ref, after, trigs, ratio_ref, inverse_ref, grads):
    left = left_lanes(CHUNK)
    for c in range(2):
        rows = slice(CHUNK * c, CHUNK * c + CHUNK)
        keys, value = [], []
        for j in range(2):
            h = 2 * p + j
            k, v = bufu[rows, at(HEADS + h, 128)], act[rows, at(h, 128)]
            high, low = halves(suffix_state(after, p, j, late_ref, c))
            gk = nn(doubled(v), jnp.concatenate([high, low], axis=0)) * trigs[1, rows]
            keys.append(gk + swap_halves(gk))
            value.append(nt(doubled(k), jnp.concatenate([high, low], axis=1)))
        cols = at(p, 128)
        gate = bufu[ROWS:WIDTH, at(2 * PAIRS + PAIRS * c + p, 128)].astype(F32)
        gk = (ratio_ref[rows, cols] + jnp.where(left, keys[0], keys[1])) * gate
        grads[rows, at(PAIRS + p, 128)] = gk.astype(BF16)
        gv = inverse_ref[rows, cols] + jnp.where(left, value[0], swap_halves(value[1]))
        grads[rows, at(2 * PAIRS + p, 128)] = gv.astype(BF16)


def layer_kernel(len_ref, bq_in, bk_in, bv_in, bo_in, gain1_in, shift1_in, bdown_in, gain2_in, shift2_in, bup_in,
                 x_hbm, wq_hbm, wk_hbm, wv_hbm, wo_hbm, wup_hbm, wdown_hbm, cot_hbm,
                 block_out, tokens_out, done_out, vec_out, act_spill, slope_spill,
                 x_ref, act, slope, bufu, bufd, trigs, early_ref, late_ref, state, before, pay, after,
                 ratio_ref, inverse_ref, normal_ref, acc_ref, scale_ref, mixed_ref, normed_ref, gffn_ref, vec_ref, rows_ref,
                 bup, turned, stage, sums, first_in, second_in, third_in, final_ref, vecs,
                 load_sem, core_send, core_recv, send, recv, keep_sem, spread_recv, spread_send, third_recv, vec_send, vec_recv, free_sem, open_sem, *scratch):
    everywhere = ("seq_0", "seq_1", "batch")
    loads = {}

    def load(name, src, dst):
        copy = pltpu.make_async_copy(src, dst, load_sem.at[len(loads)])
        copy.start()
        loads[name] = copy

    def load_shared(k, src, dst):
        pltpu.make_async_copy(src, dst, load_sem.at[k]).start()

    def ready(*names):
        with jax.named_scope("ready"):
            for name in names:
                loads[name].wait()

    def note(k, value):
        vec_ref[k : k + 1, :] += value

    load("x", x_hbm, x_ref)
    for n in range(3):
        cols = pl.ds(256 * n, 256)
        load(f"wv{n}", wv_hbm.at[:, cols], bufd.at[2 * WIDTH : 3 * WIDTH, cols])
        load(f"wk{n}", wk_hbm.at[:, cols], bufd.at[WIDTH : 2 * WIDTH, cols])
    load("wq", wq_hbm, bufd.at[0:WIDTH])
    greet(everywhere)
    for k, vector in enumerate((bq_in, bk_in, bv_in, bo_in, gain1_in, shift1_in, bdown_in, gain2_in, shift2_in)):
        load(f"row {k}", vector, rows_ref.at[k])
    load("bup", bup_in, bup.at[0])
    bq, bk, bv, bo, gain1, shift1, bdown, gain2, shift2 = (rows_ref.at[k : k + 1] for k in range(9))
    vec_ref[...] = jnp.zeros_like(vec_ref)
    length = len_ref[...].reshape(1, 1)
    start = ROWS * ((lax.axis_index("seq_0") * 4 + lax.axis_index("seq_1")) * 2 + lax.axis_index(CORE))

    def angles(r):
        both, valid = trig_block(start + 128 * r, 128, length)
        trigs[0, at(r, 128)] = both
        trigs[1, at(r, 128)] = both * valid

    loop(ROWS // 128, angles)
    ready("x", "wv0", "wk0", *(f"row {k}" for k in range(9)), "bup")
    load("wup", wup_hbm, bufu)
    wo = bufd.at[3 * WIDTH : HIDDEN]
    load("wo", wo_hbm, wo)
    load("cot", cot_hbm, gffn_ref)
    earlier_sums = Exchange(exchange_steps, state, before, *scratch[: len(EXCHANGE_SCRATCH)])
    later_sums = Exchange(quarter_steps, pay, after, *scratch[len(EXCHANGE_SCRATCH) :])

    def keys(n):
        project_values(n, x_ref, bufd.at[2 * WIDTH : 3 * WIDTH], bv, slope)
        project_soft(n, x_ref, bufd.at[WIDTH : 2 * WIDTH], bk, trigs.at[1], act, HEADS, slope, 9)
        pl.when(n == 0)(lambda: greeted(everywhere))
        pl.when(n > 0)(lambda: earlier_sums.step(1, n - 1))
        for j in range(2):
            state_sums(2 * n + j, act, slope, state, early_ref)
        earlier_sums.step(0, n)

    def queries(n):
        project_soft(n, x_ref, bufd.at[0:WIDTH], bq, trigs.at[0], act, 0, slope, 6)
        pl.when(n == 0)(lambda: earlier_sums.step(1, 2))

    def own(n):
        pl.when(n == 2)(lambda: earlier_sums.step(2, 2))
        for j in range(2):
            attend_local(2 * n + j, act, slope, ratio_ref, inverse_ref)
        pl.when(n == 0)(lambda: earlier_sums.step(2, 1))

    def earlier(n):
        pl.when(n < 2)(lambda: earlier_sums.step(3, n + 1))
        earlier_sums.step(4, n)
        for j in range(2):
            attend_earlier(2 * n + j, act, early_ref, before, ratio_ref, inverse_ref, mixed_ref)

    loop(3, keys, {n: lambda n=n: ready(f"wv{n + 1}", f"wk{n + 1}") for n in range(2)})
    ready("wq")
    loop(3, queries)
    load("wdown", wdown_hbm.at[0 : 3 * WIDTH], bufd.at[0 : 3 * WIDTH])
    load("qk_out", act, act_spill)
    load("v_out", slope, slope_spill)
    earlier_sums.step(2, 0)
    loop(3, own)
    earlier_sums.step(3, 0)
    loop(3, earlier)
    ready("wo")

    def first_norm(r):
        rows = at(r, CHUNK)
        hidden = x_ref[rows].astype(F32) + (nn(mixed_ref[rows], wo[...]) + bo[...])
        normal, scale = standard(hidden)
        normal_ref[rows] = normal
        scale_ref[rows] = jnp.broadcast_to(scale, (CHUNK, 128))
        normed_ref[rows] = (normal * gain1[...] + shift1[...]).astype(BF16)

    loop(ROWS // CHUNK, first_norm)
    load("wdown end", wdown_hbm.at[3 * WIDTH : HIDDEN], wo)
    ready("qk_out", "v_out", "wup", "wdown")

    def feed(t):
        cols = at(t, FEED)
        for r in range(2):
            rows = slice(CHUNK * r, CHUNK * r + CHUNK)
            pre = nn(normed_ref[rows], bufu[:, cols]) + bup[:, cols]
            whole, bell = normal_parts(pre)
            active = (pre * whole).astype(BF16)
            act[rows, cols] = active
            slope[rows, cols] = (whole + pre * bell).astype(BF16)
            acc_ref[rows] = nn(active, bufd[cols]) + jnp.where(t == 0, 0.0, acc_ref[rows])

    loop(2, feed, {0: lambda: ready("wdown end")})
    ready("cot")

    def second_norm(r):
        rows = at(r, CHUNK)
        hidden = normed_ref[rows].astype(F32) + (acc_ref[rows] + bdown[...])
        normal, scale = standard(hidden)
        x_ref[rows] = (normal * gain2[...] + shift2[...]).astype(BF16)
        grad = gffn_ref[rows].astype(F32)
        note(7, column(grad * normal))
        note(8, column(grad))
        back = norm_back(grad, normal, scale, gain2[...])
        acc_ref[rows] = back
        low = back.astype(BF16)
        gffn_ref[rows] = low
        note(6, column(low.astype(F32)))

    loop(ROWS // CHUNK, second_norm)
    load("block", x_ref, block_out)
    red = Reduction(stage, sums, first_in, second_in, third_in, done_out, core_send, core_recv, send, recv, keep_sem,
                    spread_recv, spread_send, third_recv, final_ref)

    def down_rows(y):
        turned[...] = act[:, at(y, WIDTH)].T
        for n in range(3):
            value = nn(turned[...], gffn_ref[:, 256 * n : 256 * n + 256]).reshape(4, 2, 4, 24, 256)
            for half in range(2):
                unit = 2 * n + half
                for side in range(2):
                    stage[unit // 3, unit % 3, side, y] = value[:, side, :, :, 128 * half : 128 * half + 128]
        for s in range(3):
            red.swap(0, s, y).start()

    loop(4, down_rows)
    red.swaps(1)
    load("v", slope_spill.at[:, 0 : 128 * HEADS], act.at[:, 0 : 128 * HEADS])

    def feed_back(k):
        t = 1 - k
        cols = at(t, TILE)
        total = jnp.zeros((1, TILE), F32)
        for r in range(2):
            rows = slice(CHUNK * r, CHUNK * r + CHUNK)
            gpre = (nt(gffn_ref[rows], bufd[cols]) * slope[rows, cols].astype(F32)).astype(BF16)
            slope[rows, cols] = gpre
            total = total + column(gpre.astype(F32))
            acc_ref[rows] += nt(gpre, bufu[:, cols])
        for half in range(2):
            vec_ref[pl.ds(9 + 2 * t + half, 1), :] = total[:, WIDTH * half : WIDTH * half + WIDTH]

    loads["wo again"] = pltpu.make_async_copy(wo_hbm, wo, load_sem.at[34])

    def down_begun():
        red.each(red.begin, 0)
        loads["wo again"].start()

    loop(2, feed_back, {0: down_begun})
    red.each(red.follow, 0)
    red.each(red.begin, 1)
    ready("block")
    load("qk", act_spill, bufu.at[0:ROWS])
    for i in range(2):
        for c in range(2):
            load_shared(36, slope_spill.at[CHUNK * c : CHUNK * c + CHUNK, pl.ds(128 * HEADS + WIDTH * i, WIDTH)],
                 bufu.at[ROWS:WIDTH, pl.ds(2 * WIDTH * i + WIDTH * c, WIDTH)])
    load("x again", x_hbm, x_ref)
    for k, w in enumerate((wq_hbm, wk_hbm, wv_hbm)):
        load_shared(35, w, bufd.at[WIDTH * k : WIDTH * k + WIDTH])

    def up_columns(b):
        for n in range(3):
            cols = pl.ds(pl.multiple_of(WIDTH * b + 256 * n, 256), 256)
            value = nn(turned[...], slope[:, cols]).reshape(4, 4, 2, 24, 256)
            for half in range(2):
                unit = 2 * n + half
                for side in range(2):
                    stage[unit // 3, unit % 3, side, :, :, b] = value[:, :, side, :, 128 * half : 128 * half + 128]
        for s in range(3):
            red.swap(2, s, b).start()

    def first_back(r):
        rows = at(r, CHUNK)
        normal = normal_ref[rows]
        scale = scale_ref[rows, 0:1]
        grad = acc_ref[rows]
        note(4, column(grad * normal))
        note(5, column(grad))
        back = norm_back(grad, normal, scale, gain1[...])
        acc_ref[rows] = back
        low = back.astype(BF16)
        gffn_ref[rows] = low
        note(3, column(low.astype(F32)))
        normal_ref[rows] = nt(low, wo[...])

    def heads_back(p):
        cols = at(p, 128)
        lane = lax.broadcasted_iota(jnp.int32, (ROWS, 128), 1)
        left = lane < 64
        gnum = (normal_ref[:, cols] * inverse_ref[:, cols]).astype(BF16).astype(F32)
        product = gnum * ratio_ref[:, cols]
        ends_of = []
        for j in range(2):
            h = 2 * p + j
            mine = jnp.where(left, product, 0.0) if j == 0 else jnp.where(left, 0.0, product)
            gden = jnp.broadcast_to(-jnp.sum(mine, axis=1, keepdims=True), (ROWS, 128))
            high = gden.astype(BF16).astype(F32)
            ends = jnp.where(lane == 64, high, jnp.where(lane == 65, gden - high, 0.0))
            grad = jnp.where(left, gnum if j == 0 else swap_halves(gnum), ends).astype(BF16)
            act[:, at(HEADS + h, 128)] = grad
            late = tn(grad[CHUNK:ROWS], bufu[CHUNK:ROWS, at(h, 128)])
            late_ref[h] = late[0:72]
            both = late + tn(grad[0:CHUNK], bufu[0:CHUNK, at(h, 128)])
            for half in range(2):
                pay[p, 2 * j + half, 0:32] = both[32 * half : 32 * half + 32]
                pay[p, 2 * j + half, 32:40] = jnp.zeros((8, 128), F32)
            ends_of.append(both[64:65] + both[65:66])
        for j in range(2):
            pay[p, 0, 32 + j : 33 + j] = ends_of[j]

    def query_back(p):
        attend_back_query(p, act, bufu, early_ref, before, trigs, slope)

    def own_back(p):
        attend_back_local(p, act, bufu, trigs, ratio_ref, inverse_ref)

    def later(p):
        attend_back_later(p, act, bufu, late_ref, after, trigs, ratio_ref, inverse_ref, slope)

    def back(r):
        rows = at(r, CHUNK)
        total = acc_ref[rows]
        for i in range(3):
            total = total + nt(slope[rows, WIDTH * i : WIDTH * i + WIDTH], bufd[WIDTH * i : WIDTH * i + WIDTH])
        acc_ref[rows] = total

    def product(rhs, base, g, b0, n):
        with jax.named_scope("product"):
            value = nn(turned[...], rhs[:, at(base + n, 256)]).reshape(4, 4, 2, 24, 256)
            for part in range(2):
                unit = 2 * n + part
                half, s = unit // 3, lax.rem(unit, 3)
                for side in range(2):
                    stage[g % 2, s, side, :, :, b0 + half] = value[:, :, side, :, 128 * part : 128 * part + 128]
                red.swap(g, s, b0 + half).start()

    def free(k):
        red.cleared(k)
        pl.semaphore_signal(free_sem.at[k], inc=1, device_id={CORE: red.other}, device_id_type=MESH)

    def freed(k):
        with jax.named_scope("freed"):
            pl.semaphore_wait(free_sem.at[k], 1)

    def release(k):
        red.sent(k)
        for axis in everywhere:
            for d in DIRECT:
                pl.semaphore_signal(open_sem.at[k], inc=1, device_id={axis: rot(lax.axis_index(axis), d)},
                                    device_id_type=MESH)

    def released(k):
        with jax.named_scope("released"):
            pl.semaphore_wait(open_sem.at[k], 9)

    ready("wo again")
    loop(ROWS // CHUNK, first_back)
    red.each(red.relay, 0)
    red.each(red.follow, 1)
    each_of(3, lambda n: earlier_sums.step(5, n))
    ready("qk", "v")

    def heads_sent(n):
        for j in range(2):
            heads_back(2 * n + j)
        later_sums.step(0, n)
        pl.when(n > 0)(lambda: later_sums.step(1, n - 1))

    loop(3, heads_sent)
    turned[...] = normed_ref[...].T

    def up_first():
        later_sums.step(1, 2)
        red.each(red.relay, 1)

    loop(4, up_columns, {0: up_first, 2: lambda: red.each(red.middle, 0)})
    red.swaps(3)
    free(0)
    arrived(bufu.at[ROWS:WIDTH], load_sem.at[36])

    def query_two(n):
        query_back(2 * n)
        query_back(2 * n + 1)

    def query_second():
        later_sums.step(2, 0)
        later_sums.step(2, 1)
        red.each(red.begin, 2)

    def query_fourth():
        later_sums.step(2, 2)
        red.each(red.middle, 1)

    loop(3, query_two, {0: query_second, 1: query_fourth})
    red.each(red.begin, 3)
    red.each(red.follow, 2)
    later_sums.step(6, 0)
    later_sums.step(6, 1)
    red.each(red.last, 0)
    free(1)
    turned[...] = mixed_ref[...].T
    freed(0)
    loop(3, lambda n: product(gffn_ref, 0, 4, 0, n))
    later_sums.step(6, 2)
    ready("x again")
    turned[...] = x_ref[...].T
    loop(3, lambda n: product(slope, 0, 4, 2, n))

    def own_two(n):
        own_back(2 * n)
        own_back(2 * n + 1)

    def own_fourth():
        red.each(red.relay, 2)
        red.each(red.follow, 3)
        red.each(red.last, 1)

    loop(3, own_two, {1: own_fourth})
    red.each(red.relay, 3)
    red.each(red.spread, 0)
    release(0)
    each_of(3, lambda n: later_sums.step(3, n))
    freed(1)

    def keys_values(n):
        later_sums.step(4, n)
        for j in range(2):
            later(2 * n + j)
        each_of(2, lambda i: product(slope, 3 + 3 * i, 5, 2 * i, n))

    def keys_first():
        released(0)
        red.each(red.begin, 4)
        red.each(red.middle, 2)

    def keys_second():
        red.each(red.follow, 4)
        red.each(red.spread, 1)
        release(1)

    loop(3, keys_values, {0: keys_first, 1: keys_second})
    for i in range(3):
        note(i, column(slope[:, WIDTH * i : WIDTH * i + WIDTH].astype(F32)))
    vector_start, vector_end = vector_steps(vec_ref, vecs, vec_send, vec_recv)
    vector_start(0)
    released(1)
    red.each(red.begin, 5)
    vector_end(0)
    vector_start(1)
    arrived(bufd.at[0 : 3 * WIDTH], load_sem.at[35])

    def back_first():
        red.each(red.relay, 4)
        red.each(red.middle, 3)
        red.each(red.last, 2)

    loop(ROWS // CHUNK, back, {0: back_first})
    load("tokens", acc_ref, tokens_out)
    red.each(red.relay, 5)
    red.each(red.follow, 5)
    red.each(red.middle, 4)
    red.each(red.last, 3)
    vector_end(1)
    vector_start(2)
    red.each(red.middle, 5)
    red.each(red.spread, 2)
    red.each(red.last, 4)
    vector_end(2)
    vector_start(3)
    red.each(red.last, 5)
    red.each(red.spread, 3)
    red.each(red.spread, 4)
    red.each(red.spread, 5)
    vector_end(3)
    vector_start(4)
    vector_end(4)
    load("vec", vec_ref, vec_out)
    for g in range(6):
        red.each(red.finish, g)
        red.spread_sent(g)
    for g in range(2, 6):
        red.cleared(g)
        red.sent(g)
    each_of(3, lambda n: later_sums.step(5, n))
    ready("tokens", "vec")


def final_kernel(done, vecs, tokens, block, block_out, tokens_out, out_q, out_bq, out_k, out_bk, out_v, out_bv, out_o,
                 out_bo, out_g1, out_s1, out_up, out_bup, out_down, out_bdown, out_g2, out_s2):
    tokens_out[...] = tokens[...]
    block_out[...] = block[...]
    for s in range(3):
        for b in range(4):
            for half in range(2):
                at_col = 384 * half + 128 * s
                out_down[24 * b : 24 * b + 24, at_col : at_col + 128] = done[half, s, b]
                out_up[:, 768 * b + at_col : 768 * b + at_col + 128] = done[2 + half, s, b]
            cols = slice(384 * (b % 2) + 128 * s, 384 * (b % 2) + 128 * s + 128)
            (out_o, out_q)[b // 2][:, cols] = done[4, s, b]
            (out_k, out_v)[b // 2][:, cols] = done[5, s, b]
    seq = (lax.axis_index("seq_0") * 4 + lax.axis_index("seq_1")) * 2 + lax.axis_index(CORE)
    values = vecs[...]
    mine = pltpu.roll(values, lax.rem(WIDTH - 24 * seq, WIDTH), 1)
    for k, out in enumerate((out_bq, out_bk, out_bv, out_bo, out_g1, out_s1, out_bdown, out_g2, out_s2)):
        out[...] = mine[k, 0:24]
    spun = pltpu.roll(values, lax.rem(WIDTH - 96 * lax.rem(seq, 8), WIDTH), 1)
    row = lax.broadcasted_iota(jnp.int32, (16, WIDTH), 0)
    out_bup[...] = jnp.sum(jnp.where(row == 9 + seq // 8, spun, 0.0), axis=0)[0:96]


def on_device(tokens, lengths, w_query, b_query, w_key, b_key, w_value, b_value, w_out, b_out, gain_one, shift_one,
              w_up, b_up, w_down, b_down, gain_two, shift_two, cotangent):
    vmem = pl.BlockSpec(memory_space=VMEM)
    anywhere = pl.BlockSpec(memory_space=pl.ANY)
    out = jax.ShapeDtypeStruct
    wide16, wide32, long16 = ((ROWS, WIDTH), BF16), ((ROWS, WIDTH), F32), ((ROWS, HIDDEN), BF16)
    per_head, packed = ((HEADS, 72, 128), F32), ((PAIRS, 136, 128), F32)
    quarters = ((PAIRS, 4, 40, 128), F32)
    vector = ((16, WIDTH), F32)
    finished = ((6, 3, 4, 24, 128), F32)
    block, tokens_grad, done, sums, _, _ = pl.pallas_call(
        layer_kernel,
        out_shape=[out(*shape) for shape in (wide16, wide32, finished, vector, long16, long16)],
        in_specs=[vmem] + [anywhere] * 18,
        out_specs=[anywhere] * 6,
        scratch_shapes=[VMEM(*shape) for shape in (
            wide16, long16, long16, ((WIDTH, HIDDEN), BF16), ((HIDDEN, WIDTH), BF16),
            ((2, ROWS, 128), F32), per_head, per_head, packed, packed, quarters, quarters,
            wide32, wide32, wide32, wide32, ((ROWS, 128), F32), wide16, wide16, wide16, vector, vector,
            ((1, HIDDEN), F32), ((WIDTH, ROWS), BF16),
            ((2, 3, 2, 4, 4, 4, 24, 128), F32), ((4, 3, 4, 4, 4, 24, 128), F32), ((4, 3, 3, 4, 4, 24, 128), F32),
            ((4, 3, 3, 4, 24, 128), F32), ((4, 3, 3, 24, 128), F32), ((6, 3, 24, 128), F32), ((11, 8, WIDTH), F32))]
        + [pltpu.SemaphoreType.DMA((37,)), pltpu.SemaphoreType.DMA((4, 3)), pltpu.SemaphoreType.DMA((4, 3)),
           pltpu.SemaphoreType.DMA((4, 3)), pltpu.SemaphoreType.DMA((4, 3, 4)), pltpu.SemaphoreType.DMA((6,)), pltpu.SemaphoreType.DMA((6,)),
           pltpu.SemaphoreType.DMA((6,)), pltpu.SemaphoreType.DMA((4,)),
           pltpu.SemaphoreType.DMA((5,)), pltpu.SemaphoreType.DMA((5,)), pltpu.SemaphoreType.REGULAR((2,)), pltpu.SemaphoreType.REGULAR((2,))]
        + EXCHANGE_SCRATCH + QUARTER_SCRATCH,
        compiler_params=pltpu.CompilerParams(collective_id=1, has_side_effects=True, vmem_limit_bytes=LIMIT),
    )(lengths, b_query, b_key, b_value, b_out, gain_one, shift_one, b_down, gain_two, shift_two, b_up,
      tokens[0], w_query, w_key, w_value, w_out, w_up, w_down, cotangent[0])
    square_share, vector_share = out((24, WIDTH), F32), out((24,), F32)
    results = pl.pallas_call(
        final_kernel,
        out_shape=[out(*wide16), out(*wide32)] + [square_share, vector_share] * 4 + [vector_share] * 2
        + [out((24, HIDDEN), F32), out((96,), F32), out((96, WIDTH), F32)] + [vector_share] * 3,
        in_specs=[vmem] * 4,
        out_specs=[vmem] * 18,
        compiler_params=pltpu.CompilerParams(vmem_limit_bytes=LIMIT),
    )(done, sums, tokens_grad, block)
    return (results[0][None], results[1][None], *results[2:])


def solution(mesh):
    torus = Mesh(mesh.devices.reshape(4, 4, 2, mesh.shape["batch"]), (*SEQ, "batch"))
    rows, shares = P("batch", SEQ, None), P(SEQ, None)
    return jax.shard_map(
        on_device,
        mesh=torus,
        in_specs=(rows, P("batch")) + (P(),) * 16 + (rows,),
        out_specs=(rows, rows) + (shares, P(SEQ)) * 4 + (P(SEQ), P(SEQ)) + (shares, P(SEQ)) * 2 + (P(SEQ), P(SEQ)),
        check_vma=False,
    )
```
